32 devices in a mesh: rows: 8 (over y, x, core), cp: 4 (over z).
Axes of the slice: x: 2, y: 2, z: 4, core: 2. Of those that a mesh axis runs over, the one named last changes fastest.
Arguments:
- tokens: bfloat16 [8, 2, 1024, 1024], P('rows', None, 'cp'), may hold values from -6 to 6
- doc_starts: int32 [8, 4], P('rows'), may hold values from 0 to 2047, as said below
- qkv_weight: bfloat16 [1024, 3072], P('rows', 'cp'), may hold values from -0.1875 to 0.1875
- out_weight: bfloat16 [1024, 1024], P('rows', 'cp'), may hold values from -0.1875 to 0.1875
- up_weight: bfloat16 [1024, 4096], P('rows', 'cp'), may hold values from -0.1875 to 0.1875
- down_weight: bfloat16 [4096, 1024], P('cp', 'rows'), may hold values from -0.09375 to 0.09375
- norm_gains: bfloat16 [4096], P(('rows', 'cp')), may hold values from 0.5 to 1.5
- cotangent: bfloat16 [8, 2, 1024, 1024], P('rows', None, 'cp'), may hold values from -6 to 6
Outputs:
- mixed: bfloat16 [8, 2, 1024, 1024], P('rows', None, 'cp')
- tokens_grad: float32 [8, 2, 1024, 1024], P('rows', None, 'cp')
- qkv_grad: float32 [1024, 3072], P('rows', 'cp')
- out_grad: float32 [1024, 1024], P('rows', 'cp')
- up_grad: float32 [1024, 4096], P('rows', 'cp')
- down_grad: float32 [4096, 1024], P('cp', 'rows')
- gains_grad: float32 [4096], P(('rows', 'cp'))
The draws below stay inside these ranges and needn't reach their ends.
Inputs may be any that keep to these rules, and one draw needn't show every extreme that they name: `doc_starts`: in each row the 4 document starts rise strictly and the first is 0; a position belongs to the document with the last start at or before it.
All inputs are finite; a program needn't handle non-finite values.
Results may differ from the reference program's by a relative error of at most 0.023.
Values may be sent and summed in bfloat16 or wider, within the bound.
No kernel may reach another device: no remote copies, remote signals or barrier semaphores. Data moves between devices by JAX's collectives and lax.ppermute only.
A program may use at most 640 MiB of HBM per device.

```python
import math
import jax
import jax.numpy as jnp
from jax import lax

D = 1024
HEADS = 16
HEAD_DIM = 64
FF = 4096
ROW_LEN = 2048
ROWS = 8
HALF = 1024
SPAN = 256


def shuffled(row_key):
    return jax.random.permutation(row_key, ROW_LEN)


def draw_doc_starts(key, part):
    key = jax.random.fold_in(key, 7)
    mode_key, early_key, end_key, late_key, tail_key, pick_key, order_key = jax.random.split(key, 7)
    mode = jax.random.randint(mode_key, (ROWS,), 0, 2)
    early_first = jax.random.randint(early_key, (ROWS,), 0, SPAN)
    early_end = jax.random.randint(end_key, (ROWS,), HALF, ROW_LEN - 2)
    late_first = jax.random.randint(late_key, (ROWS,), 3, HALF + SPAN)
    late_end = jax.random.randint(tail_key, (ROWS,), ROW_LEN - SPAN + 1, ROW_LEN + 1)
    single_row = jax.random.randint(pick_key, (), 0, ROWS)
    row_ids = jnp.arange(ROWS)
    is_single = row_ids == single_row
    first = jnp.where(is_single, 0, jnp.where(mode == 0, early_first, late_first))
    last = jnp.where(is_single, ROW_LEN - 3, jnp.where(mode == 0, early_end, late_end))
    positions = jnp.arange(ROW_LEN)[None, :]
    fixed = (positions == first[:, None]) & (first[:, None] > 0) | (positions == last[:, None])
    outside = (positions >= 1) & ((positions < first[:, None]) | (positions > last[:, None]))
    ranks = jax.vmap(shuffled)(jax.random.split(order_key, ROWS))
    priority = jnp.where(fixed, 2 * ROW_LEN + positions, jnp.where(outside, ranks, -1))
    _, chosen = lax.top_k(priority, 3)
    chosen = jnp.sort(chosen.astype(jnp.int32), axis=1)
    return jnp.concatenate([jnp.zeros((ROWS, 1), jnp.int32), chosen], axis=1).astype(jnp.int32)


def block_levels(own_key, extent, cuts, least, top_value):
    factor_of, own = 1.0, jax.random.fold_in(own_key, 6)
    for axis_at, shards_of in cuts:
        steps = jnp.exp(jax.random.uniform(jax.random.fold_in(own, axis_at), (shards_of,), jnp.float32, least / len(cuts), top_value / len(cuts)))
        factor_of = factor_of * jnp.repeat(steps, extent[axis_at] // shards_of).reshape([-1 if axis == axis_at else 1 for axis in range(len(extent))])
    return factor_of


def scatter_about(own_key, dims, width, bound, cuts=(), kind=jnp.bfloat16):
    loudness = block_levels(own_key, dims, cuts, -0.22, 0.18) if cuts else 1.0
    entries = jax.random.normal(own_key, dims, jnp.float32) * width * loudness
    return jnp.minimum(jnp.maximum(entries, -bound), bound).astype(kind)


def setup_inputs(seed: int = 0) -> dict:
    key_list = jax.random.split(jax.random.key(seed), 9)
    return {
        "tokens": scatter_about(key_list[0], (ROWS, 2, HALF, D), 1.0, 6.0, ((0, 8), (2, 4))),
        "doc_starts": draw_doc_starts(jax.random.fold_in(key_list[8], 71), 0),
        "qkv_weight": scatter_about(key_list[2], (D, 3 * D), D ** -0.5, 0.1875, ((0, 8), (1, 4))),
        "out_weight": scatter_about(key_list[3], (D, D), D ** -0.5, 0.1875, ((0, 8), (1, 4))),
        "up_weight": scatter_about(key_list[4], (D, FF), D ** -0.5, 0.1875, ((0, 8), (1, 4))),
        "down_weight": scatter_about(key_list[5], (FF, D), FF ** -0.5, 0.09375, ((0, 4), (1, 8))),
        "norm_gains": jnp.clip(1.0 + 0.1 * jax.random.normal(key_list[6], (4 * D,), jnp.float32), 0.5, 1.5).astype(jnp.bfloat16),
        "cotangent": scatter_about(key_list[7], (ROWS, 2, HALF, D), 1.0, 6.0, ((0, 8), (2, 4))),
    }


@jax.custom_vjp
def low(v):
    return lax.optimization_barrier(v.astype(jnp.bfloat16)).astype(jnp.float32)

@jax.custom_vjp
def low_back(v):
    return v

def low_keep(v):
    return (low(v), None)

def low_pass(kept, grad):
    return (grad,)

def back_keep(v):
    return (v, None)

def back_low(kept, grad):
    return (low(grad),)
low.defvjp(low_keep, low_pass)
low_back.defvjp(back_keep, back_low)

def layer_norm(values):
    average = lax.optimization_barrier(jnp.mean(values, axis=-1, keepdims=True))
    centred = values - average
    spread = lax.optimization_barrier(jnp.mean(centred * centred, axis=-1, keepdims=True))
    return centred * lax.rsqrt(spread + 1e-05)

def matmul(left, right):
    return jnp.dot(left, right, precision=lax.Precision.HIGHEST)

def rotate(values, cosine, sine_part):
    half_width = values.shape[-1] // 2
    first_half = values[..., :half_width]
    second_half = values[..., half_width:]
    return jnp.concatenate([first_half * cosine - second_half * sine_part, second_half * cosine + first_half * sine_part], axis=-1)

def layer_row(token_row, starts, qkv_w, out_w, up_w, down_w, gains):
    length = token_row.shape[0]
    gain_rows = gains.reshape(4, D)
    positions = jnp.arange(length, dtype=jnp.int32)
    start_of = lax.optimization_barrier(jnp.max(jnp.where(starts[None, :] <= positions[:, None], starts[None, :], 0), axis=1)).astype(jnp.int32)
    freq_index = jnp.arange(HEAD_DIM // 2, dtype=jnp.float32)
    inverse_freq = jnp.exp(-math.log(10000.0) * 2.0 * freq_index / HEAD_DIM)
    angles = (positions - start_of).astype(jnp.float32)[:, None] * inverse_freq[None, :]
    cosine = jnp.cos(angles)[:, None, :]
    sine_part = jnp.sin(angles)[:, None, :]
    normed = low(layer_norm(token_row) * gain_rows[0])
    linear = low_back(matmul(normed, qkv_w))
    head_shape = (length, HEADS, HEAD_DIM)
    query_rows = low_back(low(rotate(linear[:, :D].reshape(head_shape), cosine, sine_part)))
    key_rows = low_back(low(rotate(linear[:, D:2 * D].reshape(head_shape), cosine, sine_part)))
    value_rows = low_back(low(linear[:, 2 * D:].reshape(head_shape)))
    block_size = min(512, length)
    block_count = length // block_size
    score_scale = HEAD_DIM ** (-0.5)

    def attend(block_item):
        query_block, query_pos, query_start = block_item
        raw_scores = low_back(jnp.einsum('qhd,khd->hqk', query_block, key_rows, precision=lax.Precision.HIGHEST))
        allowed = (query_start[:, None] == start_of[None, :]) & (positions[None, :] <= query_pos[:, None])
        scores = jnp.where(allowed[None], raw_scores * score_scale, -1e+30)
        probs = low(jax.nn.softmax(scores, axis=-1))
        return jnp.einsum('hqk,khd->qhd', probs, value_rows, precision=lax.Precision.HIGHEST)
    attended = lax.map(jax.checkpoint(attend), (query_rows.reshape(block_count, block_size, HEADS, HEAD_DIM), positions.reshape(block_count, block_size), start_of.reshape(block_count, block_size)))
    mixed_heads = low_back(low(attended.reshape(length, D)))
    branch = low_back(matmul(mixed_heads, out_w))
    hidden = token_row + layer_norm(branch) * gain_rows[1]
    normed_mid = low(layer_norm(hidden) * gain_rows[2])
    up_proj = low_back(matmul(normed_mid, up_w))
    activation = low(jax.nn.gelu(up_proj, approximate=True))
    down_proj = low_back(matmul(activation, down_w))
    return hidden + layer_norm(down_proj) * gain_rows[3]

def natural(values):
    return jnp.concatenate([values[:, 0], values[:, 1, ::-1]], axis=1)

def folded(values):
    half_len = values.shape[1] // 2
    return jnp.stack([values[:, :half_len], values[:, half_len:][:, ::-1]], axis=1)

def reference(tokens, doc_starts, qkv_weight, out_weight, up_weight, down_weight, norm_gains, cotangent):
    params = (qkv_weight.astype(jnp.float32), out_weight.astype(jnp.float32), up_weight.astype(jnp.float32), down_weight.astype(jnp.float32), norm_gains.astype(jnp.float32))
    token_rows = natural(tokens.astype(jnp.float32))
    cotan_rows = natural(cotangent.astype(jnp.float32))

    def row_step(totals, row_item):
        token_row, cotan_row, starts = row_item

        def forward(row_in, qkv_w, out_w, up_w, down_w, gains):
            return layer_row(row_in, starts, qkv_w, out_w, up_w, down_w, gains)
        result, pull_back = jax.vjp(forward, token_row, params[0], params[1], params[2], params[3], params[4])
        gradients = pull_back(cotan_row)
        totals = tuple((running + grad_part for running, grad_part in zip(totals, gradients[1:])))
        return (totals, (result, gradients[0]))
    zeros_init = tuple((jnp.zeros_like(param_item) for param_item in params))
    totals, (results, input_grads) = lax.scan(row_step, zeros_init, (token_rows, cotan_rows, doc_starts))
    return (folded(results).astype(jnp.bfloat16), folded(input_grads), totals[0], totals[1], totals[2], totals[3], totals[4])
```

```python
import functools
import math

import jax
import jax.numpy as jnp
from jax import lax
from jax.experimental import pallas as pl
from jax.experimental.pallas import tpu as pltpu
from jax.sharding import Mesh, PartitionSpec as P

HEADS = 16
HEAD_DIM = 64


NORM_EPS = 1e-05
MASKED = -1e30


def layer_norm(values):
    average = jnp.mean(values, axis=-1, keepdims=True)
    centred = values - average
    spread = jnp.mean(centred * centred, axis=-1, keepdims=True)
    return centred * lax.rsqrt(spread + NORM_EPS)


def norm_back(values, upstream):
    _, pull_back = jax.vjp(layer_norm, values)
    return pull_back(upstream)[0]


def gelu_tanh(values):
    return jax.nn.gelu(values, approximate=True)


def rotate(values, cosine, sine_part):
    half_width = values.shape[-1] // 2
    first_half = values[..., :half_width]
    second_half = values[..., half_width:]
    return jnp.concatenate(
        [
            first_half * cosine - second_half * sine_part,
            second_half * cosine + first_half * sine_part,
        ],
        axis=-1,
    )


def rounded(values):
    return lax.optimization_barrier(values.astype(jnp.bfloat16)).astype(jnp.float32)


def doc_start_of(starts, positions):
    return jnp.max(
        jnp.where(starts[:, None, :] <= positions[None, :, None], starts[:, None, :], 0), axis=-1
    )


def general_body(tokens, doc_starts, qkv_weight, out_weight, up_weight, down_weight, norm_gains, cotangent):
    rows_count = lax.axis_size("rows")
    cp_count = lax.axis_size("cp")
    qkv_rows, out_rows, up_rows, down_rows, gain_piece = (
        lax.all_gather(qkv_weight, "rows", axis=0, tiled=True),
        lax.all_gather(out_weight, "rows", axis=0, tiled=True),
        lax.all_gather(up_weight, "rows", axis=0, tiled=True),
        lax.all_gather(down_weight, "rows", axis=1, tiled=True),
        lax.all_gather(norm_gains, "rows", axis=0, tiled=True),
    )
    qkv_full, out_full, gain_mixed = (
        lax.all_gather(qkv_rows, "cp", axis=1, tiled=True),
        lax.all_gather(out_rows, "cp", axis=1, tiled=True),
        lax.all_gather(gain_piece, "cp", axis=0, tiled=True),
    )
    gain_full = jnp.transpose(gain_mixed.reshape(cp_count, rows_count, -1), (1, 0, 2)).reshape(-1)
    row_count, _, span_len, width = tokens.shape
    half_len = span_len * cp_count
    row_len = 2 * half_len
    queries_dev = 2 * span_len
    token_total = row_count * queries_dev
    group_total = row_count * row_len
    gain_rows = gain_full.astype(jnp.float32).reshape(4, width)
    score_scale = HEAD_DIM ** (-0.5)
    local_pos = lax.axis_index("cp") * span_len + jnp.arange(span_len, dtype=jnp.int32)
    query_pos = jnp.concatenate([local_pos, row_len - 1 - local_pos])
    half_pos = jnp.arange(half_len, dtype=jnp.int32)
    key_pos = jnp.concatenate([half_pos, row_len - 1 - half_pos])
    query_start = doc_start_of(doc_starts, query_pos)
    key_start = doc_start_of(doc_starts, key_pos)
    freq_index = jnp.arange(HEAD_DIM // 2, dtype=jnp.float32)
    inverse_freq = jnp.exp(-math.log(10000.0) * 2.0 * freq_index / HEAD_DIM)
    angles = (query_pos[None, :] - query_start).astype(jnp.float32)[..., None] * inverse_freq
    cosine = jnp.cos(angles)[:, :, None, :]
    sine_part = jnp.sin(angles)[:, :, None, :]
    head_shape = (row_count, queries_dev, HEADS, HEAD_DIM)
    flat_shape = (row_count, queries_dev, width)
    fold_shape = (row_count, 2, span_len, width)
    group_shape = (row_count, 2, half_len, width)
    full_shape = (row_count, row_len, HEADS, HEAD_DIM)
    inputs = tokens.astype(jnp.float32).reshape(flat_shape)
    normed_in = layer_norm(inputs)
    normed = (normed_in * gain_rows[0]).astype(jnp.bfloat16)
    linear = jnp.dot(normed, qkv_full, preferred_element_type=jnp.float32)
    query_rows = rotate(linear[..., :width].reshape(head_shape), cosine, sine_part).astype(
        jnp.bfloat16
    )
    key_local = rotate(
        linear[..., width : 2 * width].reshape(head_shape), cosine, sine_part
    ).astype(jnp.bfloat16)
    value_local = linear[..., 2 * width :].reshape(head_shape).astype(jnp.bfloat16)
    key_sent, value_sent = (
        lax.all_gather(key_local.reshape(fold_shape), "cp", axis=2, tiled=True),
        lax.all_gather(value_local.reshape(fold_shape), "cp", axis=2, tiled=True),
    )
    key_rows = key_sent.reshape(full_shape)
    value_rows = value_sent.reshape(full_shape)
    block_size = min(512, row_len)
    block_count = row_len // block_size
    block_range = jnp.arange(block_count)

    def block_scores(block_index):
        first_key = block_index * block_size
        key_block = lax.dynamic_slice_in_dim(key_rows, first_key, block_size, 1)
        pos_block = lax.dynamic_slice_in_dim(key_pos, first_key, block_size, 0)
        start_block = lax.dynamic_slice_in_dim(key_start, first_key, block_size, 1)
        raw_scores = jnp.einsum(
            "rqhd,rkhd->rhqk", query_rows, key_block, preferred_element_type=jnp.float32
        )
        allowed = (query_start[:, None, :, None] == start_block[:, None, None, :]) & (
            pos_block[None, None, None, :] <= query_pos[None, None, :, None]
        )
        return (raw_scores * score_scale, allowed)

    def max_step(carry, block_index):
        running_max, running_sum = carry
        scores, allowed = block_scores(block_index)
        scores = jnp.where(allowed, scores, MASKED)
        new_max = jnp.maximum(running_max, jnp.max(scores, axis=-1))
        running_sum = running_sum * jnp.exp(running_max - new_max) + jnp.sum(
            jnp.where(allowed, jnp.exp(scores - new_max[..., None]), 0.0), axis=-1
        )
        return ((new_max, running_sum), None)

    stat_shape = (row_count, HEADS, queries_dev)
    (running_max, running_sum), _ = lax.scan(
        max_step,
        (jnp.full(stat_shape, MASKED, jnp.float32), jnp.zeros(stat_shape, jnp.float32)),
        block_range,
    )
    log_total = running_max + jnp.log(running_sum)

    def value_step(totals, block_index):
        scores, allowed = block_scores(block_index)
        probs = jnp.where(allowed, jnp.exp(scores - log_total[..., None]), 0.0).astype(jnp.bfloat16)
        value_block = lax.dynamic_slice_in_dim(value_rows, block_index * block_size, block_size, 1)
        return (
            totals
            + jnp.einsum("rhqk,rkhd->rqhd", probs, value_block, preferred_element_type=jnp.float32),
            None,
        )

    attended, _ = lax.scan(value_step, jnp.zeros(head_shape, jnp.float32), block_range)
    mixed_heads = attended.reshape(flat_shape).astype(jnp.bfloat16)
    branch = jnp.dot(mixed_heads, out_full, preferred_element_type=jnp.float32)
    branch_hat = layer_norm(branch)
    hidden = inputs + branch_hat * gain_rows[1]
    hidden_hat = layer_norm(hidden)
    normed_mid = (hidden_hat * gain_rows[2]).astype(jnp.bfloat16)
    ffn_in = lax.all_gather(normed_mid.reshape(fold_shape), "cp", axis=2, tiled=True).reshape(
        group_total, width
    )
    up_proj = jnp.dot(ffn_in, up_rows, preferred_element_type=jnp.float32)
    activation = gelu_tanh(up_proj).astype(jnp.bfloat16)
    down_terms = jnp.dot(activation, down_rows, preferred_element_type=jnp.float32)
    down_proj = (
        lax.psum_scatter(
            down_terms.reshape(group_shape).astype(jnp.bfloat16),
            "cp",
            scatter_dimension=2,
            tiled=True,
        )
        .astype(jnp.float32)
        .reshape(flat_shape)
    )
    down_hat = layer_norm(down_proj)
    mixed = (hidden + down_hat * gain_rows[3]).astype(jnp.bfloat16).reshape(tokens.shape)
    upstream = cotangent.astype(jnp.float32).reshape(flat_shape)
    gain_four = jnp.sum(upstream * down_hat, axis=(0, 1))
    grad_down_out = norm_back(down_proj, upstream * gain_rows[3]).astype(jnp.bfloat16)
    grad_out_rows = lax.all_gather(
        grad_down_out.reshape(fold_shape), "cp", axis=2, tiled=True
    ).reshape(group_total, width)
    down_local = jnp.einsum(
        "tf,td->fd", activation, grad_out_rows, preferred_element_type=jnp.float32
    )
    grad_act = jnp.einsum("td,fd->tf", grad_out_rows, down_rows, preferred_element_type=jnp.float32)
    _, gelu_pull = jax.vjp(gelu_tanh, up_proj)
    grad_up = gelu_pull(grad_act)[0].astype(jnp.bfloat16)
    up_local = jnp.einsum("tc,tf->cf", ffn_in, grad_up, preferred_element_type=jnp.float32)
    mid_terms = jnp.einsum("tf,cf->tc", grad_up, up_rows, preferred_element_type=jnp.float32)
    grad_mid = (
        lax.psum_scatter(
            mid_terms.reshape(group_shape).astype(jnp.bfloat16),
            "cp",
            scatter_dimension=2,
            tiled=True,
        )
        .astype(jnp.float32)
        .reshape(flat_shape)
    )
    gain_three = jnp.sum(grad_mid * hidden_hat, axis=(0, 1))
    grad_hidden = upstream + norm_back(hidden, grad_mid * gain_rows[2])
    gain_two = jnp.sum(grad_hidden * branch_hat, axis=(0, 1))
    grad_branch = norm_back(branch, grad_hidden * gain_rows[1]).astype(jnp.bfloat16)
    out_local = jnp.einsum(
        "tc,te->ce",
        mixed_heads.reshape(token_total, width),
        grad_branch.reshape(token_total, width),
        preferred_element_type=jnp.float32,
    )
    grad_heads = (
        jnp.einsum("rqe,ce->rqc", grad_branch, out_full, preferred_element_type=jnp.float32)
        .astype(jnp.bfloat16)
        .reshape(head_shape)
    )
    delta_sum = jnp.transpose(
        jnp.sum(grad_heads.astype(jnp.float32) * attended, axis=-1), (0, 2, 1)
    )

    def score_grads(block_index):
        scores, allowed = block_scores(block_index)
        probs = jnp.where(allowed, jnp.exp(scores - log_total[..., None]), 0.0)
        first_key = block_index * block_size
        key_block = lax.dynamic_slice_in_dim(key_rows, first_key, block_size, 1)
        value_block = lax.dynamic_slice_in_dim(value_rows, first_key, block_size, 1)
        grad_probs = jnp.einsum(
            "rqhd,rkhd->rhqk", grad_heads, value_block, preferred_element_type=jnp.float32
        )
        grad_scores = (probs * (grad_probs - delta_sum[..., None]) * score_scale).astype(
            jnp.bfloat16
        )
        return (probs, grad_scores, key_block)

    def grad_step(grad_query, block_index):
        probs, grad_scores, key_block = score_grads(block_index)
        grad_query = grad_query + jnp.einsum(
            "rhqk,rkhd->rqhd", grad_scores, key_block, preferred_element_type=jnp.float32
        )
        key_part = jnp.einsum(
            "rhqk,rqhd->rkhd", grad_scores, query_rows, preferred_element_type=jnp.float32
        )
        value_part = jnp.einsum(
            "rhqk,rqhd->rkhd",
            probs.astype(jnp.bfloat16),
            grad_heads,
            preferred_element_type=jnp.float32,
        )
        return (grad_query, (key_part, value_part))

    grad_query, (key_parts, value_parts) = lax.scan(
        grad_step, jnp.zeros(head_shape, jnp.float32), block_range
    )
    key_terms = jnp.moveaxis(key_parts, 0, 1).reshape(group_shape)
    value_terms = jnp.moveaxis(value_parts, 0, 1).reshape(group_shape)
    key_sum, value_sum = (
        lax.psum_scatter(
            key_terms.astype(jnp.bfloat16), "cp", scatter_dimension=2, tiled=True
        ).astype(jnp.float32),
        lax.psum_scatter(
            value_terms.astype(jnp.bfloat16), "cp", scatter_dimension=2, tiled=True
        ).astype(jnp.float32),
    )
    query_unturned = rotate(rounded(grad_query), cosine, -sine_part).reshape(flat_shape)
    key_unturned = rotate(rounded(key_sum.reshape(head_shape)), cosine, -sine_part).reshape(
        flat_shape
    )
    grad_linear = jnp.concatenate(
        [query_unturned, key_unturned, value_sum.reshape(flat_shape)], axis=-1
    ).astype(jnp.bfloat16)
    qkv_local = jnp.einsum(
        "tc,te->ce",
        normed.reshape(token_total, width),
        grad_linear.reshape(token_total, 3 * width),
        preferred_element_type=jnp.float32,
    )
    grad_normed = jnp.einsum(
        "rqe,ce->rqc", grad_linear, qkv_full, preferred_element_type=jnp.float32
    )
    gain_one = jnp.sum(grad_normed * normed_in, axis=(0, 1))
    tokens_grad = (grad_hidden + norm_back(inputs, grad_normed * gain_rows[0])).reshape(
        tokens.shape
    )
    gain_local = jnp.concatenate([gain_one, gain_two, gain_three, gain_four])
    gain_order = jnp.transpose(gain_local.reshape(rows_count, cp_count, -1), (1, 0, 2)).reshape(-1)
    qkv_mid, out_mid, gain_mid = (
        lax.psum_scatter(
            qkv_local.astype(jnp.bfloat16), "cp", scatter_dimension=1, tiled=True
        ).astype(jnp.float32),
        lax.psum_scatter(
            out_local.astype(jnp.bfloat16), "cp", scatter_dimension=1, tiled=True
        ).astype(jnp.float32),
        lax.psum_scatter(
            gain_order.astype(jnp.bfloat16), "cp", scatter_dimension=0, tiled=True
        ).astype(jnp.float32),
    )
    qkv_sum, out_sum, up_sum, down_sum, gain_sum = (
        lax.psum_scatter(
            qkv_mid.astype(jnp.bfloat16), "rows", scatter_dimension=0, tiled=True
        ).astype(jnp.float32),
        lax.psum_scatter(
            out_mid.astype(jnp.bfloat16), "rows", scatter_dimension=0, tiled=True
        ).astype(jnp.float32),
        lax.psum_scatter(
            up_local.astype(jnp.bfloat16), "rows", scatter_dimension=0, tiled=True
        ).astype(jnp.float32),
        lax.psum_scatter(
            down_local.astype(jnp.bfloat16), "rows", scatter_dimension=1, tiled=True
        ).astype(jnp.float32),
        lax.psum_scatter(
            gain_mid.astype(jnp.bfloat16), "rows", scatter_dimension=0, tiled=True
        ).astype(jnp.float32),
    )
    return (mixed, tokens_grad, qkv_sum, out_sum, up_sum, down_sum, gain_sum)


F32 = jnp.float32
BF16 = jnp.bfloat16
VMEM = 56 * 1024 * 1024


def params(grid_rank):
    return pltpu.CompilerParams(
        dimension_semantics=("arbitrary",) * grid_rank, vmem_limit_bytes=VMEM
    )


def turned(x, cosine, sine):
    lane = lax.broadcasted_iota(jnp.int32, x.shape, 1)
    other = jnp.where((lane & 32) == 0, pltpu.roll(x, 96, 1), pltpu.roll(x, 32, 1))
    return x * cosine + other * sine


def attend_kernel(tile, bounds, q_ref, k_ref, v_ref, pcol_ref, prow_ref, srow_ref,
                  o_ref, ob_ref, lse_ref, vt_ref):
    i = pl.program_id(1)

    @pl.when(i == 0)
    def _():
        vt_ref[...] = v_ref[...].astype(F32).T.astype(BF16)

    qt = q_ref[...].astype(F32).T
    row = lax.broadcasted_iota(jnp.int32, qt.shape, 0)
    lo = bounds[0, i]
    mid = jnp.minimum(bounds[1, i], i)
    qpos = prow_ref[...]
    qstart = srow_ref[...]
    qh = [jnp.where((row >= 64) == (h == 1), qt, 0.0).astype(BF16) for h in range(2)]

    def step(j, carry, masked):
        at = pl.multiple_of(j * tile, tile)
        k = k_ref[pl.ds(at, tile), :]
        scores = [jnp.dot(k, qh[h], preferred_element_type=F32) for h in range(2)]
        if masked:
            kpos = pcol_ref[pl.ds(at, tile), :]
            allowed = (kpos >= qstart) & (kpos <= qpos)
            scores = [jnp.where(allowed, s, MASKED) for s in scores]
        out = []
        for h in range(2):
            top, total, acc = carry[h]
            new = jnp.maximum(top, jnp.max(scores[h], axis=0, keepdims=True))
            p = jnp.exp(scores[h] - new)
            keep = jnp.exp(top - new)
            total = total * keep + jnp.sum(p, axis=0, keepdims=True)
            acc = acc * keep + jnp.dot(
                vt_ref[h * 64 : h * 64 + 64, pl.ds(at, tile)], p.astype(BF16),
                preferred_element_type=F32,
            )
            out.append((new, total, acc))
        return tuple(out)

    start = (
        jnp.full((1, tile), MASKED, F32), jnp.zeros((1, tile), F32), jnp.zeros((64, tile), F32)
    )
    carry = step(i, (start, start), True)
    carry = lax.fori_loop(lo, mid, functools.partial(step, masked=True), carry)
    carry = lax.fori_loop(mid, i, functools.partial(step, masked=False), carry)
    parts = []
    for h in range(2):
        top, total, acc = carry[h]
        lse_ref[0, h : h + 1, :] = top + jnp.log(total)
        parts.append(acc / total)
    out = jnp.concatenate(parts, axis=0).T
    o_ref[...] = out
    ob_ref[...] = out.astype(BF16)


def attend(q, k, v, pcol, prow, srow, bounds, tile):
    rows, width = q.shape
    pairs = width // 128
    count = rows // tile
    grid_spec = pltpu.PrefetchScalarGridSpec(
        num_scalar_prefetch=1,
        grid=(pairs, count),
        in_specs=[
            pl.BlockSpec((tile, 128), lambda p, i, b: (i, p)),
            pl.BlockSpec((rows, 128), lambda p, i, b: (0, p)),
            pl.BlockSpec((rows, 128), lambda p, i, b: (0, p)),
            pl.BlockSpec((rows, 1), lambda p, i, b: (0, 0)),
            pl.BlockSpec((1, tile), lambda p, i, b: (0, i)),
            pl.BlockSpec((1, tile), lambda p, i, b: (0, i)),
        ],
        out_specs=[
            pl.BlockSpec((tile, 128), lambda p, i, b: (i, p)),
            pl.BlockSpec((tile, 128), lambda p, i, b: (i, p)),
            pl.BlockSpec((1, 2, tile), lambda p, i, b: (p, 0, i)),
        ],
        scratch_shapes=[pltpu.VMEM((128, rows), BF16)],
    )
    return pl.pallas_call(
        functools.partial(attend_kernel, tile),
        grid_spec=grid_spec,
        out_shape=[
            jax.ShapeDtypeStruct((rows, width), F32),
            jax.ShapeDtypeStruct((rows, width), BF16),
            jax.ShapeDtypeStruct((pairs, 2, rows), F32),
        ],
        compiler_params=params(2),
        name="attend",
    )(bounds, q, k, v, pcol, prow, srow)


def attend_back_kernel(tile, bounds, q_ref, k_ref, v_ref, do_ref, o_ref, lse_ref, pcol_ref,
                       prow_ref, srow_ref, cos_ref, sin_ref, g_ref,
                       qm, dom, qtm, dotm, delta, dqt):
    j = pl.program_id(1)
    count = pl.num_programs(1)
    rows = q_ref.shape[0]

    @pl.when(j == 0)
    def _():
        for t in range(rows // tile):
            part = pl.ds(t * tile, tile)
            q = q_ref[part, :].astype(F32)
            do = do_ref[part, :].astype(F32)
            qt, dot = q.T, do.T
            lane = lax.broadcasted_iota(jnp.int32, q.shape, 1)
            row = lax.broadcasted_iota(jnp.int32, qt.shape, 0)
            prod = dot * o_ref[part, :].T
            for h in range(2):
                mine = (lane >= 64) == (h == 1)
                mine_t = (row >= 64) == (h == 1)
                qm[h, part, :] = jnp.where(mine, q, 0.0).astype(BF16)
                dom[h, part, :] = jnp.where(mine, do, 0.0).astype(BF16)
                qtm[h, :, part] = jnp.where(mine_t, qt, 0.0).astype(BF16)
                dotm[h, :, part] = jnp.where(mine_t, dot, 0.0).astype(BF16)
                delta[h : h + 1, part] = jnp.sum(
                    prod[h * 64 : h * 64 + 64], axis=0, keepdims=True
                )
        dqt[...] = jnp.zeros_like(dqt)

    here = pl.ds(pl.multiple_of(j * tile, tile), tile)
    k = k_ref[here, :]
    v = v_ref[here, :]
    kt = k.astype(F32).T.astype(BF16)
    kpos = pcol_ref[here, :]
    full = jnp.maximum(bounds[2, j], j + 1)
    end = bounds[3, j]

    def step(i, carry, masked):
        dk, dv = carry
        part = pl.ds(pl.multiple_of(i * tile, tile), tile)
        if masked:
            allowed = (kpos >= srow_ref[:, part]) & (kpos <= prow_ref[:, part])
        for h in range(2):
            s = jnp.dot(k, qtm[h, :, part], preferred_element_type=F32)
            p = jnp.exp(s - lse_ref[0, h : h + 1, part])
            if masked:
                p = jnp.where(allowed, p, 0.0)
            dp = jnp.dot(v, dotm[h, :, part], preferred_element_type=F32)
            ds = (p * (dp - delta[h : h + 1, part])).astype(BF16)
            dv = dv + jnp.dot(p.astype(BF16), dom[h, part, :], preferred_element_type=F32)
            dk = dk + jnp.dot(ds, qm[h, part, :], preferred_element_type=F32)
            dqt[h * 64 : h * 64 + 64, part] += jnp.dot(
                kt[h * 64 : h * 64 + 64, :], ds, preferred_element_type=F32
            )
        return dk, dv

    carry = (jnp.zeros((tile, 128), F32), jnp.zeros((tile, 128), F32))
    carry = step(j, carry, True)
    carry = lax.fori_loop(j + 1, full, functools.partial(step, masked=False), carry)
    carry = lax.fori_loop(full, end, functools.partial(step, masked=True), carry)
    dk, dv = carry

    def unturned(x, at):
        x = x.astype(BF16).astype(F32)
        return turned(x, cos_ref[at, :], -sin_ref[at, :]).astype(BF16)

    g_ref[1, here, :] = unturned(dk, here)
    g_ref[2, here, :] = dv.astype(BF16)

    @pl.when(j == count - 1)
    def _():
        for t in range(rows // tile):
            part = pl.ds(t * tile, tile)
            g_ref[0, part, :] = unturned(dqt[:, part].T * 0.125, part)


def attend_back(q, k, v, do, o, lse, pcol, prow, srow, cosine, sine, bounds, tile):
    rows, width = q.shape
    pairs = width // 128
    count = rows // tile
    whole = pl.BlockSpec((rows, 128), lambda p, j, b: (0, p))
    table = pl.BlockSpec((rows, 128), lambda p, j, b: (0, 0))
    line = pl.BlockSpec((1, rows), lambda p, j, b: (0, 0))
    grid_spec = pltpu.PrefetchScalarGridSpec(
        num_scalar_prefetch=1,
        grid=(pairs, count),
        in_specs=[
            whole, whole, whole, whole, whole,
            pl.BlockSpec((1, 2, rows), lambda p, j, b: (p, 0, 0)),
            pl.BlockSpec((rows, 1), lambda p, j, b: (0, 0)),
            line, line, table, table,
        ],
        out_specs=pl.BlockSpec((3, rows, 128), lambda p, j, b: (0, 0, p)),
        scratch_shapes=[
            pltpu.VMEM((2, rows, 128), BF16), pltpu.VMEM((2, rows, 128), BF16),
            pltpu.VMEM((2, 128, rows), BF16), pltpu.VMEM((2, 128, rows), BF16),
            pltpu.VMEM((2, rows), F32), pltpu.VMEM((128, rows), F32),
        ],
    )
    return pl.pallas_call(
        functools.partial(attend_back_kernel, tile),
        grid_spec=grid_spec,
        out_shape=jax.ShapeDtypeStruct((3, rows, width), BF16),
        compiler_params=params(2),
        name="attend_back",
    )(bounds, q, k, v, do, o, lse, pcol, prow, srow, cosine, sine)


def tile_bounds(starts_nat, tile):
    rows = starts_nat.shape[0]
    count = rows // tile
    tiles = starts_nat.reshape(count, tile)
    first, last = tiles[:, 0], tiles[:, -1]
    at = jnp.arange(count, dtype=jnp.int32) * tile
    lo = first // tile
    mid = (last + tile - 1) // tile
    full = jnp.sum((last[None, :] <= at[:, None]).astype(jnp.int32), axis=1)
    end = jnp.sum((first[None, :] <= at[:, None] + tile - 1).astype(jnp.int32), axis=1)
    return jnp.stack([lo, mid, full, end]).astype(jnp.int32)


def reorder_kernel(table, x_ref, o_ref):
    o_ref[...] = x_ref[...]


def reorder(x, table):
    count, rows, width = x.shape
    block = (1, rows, width)
    return pl.pallas_call(
        reorder_kernel,
        grid_spec=pltpu.PrefetchScalarGridSpec(
            num_scalar_prefetch=1,
            grid=(count,),
            in_specs=[pl.BlockSpec(block, lambda i, t: (t[i], 0, 0))],
            out_specs=pl.BlockSpec(block, lambda i, t: (i, 0, 0)),
        ),
        out_shape=jax.ShapeDtypeStruct(x.shape, x.dtype),
        compiler_params=params(1),
        name="reorder",
    )(table, x)


def project_kernel(table, x_ref, w_ref, cos_ref, sin_ref, q_ref, k_ref, v_ref):
    width = q_ref.shape[1]
    linear = jnp.dot(x_ref[0], w_ref[...], preferred_element_type=F32)
    for at in range(0, width, 128):
        q = turned(linear[:, at : at + 128], cos_ref[...], sin_ref[...])
        k = turned(linear[:, width + at : width + at + 128], cos_ref[...], sin_ref[...])
        q_ref[:, at : at + 128] = q.astype(BF16) * jnp.asarray(0.125, BF16)
        k_ref[:, at : at + 128] = k.astype(BF16)
    v_ref[...] = linear[:, 2 * width :].astype(BF16)


def project(x, w, cosine, sine, table):
    count, rows, depth = x.shape
    width = w.shape[1] // 3
    out = pl.BlockSpec((rows, width), lambda i, t: (i, 0))
    angle = pl.BlockSpec((rows, 128), lambda i, t: (i, 0))
    return pl.pallas_call(
        project_kernel,
        grid_spec=pltpu.PrefetchScalarGridSpec(
            num_scalar_prefetch=1,
            grid=(count,),
            in_specs=[
                pl.BlockSpec((1, rows, depth), lambda i, t: (t[i], 0, 0)),
                pl.BlockSpec(w.shape, lambda i, t: (0, 0)),
                angle, angle,
            ],
            out_specs=[out, out, out],
        ),
        out_shape=[jax.ShapeDtypeStruct((count * rows, width), BF16)] * 3,
        compiler_params=params(1),
        name="project",
    )(table, x, w, cosine, sine)


def project_back_kernel(table, g_ref, w_ref, o_ref):
    g = jnp.concatenate([g_ref[0], g_ref[1], g_ref[2]], axis=1)
    o_ref[0] = lax.dot_general(
        g, w_ref[...], (((1,), (1,)), ((), ())), preferred_element_type=F32
    ).astype(BF16)


def project_back(grads, w, table):
    count = table.shape[0]
    _, total, width = grads.shape
    rows = total // count
    depth = w.shape[0]
    return pl.pallas_call(
        project_back_kernel,
        grid_spec=pltpu.PrefetchScalarGridSpec(
            num_scalar_prefetch=1,
            grid=(count,),
            in_specs=[
                pl.BlockSpec((3, rows, width), lambda i, t: (0, i, 0)),
                pl.BlockSpec(w.shape, lambda i, t: (0, 0)),
            ],
            out_specs=pl.BlockSpec((1, rows, depth), lambda i, t: (t[i], 0, 0)),
        ),
        out_shape=jax.ShapeDtypeStruct((count, rows, depth), BF16),
        compiler_params=params(1),
        name="project_back",
    )(table, grads, w)


def project_weights_kernel(table, x_ref, g_ref, o_ref, total):
    i = pl.program_id(0)

    @pl.when(i == 0)
    def _():
        total[...] = jnp.zeros_like(total)

    g = jnp.concatenate([g_ref[0], g_ref[1], g_ref[2]], axis=1)
    total[...] += lax.dot_general(
        x_ref[0], g, (((0,), (0,)), ((), ())), preferred_element_type=F32
    )

    @pl.when(i == pl.num_programs(0) - 1)
    def _():
        o_ref[...] = total[...].astype(BF16)


def project_weights(x, grads, table):
    count, rows, depth = x.shape
    width = grads.shape[2]
    return pl.pallas_call(
        project_weights_kernel,
        grid_spec=pltpu.PrefetchScalarGridSpec(
            num_scalar_prefetch=1,
            grid=(count,),
            in_specs=[
                pl.BlockSpec((1, rows, depth), lambda i, t: (t[i], 0, 0)),
                pl.BlockSpec((3, rows, width), lambda i, t: (0, i, 0)),
            ],
            out_specs=pl.BlockSpec((depth, 3 * width), lambda i, t: (0, 0)),
            scratch_shapes=[pltpu.VMEM((depth, 3 * width), F32)],
        ),
        out_shape=jax.ShapeDtypeStruct((depth, 3 * width), BF16),
        compiler_params=params(1),
        name="project_weights",
    )(table, x, grads)


def flip(x, axis, bit):
    return lax.ppermute(x, axis, [(i, i ^ bit) for i in range(lax.axis_size(axis))])


def swap(x):
    cp = lax.axis_size("cp")
    half = cp // 2
    pairs = []
    for z in range(half):
        low, high = cp + z, z + half
        pairs += [(low, high), (high, low), (z, z), (cp + high, cp + high)]
    return lax.ppermute(x, ("core", "cp"), pairs)


def ordered(first, mine, other, axis):
    return jnp.concatenate(
        [jnp.where(first, mine, other), jnp.where(first, other, mine)], axis=axis
    )


def dot(a, b, dims):
    return lax.dot_general(a, b, ((dims[:1], dims[1:]), ((), ())), preferred_element_type=F32)


def gelu_and_slope(u):
    inner = math.sqrt(2.0 / math.pi) * (u + 0.044715 * u * u * u)
    t = jnp.tanh(inner)
    slope = 0.5 * (1.0 + t) + 0.5 * u * (1.0 - t * t) * math.sqrt(2.0 / math.pi) * (
        1.0 + 3.0 * 0.044715 * u * u
    )
    return 0.5 * u * (1.0 + t), slope


def body(tokens, doc_starts, qkv_weight, out_weight, up_weight, down_weight, norm_gains, cotangent):
    xy, core, z = lax.axis_index("xy"), lax.axis_index("core"), lax.axis_index("cp")
    xy_count, cp_count = lax.axis_size("xy"), lax.axis_size("cp")
    _, _, span, width = tokens.shape
    blocks = 2 * cp_count
    row_len = blocks * span
    own = 2 * span
    parity = z & 1
    group = 2 * parity + core
    part = width // cp_count
    hidden_part = up_weight.shape[1] // 2

    inputs = swap(tokens.reshape(own, width)).astype(F32)
    upstream = swap(cotangent.reshape(own, width)).astype(F32)
    other_starts = flip(doc_starts, "core", 1)
    starts = jnp.where(core == z // (cp_count // 2), doc_starts, other_starts)[0]
    gains = lax.all_gather(norm_gains, ("xy", "core", "cp"), axis=0, tiled=True)
    gains = gains.astype(F32).reshape(4, width)

    w = qkv_weight
    for bit, at in ((2, 0), (1, 1)):
        other = flip(w, "cp", bit)
        w = ordered((z & bit) == 0, jnp.expand_dims(w, at), jnp.expand_dims(other, at), at)

    def columns(of):
        picked = []
        for third in range(3):
            block = third * cp_count + of
            picked.append(
                lax.dynamic_slice(
                    w, (block // 6, (block // 3) & 1, 0, (block % 3) * part), (1, 1, w.shape[2], part)
                )[0, 0]
            )
        return jnp.concatenate(picked, axis=1)

    mine = columns(group)
    other = flip(columns(group ^ 1), "core", 1)
    qkv = ordered(core == 0, mine, other, 0)
    for bit in (1, 2):
        other = flip(qkv, "xy", bit)
        qkv = ordered((xy & bit) == 0, qkv, other, 0)

    def half_of(which):
        up = lax.dynamic_slice_in_dim(up_weight, which * hidden_part, hidden_part, 1)
        down = lax.dynamic_slice_in_dim(down_weight, which * hidden_part, hidden_part, 0)
        return jnp.stack([up, down.T])

    both = ordered(core == 0, half_of(core), flip(half_of(1 - core), "core", 1), 1)
    ffn = lax.all_gather(both, ("xy", "cp"), axis=0)
    ffn = ffn.reshape(xy_count, cp_count, 2, -1, hidden_part).transpose(2, 0, 3, 1, 4)
    ffn = ffn.reshape(2, width, cp_count * hidden_part)
    up_half, down_half = ffn[0], ffn[1]

    out_w = out_weight
    for bit in (1, 2):
        other = flip(out_w, "cp", bit)
        out_w = ordered((z & bit) == 0, out_w, other, 1)
    out_w = out_w[None]
    for bit in (1, 2):
        other = flip(out_w, "xy", bit)
        out_w = ordered((xy & bit) == 0, out_w, other, 0)
    other = flip(out_w, "core", 1)
    out_w = ordered(core == 0, out_w[:, None], other[:, None], 1).reshape(width, width)

    block_id = jnp.arange(blocks, dtype=jnp.int32)[:, None]
    inside = jnp.arange(span, dtype=jnp.int32)[None, :]
    late = block_id >= cp_count
    positions = (block_id * span + jnp.where(late, span - 1 - inside, inside)).reshape(-1)

    def starts_at(at):
        return jnp.max(jnp.where(starts[None, :] <= at[:, None], starts[None, :], 0), axis=1)

    row_start = starts_at(positions)
    tile = min(512, row_len)
    bounds = tile_bounds(starts_at(jnp.arange(row_len, dtype=jnp.int32)), tile)
    freq = jnp.exp(
        -math.log(10000.0) * 2.0 * jnp.arange(HEAD_DIM // 2, dtype=F32) / HEAD_DIM
    )
    angles = (positions - row_start).astype(F32)[:, None] * freq
    cosine, sine = jnp.cos(angles), jnp.sin(angles)
    cosine = jnp.tile(cosine, (1, 4))
    sine = jnp.tile(jnp.concatenate([-sine, sine], axis=1), (1, 2))
    pcol, prow, srow = positions[:, None], positions[None, :], row_start[None, :]
    chunk = jnp.arange(blocks, dtype=jnp.int32)
    chunk = jnp.where(chunk < cp_count, chunk, blocks - 1 - chunk)
    slot_of = (
        2 * (2 * ((chunk >> 1) ^ core) + ((chunk & 1) ^ parity))
        + (jnp.arange(blocks) >= cp_count)
    ).astype(jnp.int32)
    slot = jnp.arange(blocks, dtype=jnp.int32)
    relative = slot >> 1
    chunk_of = 2 * ((relative >> 1) ^ core) + ((relative & 1) ^ parity)
    block_of = jnp.where(slot & 1 == 0, chunk_of, blocks - 1 - chunk_of).astype(jnp.int32)

    normed_in = layer_norm(inputs)
    normed = (normed_in * gains[0]).astype(BF16).reshape(2, span, width)
    pair = jnp.concatenate([normed, flip(normed, "cp", 1)], axis=0)
    slots = jnp.concatenate([pair, flip(pair, "core", 1)], axis=0)
    q, k, v = project(slots, qkv, cosine, sine, slot_of)
    attended, attended_low, lse = attend(q, k, v, pcol, prow, srow, bounds, tile)
    local = reorder(attended_low.reshape(blocks, span, part), block_of)
    from_core = flip(local[4:], "core", 1)
    from_chip = flip(jnp.stack([local[2:4], from_core[2:4]]), "cp", 1)
    pieces = jnp.concatenate([jnp.stack([local[:2], from_core[:2]]), from_chip]).reshape(
        4, own, part
    )
    heads = jnp.concatenate(
        [lax.dynamic_index_in_dim(pieces, g ^ group, 0, False) for g in range(4)], axis=1
    )
    branch = dot(heads, out_w, (1, 0))
    branch_hat = layer_norm(branch)
    hidden = inputs + branch_hat * gains[1]
    hidden_hat = layer_norm(hidden)
    normed_mid = (hidden_hat * gains[2]).astype(BF16)

    ffn_in = jnp.concatenate([normed_mid, flip(normed_mid, "core", 1)])
    act, slope = gelu_and_slope(dot(ffn_in, up_half, (1, 0)))
    act, slope = act.astype(BF16), slope.astype(BF16)
    terms = dot(act, down_half, (1, 1))
    down = terms[:own] + flip(terms[own:].astype(BF16), "core", 1).astype(F32)
    down_hat = layer_norm(down)
    mixed = swap((hidden + down_hat * gains[3]).astype(BF16)).reshape(tokens.shape)

    gain_four = jnp.sum(upstream * down_hat, axis=0)
    grad_down = norm_back(down, upstream * gains[3]).astype(BF16)
    grad_down = jnp.concatenate([grad_down, flip(grad_down, "core", 1)])
    grad_up = (dot(grad_down, down_half, (1, 0)) * slope.astype(F32)).astype(BF16)
    terms = dot(grad_up, up_half, (1, 1))
    grad_mid = terms[:own] + flip(terms[own:].astype(BF16), "core", 1).astype(F32)
    up_local = dot(ffn_in, grad_up, (0, 0)).astype(BF16)
    down_local = dot(grad_down, act, (0, 0)).astype(BF16)

    gain_three = jnp.sum(grad_mid * hidden_hat, axis=0)
    grad_hidden = upstream + norm_back(hidden, grad_mid * gains[2])
    gain_two = jnp.sum(grad_hidden * branch_hat, axis=0)
    grad_branch = norm_back(branch, grad_hidden * gains[1]).astype(BF16)
    grad_heads = dot(grad_branch, out_w, (1, 1)).astype(BF16)
    out_local = dot(heads, grad_branch, (0, 0)).astype(BF16)

    cut = jnp.transpose(grad_heads.reshape(2, span, 4, part), (2, 0, 1, 3))
    near = [lax.dynamic_index_in_dim(cut, group ^ r, 0, False) for r in range(4)]
    from_chip = flip(jnp.stack([near[2], near[3]]), "cp", 1)
    from_core = flip(jnp.concatenate([near[1], from_chip[1]]), "core", 1)
    grad_local = jnp.concatenate([near[0], from_chip[0], from_core])
    grad_local = reorder(grad_local, slot_of).reshape(row_len, part)
    grad_linear = attend_back(
        q, k, v, grad_local, attended, lse, pcol, prow, srow, cosine, sine, bounds, tile
    )
    terms = project_back(grad_linear, qkv, slot_of)
    pair = terms[:4].astype(F32) + flip(terms[4:], "core", 1).astype(F32)
    grad_normed = pair[:2] + flip(pair[2:].astype(BF16), "cp", 1).astype(F32)
    grad_normed = grad_normed.reshape(own, width)
    gain_one = jnp.sum(grad_normed * normed_in, axis=0)
    tokens_grad = grad_hidden + norm_back(inputs, grad_normed * gains[0])
    tokens_grad = swap(tokens_grad.astype(BF16)).astype(F32).reshape(tokens.shape)

    out_local = out_local.reshape(xy_count, 2, width // xy_count // 2, width)
    out_mine = lax.dynamic_index_in_dim(out_local, core, 1, False)
    out_other = lax.dynamic_index_in_dim(out_local, 1 - core, 1, False)
    out_pair = (out_mine.astype(F32) + flip(out_other, "core", 1).astype(F32)).astype(BF16)
    out_rows = out_pair.shape[1]
    out_pair = out_pair.reshape(xy_count, out_rows, cp_count, -1).transpose(0, 2, 1, 3)
    out_cols = out_pair.shape[3]
    rows_each = width // xy_count
    sent = jnp.stack([up_local, down_local]).reshape(
        2, xy_count, rows_each, cp_count, hidden_part
    )
    sent = sent.transpose(1, 3, 0, 2, 4).reshape(xy_count, cp_count, 2 * rows_each, hidden_part)
    sent = jnp.concatenate([sent, out_pair.reshape(xy_count, cp_count, -1, hidden_part)], axis=2)
    sent = lax.psum_scatter(sent, "xy", scatter_dimension=0)
    sent = lax.psum_scatter(sent, "cp", scatter_dimension=0)
    out_grad = sent[2 * rows_each :].reshape(out_rows, out_cols).astype(F32)
    sent = sent[: 2 * rows_each].reshape(2, 2, rows_each // 2, hidden_part)
    mine = lax.dynamic_index_in_dim(sent, core, 1, False)
    other = flip(lax.dynamic_index_in_dim(sent, 1 - core, 1, False), "core", 1)
    up_grad = ordered(core == 0, mine[0], other[0], 1).astype(F32)
    down_grad = ordered(core == 0, mine[1], other[1], 1).T.astype(F32)

    qkv_local = project_weights(slots, grad_linear, slot_of)
    qkv_local = qkv_local.reshape(xy_count, 2, rows_each // 2, 3 * part)
    qkv_sum = lax.psum_scatter(qkv_local, "xy", scatter_dimension=0)
    mine = lax.dynamic_index_in_dim(qkv_sum, core, 0, False)
    other = flip(lax.dynamic_index_in_dim(qkv_sum, 1 - core, 0, False), "core", 1)
    both = ordered(core == 0, mine[None], other[None], 0)
    both = (both.astype(F32) + flip(both, "cp", 2).astype(F32)).astype(BF16)
    every = ordered(parity == 0, both, flip(both, "cp", 1), 0)
    every = every.reshape(4, rows_each // 2, 3, part).transpose(1, 2, 0, 3)
    qkv_grad = lax.dynamic_slice_in_dim(
        every.reshape(rows_each // 2, 3 * width), z * 3 * part, 3 * part, 1
    ).astype(F32)

    gain_local = jnp.concatenate([gain_one, gain_two, gain_three, gain_four]).reshape(-1, 128)
    for axis, bit in (("core", 1), ("xy", 1), ("xy", 2), ("cp", 1), ("cp", 2)):
        gain_local = gain_local + flip(gain_local, axis, bit)
    gains_grad = lax.dynamic_index_in_dim(
        gain_local, (2 * xy + core) * cp_count + z, 0, False
    )
    return mixed, tokens_grad, qkv_grad, out_grad, up_grad, down_grad, gains_grad


def solution(mesh):
    rows, cp = mesh.shape["rows"], mesh.shape["cp"]
    if (rows, cp) == (8, 4):
        grid = Mesh(mesh.devices.reshape(rows // 2, 2, cp), ("xy", "core", "cp"))
        run, lines = body, ("xy", "core")
    else:
        grid, run, lines = mesh, general_body, ("rows",)
    tokens = P(lines, None, "cp", None)
    weight, down, gains = P(lines, "cp"), P("cp", lines), P(lines + ("cp",))
    return jax.shard_map(
        run,
        mesh=grid,
        in_specs=(tokens, P(lines, None), weight, weight, weight, down, gains, tokens),
        out_specs=(tokens, tokens, weight, weight, weight, down, gains),
        check_vma=False,
    )
```

```python
import functools
import math

import jax
import jax.numpy as jnp
from jax import lax
from jax.experimental import pallas as pl
from jax.experimental.layout import Layout, with_layout_constraint
from jax.experimental.pallas import tpu as pltpu
from jax.sharding import Mesh, PartitionSpec as P

HEADS = 16
HEAD_DIM = 64


NORM_EPS = 1e-05
MASKED = -1e30


def layer_norm(values):
    average = jnp.mean(values, axis=-1, keepdims=True)
    centred = values - average
    spread = jnp.mean(centred * centred, axis=-1, keepdims=True)
    return centred * lax.rsqrt(spread + NORM_EPS)


def norm_back(values, upstream):
    _, pull_back = jax.vjp(layer_norm, values)
    return pull_back(upstream)[0]


def gelu_tanh(values):
    return jax.nn.gelu(values, approximate=True)


def rotate(values, cosine, sine_part):
    half_width = values.shape[-1] // 2
    first_half = values[..., :half_width]
    second_half = values[..., half_width:]
    return jnp.concatenate(
        [
            first_half * cosine - second_half * sine_part,
            second_half * cosine + first_half * sine_part,
        ],
        axis=-1,
    )


def rounded(values):
    return lax.optimization_barrier(values.astype(jnp.bfloat16)).astype(jnp.float32)


def doc_start_of(starts, positions):
    return jnp.max(
        jnp.where(starts[:, None, :] <= positions[None, :, None], starts[:, None, :], 0), axis=-1
    )


def general_body(tokens, doc_starts, qkv_weight, out_weight, up_weight, down_weight, norm_gains, cotangent):
    rows_count = lax.axis_size("rows")
    cp_count = lax.axis_size("cp")
    qkv_rows, out_rows, up_rows, down_rows, gain_piece = (
        lax.all_gather(qkv_weight, "rows", axis=0, tiled=True),
        lax.all_gather(out_weight, "rows", axis=0, tiled=True),
        lax.all_gather(up_weight, "rows", axis=0, tiled=True),
        lax.all_gather(down_weight, "rows", axis=1, tiled=True),
        lax.all_gather(norm_gains, "rows", axis=0, tiled=True),
    )
    qkv_full, out_full, gain_mixed = (
        lax.all_gather(qkv_rows, "cp", axis=1, tiled=True),
        lax.all_gather(out_rows, "cp", axis=1, tiled=True),
        lax.all_gather(gain_piece, "cp", axis=0, tiled=True),
    )
    gain_full = jnp.transpose(gain_mixed.reshape(cp_count, rows_count, -1), (1, 0, 2)).reshape(-1)
    row_count, _, span_len, width = tokens.shape
    half_len = span_len * cp_count
    row_len = 2 * half_len
    queries_dev = 2 * span_len
    token_total = row_count * queries_dev
    group_total = row_count * row_len
    gain_rows = gain_full.astype(jnp.float32).reshape(4, width)
    score_scale = HEAD_DIM ** (-0.5)
    local_pos = lax.axis_index("cp") * span_len + jnp.arange(span_len, dtype=jnp.int32)
    query_pos = jnp.concatenate([local_pos, row_len - 1 - local_pos])
    half_pos = jnp.arange(half_len, dtype=jnp.int32)
    key_pos = jnp.concatenate([half_pos, row_len - 1 - half_pos])
    query_start = doc_start_of(doc_starts, query_pos)
    key_start = doc_start_of(doc_starts, key_pos)
    freq_index = jnp.arange(HEAD_DIM // 2, dtype=jnp.float32)
    inverse_freq = jnp.exp(-math.log(10000.0) * 2.0 * freq_index / HEAD_DIM)
    angles = (query_pos[None, :] - query_start).astype(jnp.float32)[..., None] * inverse_freq
    cosine = jnp.cos(angles)[:, :, None, :]
    sine_part = jnp.sin(angles)[:, :, None, :]
    head_shape = (row_count, queries_dev, HEADS, HEAD_DIM)
    flat_shape = (row_count, queries_dev, width)
    fold_shape = (row_count, 2, span_len, width)
    group_shape = (row_count, 2, half_len, width)
    full_shape = (row_count, row_len, HEADS, HEAD_DIM)
    inputs = tokens.astype(jnp.float32).reshape(flat_shape)
    normed_in = layer_norm(inputs)
    normed = (normed_in * gain_rows[0]).astype(jnp.bfloat16)
    linear = jnp.dot(normed, qkv_full, preferred_element_type=jnp.float32)
    query_rows = rotate(linear[..., :width].reshape(head_shape), cosine, sine_part).astype(
        jnp.bfloat16
    )
    key_local = rotate(
        linear[..., width : 2 * width].reshape(head_shape), cosine, sine_part
    ).astype(jnp.bfloat16)
    value_local = linear[..., 2 * width :].reshape(head_shape).astype(jnp.bfloat16)
    key_sent, value_sent = (
        lax.all_gather(key_local.reshape(fold_shape), "cp", axis=2, tiled=True),
        lax.all_gather(value_local.reshape(fold_shape), "cp", axis=2, tiled=True),
    )
    key_rows = key_sent.reshape(full_shape)
    value_rows = value_sent.reshape(full_shape)
    block_size = min(512, row_len)
    block_count = row_len // block_size
    block_range = jnp.arange(block_count)

    def block_scores(block_index):
        first_key = block_index * block_size
        key_block = lax.dynamic_slice_in_dim(key_rows, first_key, block_size, 1)
        pos_block = lax.dynamic_slice_in_dim(key_pos, first_key, block_size, 0)
        start_block = lax.dynamic_slice_in_dim(key_start, first_key, block_size, 1)
        raw_scores = jnp.einsum(
            "rqhd,rkhd->rhqk", query_rows, key_block, preferred_element_type=jnp.float32
        )
        allowed = (query_start[:, None, :, None] == start_block[:, None, None, :]) & (
            pos_block[None, None, None, :] <= query_pos[None, None, :, None]
        )
        return (raw_scores * score_scale, allowed)

    def max_step(carry, block_index):
        running_max, running_sum = carry
        scores, allowed = block_scores(block_index)
        scores = jnp.where(allowed, scores, MASKED)
        new_max = jnp.maximum(running_max, jnp.max(scores, axis=-1))
        running_sum = running_sum * jnp.exp(running_max - new_max) + jnp.sum(
            jnp.where(allowed, jnp.exp(scores - new_max[..., None]), 0.0), axis=-1
        )
        return ((new_max, running_sum), None)

    stat_shape = (row_count, HEADS, queries_dev)
    (running_max, running_sum), _ = lax.scan(
        max_step,
        (jnp.full(stat_shape, MASKED, jnp.float32), jnp.zeros(stat_shape, jnp.float32)),
        block_range,
    )
    log_total = running_max + jnp.log(running_sum)

    def value_step(totals, block_index):
        scores, allowed = block_scores(block_index)
        probs = jnp.where(allowed, jnp.exp(scores - log_total[..., None]), 0.0).astype(jnp.bfloat16)
        value_block = lax.dynamic_slice_in_dim(value_rows, block_index * block_size, block_size, 1)
        return (
            totals
            + jnp.einsum("rhqk,rkhd->rqhd", probs, value_block, preferred_element_type=jnp.float32),
            None,
        )

    attended, _ = lax.scan(value_step, jnp.zeros(head_shape, jnp.float32), block_range)
    mixed_heads = attended.reshape(flat_shape).astype(jnp.bfloat16)
    branch = jnp.dot(mixed_heads, out_full, preferred_element_type=jnp.float32)
    branch_hat = layer_norm(branch)
    hidden = inputs + branch_hat * gain_rows[1]
    hidden_hat = layer_norm(hidden)
    normed_mid = (hidden_hat * gain_rows[2]).astype(jnp.bfloat16)
    ffn_in = lax.all_gather(normed_mid.reshape(fold_shape), "cp", axis=2, tiled=True).reshape(
        group_total, width
    )
    up_proj = jnp.dot(ffn_in, up_rows, preferred_element_type=jnp.float32)
    activation = gelu_tanh(up_proj).astype(jnp.bfloat16)
    down_terms = jnp.dot(activation, down_rows, preferred_element_type=jnp.float32)
    down_proj = (
        lax.psum_scatter(
            down_terms.reshape(group_shape).astype(jnp.bfloat16),
            "cp",
            scatter_dimension=2,
            tiled=True,
        )
        .astype(jnp.float32)
        .reshape(flat_shape)
    )
    down_hat = layer_norm(down_proj)
    mixed = (hidden + down_hat * gain_rows[3]).astype(jnp.bfloat16).reshape(tokens.shape)
    upstream = cotangent.astype(jnp.float32).reshape(flat_shape)
    gain_four = jnp.sum(upstream * down_hat, axis=(0, 1))
    grad_down_out = norm_back(down_proj, upstream * gain_rows[3]).astype(jnp.bfloat16)
    grad_out_rows = lax.all_gather(
        grad_down_out.reshape(fold_shape), "cp", axis=2, tiled=True
    ).reshape(group_total, width)
    down_local = jnp.einsum(
        "tf,td->fd", activation, grad_out_rows, preferred_element_type=jnp.float32
    )
    grad_act = jnp.einsum("td,fd->tf", grad_out_rows, down_rows, preferred_element_type=jnp.float32)
    _, gelu_pull = jax.vjp(gelu_tanh, up_proj)
    grad_up = gelu_pull(grad_act)[0].astype(jnp.bfloat16)
    up_local = jnp.einsum("tc,tf->cf", ffn_in, grad_up, preferred_element_type=jnp.float32)
    mid_terms = jnp.einsum("tf,cf->tc", grad_up, up_rows, preferred_element_type=jnp.float32)
    grad_mid = (
        lax.psum_scatter(
            mid_terms.reshape(group_shape).astype(jnp.bfloat16),
            "cp",
            scatter_dimension=2,
            tiled=True,
        )
        .astype(jnp.float32)
        .reshape(flat_shape)
    )
    gain_three = jnp.sum(grad_mid * hidden_hat, axis=(0, 1))
    grad_hidden = upstream + norm_back(hidden, grad_mid * gain_rows[2])
    gain_two = jnp.sum(grad_hidden * branch_hat, axis=(0, 1))
    grad_branch = norm_back(branch, grad_hidden * gain_rows[1]).astype(jnp.bfloat16)
    out_local = jnp.einsum(
        "tc,te->ce",
        mixed_heads.reshape(token_total, width),
        grad_branch.reshape(token_total, width),
        preferred_element_type=jnp.float32,
    )
    grad_heads = (
        jnp.einsum("rqe,ce->rqc", grad_branch, out_full, preferred_element_type=jnp.float32)
        .astype(jnp.bfloat16)
        .reshape(head_shape)
    )
    delta_sum = jnp.transpose(
        jnp.sum(grad_heads.astype(jnp.float32) * attended, axis=-1), (0, 2, 1)
    )

    def score_grads(block_index):
        scores, allowed = block_scores(block_index)
        probs = jnp.where(allowed, jnp.exp(scores - log_total[..., None]), 0.0)
        first_key = block_index * block_size
        key_block = lax.dynamic_slice_in_dim(key_rows, first_key, block_size, 1)
        value_block = lax.dynamic_slice_in_dim(value_rows, first_key, block_size, 1)
        grad_probs = jnp.einsum(
            "rqhd,rkhd->rhqk", grad_heads, value_block, preferred_element_type=jnp.float32
        )
        grad_scores = (probs * (grad_probs - delta_sum[..., None]) * score_scale).astype(
            jnp.bfloat16
        )
        return (probs, grad_scores, key_block)

    def grad_step(grad_query, block_index):
        probs, grad_scores, key_block = score_grads(block_index)
        grad_query = grad_query + jnp.einsum(
            "rhqk,rkhd->rqhd", grad_scores, key_block, preferred_element_type=jnp.float32
        )
        key_part = jnp.einsum(
            "rhqk,rqhd->rkhd", grad_scores, query_rows, preferred_element_type=jnp.float32
        )
        value_part = jnp.einsum(
            "rhqk,rqhd->rkhd",
            probs.astype(jnp.bfloat16),
            grad_heads,
            preferred_element_type=jnp.float32,
        )
        return (grad_query, (key_part, value_part))

    grad_query, (key_parts, value_parts) = lax.scan(
        grad_step, jnp.zeros(head_shape, jnp.float32), block_range
    )
    key_terms = jnp.moveaxis(key_parts, 0, 1).reshape(group_shape)
    value_terms = jnp.moveaxis(value_parts, 0, 1).reshape(group_shape)
    key_sum, value_sum = (
        lax.psum_scatter(
            key_terms.astype(jnp.bfloat16), "cp", scatter_dimension=2, tiled=True
        ).astype(jnp.float32),
        lax.psum_scatter(
            value_terms.astype(jnp.bfloat16), "cp", scatter_dimension=2, tiled=True
        ).astype(jnp.float32),
    )
    query_unturned = rotate(rounded(grad_query), cosine, -sine_part).reshape(flat_shape)
    key_unturned = rotate(rounded(key_sum.reshape(head_shape)), cosine, -sine_part).reshape(
        flat_shape
    )
    grad_linear = jnp.concatenate(
        [query_unturned, key_unturned, value_sum.reshape(flat_shape)], axis=-1
    ).astype(jnp.bfloat16)
    qkv_local = jnp.einsum(
        "tc,te->ce",
        normed.reshape(token_total, width),
        grad_linear.reshape(token_total, 3 * width),
        preferred_element_type=jnp.float32,
    )
    grad_normed = jnp.einsum(
        "rqe,ce->rqc", grad_linear, qkv_full, preferred_element_type=jnp.float32
    )
    gain_one = jnp.sum(grad_normed * normed_in, axis=(0, 1))
    tokens_grad = (grad_hidden + norm_back(inputs, grad_normed * gain_rows[0])).reshape(
        tokens.shape
    )
    gain_local = jnp.concatenate([gain_one, gain_two, gain_three, gain_four])
    gain_order = jnp.transpose(gain_local.reshape(rows_count, cp_count, -1), (1, 0, 2)).reshape(-1)
    qkv_mid, out_mid, gain_mid = (
        lax.psum_scatter(
            qkv_local.astype(jnp.bfloat16), "cp", scatter_dimension=1, tiled=True
        ).astype(jnp.float32),
        lax.psum_scatter(
            out_local.astype(jnp.bfloat16), "cp", scatter_dimension=1, tiled=True
        ).astype(jnp.float32),
        lax.psum_scatter(
            gain_order.astype(jnp.bfloat16), "cp", scatter_dimension=0, tiled=True
        ).astype(jnp.float32),
    )
    qkv_sum, out_sum, up_sum, down_sum, gain_sum = (
        lax.psum_scatter(
            qkv_mid.astype(jnp.bfloat16), "rows", scatter_dimension=0, tiled=True
        ).astype(jnp.float32),
        lax.psum_scatter(
            out_mid.astype(jnp.bfloat16), "rows", scatter_dimension=0, tiled=True
        ).astype(jnp.float32),
        lax.psum_scatter(
            up_local.astype(jnp.bfloat16), "rows", scatter_dimension=0, tiled=True
        ).astype(jnp.float32),
        lax.psum_scatter(
            down_local.astype(jnp.bfloat16), "rows", scatter_dimension=1, tiled=True
        ).astype(jnp.float32),
        lax.psum_scatter(
            gain_mid.astype(jnp.bfloat16), "rows", scatter_dimension=0, tiled=True
        ).astype(jnp.float32),
    )
    return (mixed, tokens_grad, qkv_sum, out_sum, up_sum, down_sum, gain_sum)


F32 = jnp.float32
BF16 = jnp.bfloat16
VMEM = 56 * 1024 * 1024


def params(grid_rank):
    return pltpu.CompilerParams(
        dimension_semantics=("arbitrary",) * grid_rank, vmem_limit_bytes=VMEM
    )


def work(flops, moved):
    return pl.CostEstimate(flops=flops, bytes_accessed=moved, transcendentals=0)


def turned(x, cosine, sine):
    lane = lax.broadcasted_iota(jnp.int32, x.shape, 1)
    other = jnp.where((lane & 32) == 0, pltpu.roll(x, 96, 1), pltpu.roll(x, 32, 1))
    return x * cosine + other * sine


def attend_kernel(tile, bounds, slot_of, q_ref, k_ref, v_ref, pcol_ref, prow_ref, srow_ref,
                  o_ref, ob_ref, lse_ref, vt_ref):
    i = pl.program_id(1)

    @pl.when(i == 0)
    def _():
        vt_ref[...] = v_ref[...].astype(F32).T.astype(BF16)

    qt = q_ref[...].astype(F32).T
    row = lax.broadcasted_iota(jnp.int32, qt.shape, 0)
    lo = bounds[0, i]
    mid = jnp.minimum(bounds[1, i], i)
    qpos = prow_ref[...]
    qstart = srow_ref[...]
    qh = [jnp.where((row >= 64) == (h == 1), qt, 0.0).astype(BF16) for h in range(2)]

    def step(j, carry, masked):
        at = pl.multiple_of(j * tile, tile)
        k = k_ref[pl.ds(at, tile), :]
        scores = [jnp.dot(k, qh[h], preferred_element_type=F32) for h in range(2)]
        if masked:
            kpos = pcol_ref[pl.ds(at, tile), :]
            allowed = (kpos >= qstart) & (kpos <= qpos)
            scores = [jnp.where(allowed, s, MASKED) for s in scores]
        out = []
        for h in range(2):
            top, total, acc = carry[h]
            new = jnp.maximum(top, jnp.max(scores[h], axis=0, keepdims=True))
            p = jnp.exp(scores[h] - new)
            keep = jnp.exp(top - new)
            total = total * keep + jnp.sum(p, axis=0, keepdims=True)
            acc = acc * keep + jnp.dot(
                vt_ref[h * 64 : h * 64 + 64, pl.ds(at, tile)], p.astype(BF16),
                preferred_element_type=F32,
            )
            out.append((new, total, acc))
        return tuple(out)

    start = (
        jnp.full((1, tile), MASKED, F32), jnp.zeros((1, tile), F32), jnp.zeros((64, tile), F32)
    )
    carry = step(i, (start, start), True)
    carry = lax.fori_loop(lo, mid, functools.partial(step, masked=True), carry)
    carry = lax.fori_loop(mid, i, functools.partial(step, masked=False), carry)
    parts = []
    for h in range(2):
        top, total, acc = carry[h]
        lse_ref[0, h : h + 1, :] = top + jnp.log(total)
        parts.append(acc / total)
    out = jnp.concatenate(parts, axis=0).T
    o_ref[...] = out
    span = ob_ref.shape[1]
    for b in range(tile // span):
        ob_ref[slot_of[i * (tile // span) + b]] = out[b * span : (b + 1) * span].astype(BF16)


def attend(q, k, v, pcol, prow, srow, bounds, slot_of, tile):
    rows, width = q.shape
    blocks = slot_of.shape[0]
    span = rows // blocks
    pairs = width // 128
    count = rows // tile
    grid_spec = pltpu.PrefetchScalarGridSpec(
        num_scalar_prefetch=2,
        grid=(pairs, count),
        in_specs=[
            pl.BlockSpec((tile, 128), lambda p, i, b, t: (i, p)),
            pl.BlockSpec((rows, 128), lambda p, i, b, t: (0, p)),
            pl.BlockSpec((rows, 128), lambda p, i, b, t: (0, p)),
            pl.BlockSpec((rows, 1), lambda p, i, b, t: (0, 0)),
            pl.BlockSpec((1, tile), lambda p, i, b, t: (0, i)),
            pl.BlockSpec((1, tile), lambda p, i, b, t: (0, i)),
        ],
        out_specs=[
            pl.BlockSpec((tile, 128), lambda p, i, b, t: (i, p)),
            pl.BlockSpec((blocks, span, 128), lambda p, i, b, t: (0, 0, p)),
            pl.BlockSpec((1, 2, tile), lambda p, i, b, t: (p, 0, i)),
        ],
        scratch_shapes=[pltpu.VMEM((128, rows), BF16)],
    )
    return pl.pallas_call(
        functools.partial(attend_kernel, tile),
        grid_spec=grid_spec,
        out_shape=[
            jax.ShapeDtypeStruct((rows, width), F32),
            jax.ShapeDtypeStruct((blocks, span, width), BF16),
            jax.ShapeDtypeStruct((pairs, 2, rows), F32),
        ],
        compiler_params=params(2),
        cost_estimate=work(3 * rows * rows * width, 8 * rows * width),
        name="attend",
    )(bounds, slot_of, q, k, v, pcol, prow, srow)


def attend_back_kernel(tile, bounds, slot_of, q_ref, k_ref, v_ref, do_ref, o_ref, lse_ref, pcol_ref,
                       prow_ref, srow_ref, cos_ref, sin_ref, g_ref,
                       qm, dom, qtm, dotm, delta, dqt):
    j = pl.program_id(1)
    count = pl.num_programs(1)
    rows = q_ref.shape[0]

    span = do_ref.shape[1]

    @pl.when(j == 0)
    def _():
        for t in range(rows // tile):
            part = pl.ds(t * tile, tile)
            q = q_ref[part, :].astype(F32)
            do = jnp.concatenate(
                [do_ref[slot_of[t * tile // span + b]] for b in range(tile // span)], axis=0
            ).astype(F32)
            qt, dot = q.T, do.T
            lane = lax.broadcasted_iota(jnp.int32, q.shape, 1)
            row = lax.broadcasted_iota(jnp.int32, qt.shape, 0)
            prod = dot * o_ref[part, :].T
            for h in range(2):
                mine = (lane >= 64) == (h == 1)
                mine_t = (row >= 64) == (h == 1)
                qm[h, part, :] = jnp.where(mine, q, 0.0).astype(BF16)
                dom[h, part, :] = jnp.where(mine, do, 0.0).astype(BF16)
                qtm[h, :, part] = jnp.where(mine_t, qt, 0.0).astype(BF16)
                dotm[h, :, part] = jnp.where(mine_t, dot, 0.0).astype(BF16)
                delta[h : h + 1, part] = jnp.sum(
                    prod[h * 64 : h * 64 + 64], axis=0, keepdims=True
                )
        dqt[...] = jnp.zeros_like(dqt)

    here = pl.ds(pl.multiple_of(j * tile, tile), tile)
    k = k_ref[here, :]
    v = v_ref[here, :]
    kt = k.astype(F32).T.astype(BF16)
    kpos = pcol_ref[here, :]
    full = jnp.maximum(bounds[2, j], j + 1)
    end = bounds[3, j]

    def step(i, carry, masked):
        dk, dv = carry
        part = pl.ds(pl.multiple_of(i * tile, tile), tile)
        if masked:
            allowed = (kpos >= srow_ref[:, part]) & (kpos <= prow_ref[:, part])
        for h in range(2):
            s = jnp.dot(k, qtm[h, :, part], preferred_element_type=F32)
            p = jnp.exp(s - lse_ref[0, h : h + 1, part])
            if masked:
                p = jnp.where(allowed, p, 0.0)
            dp = jnp.dot(v, dotm[h, :, part], preferred_element_type=F32)
            ds = (p * (dp - delta[h : h + 1, part])).astype(BF16)
            dv = dv + jnp.dot(p.astype(BF16), dom[h, part, :], preferred_element_type=F32)
            dk = dk + jnp.dot(ds, qm[h, part, :], preferred_element_type=F32)
            dqt[h * 64 : h * 64 + 64, part] += jnp.dot(
                kt[h * 64 : h * 64 + 64, :], ds, preferred_element_type=F32
            )
        return dk, dv

    carry = (jnp.zeros((tile, 128), F32), jnp.zeros((tile, 128), F32))
    carry = step(j, carry, True)
    carry = lax.fori_loop(j + 1, full, functools.partial(step, masked=False), carry)
    carry = lax.fori_loop(full, end, functools.partial(step, masked=True), carry)
    dk, dv = carry

    def unturned(x, at):
        x = x.astype(BF16).astype(F32)
        return turned(x, cos_ref[at, :], -sin_ref[at, :]).astype(BF16)

    g_ref[1, here, :] = unturned(dk, here)
    g_ref[2, here, :] = dv.astype(BF16)

    @pl.when(j == count - 1)
    def _():
        for t in range(rows // tile):
            part = pl.ds(t * tile, tile)
            g_ref[0, part, :] = unturned(dqt[:, part].T * 0.125, part)


def attend_back(pair, q, k, v, do, o, lse, pcol, prow, srow, cosine, sine, bounds, slot_of, tile):
    rows, width = q.shape
    blocks, span, _ = do.shape
    count = rows // tile
    whole = pl.BlockSpec((rows, 128), lambda p, j, b, t: (0, pair))
    table = pl.BlockSpec((rows, 128), lambda p, j, b, t: (0, 0))
    line = pl.BlockSpec((1, rows), lambda p, j, b, t: (0, 0))
    grid_spec = pltpu.PrefetchScalarGridSpec(
        num_scalar_prefetch=2,
        grid=(1, count),
        in_specs=[
            whole, whole, whole,
            pl.BlockSpec((blocks, span, 128), lambda p, j, b, t: (0, 0, pair)),
            whole,
            pl.BlockSpec((1, 2, rows), lambda p, j, b, t: (pair, 0, 0)),
            pl.BlockSpec((rows, 1), lambda p, j, b, t: (0, 0)),
            line, line, table, table,
        ],
        out_specs=pl.BlockSpec((3, rows, 128), lambda p, j, b, t: (0, 0, 0)),
        scratch_shapes=[
            pltpu.VMEM((2, rows, 128), BF16), pltpu.VMEM((2, rows, 128), BF16),
            pltpu.VMEM((2, 128, rows), BF16), pltpu.VMEM((2, 128, rows), BF16),
            pltpu.VMEM((2, rows), F32), pltpu.VMEM((128, rows), F32),
        ],
    )
    return pl.pallas_call(
        functools.partial(attend_back_kernel, tile),
        grid_spec=grid_spec,
        out_shape=jax.ShapeDtypeStruct((3, rows, 128), BF16),
        compiler_params=params(2),
        cost_estimate=work(7 * rows * rows * 128, 18 * rows * 128),
        name="attend_back",
    )(bounds, slot_of, q, k, v, do, o, lse, pcol, prow, srow, cosine, sine)


def tile_bounds(starts_nat, tile):
    rows = starts_nat.shape[0]
    count = rows // tile
    tiles = starts_nat.reshape(count, tile)
    first, last = tiles[:, 0], tiles[:, -1]
    at = jnp.arange(count, dtype=jnp.int32) * tile
    lo = first // tile
    mid = (last + tile - 1) // tile
    full = jnp.sum((last[None, :] <= at[:, None]).astype(jnp.int32), axis=1)
    end = jnp.sum((first[None, :] <= at[:, None] + tile - 1).astype(jnp.int32), axis=1)
    return jnp.stack([lo, mid, full, end]).astype(jnp.int32)


def normalized(x):
    centred = x - jnp.mean(x, axis=1, keepdims=True)
    scale = lax.rsqrt(jnp.mean(centred * centred, axis=1, keepdims=True) + NORM_EPS)
    return centred * scale, scale


def normalized_back(hat, scale, upstream):
    level = jnp.mean(upstream, axis=1, keepdims=True)
    slant = jnp.mean(upstream * hat, axis=1, keepdims=True)
    return scale * (upstream - level - hat * slant)


def dot_nt(a, b):
    return lax.dot_general(a, b, (((1,), (1,)), ((), ())), preferred_element_type=F32)


def call(kernel, name, grid, tables, ins, outs, scratch, flops, *arrays):
    moved = sum(math.prod(a.shape) * a.dtype.itemsize for a in arrays)
    moved += sum(math.prod(s.shape) * s.dtype.itemsize for s, _ in outs)
    return pl.pallas_call(
        kernel,
        grid_spec=pltpu.PrefetchScalarGridSpec(
            num_scalar_prefetch=len(tables),
            grid=grid,
            in_specs=ins,
            out_specs=[spec for _, spec in outs],
            scratch_shapes=scratch,
        ),
        out_shape=[shape for shape, _ in outs],
        compiler_params=params(len(grid)),
        cost_estimate=work(flops, moved),
        name=name,
    )(*tables, *arrays)


def shaped(dtype, *shape):
    return jax.ShapeDtypeStruct(shape, dtype)


def fixed(*shape):
    return pl.BlockSpec(shape, lambda *_: (0,) * len(shape))


def project_kernel(slot_of, x0, x1, x2, x3, gain_ref, w_ref, cos_ref, sin_ref,
                   q_ref, k_ref, v_ref, n_ref):
    which = slot_of[pl.program_id(0)] >> 1
    width = q_ref.shape[1]
    near = jnp.where(which == 0, x0[0], x1[0])
    far = jnp.where(which == 2, x2[0], x3[0])
    x = jnp.where(which < 2, near, far).astype(F32)
    normed = (normalized(x)[0] * gain_ref[0:1, :]).astype(BF16)
    n_ref[0] = normed
    linear = jnp.dot(normed, w_ref[...], preferred_element_type=F32)
    for at in range(0, width, 128):
        q = turned(linear[:, at : at + 128], cos_ref[...], sin_ref[...])
        k = turned(linear[:, width + at : width + at + 128], cos_ref[...], sin_ref[...])
        q_ref[:, at : at + 128] = q.astype(BF16) * jnp.asarray(0.125, BF16)
        k_ref[:, at : at + 128] = k.astype(BF16)
    v_ref[...] = linear[:, 2 * width :].astype(BF16)


def project(parts, gains, w, cosine, sine, slot_of):
    count = slot_of.shape[0]
    _, rows, depth = parts[0].shape
    width = w.shape[1] // 3
    piece = pl.BlockSpec((1, rows, depth), lambda i, t: (t[i] & 1, 0, 0))
    angle = pl.BlockSpec((rows, 128), lambda i, t: (i, 0))
    out = shaped(BF16, count * rows, width), pl.BlockSpec((rows, width), lambda i, t: (i, 0))
    normed = (
        shaped(BF16, count, rows, depth),
        pl.BlockSpec((1, rows, depth), lambda i, t: (t[i], 0, 0)),
    )
    return call(
        project_kernel, "project", (count,), [slot_of],
        [piece] * 4 + [fixed(*gains.shape), fixed(*w.shape), angle, angle],
        [out, out, out, normed], [], 2 * count * rows * depth * 3 * width,
        *parts, gains, w, cosine, sine,
    )


def side_by_side(first, second):
    return jnp.concatenate([half[n] for n in range(3) for half in (first, second)], axis=1)


def project_back_kernel(table, g0_ref, g1_ref, w_ref, o_ref):
    g = side_by_side(g0_ref, g1_ref)
    o_ref[0] = dot_nt(g, w_ref[...]).astype(o_ref.dtype)


def project_back(grads, w, table, rows, dtype):
    count = table.shape[0]
    depth, width = w.shape
    piece = pl.BlockSpec((3, rows, width // 6), lambda i, t: (0, t[i], 0))
    return call(
        project_back_kernel, "project_back", (count,), [table],
        [piece, piece, fixed(*w.shape)],
        [(shaped(dtype, count, rows, depth), pl.BlockSpec((1, rows, depth), lambda i, t: (i, 0, 0)))],
        [], 2 * count * rows * depth * width, *grads, w,
    )[0]


def project_weights_kernel(slot_of, place, x_ref, g0_ref, g1_ref, w_ref, ac, as_, bc, bs, gain_ref, total):
    i = pl.program_id(0)

    @pl.when(i == 0)
    def _():
        total[...] = jnp.zeros_like(total)

    g = side_by_side(g0_ref, g1_ref)
    total[...] += lax.dot_general(
        x_ref[0], g, (((0,), (0,)), ((), ())), preferred_element_type=F32
    )

    @pl.when(i == pl.num_programs(0) - 1)
    def _():
        rows, half = ac.shape[1:]
        for r in range(2):
            for out, flips in ((ac, 2 * r), (as_, 1 + 2 * r)):
                at = pl.ds(pl.multiple_of((place[0] ^ flips) * rows, rows), rows)
                out[r] = total[at, :half].astype(BF16)
            for out, flips in ((bc, r), (bs, 2 + r)):
                at = pl.ds(pl.multiple_of((place[0] ^ flips) * rows, rows), rows)
                out[r] = total[at, half:].astype(BF16)
        gain_ref[...] = jnp.sum(total[...] * w_ref[...].astype(F32), axis=1, keepdims=True)


def project_weights(x, grads, w, slot_of, place):
    count, rows, depth = x.shape
    width = w.shape[1]
    grad = pl.BlockSpec((3, rows, width // 6), lambda i, t, p: (0, i, 0))
    quarter = depth // 4
    piece = shaped(BF16, 2, quarter, width // 2), fixed(2, quarter, width // 2)
    return call(
        project_weights_kernel, "project_weights", (count,), [slot_of, place],
        [
            pl.BlockSpec((1, rows, depth), lambda i, t, p: (t[i], 0, 0)),
            grad, grad, fixed(*w.shape),
        ],
        [piece, piece, piece, piece, (shaped(F32, depth, 1), fixed(depth, 1))],
        [pltpu.VMEM((depth, width), F32)], 2 * count * rows * depth * width,
        x, *grads, w,
    )


def mix_kernel(group, own, near, far, both, w_ref, x_ref, gain_ref,
               heads_ref, hat_ref, scale_ref, hidden_ref, mid_ref):
    width = own.shape[2]
    for r, piece in enumerate((own[0], near[0], far[0], both[0])):
        at = pl.ds(pl.multiple_of((group[0] ^ r) * width, width), width)
        heads_ref[:, at] = piece
    branch = jnp.dot(heads_ref[...], w_ref[...], preferred_element_type=F32)
    hat, scale = normalized(branch)
    hidden = x_ref[0].astype(F32) + hat * gain_ref[1:2, :]
    hat_ref[...] = hat
    scale_ref[...] = scale
    hidden_ref[...] = hidden
    mid_ref[...] = (normalized(hidden)[0] * gain_ref[2:3, :]).astype(BF16)


def mix(group, local, near, far, both, w, x, gains):
    _, rows, part = local.shape
    count, _, width = x.shape
    block = pl.BlockSpec((1, rows, part), lambda i, g: (i, 0, 0))
    row = pl.BlockSpec((rows, width), lambda i, g: (i, 0))
    total = count * rows
    return call(
        mix_kernel, "mix", (count,), [group],
        [
            block, block, block, block, fixed(*w.shape), pl.BlockSpec((1, rows, width), lambda i, g: (i, 0, 0)),
            fixed(*gains.shape),
        ],
        [
            (shaped(BF16, total, width), row),
            (shaped(F32, total, width), row),
            (shaped(F32, total, 1), pl.BlockSpec((rows, 1), lambda i, g: (i, 0))),
            (shaped(F32, total, width), row),
            (shaped(BF16, total, width), row),
        ],
        [], 2 * total * width * width, local, near, far, both, w, x, gains,
    )


def finish_kernel(terms_ref, sent_ref, hidden_ref, dy_ref, gain_ref, mixed_ref, grad_ref, sum_ref):
    down = terms_ref[...] + sent_ref[...].astype(F32)
    hat, scale = normalized(down)
    gain = gain_ref[3:4, :]
    dy = dy_ref[...].astype(F32)
    mixed_ref[...] = (hidden_ref[...] + hat * gain).astype(BF16)
    grad_ref[...] = normalized_back(hat, scale, dy * gain).astype(BF16)

    @pl.when(pl.program_id(0) == 0)
    def _():
        sum_ref[...] = jnp.zeros_like(sum_ref)

    sum_ref[...] += jnp.sum(dy * hat, axis=0, keepdims=True)


def finish(terms, sent, hidden, dy, gains):
    total, width = terms.shape
    rows = total // 2
    row = pl.BlockSpec((rows, width), lambda i: (i, 0))
    return call(
        finish_kernel, "finish", (2,), [],
        [row, row, row, row, fixed(*gains.shape)],
        [
            (shaped(BF16, total, width), row), (shaped(BF16, total, width), row),
            (shaped(F32, 1, width), fixed(1, width)),
        ],
        [], 20 * total * width, terms, sent, hidden, dy, gains,
    )


def turn_kernel(group, terms_ref, sent_ref, hidden_ref, dy_ref, hat_ref, scale_ref, w_ref, gain_ref,
                keep_ref, branch_ref, heads_ref, three_ref, two_ref):
    upstream = terms_ref[...] + sent_ref[...].astype(F32)
    hat, scale = normalized(hidden_ref[...])

    @pl.when(pl.program_id(0) == 0)
    def _():
        three_ref[...] = jnp.zeros_like(three_ref)
        two_ref[...] = jnp.zeros_like(two_ref)

    three_ref[...] += jnp.sum(upstream * hat, axis=0, keepdims=True)
    grad = dy_ref[...].astype(F32) + normalized_back(hat, scale, upstream * gain_ref[2:3, :])
    keep_ref[...] = grad
    branch_hat = hat_ref[...]
    two_ref[...] += jnp.sum(grad * branch_hat, axis=0, keepdims=True)
    branch = normalized_back(branch_hat, scale_ref[...], grad * gain_ref[1:2, :]).astype(BF16)
    branch_ref[...] = branch
    part = heads_ref.shape[3]
    for r in range(4):
        at = pl.ds(pl.multiple_of((group[0] ^ r) * part, part), part)
        heads_ref[r, 0] = dot_nt(branch, w_ref[at, :]).astype(BF16)


def turn(group, terms, sent, hidden, dy, hat, scale, w, gains):
    total, width = terms.shape
    rows = total // 2
    part = width // 4
    row = pl.BlockSpec((rows, width), lambda i, g: (i, 0))
    return call(
        turn_kernel, "turn", (2,), [group],
        [
            row, row, row, row, row, pl.BlockSpec((rows, 1), lambda i, g: (i, 0)),
            fixed(*w.shape), fixed(*gains.shape),
        ],
        [
            (shaped(F32, total, width), row), (shaped(BF16, total, width), row),
            (
                shaped(BF16, 4, 2, rows, part),
                pl.BlockSpec((4, 1, rows, part), lambda i, g: (0, i, 0, 0)),
            ),
            (shaped(F32, 1, width), fixed(1, width)), (shaped(F32, 1, width), fixed(1, width)),
        ],
        [], 2 * total * width * width, terms, sent, hidden, dy, hat, scale, w, gains,
    )


def end_kernel(keep_ref, near_ref, far_ref, x_ref, grad_ref, gain_ref, o_ref):
    upstream = keep_ref[...] + near_ref[...].astype(F32) + far_ref[...].astype(F32)
    hat, scale = normalized(x_ref[...].astype(F32))
    grad = grad_ref[...] + normalized_back(hat, scale, upstream * gain_ref[0:1, :])
    o_ref[...] = grad.astype(BF16)


def end(keep, near, far, x, grad, gains):
    rows, width = x.shape
    return call(
        end_kernel, "end", (1,), [],
        [fixed(rows, width)] * 5 + [fixed(*gains.shape)],
        [(shaped(BF16, rows, width), fixed(rows, width))],
        [], 20 * rows * width, keep, near, far, x, grad, gains,
    )[0]


def flip(x, axis, bit):
    return lax.ppermute(x, axis, [(i, i ^ bit) for i in range(lax.axis_size(axis))])


def swap(x):
    cp = lax.axis_size("cp")
    half = cp // 2
    pairs = []
    for z in range(half):
        low, high = cp + z, z + half
        pairs += [(low, high), (high, low), (z, z), (cp + high, cp + high)]
    return lax.ppermute(x, ("core", "cp"), pairs)


def ordered(first, mine, other, axis):
    return jnp.concatenate(
        [jnp.where(first, mine, other), jnp.where(first, other, mine)], axis=axis
    )


def placed(first, mine, other, at):
    return ordered(first, jnp.expand_dims(mine, at), jnp.expand_dims(other, at), at)


def after(x, *others):
    return lax.optimization_barrier((x, *others))[0]


def all_after(group, *others):
    return lax.optimization_barrier((*group, *others))[: len(group)]


def plain(x):
    return with_layout_constraint(x, Layout(tuple(range(x.ndim))))


def total(a, b):
    return (a.astype(F32) + b.astype(F32)).astype(BF16)


def flip_both(x):
    cp = lax.axis_size("cp")
    return lax.ppermute(
        x, ("core", "cp"), [(c * cp + z, (1 - c) * cp + (z ^ 1)) for c in range(2) for z in range(cp)]
    )


def dot(a, b, dims):
    return lax.dot_general(a, b, ((dims[:1], dims[1:]), ((), ())), preferred_element_type=F32)


def gelu_and_slope(u):
    c = math.sqrt(2.0 / math.pi)
    square = u * u
    t = jnp.tanh(u * (c + (c * 0.044715) * square))
    half = 0.5 + 0.5 * t
    slope = half + (0.5 * u) * (1.0 - t * t) * (c + (3.0 * 0.044715 * c) * square)
    return lax.optimization_barrier(((u * half).astype(BF16), slope.astype(BF16)))


def pick(x, at, axis):
    return lax.dynamic_index_in_dim(x, at, axis, False)


def widened(z, x):
    other = flip(x, "cp", 1)
    first, second = jnp.where(z & 1 == 0, x, other), jnp.where(z & 1 == 0, other, x)
    half = x.shape[1] // 2
    return jnp.concatenate(
        [first[:, :half], second[:, :half], first[:, half:], second[:, half:]], axis=1
    )


def body(tokens, doc_starts, qkv_weight, out_weight, up_weight, down_weight, norm_gains, cotangent):
    xy, core, z = lax.axis_index("xy"), lax.axis_index("core"), lax.axis_index("cp")
    xy_count, cp_count = lax.axis_size("xy"), lax.axis_size("cp")
    _, _, span, width = tokens.shape
    blocks = 2 * cp_count
    row_len = blocks * span
    own = 2 * span
    parity = z & 1
    group = 2 * parity + core
    part = width // cp_count
    hidden_part = up_weight.shape[1] // 2
    lines_each = width // xy_count
    lines = lines_each // 2
    here = jnp.reshape(xy, (1,)).astype(jnp.int32)
    group_at = jnp.reshape(group, (1,)).astype(jnp.int32)

    w = jnp.concatenate([qkv_weight, out_weight], axis=1)
    gain_rows = jnp.zeros((16, w.shape[1]), BF16)
    gain_rows = lax.dynamic_update_slice(gain_rows, norm_gains[None], (0, 0))
    w = jnp.concatenate([w, gain_rows])
    x = tokens[0]
    w_far = flip(w, "cp", 2)
    x_half = [swap(x[0]), swap(x[1])]

    up_weight, down_weight = all_after((up_weight, down_weight), w_far)

    def half_of(which):
        up = lax.dynamic_slice_in_dim(up_weight, which * hidden_part, hidden_part, 1)
        down = lax.dynamic_slice_in_dim(down_weight, which * hidden_part, hidden_part, 0)
        return plain(jnp.stack([up, down.T]))

    ffn = ordered(core == 0, half_of(core), flip(half_of(1 - core), "core", 1), 1)

    def paired(mine, other):
        return jnp.concatenate(
            [jnp.where(z & 2 == 0, mine, other), jnp.where(z & 2 == 0, other, mine)], axis=1
        )

    w = placed(z & 2 == 0, w, w_far, 0)
    w = placed(z & 1 == 0, w, flip(w, "cp", 1), 1)
    x_half[0] = after(x_half[0], w)
    z_half = [flip(x_half[0], "cp", 1), flip(x_half[1], "cp", 1)]
    up_lines = after(ffn[0], x_half[1])
    up_lines = paired(up_lines, flip(up_lines, "cp", 2))

    gain_rows = jnp.zeros((16, 3 * part), BF16)
    gain_rows = lax.dynamic_update_slice(
        gain_rows, w[:, :, lines, : norm_gains.shape[0]].reshape(cp_count, -1), (0, 0)
    )
    out_w = jnp.concatenate([w[a, b, :lines, 3 * part :] for a in range(2) for b in range(2)], axis=1)

    def columns(of):
        picked = []
        for third in range(3):
            block = third * cp_count + of
            at = (block // 6, (block // 3) & 1, 0, (block % 3) * part)
            picked.append(lax.dynamic_slice(w, at, (1, 1, lines, part))[0, 0])
        return jnp.concatenate([jnp.concatenate(picked, axis=1), gain_rows])

    qkv = placed(core == 0, columns(group), flip(columns(group ^ 1), "core", 1), 0)
    cut = qkv.shape[2] // 2
    low, high = qkv[:, :, :cut], qkv[:, :, cut:]
    low = placed(xy & 1 == 0, low, flip(low, "xy", 1), 0)
    high = placed(xy & 2 == 0, high, flip(high, "xy", 2), 0)
    low = placed(xy & 2 == 0, low, flip(low, "xy", 2), 0)
    high = placed(xy & 1 == 0, high, flip(high, "xy", 1), 1)
    qkv = jnp.concatenate([low[:, :, :, :lines], high[:, :, :, :lines]], axis=4)
    qkv = qkv.reshape(width, 3 * part)
    gains = low[:, :, :, lines : lines + cp_count, : norm_gains.shape[0]]
    gains = gains.reshape(4, width).astype(F32)

    x = jnp.stack(x_half)
    x_core = flip(x, "core", 1)
    x_chip = jnp.stack(z_half)
    x_both = flip(x_chip, "core", 1)
    other_starts = flip(after(doc_starts, w_far), "core", 1)
    starts = jnp.where(core == z // (cp_count // 2), doc_starts, other_starts)[0]

    up_lines = widened(z, after(up_lines, x_chip))
    up_full = lax.all_gather(after(up_lines, qkv), "xy", axis=0, tiled=True)
    down_lines = after(ffn[1], x_chip)
    down_lines = paired(down_lines, flip(down_lines, "cp", 2))
    out_w = after(out_w, x_chip)[None]
    out_w = ordered(xy & 1 == 0, out_w, flip(out_w, "xy", 1), 0)

    block_id = jnp.arange(blocks, dtype=jnp.int32)[:, None]
    inside = jnp.arange(span, dtype=jnp.int32)[None, :]
    late = block_id >= cp_count
    positions = (block_id * span + jnp.where(late, span - 1 - inside, inside)).reshape(-1)

    def starts_at(at):
        return jnp.max(jnp.where(starts[None, :] <= at[:, None], starts[None, :], 0), axis=1)

    row_start = starts_at(positions)
    tile = min(512, row_len)
    bounds = tile_bounds(starts_at(jnp.arange(row_len, dtype=jnp.int32)), tile)
    freq = jnp.exp(
        -math.log(10000.0) * 2.0 * jnp.arange(HEAD_DIM // 2, dtype=F32) / HEAD_DIM
    )
    angles = (positions - row_start).astype(F32)[:, None] * freq
    cosine, sine = jnp.cos(angles), jnp.sin(angles)
    cosine = jnp.tile(cosine, (1, 4))
    sine = jnp.tile(jnp.concatenate([-sine, sine], axis=1), (1, 2))
    pcol, prow, srow = positions[:, None], positions[None, :], row_start[None, :]
    chunk = jnp.arange(blocks, dtype=jnp.int32)
    chunk = jnp.where(chunk < cp_count, chunk, blocks - 1 - chunk)
    slot_of = (
        2 * (2 * ((chunk >> 1) ^ core) + ((chunk & 1) ^ parity))
        + (jnp.arange(blocks) >= cp_count)
    ).astype(jnp.int32)
    slot = jnp.arange(blocks, dtype=jnp.int32)
    relative = slot >> 1
    chunk_of = 2 * ((relative >> 1) ^ core) + ((relative & 1) ^ parity)
    block_of = jnp.where(slot & 1 == 0, chunk_of, blocks - 1 - chunk_of).astype(jnp.int32)

    q, k, v, normed = project([x, x_chip, x_core, x_both], gains, qkv, cosine, sine, slot_of)
    down_lines, out_w = all_after((down_lines, out_w), q)
    down_lines = widened(z, down_lines)
    out_w = ordered(xy & 2 == 0, out_w, flip(out_w, "xy", 2), 0)
    attended, local, lse = attend(q, k, v, pcol, prow, srow, bounds, slot_of, tile)
    down_lines, out_w, dy = all_after((down_lines, out_w, cotangent), local)
    down_full = lax.all_gather(down_lines, "xy", axis=0, tiled=True)
    out_w = placed(core == 0, out_w, flip(out_w, "core", 1), 1).reshape(width, width)
    heads, branch_hat, branch_scale, hidden, mid = mix(
        group_at, local[:2], flip(local[4:6], "core", 1), flip(local[2:4], "cp", 1),
        flip_both(local[6:]), out_w, x, gains,
    )

    dy = swap(after(dy.reshape(own, width), mid))

    ffn_in = jnp.concatenate([mid, flip(mid, "core", 1)])
    act, slope = gelu_and_slope(dot(ffn_in, up_full, (1, 0)))
    sent = flip(dot(act[own:], down_full, (1, 1)).astype(BF16), "core", 1)
    terms = dot(act[:own], down_full, (1, 1))
    mixed, grad_down, gain_four = finish(terms, sent, hidden, dy, gains)
    grad_down = jnp.concatenate([grad_down, flip(grad_down, "core", 1)])

    x_bit, y_bit = xy & 1, xy >> 1

    def cut_first(grads, extra):
        grads = grads.reshape(2, 2, 2, lines, -1)
        low, high = grads[:, :, 0], grads[:, :, 1]
        if extra is not None:
            extra = extra.reshape(2, 2, 2, -1, extra.shape[-1])
            low = jnp.concatenate([low, extra[:, :, 0]], axis=2)
            high = jnp.concatenate([high, extra[:, :, 1]], axis=2)
        away = pick(low, 1 - x_bit, 1), pick(high, 1 - y_bit, 0)
        return (pick(low, x_bit, 1), pick(high, y_bit, 0)), away

    def send_first(away):
        return flip(away[0], "xy", 1), flip(away[1], "xy", 2)

    def cut_second(near, far):
        away = (
            total(pick(near[0], 1 - y_bit, 0), pick(far[0], 1 - y_bit, 0)),
            total(pick(near[1], 1 - x_bit, 0), pick(far[1], 1 - x_bit, 0)),
        )
        near = (
            total(pick(near[0], y_bit, 0), pick(far[0], y_bit, 0)),
            total(pick(near[1], x_bit, 0), pick(far[1], x_bit, 0)),
        )
        return near, away

    def send_second(away):
        return flip(away[0], "xy", 2), flip(away[1], "xy", 1)

    def cut_third(near, far):
        sums = jnp.concatenate([total(a, b) for a, b in zip(near, far)])
        blocks_of = [sums[:, n * hidden_part : (n + 1) * hidden_part] for n in range(cp_count)]
        odd = jnp.stack([blocks_of[1], blocks_of[3]])
        even = jnp.stack([blocks_of[0], blocks_of[2]])
        return jnp.where(parity == 0, even, odd), jnp.where(parity == 0, odd, even)

    def cut_fourth(near, far):
        return (
            total(pick(near, z >> 1, 0), pick(far, z >> 1, 0)),
            total(pick(near, 1 - (z >> 1), 0), pick(far, 1 - (z >> 1), 0)),
        )

    down_local = plain(dot(grad_down, act, (0, 0)).astype(BF16))
    down_near, down_away = cut_first(down_local, None)
    down_far = send_first(down_away)
    grad_up = dot(after(grad_down, *down_away), down_full, (1, 0)) * slope.astype(F32)
    grad_up = grad_up.astype(BF16)
    sent = flip(dot(grad_up[own:], up_full, (1, 1)).astype(BF16), "core", 1)
    terms = dot(grad_up[:own], up_full, (1, 1))
    grad_hidden, grad_branch, grad_heads, gain_three, gain_two = turn(
        group_at, terms, sent, hidden, dy, branch_hat, branch_scale, out_w, gains
    )

    grad_local = [
        grad_heads[0], flip(grad_heads[2], "cp", 1), flip(grad_heads[1], "core", 1),
        flip_both(grad_heads[3]),
    ]
    out_local = dot(heads, grad_branch, (0, 0)).astype(BF16)
    out_local = out_local.reshape(xy_count, 2, lines, width)
    out_away = pick(out_local, 1 - core, 1)
    out_sum = flip(out_away, "core", 1)
    down_far = all_after(down_far, grad_heads)
    down_near, down_away = cut_second(down_near, down_far)
    down_far = send_second(down_away)
    up_local = plain(dot(after(ffn_in, out_away), grad_up, (0, 0)).astype(BF16))
    out_sum = total(pick(out_local, core, 1), out_sum)
    out_sum = out_sum.reshape(xy_count, 2, lines // 2, cp_count, part)
    out_sum = jnp.concatenate(
        [out_sum[:, h, :, n] for n in range(cp_count) for h in range(2)], axis=-1
    )
    up_near, up_away = cut_first(up_local, out_sum)
    up_far = send_first(up_away)
    grad_local = after(jnp.concatenate(grad_local), *up_away, *down_away)

    tables = (pcol, prow, srow, cosine, sine, bounds, slot_of, tile)
    first = attend_back(0, q, k, v, grad_local, attended, lse, *tables)
    down_far = all_after(down_far, first)
    down_near, down_away = cut_third(down_near, down_far)
    down_far = flip(down_away, "cp", 1)
    second = attend_back(1, q, k, v, after(grad_local, first, down_away), attended, lse, *tables)
    send = project_back((first, second), qkv, block_of[4:], span, BF16)
    sent = flip(send, "core", 1)
    up_far = all_after(up_far, send)
    up_near, up_away = cut_second(up_near, up_far)
    up_far = send_second(up_away)
    down_far = after(down_far, send)
    down_near, down_away = cut_fourth(down_near, down_far)
    down_far = flip(down_away, "cp", 2)
    keep = project_back((after(first, send, *up_away, down_away), second), qkv, block_of[:4], span, F32)
    far_away = [total(keep[2 + h], sent[2 + h]) for h in range(2)]
    far = [flip(a, "cp", 1) for a in far_away]
    low, low_send, high, high_send, gain_one = project_weights(
        normed, (after(first, *far_away), second), qkv, slot_of, here
    )
    low_far, high_far = flip(low_send, "xy", 1), flip(high_send, "xy", 2)
    up_far = all_after(up_far, low_send)
    up_near, up_away = cut_third(up_near, up_far)
    up_far = flip(up_away, "cp", 1)
    tokens_grad = []
    for h in range(2):
        grad = end(
            keep[h], sent[h], far[h], x[h], grad_hidden[h * span : (h + 1) * span], gains
        )
        tokens_grad.append(grad)
    ended = tuple(tokens_grad)
    tokens_grad = [swap(grad) for grad in tokens_grad]
    tokens_grad = jnp.stack(tokens_grad).astype(F32).reshape(tokens.shape)
    mixed = swap(after(mixed, send)).reshape(tokens.shape)

    low_send, low = total(low[1], low_far[1]), total(low[0], low_far[0])
    high_send, high = total(high[1], high_far[1]), total(high[0], high_far[0])
    low = total(low, flip(low_send, "xy", 2))
    high = total(high, flip(high_send, "xy", 1))
    both = jnp.concatenate([low, high], axis=1).reshape(2, lines, 3 * part)
    mine, other = pick(both, core, 0), flip(pick(both, 1 - core, 0), "core", 1)
    both = placed(core == 0, mine, other, 0).reshape(2, lines, 3, part).transpose(2, 0, 1, 3)
    right = z >= 2
    even = parity == 0
    send_at = (
        jnp.where(right, 0, jnp.where(even, 2, 1)), jnp.where(right, jnp.where(even, 1, 0), 2)
    )
    keep_at = (
        jnp.where(right, jnp.where(even, 2, 1), 0), jnp.where(right, 2, jnp.where(even, 1, 0))
    )
    sent = flip(jnp.stack([pick(both, at, 0) for at in send_at]), "cp", 2)
    both = total(jnp.stack([pick(both, at, 0) for at in keep_at]), sent)
    sent = flip(pick(both, jnp.where(z == 0, 1, 0), 0), "cp", 1)

    def choice(*four):
        return jnp.where(
            z == 0, four[0], jnp.where(z == 1, four[1], jnp.where(z == 2, four[2], four[3]))
        )

    qkv_grad = jnp.concatenate(
        [
            choice(both[0, 0], both[0, 1], sent[0], sent[1]),
            choice(both[0, 1], sent[0], sent[1], both[1, 0]),
            choice(sent[0], sent[1], both[0, 0], both[1, 1]),
        ],
        axis=1,
    ).astype(F32)

    up_near, up_away = cut_fourth(up_near, up_far)
    up_sums = total(up_near, flip(up_away, "cp", 2))
    down_sums = plain(total(down_near, down_far))
    extra = lines // 4
    out_grad = jnp.concatenate([up_sums[lines : lines + extra], up_sums[2 * lines + extra :]])
    out_grad = jnp.concatenate([out_grad[:, :part], out_grad[:, part:]]).astype(F32)
    both = jnp.stack([
        jnp.stack([up_sums[:lines], up_sums[lines + extra : 2 * lines + extra]]),
        down_sums.reshape(2, lines, hidden_part),
    ], axis=1)
    mine, other = pick(both, core, 0), flip(pick(both, 1 - core, 0), "core", 1)
    up_grad = ordered(core == 0, mine[0], other[0], 1).astype(F32)
    down_grad = ordered(core == 0, mine[1], other[1], 1).T.astype(F32)

    gain_one = gain_one.reshape(1, width) / gains[0:1]
    gain_sum = jnp.concatenate([gain_one, gain_two, gain_three, gain_four]).reshape(-1, 128)
    gain_sum = after(gain_sum, *ended)
    for axis, bit in (("core", 1), ("xy", 1), ("xy", 2), ("cp", 1), ("cp", 2)):
        gain_sum = gain_sum + flip(gain_sum, axis, bit)
    gains_grad = pick(gain_sum, (2 * xy + core) * cp_count + z, 0)
    return mixed, tokens_grad, qkv_grad, out_grad, up_grad, down_grad, gains_grad


def solution(mesh):
    rows, cp = mesh.shape["rows"], mesh.shape["cp"]
    if (rows, cp) == (8, 4):
        grid = Mesh(mesh.devices.reshape(rows // 2, 2, cp), ("xy", "core", "cp"))
        run, lines = body, ("xy", "core")
    else:
        grid, run, lines = mesh, general_body, ("rows",)
    tokens = P(lines, None, "cp", None)
    weight, down, gains = P(lines, "cp"), P("cp", lines), P(lines + ("cp",))
    return jax.shard_map(
        run,
        mesh=grid,
        in_specs=(tokens, P(lines, None), weight, weight, weight, down, gains, tokens),
        out_specs=(tokens, tokens, weight, weight, weight, down, gains),
        check_vma=False,
    )
```

```python
import functools
import math

import jax
import jax.numpy as jnp
from jax import lax
from jax.experimental import pallas as pl
from jax.experimental.layout import Layout, with_layout_constraint
from jax.experimental.pallas import tpu as pltpu
from jax.sharding import Mesh, PartitionSpec as P

HEADS = 16
HEAD_DIM = 64


NORM_EPS = 1e-05
MASKED = -1e30


def layer_norm(values):
    average = jnp.mean(values, axis=-1, keepdims=True)
    centred = values - average
    spread = jnp.mean(centred * centred, axis=-1, keepdims=True)
    return centred * lax.rsqrt(spread + NORM_EPS)


def norm_back(values, upstream):
    _, pull_back = jax.vjp(layer_norm, values)
    return pull_back(upstream)[0]


def gelu_tanh(values):
    return jax.nn.gelu(values, approximate=True)


def rotate(values, cosine, sine_part):
    half_width = values.shape[-1] // 2
    first_half = values[..., :half_width]
    second_half = values[..., half_width:]
    return jnp.concatenate(
        [
            first_half * cosine - second_half * sine_part,
            second_half * cosine + first_half * sine_part,
        ],
        axis=-1,
    )


def rounded(values):
    return lax.optimization_barrier(values.astype(jnp.bfloat16)).astype(jnp.float32)


def doc_start_of(starts, positions):
    return jnp.max(
        jnp.where(starts[:, None, :] <= positions[None, :, None], starts[:, None, :], 0), axis=-1
    )


def general_body(tokens, doc_starts, qkv_weight, out_weight, up_weight, down_weight, norm_gains, cotangent):
    rows_count = lax.axis_size("rows")
    cp_count = lax.axis_size("cp")
    qkv_rows, out_rows, up_rows, down_rows, gain_piece = (
        lax.all_gather(qkv_weight, "rows", axis=0, tiled=True),
        lax.all_gather(out_weight, "rows", axis=0, tiled=True),
        lax.all_gather(up_weight, "rows", axis=0, tiled=True),
        lax.all_gather(down_weight, "rows", axis=1, tiled=True),
        lax.all_gather(norm_gains, "rows", axis=0, tiled=True),
    )
    qkv_full, out_full, gain_mixed = (
        lax.all_gather(qkv_rows, "cp", axis=1, tiled=True),
        lax.all_gather(out_rows, "cp", axis=1, tiled=True),
        lax.all_gather(gain_piece, "cp", axis=0, tiled=True),
    )
    gain_full = jnp.transpose(gain_mixed.reshape(cp_count, rows_count, -1), (1, 0, 2)).reshape(-1)
    row_count, _, span_len, width = tokens.shape
    half_len = span_len * cp_count
    row_len = 2 * half_len
    queries_dev = 2 * span_len
    token_total = row_count * queries_dev
    group_total = row_count * row_len
    gain_rows = gain_full.astype(jnp.float32).reshape(4, width)
    score_scale = HEAD_DIM ** (-0.5)
    local_pos = lax.axis_index("cp") * span_len + jnp.arange(span_len, dtype=jnp.int32)
    query_pos = jnp.concatenate([local_pos, row_len - 1 - local_pos])
    half_pos = jnp.arange(half_len, dtype=jnp.int32)
    key_pos = jnp.concatenate([half_pos, row_len - 1 - half_pos])
    query_start = doc_start_of(doc_starts, query_pos)
    key_start = doc_start_of(doc_starts, key_pos)
    freq_index = jnp.arange(HEAD_DIM // 2, dtype=jnp.float32)
    inverse_freq = jnp.exp(-math.log(10000.0) * 2.0 * freq_index / HEAD_DIM)
    angles = (query_pos[None, :] - query_start).astype(jnp.float32)[..., None] * inverse_freq
    cosine = jnp.cos(angles)[:, :, None, :]
    sine_part = jnp.sin(angles)[:, :, None, :]
    head_shape = (row_count, queries_dev, HEADS, HEAD_DIM)
    flat_shape = (row_count, queries_dev, width)
    fold_shape = (row_count, 2, span_len, width)
    group_shape = (row_count, 2, half_len, width)
    full_shape = (row_count, row_len, HEADS, HEAD_DIM)
    inputs = tokens.astype(jnp.float32).reshape(flat_shape)
    normed_in = layer_norm(inputs)
    normed = (normed_in * gain_rows[0]).astype(jnp.bfloat16)
    linear = jnp.dot(normed, qkv_full, preferred_element_type=jnp.float32)
    query_rows = rotate(linear[..., :width].reshape(head_shape), cosine, sine_part).astype(
        jnp.bfloat16
    )
    key_local = rotate(
        linear[..., width : 2 * width].reshape(head_shape), cosine, sine_part
    ).astype(jnp.bfloat16)
    value_local = linear[..., 2 * width :].reshape(head_shape).astype(jnp.bfloat16)
    key_sent, value_sent = (
        lax.all_gather(key_local.reshape(fold_shape), "cp", axis=2, tiled=True),
        lax.all_gather(value_local.reshape(fold_shape), "cp", axis=2, tiled=True),
    )
    key_rows = key_sent.reshape(full_shape)
    value_rows = value_sent.reshape(full_shape)
    block_size = min(512, row_len)
    block_count = row_len // block_size
    block_range = jnp.arange(block_count)

    def block_scores(block_index):
        first_key = block_index * block_size
        key_block = lax.dynamic_slice_in_dim(key_rows, first_key, block_size, 1)
        pos_block = lax.dynamic_slice_in_dim(key_pos, first_key, block_size, 0)
        start_block = lax.dynamic_slice_in_dim(key_start, first_key, block_size, 1)
        raw_scores = jnp.einsum(
            "rqhd,rkhd->rhqk", query_rows, key_block, preferred_element_type=jnp.float32
        )
        allowed = (query_start[:, None, :, None] == start_block[:, None, None, :]) & (
            pos_block[None, None, None, :] <= query_pos[None, None, :, None]
        )
        return (raw_scores * score_scale, allowed)

    def max_step(carry, block_index):
        running_max, running_sum = carry
        scores, allowed = block_scores(block_index)
        scores = jnp.where(allowed, scores, MASKED)
        new_max = jnp.maximum(running_max, jnp.max(scores, axis=-1))
        running_sum = running_sum * jnp.exp(running_max - new_max) + jnp.sum(
            jnp.where(allowed, jnp.exp(scores - new_max[..., None]), 0.0), axis=-1
        )
        return ((new_max, running_sum), None)

    stat_shape = (row_count, HEADS, queries_dev)
    (running_max, running_sum), _ = lax.scan(
        max_step,
        (jnp.full(stat_shape, MASKED, jnp.float32), jnp.zeros(stat_shape, jnp.float32)),
        block_range,
    )
    log_total = running_max + jnp.log(running_sum)

    def value_step(totals, block_index):
        scores, allowed = block_scores(block_index)
        probs = jnp.where(allowed, jnp.exp(scores - log_total[..., None]), 0.0).astype(jnp.bfloat16)
        value_block = lax.dynamic_slice_in_dim(value_rows, block_index * block_size, block_size, 1)
        return (
            totals
            + jnp.einsum("rhqk,rkhd->rqhd", probs, value_block, preferred_element_type=jnp.float32),
            None,
        )

    attended, _ = lax.scan(value_step, jnp.zeros(head_shape, jnp.float32), block_range)
    mixed_heads = attended.reshape(flat_shape).astype(jnp.bfloat16)
    branch = jnp.dot(mixed_heads, out_full, preferred_element_type=jnp.float32)
    branch_hat = layer_norm(branch)
    hidden = inputs + branch_hat * gain_rows[1]
    hidden_hat = layer_norm(hidden)
    normed_mid = (hidden_hat * gain_rows[2]).astype(jnp.bfloat16)
    ffn_in = lax.all_gather(normed_mid.reshape(fold_shape), "cp", axis=2, tiled=True).reshape(
        group_total, width
    )
    up_proj = jnp.dot(ffn_in, up_rows, preferred_element_type=jnp.float32)
    activation = gelu_tanh(up_proj).astype(jnp.bfloat16)
    down_terms = jnp.dot(activation, down_rows, preferred_element_type=jnp.float32)
    down_proj = (
        lax.psum_scatter(
            down_terms.reshape(group_shape).astype(jnp.bfloat16),
            "cp",
            scatter_dimension=2,
            tiled=True,
        )
        .astype(jnp.float32)
        .reshape(flat_shape)
    )
    down_hat = layer_norm(down_proj)
    mixed = (hidden + down_hat * gain_rows[3]).astype(jnp.bfloat16).reshape(tokens.shape)
    upstream = cotangent.astype(jnp.float32).reshape(flat_shape)
    gain_four = jnp.sum(upstream * down_hat, axis=(0, 1))
    grad_down_out = norm_back(down_proj, upstream * gain_rows[3]).astype(jnp.bfloat16)
    grad_out_rows = lax.all_gather(
        grad_down_out.reshape(fold_shape), "cp", axis=2, tiled=True
    ).reshape(group_total, width)
    down_local = jnp.einsum(
        "tf,td->fd", activation, grad_out_rows, preferred_element_type=jnp.float32
    )
    grad_act = jnp.einsum("td,fd->tf", grad_out_rows, down_rows, preferred_element_type=jnp.float32)
    _, gelu_pull = jax.vjp(gelu_tanh, up_proj)
    grad_up = gelu_pull(grad_act)[0].astype(jnp.bfloat16)
    up_local = jnp.einsum("tc,tf->cf", ffn_in, grad_up, preferred_element_type=jnp.float32)
    mid_terms = jnp.einsum("tf,cf->tc", grad_up, up_rows, preferred_element_type=jnp.float32)
    grad_mid = (
        lax.psum_scatter(
            mid_terms.reshape(group_shape).astype(jnp.bfloat16),
            "cp",
            scatter_dimension=2,
            tiled=True,
        )
        .astype(jnp.float32)
        .reshape(flat_shape)
    )
    gain_three = jnp.sum(grad_mid * hidden_hat, axis=(0, 1))
    grad_hidden = upstream + norm_back(hidden, grad_mid * gain_rows[2])
    gain_two = jnp.sum(grad_hidden * branch_hat, axis=(0, 1))
    grad_branch = norm_back(branch, grad_hidden * gain_rows[1]).astype(jnp.bfloat16)
    out_local = jnp.einsum(
        "tc,te->ce",
        mixed_heads.reshape(token_total, width),
        grad_branch.reshape(token_total, width),
        preferred_element_type=jnp.float32,
    )
    grad_heads = (
        jnp.einsum("rqe,ce->rqc", grad_branch, out_full, preferred_element_type=jnp.float32)
        .astype(jnp.bfloat16)
        .reshape(head_shape)
    )
    delta_sum = jnp.transpose(
        jnp.sum(grad_heads.astype(jnp.float32) * attended, axis=-1), (0, 2, 1)
    )

    def score_grads(block_index):
        scores, allowed = block_scores(block_index)
        probs = jnp.where(allowed, jnp.exp(scores - log_total[..., None]), 0.0)
        first_key = block_index * block_size
        key_block = lax.dynamic_slice_in_dim(key_rows, first_key, block_size, 1)
        value_block = lax.dynamic_slice_in_dim(value_rows, first_key, block_size, 1)
        grad_probs = jnp.einsum(
            "rqhd,rkhd->rhqk", grad_heads, value_block, preferred_element_type=jnp.float32
        )
        grad_scores = (probs * (grad_probs - delta_sum[..., None]) * score_scale).astype(
            jnp.bfloat16
        )
        return (probs, grad_scores, key_block)

    def grad_step(grad_query, block_index):
        probs, grad_scores, key_block = score_grads(block_index)
        grad_query = grad_query + jnp.einsum(
            "rhqk,rkhd->rqhd", grad_scores, key_block, preferred_element_type=jnp.float32
        )
        key_part = jnp.einsum(
            "rhqk,rqhd->rkhd", grad_scores, query_rows, preferred_element_type=jnp.float32
        )
        value_part = jnp.einsum(
            "rhqk,rqhd->rkhd",
            probs.astype(jnp.bfloat16),
            grad_heads,
            preferred_element_type=jnp.float32,
        )
        return (grad_query, (key_part, value_part))

    grad_query, (key_parts, value_parts) = lax.scan(
        grad_step, jnp.zeros(head_shape, jnp.float32), block_range
    )
    key_terms = jnp.moveaxis(key_parts, 0, 1).reshape(group_shape)
    value_terms = jnp.moveaxis(value_parts, 0, 1).reshape(group_shape)
    key_sum, value_sum = (
        lax.psum_scatter(
            key_terms.astype(jnp.bfloat16), "cp", scatter_dimension=2, tiled=True
        ).astype(jnp.float32),
        lax.psum_scatter(
            value_terms.astype(jnp.bfloat16), "cp", scatter_dimension=2, tiled=True
        ).astype(jnp.float32),
    )
    query_unturned = rotate(rounded(grad_query), cosine, -sine_part).reshape(flat_shape)
    key_unturned = rotate(rounded(key_sum.reshape(head_shape)), cosine, -sine_part).reshape(
        flat_shape
    )
    grad_linear = jnp.concatenate(
        [query_unturned, key_unturned, value_sum.reshape(flat_shape)], axis=-1
    ).astype(jnp.bfloat16)
    qkv_local = jnp.einsum(
        "tc,te->ce",
        normed.reshape(token_total, width),
        grad_linear.reshape(token_total, 3 * width),
        preferred_element_type=jnp.float32,
    )
    grad_normed = jnp.einsum(
        "rqe,ce->rqc", grad_linear, qkv_full, preferred_element_type=jnp.float32
    )
    gain_one = jnp.sum(grad_normed * normed_in, axis=(0, 1))
    tokens_grad = (grad_hidden + norm_back(inputs, grad_normed * gain_rows[0])).reshape(
        tokens.shape
    )
    gain_local = jnp.concatenate([gain_one, gain_two, gain_three, gain_four])
    gain_order = jnp.transpose(gain_local.reshape(rows_count, cp_count, -1), (1, 0, 2)).reshape(-1)
    qkv_mid, out_mid, gain_mid = (
        lax.psum_scatter(
            qkv_local.astype(jnp.bfloat16), "cp", scatter_dimension=1, tiled=True
        ).astype(jnp.float32),
        lax.psum_scatter(
            out_local.astype(jnp.bfloat16), "cp", scatter_dimension=1, tiled=True
        ).astype(jnp.float32),
        lax.psum_scatter(
            gain_order.astype(jnp.bfloat16), "cp", scatter_dimension=0, tiled=True
        ).astype(jnp.float32),
    )
    qkv_sum, out_sum, up_sum, down_sum, gain_sum = (
        lax.psum_scatter(
            qkv_mid.astype(jnp.bfloat16), "rows", scatter_dimension=0, tiled=True
        ).astype(jnp.float32),
        lax.psum_scatter(
            out_mid.astype(jnp.bfloat16), "rows", scatter_dimension=0, tiled=True
        ).astype(jnp.float32),
        lax.psum_scatter(
            up_local.astype(jnp.bfloat16), "rows", scatter_dimension=0, tiled=True
        ).astype(jnp.float32),
        lax.psum_scatter(
            down_local.astype(jnp.bfloat16), "rows", scatter_dimension=1, tiled=True
        ).astype(jnp.float32),
        lax.psum_scatter(
            gain_mid.astype(jnp.bfloat16), "rows", scatter_dimension=0, tiled=True
        ).astype(jnp.float32),
    )
    return (mixed, tokens_grad, qkv_sum, out_sum, up_sum, down_sum, gain_sum)


F32 = jnp.float32
BF16 = jnp.bfloat16
VMEM = 56 * 1024 * 1024


def params(grid_rank):
    return pltpu.CompilerParams(
        dimension_semantics=("arbitrary",) * grid_rank, vmem_limit_bytes=VMEM
    )


def lasting(microseconds):
    return pl.CostEstimate(
        flops=int(microseconds * 1e7), bytes_accessed=1024, transcendentals=0
    )


def turned(x, cosine, sine):
    lane = lax.broadcasted_iota(jnp.int32, x.shape, 1)
    other = jnp.where((lane & 32) == 0, pltpu.roll(x, 96, 1), pltpu.roll(x, 32, 1))
    return x * cosine + other * sine


def attend_kernel(tile, bounds, slot_of, q_ref, k_ref, v_ref, pcol_ref, prow_ref, srow_ref,
                  o_ref, ob_ref, lse_ref, vt_ref):
    i = pl.program_id(1)

    @pl.when(i == 0)
    def _():
        vt_ref[...] = v_ref[...].astype(F32).T.astype(BF16)

    qt = q_ref[...].astype(F32).T
    row = lax.broadcasted_iota(jnp.int32, qt.shape, 0)
    lo = bounds[0, i]
    mid = jnp.minimum(bounds[1, i], i)
    qpos = prow_ref[...]
    qstart = srow_ref[...]
    qh = [jnp.where((row >= 64) == (h == 1), qt, 0.0).astype(BF16) for h in range(2)]

    def step(j, carry, masked):
        at = pl.multiple_of(j * tile, tile)
        k = k_ref[pl.ds(at, tile), :]
        scores = [jnp.dot(k, qh[h], preferred_element_type=F32) for h in range(2)]
        if masked:
            kpos = pcol_ref[pl.ds(at, tile), :]
            allowed = (kpos >= qstart) & (kpos <= qpos)
            scores = [jnp.where(allowed, s, MASKED) for s in scores]
        out = []
        for h in range(2):
            top, total, acc = carry[h]
            new = jnp.maximum(top, jnp.max(scores[h], axis=0, keepdims=True))
            p = jnp.exp(scores[h] - new)
            keep = jnp.exp(top - new)
            total = total * keep + jnp.sum(p, axis=0, keepdims=True)
            acc = acc * keep + jnp.dot(
                vt_ref[h * 64 : h * 64 + 64, pl.ds(at, tile)], p.astype(BF16),
                preferred_element_type=F32,
            )
            out.append((new, total, acc))
        return tuple(out)

    start = (
        jnp.full((1, tile), MASKED, F32), jnp.zeros((1, tile), F32), jnp.zeros((64, tile), F32)
    )
    carry = step(i, (start, start), True)
    carry = lax.fori_loop(lo, mid, functools.partial(step, masked=True), carry)
    carry = lax.fori_loop(mid, i, functools.partial(step, masked=False), carry)
    parts = []
    for h in range(2):
        top, total, acc = carry[h]
        lse_ref[0, h : h + 1, :] = top + jnp.log(total)
        parts.append(acc / total)
    out = jnp.concatenate(parts, axis=0).T
    o_ref[...] = out
    span = ob_ref.shape[1]
    for b in range(tile // span):
        ob_ref[slot_of[i * (tile // span) + b]] = out[b * span : (b + 1) * span].astype(BF16)


def attend(pair, q, k, v, pcol, prow, srow, bounds, slot_of, tile):
    rows, width = q.shape
    blocks = slot_of.shape[0]
    span = rows // blocks
    count = rows // tile
    grid_spec = pltpu.PrefetchScalarGridSpec(
        num_scalar_prefetch=2,
        grid=(1, count),
        in_specs=[
            pl.BlockSpec((tile, 128), lambda p, i, b, t: (i, pair)),
            pl.BlockSpec((rows, 128), lambda p, i, b, t: (0, pair)),
            pl.BlockSpec((rows, 128), lambda p, i, b, t: (0, pair)),
            pl.BlockSpec((rows, 1), lambda p, i, b, t: (0, 0)),
            pl.BlockSpec((1, tile), lambda p, i, b, t: (0, i)),
            pl.BlockSpec((1, tile), lambda p, i, b, t: (0, i)),
        ],
        out_specs=[
            pl.BlockSpec((tile, 128), lambda p, i, b, t: (i, p)),
            pl.BlockSpec((blocks, span, 128), lambda p, i, b, t: (0, 0, p)),
            pl.BlockSpec((1, 2, tile), lambda p, i, b, t: (p, 0, i)),
        ],
        scratch_shapes=[pltpu.VMEM((128, rows), BF16)],
    )
    return pl.pallas_call(
        functools.partial(attend_kernel, tile),
        grid_spec=grid_spec,
        out_shape=[
            jax.ShapeDtypeStruct((rows, 128), F32),
            jax.ShapeDtypeStruct((blocks, span, 128), BF16),
            jax.ShapeDtypeStruct((1, 2, rows), F32),
        ],
        compiler_params=params(2),
        cost_estimate=lasting(14),
        name="attend",
    )(bounds, slot_of, q, k, v, pcol, prow, srow)


def attend_back_kernel(tile, bounds, slot_of, q_ref, k_ref, v_ref, do_ref, o_ref, lse_ref, pcol_ref,
                       prow_ref, srow_ref, cos_ref, sin_ref, g_ref,
                       qm, dom, qtm, dotm, delta, dqt):
    j = pl.program_id(1)
    count = pl.num_programs(1)
    rows = q_ref.shape[0]

    span = do_ref.shape[1]

    @pl.when(j == 0)
    def _():
        for t in range(rows // tile):
            part = pl.ds(t * tile, tile)
            q = q_ref[part, :].astype(F32)
            do = jnp.concatenate(
                [do_ref[slot_of[t * tile // span + b]] for b in range(tile // span)], axis=0
            ).astype(F32)
            qt, dot = q.T, do.T
            lane = lax.broadcasted_iota(jnp.int32, q.shape, 1)
            row = lax.broadcasted_iota(jnp.int32, qt.shape, 0)
            prod = dot * o_ref[part, :].T
            for h in range(2):
                mine = (lane >= 64) == (h == 1)
                mine_t = (row >= 64) == (h == 1)
                qm[h, part, :] = jnp.where(mine, q, 0.0).astype(BF16)
                dom[h, part, :] = jnp.where(mine, do, 0.0).astype(BF16)
                qtm[h, :, part] = jnp.where(mine_t, qt, 0.0).astype(BF16)
                dotm[h, :, part] = jnp.where(mine_t, dot, 0.0).astype(BF16)
                delta[h : h + 1, part] = jnp.sum(
                    prod[h * 64 : h * 64 + 64], axis=0, keepdims=True
                )
        dqt[...] = jnp.zeros_like(dqt)

    here = pl.ds(pl.multiple_of(j * tile, tile), tile)
    k = k_ref[here, :]
    v = v_ref[here, :]
    kt = k.astype(F32).T.astype(BF16)
    kpos = pcol_ref[here, :]
    full = jnp.maximum(bounds[2, j], j + 1)
    end = bounds[3, j]

    def step(i, carry, masked):
        dk, dv = carry
        part = pl.ds(pl.multiple_of(i * tile, tile), tile)
        if masked:
            allowed = (kpos >= srow_ref[:, part]) & (kpos <= prow_ref[:, part])
        for h in range(2):
            s = jnp.dot(k, qtm[h, :, part], preferred_element_type=F32)
            p = jnp.exp(s - lse_ref[0, h : h + 1, part])
            if masked:
                p = jnp.where(allowed, p, 0.0)
            dp = jnp.dot(v, dotm[h, :, part], preferred_element_type=F32)
            ds = (p * (dp - delta[h : h + 1, part])).astype(BF16)
            dv = dv + jnp.dot(p.astype(BF16), dom[h, part, :], preferred_element_type=F32)
            dk = dk + jnp.dot(ds, qm[h, part, :], preferred_element_type=F32)
            dqt[h * 64 : h * 64 + 64, part] += jnp.dot(
                kt[h * 64 : h * 64 + 64, :], ds, preferred_element_type=F32
            )
        return dk, dv

    carry = (jnp.zeros((tile, 128), F32), jnp.zeros((tile, 128), F32))
    carry = step(j, carry, True)
    carry = lax.fori_loop(j + 1, full, functools.partial(step, masked=False), carry)
    carry = lax.fori_loop(full, end, functools.partial(step, masked=True), carry)
    dk, dv = carry

    def unturned(x, at):
        x = x.astype(BF16).astype(F32)
        return turned(x, cos_ref[at, :], -sin_ref[at, :]).astype(BF16)

    grad_k, grad_v = unturned(dk, here), dv.astype(BF16)
    for b in range(tile // span):
        at = slot_of[j * (tile // span) + b]
        g_ref[1, at] = grad_k[b * span : (b + 1) * span]
        g_ref[2, at] = grad_v[b * span : (b + 1) * span]

    @pl.when(j == count - 1)
    def _():
        for t in range(rows // tile):
            part = pl.ds(t * tile, tile)
            grad_q = unturned(dqt[:, part].T * 0.125, part)
            for b in range(tile // span):
                at = slot_of[t * (tile // span) + b]
                g_ref[0, at] = grad_q[b * span : (b + 1) * span]


def attend_back(pair, q, k, v, do, o, lse, pcol, prow, srow, cosine, sine, bounds, slot_of, tile):
    rows, width = q.shape
    blocks, span, _ = do.shape
    count = rows // tile
    whole = pl.BlockSpec((rows, 128), lambda p, j, b, t: (0, pair))
    table = pl.BlockSpec((rows, 128), lambda p, j, b, t: (0, 0))
    line = pl.BlockSpec((1, rows), lambda p, j, b, t: (0, 0))
    grid_spec = pltpu.PrefetchScalarGridSpec(
        num_scalar_prefetch=2,
        grid=(1, count),
        in_specs=[
            whole, whole, whole,
            pl.BlockSpec((blocks, span, 128), lambda p, j, b, t: (0, 0, pair)),
            table,
            pl.BlockSpec((1, 2, rows), lambda p, j, b, t: (0, 0, 0)),
            pl.BlockSpec((rows, 1), lambda p, j, b, t: (0, 0)),
            line, line, table, table,
        ],
        out_specs=pl.BlockSpec((3, blocks, span, 128), lambda p, j, b, t: (0, 0, 0, 0)),
        scratch_shapes=[
            pltpu.VMEM((2, rows, 128), BF16), pltpu.VMEM((2, rows, 128), BF16),
            pltpu.VMEM((2, 128, rows), BF16), pltpu.VMEM((2, 128, rows), BF16),
            pltpu.VMEM((2, rows), F32), pltpu.VMEM((128, rows), F32),
        ],
    )
    return pl.pallas_call(
        functools.partial(attend_back_kernel, tile),
        grid_spec=grid_spec,
        out_shape=jax.ShapeDtypeStruct((3, blocks, span, 128), BF16),
        compiler_params=params(2),
        cost_estimate=lasting(23),
        name="attend_back",
    )(bounds, slot_of, q, k, v, do, o, lse, pcol, prow, srow, cosine, sine)


def tile_bounds(starts_nat, tile):
    rows = starts_nat.shape[0]
    count = rows // tile
    tiles = starts_nat.reshape(count, tile)
    first, last = tiles[:, 0], tiles[:, -1]
    at = jnp.arange(count, dtype=jnp.int32) * tile
    lo = first // tile
    mid = (last + tile - 1) // tile
    full = jnp.sum((last[None, :] <= at[:, None]).astype(jnp.int32), axis=1)
    end = jnp.sum((first[None, :] <= at[:, None] + tile - 1).astype(jnp.int32), axis=1)
    return jnp.stack([lo, mid, full, end]).astype(jnp.int32)


def normalized(x):
    centred = x - jnp.mean(x, axis=1, keepdims=True)
    scale = lax.rsqrt(jnp.mean(centred * centred, axis=1, keepdims=True) + NORM_EPS)
    return centred * scale, scale


def normalized_back(hat, scale, upstream):
    level = jnp.mean(upstream, axis=1, keepdims=True)
    slant = jnp.mean(upstream * hat, axis=1, keepdims=True)
    return scale * (upstream - level - hat * slant)


def dot_nt(a, b):
    return lax.dot_general(a, b, (((1,), (1,)), ((), ())), preferred_element_type=F32)


def call(kernel, name, grid, tables, ins, outs, microseconds, *arrays):
    return pl.pallas_call(
        kernel,
        grid_spec=pltpu.PrefetchScalarGridSpec(
            num_scalar_prefetch=len(tables),
            grid=grid,
            in_specs=ins,
            out_specs=[spec for _, spec in outs],
        ),
        out_shape=[shape for shape, _ in outs],
        compiler_params=params(len(grid)),
        cost_estimate=lasting(microseconds),
        name=name,
    )(*tables, *arrays)


def shaped(dtype, *shape):
    return jax.ShapeDtypeStruct(shape, dtype)


def fixed(*shape):
    return pl.BlockSpec(shape, lambda *_: (0,) * len(shape))


def project_kernel(slot_of, x0, x1, x2, x3, gain_ref, w_ref, cos_ref, sin_ref,
                   q_ref, k_ref, v_ref, n_ref):
    which = slot_of[pl.program_id(0)] >> 1
    width = q_ref.shape[1]
    near = jnp.where(which == 0, x0[0], x1[0])
    far = jnp.where(which == 2, x2[0], x3[0])
    x = jnp.where(which < 2, near, far).astype(F32)
    normed = (normalized(x)[0] * gain_ref[0:1, :]).astype(BF16)
    n_ref[0] = normed
    linear = jnp.dot(normed, w_ref[...], preferred_element_type=F32)
    for at in range(0, width, 128):
        q = turned(linear[:, at : at + 128], cos_ref[...], sin_ref[...])
        k = turned(linear[:, width + at : width + at + 128], cos_ref[...], sin_ref[...])
        q_ref[:, at : at + 128] = q.astype(BF16) * jnp.asarray(0.125, BF16)
        k_ref[:, at : at + 128] = k.astype(BF16)
    v_ref[...] = linear[:, 2 * width :].astype(BF16)


def project(parts, gains, w, cosine, sine, slot_of):
    count = slot_of.shape[0]
    _, rows, depth = parts[0].shape
    width = w.shape[1] // 3
    piece = pl.BlockSpec((1, rows, depth), lambda i, t: (t[i] & 1, 0, 0))
    angle = pl.BlockSpec((rows, 128), lambda i, t: (i, 0))
    out = shaped(BF16, count * rows, width), pl.BlockSpec((rows, width), lambda i, t: (i, 0))
    normed = (
        shaped(BF16, count, rows, depth),
        pl.BlockSpec((1, rows, depth), lambda i, t: (t[i], 0, 0)),
    )
    return call(
        project_kernel, "project", (count,), [slot_of],
        [piece] * 4 + [fixed(*gains.shape), fixed(*w.shape), angle, angle],
        [out, out, out, normed], 13, *parts, gains, w, cosine, sine,
    )


def mix_kernel(group, own, near, far, both, w_ref, x_ref, gain_ref,
               heads_ref, hat_ref, scale_ref, hidden_ref, mid_ref):
    width = own.shape[2]
    for r, piece in enumerate((own[0], near[0], far[0], both[0])):
        at = pl.ds(pl.multiple_of((group[0] ^ r) * width, width), width)
        heads_ref[:, at] = piece
    branch = jnp.dot(heads_ref[...], w_ref[...], preferred_element_type=F32)
    hat, scale = normalized(branch)
    hidden = x_ref[0].astype(F32) + hat * gain_ref[1:2, :]
    hat_ref[...] = hat
    scale_ref[...] = scale
    hidden_ref[...] = hidden
    mid_ref[...] = (normalized(hidden)[0] * gain_ref[2:3, :]).astype(BF16)


def mix(group, local, near, far, both, w, x, gains):
    _, rows, part = local.shape
    count, _, width = x.shape
    block = pl.BlockSpec((1, rows, part), lambda i, g: (i, 0, 0))
    row = pl.BlockSpec((rows, width), lambda i, g: (i, 0))
    total = count * rows
    return call(
        mix_kernel, "mix", (count,), [group],
        [
            block, block, block, block, fixed(*w.shape), pl.BlockSpec((1, rows, width), lambda i, g: (i, 0, 0)),
            fixed(*gains.shape),
        ],
        [
            (shaped(BF16, total, width), row),
            (shaped(F32, total, width), row),
            (shaped(F32, total, 1), pl.BlockSpec((rows, 1), lambda i, g: (i, 0))),
            (shaped(F32, total, width), row),
            (shaped(BF16, total, width), row),
        ],
        6, local, near, far, both, w, x, gains,
    )


def finish_kernel(terms_ref, sent_ref, hidden_ref, dy_ref, gain_ref, mixed_ref, grad_ref, sum_ref):
    down = terms_ref[...] + sent_ref[...].astype(F32)
    hat, scale = normalized(down)
    gain = gain_ref[3:4, :]
    dy = dy_ref[...].astype(F32)
    mixed_ref[...] = (hidden_ref[...] + hat * gain).astype(BF16)
    grad_ref[...] = normalized_back(hat, scale, dy * gain).astype(BF16)

    @pl.when(pl.program_id(0) == 0)
    def _():
        sum_ref[...] = jnp.zeros_like(sum_ref)

    sum_ref[...] += jnp.sum(dy * hat, axis=0, keepdims=True)


def finish(terms, sent, hidden, dy, gains):
    total, width = terms.shape
    rows = total // 2
    row = pl.BlockSpec((rows, width), lambda i: (i, 0))
    return call(
        finish_kernel, "finish", (2,), [],
        [row, row, row, row, fixed(*gains.shape)],
        [
            (shaped(BF16, total, width), row), (shaped(BF16, total, width), row),
            (shaped(F32, 1, width), fixed(1, width)),
        ],
        5, terms, sent, hidden, dy, gains,
    )


def turn_kernel(group, terms_ref, sent_ref, hidden_ref, dy_ref, hat_ref, scale_ref, w_ref, gain_ref,
                keep_ref, branch_ref, heads_ref, three_ref, two_ref):
    upstream = terms_ref[...] + sent_ref[...].astype(F32)
    hat, scale = normalized(hidden_ref[...])

    @pl.when(pl.program_id(0) == 0)
    def _():
        three_ref[...] = jnp.zeros_like(three_ref)
        two_ref[...] = jnp.zeros_like(two_ref)

    three_ref[...] += jnp.sum(upstream * hat, axis=0, keepdims=True)
    grad = dy_ref[...].astype(F32) + normalized_back(hat, scale, upstream * gain_ref[2:3, :])
    keep_ref[...] = grad
    branch_hat = hat_ref[...]
    two_ref[...] += jnp.sum(grad * branch_hat, axis=0, keepdims=True)
    branch = normalized_back(branch_hat, scale_ref[...], grad * gain_ref[1:2, :]).astype(BF16)
    branch_ref[...] = branch
    part = heads_ref.shape[3]
    for r in range(4):
        at = pl.ds(pl.multiple_of((group[0] ^ r) * part, part), part)
        heads_ref[r, 0] = dot_nt(branch, w_ref[at, :]).astype(BF16)


def turn(group, terms, sent, hidden, dy, hat, scale, w, gains):
    total, width = terms.shape
    rows = total // 2
    part = width // 4
    row = pl.BlockSpec((rows, width), lambda i, g: (i, 0))
    return call(
        turn_kernel, "turn", (2,), [group],
        [
            row, row, row, row, row, pl.BlockSpec((rows, 1), lambda i, g: (i, 0)),
            fixed(*w.shape), fixed(*gains.shape),
        ],
        [
            (shaped(F32, total, width), row), (shaped(BF16, total, width), row),
            (
                shaped(BF16, 4, 2, rows, part),
                pl.BlockSpec((4, 1, rows, part), lambda i, g: (0, i, 0, 0)),
            ),
            (shaped(F32, 1, width), fixed(1, width)), (shaped(F32, 1, width), fixed(1, width)),
        ],
        8, terms, sent, hidden, dy, hat, scale, w, gains,
    )


def end_kernel(keep_ref, near_ref, far_ref, x_ref, grad_ref, gain_ref, o_ref):
    upstream = keep_ref[...] + near_ref[...].astype(F32) + far_ref[...].astype(F32)
    hat, scale = normalized(x_ref[...].astype(F32))
    grad = grad_ref[...] + normalized_back(hat, scale, upstream * gain_ref[0:1, :])
    o_ref[...] = grad.astype(BF16)


def end(keep, near, far, x, grad, gains):
    total, width = x.shape
    rows = total // 2
    row = pl.BlockSpec((rows, width), lambda i: (i, 0))
    return call(
        end_kernel, "end", (2,), [], [row] * 5 + [fixed(*gains.shape)],
        [(shaped(BF16, total, width), row)], 20, keep, near, far, x, grad, gains,
    )[0]


def plain(x):
    return with_layout_constraint(x, Layout(tuple(range(x.ndim))))


def flip(x, axis, bit):
    return lax.ppermute(plain(x), axis, [(i, i ^ bit) for i in range(lax.axis_size(axis))])


def swap(x):
    cp = lax.axis_size("cp")
    half = cp // 2
    pairs = []
    for z in range(half):
        low, high = cp + z, z + half
        pairs += [(low, high), (high, low), (z, z), (cp + high, cp + high)]
    return lax.ppermute(plain(x), ("core", "cp"), pairs)


def ordered(first, mine, other, axis):
    return jnp.concatenate(
        [jnp.where(first, mine, other), jnp.where(first, other, mine)], axis=axis
    )


def placed(first, mine, other, at):
    return ordered(first, jnp.expand_dims(mine, at), jnp.expand_dims(other, at), at)


def after(x, *others):
    return lax.optimization_barrier((x, *others))[0]


def all_after(group, *others):
    return lax.optimization_barrier((*group, *others))[: len(group)]


def total(a, b):
    return (a.astype(F32) + b.astype(F32)).astype(BF16)


def flip_both(x):
    cp = lax.axis_size("cp")
    return lax.ppermute(
        x, ("core", "cp"), [(c * cp + z, (1 - c) * cp + (z ^ 1)) for c in range(2) for z in range(cp)]
    )


def dot(a, b, dims):
    return lax.dot_general(a, b, ((dims[:1], dims[1:]), ((), ())), preferred_element_type=F32)


def gelu_and_slope(u):
    c = math.sqrt(2.0 / math.pi)
    square = u * u
    t = jnp.tanh(u * (c + (c * 0.044715) * square))
    half = 0.5 + 0.5 * t
    slope = half + (0.5 * u) * (1.0 - t * t) * (c + (3.0 * 0.044715 * c) * square)
    return lax.optimization_barrier(((u * half).astype(BF16), slope.astype(BF16)))


def pick(x, at, axis):
    return lax.dynamic_index_in_dim(x, at, axis, False)


def widened(z, x, other):
    first, second = jnp.where(z & 1 == 0, x, other), jnp.where(z & 1 == 0, other, x)
    half = x.shape[1] // 2
    return jnp.concatenate(
        [first[:, :half], second[:, :half], first[:, half:], second[:, half:]], axis=1
    )


def body(tokens, doc_starts, qkv_weight, out_weight, up_weight, down_weight, norm_gains, cotangent):
    xy, core, z = lax.axis_index("xy"), lax.axis_index("core"), lax.axis_index("cp")
    xy_count, cp_count = lax.axis_size("xy"), lax.axis_size("cp")
    _, _, span, width = tokens.shape
    blocks = 2 * cp_count
    row_len = blocks * span
    own = 2 * span
    parity = z & 1
    group = 2 * parity + core
    part = width // cp_count
    hidden_part = up_weight.shape[1] // 2
    lines_each = width // xy_count
    lines = lines_each // 2
    here = jnp.reshape(xy, (1,)).astype(jnp.int32)
    group_at = jnp.reshape(group, (1,)).astype(jnp.int32)

    gain_rows = jnp.zeros((16, qkv_weight.shape[1]), BF16)
    gain_rows = lax.dynamic_update_slice(gain_rows, norm_gains[None], (0, 0))
    w = jnp.concatenate([qkv_weight, gain_rows])
    w_far = flip(w, "cp", 2)
    x = swap(after(tokens, w_far)[0])

    up_weight, down_weight, out_weight = all_after((up_weight, down_weight, out_weight), w_far)

    def half_of(which):
        up = lax.dynamic_slice_in_dim(up_weight, which * hidden_part, hidden_part, 1)
        down = lax.dynamic_slice_in_dim(down_weight, which * hidden_part, hidden_part, 0)
        return plain(jnp.stack([up, down.T]))

    ffn = ordered(core == 0, half_of(core), flip(half_of(1 - core), "core", 1), 1)

    def paired(mine, other):
        return jnp.concatenate(
            [jnp.where(z & 2 == 0, mine, other), jnp.where(z & 2 == 0, other, mine)], axis=1
        )

    out_far = flip(out_weight, "cp", 2)
    w, w_far = jnp.where(z & 2 == 0, w, w_far), jnp.where(z & 2 == 0, w_far, w)
    near = [w[:, n * part : (n + 1) * part] for n in range(3)]
    near += [w_far[:, n * part : (n + 1) * part] for n in range(3)]
    even = parity == 0
    sent = jnp.concatenate(
        [jnp.where(even, near[a], near[b]) for a, b in ((2, 1), (3, 2), (4, 3))], axis=1
    )
    gain_near = jnp.stack([w[lines, :128], w_far[lines, :128]])
    sent = lax.dynamic_update_slice(sent, gain_near, (lines, 0))
    far = flip(sent, "cp", 1)
    gain_far = far[lines : lines + 2, :128]
    gain_near, gain_far = (
        jnp.where(even, gain_near, gain_far), jnp.where(even, gain_far, gain_near)
    )
    gain_rows = jnp.stack([gain_near[0], gain_far[0], gain_near[1], gain_far[1]])
    far = [far[:lines, n * part : (n + 1) * part] for n in range(3)]
    near = [block[:lines] for block in near]
    first_group = jnp.concatenate(
        [jnp.where(even, a, b) for a, b in ((near[0], far[0]), (far[0], far[1]), (near[5], near[4]))],
        axis=1,
    )
    second_group = jnp.concatenate(
        [jnp.where(even, a, b) for a, b in ((near[1], near[0]), (far[1], far[2]), (far[2], near[5]))],
        axis=1,
    )
    gain_block = jnp.zeros((16, 3 * part), BF16)
    gain_block = lax.dynamic_update_slice(gain_block, gain_rows, (0, 0))
    mine = jnp.concatenate([jnp.where(core == 0, first_group, second_group), gain_block])
    other = jnp.concatenate([jnp.where(core == 0, second_group, first_group), gain_block])

    other_starts = flip(after(doc_starts, w_far), "core", 1)
    starts = jnp.where(core == z // (cp_count // 2), doc_starts, other_starts)[0]

    block_id = jnp.arange(blocks, dtype=jnp.int32)[:, None]
    inside = jnp.arange(span, dtype=jnp.int32)[None, :]
    late = block_id >= cp_count
    positions = (block_id * span + jnp.where(late, span - 1 - inside, inside)).reshape(-1)

    def starts_at(at):
        return jnp.max(jnp.where(starts[None, :] <= at[:, None], starts[None, :], 0), axis=1)

    row_start = starts_at(positions)
    tile = min(512, row_len)
    bounds = tile_bounds(starts_at(jnp.arange(row_len, dtype=jnp.int32)), tile)
    freq = jnp.exp(
        -math.log(10000.0) * 2.0 * jnp.arange(HEAD_DIM // 2, dtype=F32) / HEAD_DIM
    )
    angles = (positions - row_start).astype(F32)[:, None] * freq
    cosine, sine = jnp.cos(angles), jnp.sin(angles)
    cosine = plain(jnp.tile(cosine, (1, 4)))
    sine = plain(jnp.tile(jnp.concatenate([-sine, sine], axis=1), (1, 2)))
    pcol, prow, srow = positions[:, None], positions[None, :], row_start[None, :]
    chunk = jnp.arange(blocks, dtype=jnp.int32)
    chunk = jnp.where(chunk < cp_count, chunk, blocks - 1 - chunk)
    slot_of = (
        2 * (2 * ((chunk >> 1) ^ core) + ((chunk & 1) ^ parity))
        + (jnp.arange(blocks) >= cp_count)
    ).astype(jnp.int32)
    slot = jnp.arange(blocks, dtype=jnp.int32)
    relative = slot >> 1
    chunk_of = 2 * ((relative >> 1) ^ core) + ((relative & 1) ^ parity)
    block_of = jnp.where(slot & 1 == 0, chunk_of, blocks - 1 - chunk_of).astype(jnp.int32)

    x = after(x, sent, cosine, sine)
    x_chip = flip(x, "cp", 1)
    x_core = flip(x, "core", 1)
    up_lines, out_w, out_far = all_after((ffn[0], out_weight, out_far), x)
    up_far = flip(up_lines, "cp", 2)
    out_w = paired(out_w, out_far)
    out_far = flip(out_w, "cp", 1)

    qkv = placed(core == 0, mine, flip(other, "core", 1), 0)
    cut = qkv.shape[2] // 2
    low, high = qkv[:, :, :cut], qkv[:, :, cut:]
    low = placed(xy & 1 == 0, low, flip(low, "xy", 1), 0)
    high = placed(xy & 2 == 0, high, flip(high, "xy", 2), 0)
    low = placed(xy & 2 == 0, low, flip(low, "xy", 2), 0)
    high = placed(xy & 1 == 0, high, flip(high, "xy", 1), 1)
    qkv = jnp.concatenate([low[:, :, :, :lines], high[:, :, :, :lines]], axis=4)
    qkv = qkv.reshape(width, 3 * part)
    gains = low[:, :, :, lines : lines + cp_count, :128]
    gains = gains.reshape(4, width).astype(F32)

    x_both = flip(x_chip, "core", 1)
    x_chip, up_far = lax.optimization_barrier((x_chip, up_far))
    up_lines, up_far, down_lines, out_w, out_far = all_after(
        (up_lines, up_far, ffn[1], out_w, out_far), x_chip, qkv
    )
    up_lines, out_w = paired(up_lines, up_far), widened(z, out_w, out_far)[None]
    up_far = flip(up_lines, "cp", 1)
    down_far = flip(down_lines, "cp", 2)
    out_far = flip(out_w, "xy", 1)

    def halves(x):
        return x[None, :lines], x[None, lines:]

    def send_lines(low, high):
        return flip(low, "xy", 1), flip(high, "xy", 2)

    def join_lines(low, high, low_far, high_far):
        low = ordered(xy & 1 == 0, low, low_far, 0)
        high = jnp.expand_dims(ordered(xy & 2 == 0, high, high_far, 0), 1)
        return low, high

    def send_more(low, high):
        return flip(low, "xy", 2), flip(high, "xy", 1)

    def join_all(low, high, low_far, high_far):
        low = ordered(xy & 2 == 0, low, low_far, 0)
        high = ordered(xy & 1 == 0, high, high_far, 1).reshape(low.shape)
        return jnp.stack([low, high], axis=1).reshape(width, -1)

    q, k, v, normed = project([x, x_chip, x_core, x_both], gains, qkv, cosine, sine, slot_of)
    up_lines, up_far, down_lines, down_far, out_w, out_far = all_after(
        (up_lines, up_far, down_lines, down_far, out_w, out_far), q
    )
    up_pair = halves(widened(z, up_lines, up_far))
    up_far = send_lines(*up_pair)
    down_lines = paired(down_lines, down_far)
    down_far = flip(down_lines, "cp", 1)
    out_w = ordered(xy & 1 == 0, out_w, out_far, 0)
    out_far = flip(out_w, "xy", 2)
    q = after(q, *up_pair, down_lines, out_w)
    first = attend(0, q, k, v, pcol, prow, srow, bounds, slot_of, tile)
    up_pair, up_far = all_after(up_pair, first[0]), all_after(up_far, first[0])
    down_lines, down_far, out_w, out_far = all_after(
        (down_lines, down_far, out_w, out_far), first[0]
    )
    up_pair = join_lines(*up_pair, *up_far)
    up_far = send_more(*up_pair)
    out_w = ordered(xy & 2 == 0, out_w, out_far, 0)
    out_far = flip(out_w, "core", 1)
    down_pair = halves(widened(z, down_lines, down_far))
    down_far = send_lines(*all_after(down_pair, *up_pair))
    q = after(q, first[0], *down_pair, *up_pair, out_w)
    second = attend(1, q, k, v, pcol, prow, srow, bounds, slot_of, tile)
    attended, local, lse = zip(first, second)
    local = jnp.concatenate(local, axis=2)
    out_w, out_far = all_after((out_w, out_far), local)
    out_w = placed(core == 0, out_w, out_far, 1).reshape(width, width)
    heads, branch_hat, branch_scale, hidden, mid = mix(
        group_at, local[:2], flip(local[4:6], "core", 1), flip(local[2:4], "cp", 1),
        flip_both(local[6:]), out_w, x, gains,
    )

    dy = swap(after(cotangent.reshape(own, width), mid))

    ffn_in = jnp.concatenate([mid, flip(mid, "core", 1)])
    down_pair, down_far = all_after(down_pair, mid), all_after(down_far, mid)
    down_pair = join_lines(*down_pair, *down_far)
    down_far = send_more(*down_pair)
    up_full = join_all(*up_pair, *all_after(up_far, *down_pair))
    act, slope = gelu_and_slope(dot(ffn_in, up_full, (1, 0)))
    down_full = join_all(*down_pair, *all_after(down_far, act))
    sent = flip(dot(act[own:], down_full, (1, 1)).astype(BF16), "core", 1)
    terms = dot(act[:own], down_full, (1, 1))
    mixed, grad_down, gain_four = finish(terms, sent, hidden, dy, gains)
    grad_down = jnp.concatenate([grad_down, flip(grad_down, "core", 1)])

    x_bit, y_bit = xy & 1, xy >> 1

    def cut_first(grads):
        grads = [g.reshape(2, 2, 2, lines, -1) for g in grads]
        low = [g[:, :, 0] for g in grads]
        high = [g[:, :, 1] for g in grads]

        def both(parts, at, axis):
            return jnp.concatenate([pick(part_of, at, axis) for part_of in parts], axis=1)

        away = both(low, 1 - x_bit, 1), both(high, 1 - y_bit, 0)
        return (both(low, x_bit, 1), both(high, y_bit, 0)), away

    def send_first(away):
        return flip(away[0], "xy", 1), flip(away[1], "xy", 2)

    def cut_second(near, far):
        away = (
            total(pick(near[0], 1 - y_bit, 0), pick(far[0], 1 - y_bit, 0)),
            total(pick(near[1], 1 - x_bit, 0), pick(far[1], 1 - x_bit, 0)),
        )
        near = (
            total(pick(near[0], y_bit, 0), pick(far[0], y_bit, 0)),
            total(pick(near[1], x_bit, 0), pick(far[1], x_bit, 0)),
        )
        return near, away

    def send_second(away):
        return flip(away[0], "xy", 2), flip(away[1], "xy", 1)

    def cut_third(near, far):
        return split_columns(
            jnp.concatenate([total(a, b) for a, b in zip(near, far)]), hidden_part
        )

    def split_columns(sums, each):
        blocks_of = [sums[:, n * each : (n + 1) * each] for n in range(cp_count)]
        odd = jnp.stack([blocks_of[1], blocks_of[3]])
        even = jnp.stack([blocks_of[0], blocks_of[2]])
        return jnp.where(parity == 0, even, odd), jnp.where(parity == 0, odd, even)

    def cut_fourth(near, far):
        return (
            total(pick(near, z >> 1, 0), pick(far, z >> 1, 0)),
            total(pick(near, 1 - (z >> 1), 0), pick(far, 1 - (z >> 1), 0)),
        )

    down_local = plain(dot(grad_down, act, (0, 0)).astype(BF16))
    grad_up = dot(after(grad_down, down_local), down_full, (1, 0)) * slope.astype(F32)
    grad_up = grad_up.astype(BF16)
    sent = flip(dot(grad_up[own:], up_full, (1, 1)).astype(BF16), "core", 1)
    up_local = plain(dot(ffn_in, grad_up, (0, 0)).astype(BF16))
    grad_near, grad_away = cut_first((up_local, down_local))
    grad_far = send_first(grad_away)
    terms = dot(after(grad_up, *grad_away)[:own], up_full, (1, 1))
    grad_hidden, grad_branch, grad_heads, gain_three, gain_two = turn(
        group_at, terms, sent, hidden, dy, branch_hat, branch_scale, out_w, gains
    )

    grad_local = [
        grad_heads[0], flip(grad_heads[2], "cp", 1), flip(grad_heads[1], "core", 1),
        flip_both(grad_heads[3]),
    ]
    out_local = dot(after(heads, grad_heads), grad_branch, (0, 0)).astype(BF16)
    out_local = out_local.reshape(xy_count, 2, lines, width)
    out_away = pick(out_local, 1 - core, 1)
    grad_local = plain(jnp.concatenate(grad_local))
    out_away, mixed = all_after((out_away, mixed), grad_local)
    out_far = flip(out_away, "core", 1)
    mixed = swap(mixed).reshape(tokens.shape)
    grad_local = after(grad_local, out_away)

    tables = (pcol, prow, srow, cosine, sine, bounds, slot_of, tile)
    first = attend_back(0, q, k, v, grad_local, attended[0], lse[0], *tables)
    grad_far = all_after(grad_far, first)
    grad_near, grad_away = cut_second(grad_near, grad_far)
    grad_far = send_second(grad_away)
    out_near, out_away = split_columns(
        total(pick(out_local, core, 1), after(out_far, first)).reshape(-1, width), part
    )
    out_far = flip(out_away, "cp", 1)
    second = attend_back(
        1, q, k, v, after(grad_local, first, *grad_away, out_away, mixed), attended[1], lse[1],
        *tables,
    )
    first, second, grad_far, out_far = lax.optimization_barrier((first, second, grad_far, out_far))

    def rows_of(low, high):
        return jnp.concatenate(
            [half[n, low:high].reshape(-1, 128) for n in range(3) for half in (first, second)],
            axis=1,
        )

    half_rows = row_len // 2
    grad_rows = rows_of(0, blocks)
    send = dot(grad_rows[half_rows:], qkv, (1, 1)).astype(BF16)
    sent = flip(send, "core", 1)
    grad_near, grad_away = cut_third(grad_near, all_after(grad_far, send))
    grad_far = flip(grad_away, "cp", 1)
    out_near, out_away = cut_fourth(out_near, after(out_far, send))
    out_far = flip(out_away, "cp", 2)
    grad_rows = after(grad_rows, send, grad_away, out_away)
    qkv_local = dot(normed.reshape(row_len, width), grad_rows, (0, 0)).astype(BF16)
    gain_one = jnp.sum(qkv_local.astype(F32) * qkv.astype(F32), axis=1) / gains[0]
    gain_sum = jnp.concatenate([gain_one[None], gain_two, gain_three, gain_four])
    gain_sum = gain_sum.reshape(2 * xy_count, cp_count, 128).astype(BF16)
    gain_sum = jnp.pad(gain_sum, ((0, 0), (0, lines - cp_count), (0, 0)))
    rest = plain(jnp.concatenate([qkv_local, gain_sum.reshape(width, 128)], axis=1))
    rest = rest.reshape(xy_count, 2, lines, -1)
    rest_near, rest_away = pick(rest, core, 1), pick(rest, 1 - core, 1)
    rest_far = flip(rest_away, "core", 1)
    grad_rows = after(grad_rows, rest_away)
    far_away = total(dot(grad_rows[own:half_rows], qkv, (1, 1)), sent[own:])
    far = flip(far_away, "cp", 1)
    keep = dot(after(grad_rows, far_away)[:own], qkv, (1, 1))

    out_sum = total(out_near, out_far).reshape(xy_count, lines, part)
    rest_far = after(rest_far, far_away)
    three = 3 * part
    summed = total(rest_near[..., three:], rest_far[..., three:])
    rest_near, rest_far = rest_near[..., :three], rest_far[..., :three]
    rest = jnp.concatenate(
        [
            jnp.where(core == 0, rest_near, rest_far), jnp.where(core == 0, rest_far, rest_near),
            out_sum, summed,
        ],
        axis=2,
    )
    rest = plain(rest).reshape(2, 2, lines, -1)
    cut = rest.shape[3] // 256 * 128
    low, high = rest[..., :cut], rest[..., cut:]
    rest_near = pick(low, x_bit, 1), pick(high, y_bit, 0)
    rest_away = pick(low, 1 - x_bit, 1), pick(high, 1 - y_bit, 0)
    rest_far = send_first(rest_away)
    grad_near, grad_away = cut_fourth(grad_near, after(grad_far, *rest_away))
    grad_far = flip(grad_away, "cp", 2)
    far = after(far, grad_away)
    tokens_grad = end(keep, sent[:own], far, x.reshape(own, width), grad_hidden, gains)
    ended = tokens_grad
    tokens_grad = swap(tokens_grad)

    rest_far = all_after(rest_far, far)
    rest_near, rest_away = cut_second(rest_near, rest_far)
    rest_far = send_second(rest_away)
    rest = jnp.concatenate([total(a, b) for a, b in zip(rest_near, rest_far)], axis=1)
    qkv_sum = rest[:, : 2 * three].reshape(lines, 2, 3, part).transpose(2, 1, 0, 3)
    out_grad = rest[:, 2 * three : 2 * three + part].astype(F32)
    gain_sum = rest[:, 2 * three + part :]
    right = z >= 2
    even = parity == 0
    send_at = (
        jnp.where(right, 0, jnp.where(even, 2, 1)), jnp.where(right, jnp.where(even, 1, 0), 2)
    )
    keep_at = (
        jnp.where(right, jnp.where(even, 2, 1), 0), jnp.where(right, 2, jnp.where(even, 1, 0))
    )

    def flat(qkv_blocks, gain_block):
        return jnp.concatenate([*qkv_blocks.reshape(-1, lines, part), gain_block], axis=1)

    rest = flat(jnp.stack([pick(qkv_sum, at, 0) for at in keep_at]), gain_sum)
    rest_away = flat(jnp.stack([pick(qkv_sum, at, 0) for at in send_at]), gain_sum)
    rest = total(rest, flip(rest_away, "cp", 2))
    blocks_of = [rest[:, n * part : (n + 1) * part] for n in range(4)]
    gain_sum = rest[:, 4 * part :]
    slots = jnp.stack([jnp.stack(blocks_of[:2]), jnp.stack(blocks_of[2:4])])
    rest_away = flat(pick(slots, jnp.where(z == 0, 1, 0), 0), gain_sum)
    rest_far = flip(rest_away, "cp", 1)
    sent = [rest_far[:, :part], rest_far[:, part : 2 * part]]

    def choice(*four):
        return jnp.where(
            z == 0, four[0], jnp.where(z == 1, four[1], jnp.where(z == 2, four[2], four[3]))
        )

    qkv_grad = jnp.concatenate(
        [
            choice(slots[0, 0], slots[0, 1], sent[0], sent[1]),
            choice(slots[0, 1], sent[0], sent[1], slots[1, 0]),
            choice(sent[0], sent[1], slots[0, 0], slots[1, 1]),
        ],
        axis=1,
    ).astype(F32)
    gains_grad = pick(gain_sum.astype(F32) + rest_far[:, 2 * part :].astype(F32), z, 0)
    tokens_grad = after(tokens_grad, rest_away).astype(F32).reshape(tokens.shape)

    both = plain(total(grad_near, after(grad_far, ended))).reshape(2, 2, lines, hidden_part)
    mine, other = pick(both, core, 0), flip(pick(both, 1 - core, 0), "core", 1)
    up_grad = ordered(core == 0, mine[0], other[0], 1).astype(F32)
    down_grad = ordered(core == 0, mine[1], other[1], 1).T.astype(F32)
    return mixed, tokens_grad, qkv_grad, out_grad, up_grad, down_grad, gains_grad


def solution(mesh):
    rows, cp = mesh.shape["rows"], mesh.shape["cp"]
    if (rows, cp) == (8, 4):
        grid = Mesh(mesh.devices.reshape(rows // 2, 2, cp), ("xy", "core", "cp"))
        run, lines = body, ("xy", "core")
    else:
        grid, run, lines = mesh, general_body, ("rows",)
    tokens = P(lines, None, "cp", None)
    weight, down, gains = P(lines, "cp"), P("cp", lines), P(lines + ("cp",))
    return jax.shard_map(
        run,
        mesh=grid,
        in_specs=(tokens, P(lines, None), weight, weight, weight, down, gains, tokens),
        out_specs=(tokens, tokens, weight, weight, weight, down, gains),
        check_vma=False,
    )
```

```python
import functools
import math

import jax
import jax.numpy as jnp
from jax import lax
from jax.experimental import pallas as pl
from jax.experimental.layout import Layout, with_layout_constraint
from jax.experimental.pallas import tpu as pltpu
from jax.sharding import Mesh, PartitionSpec as P

HEADS = 16
HEAD_DIM = 64


NORM_EPS = 1e-05
MASKED = -1e30


def layer_norm(values):
    average = jnp.mean(values, axis=-1, keepdims=True)
    centred = values - average
    spread = jnp.mean(centred * centred, axis=-1, keepdims=True)
    return centred * lax.rsqrt(spread + NORM_EPS)


def norm_back(values, upstream):
    _, pull_back = jax.vjp(layer_norm, values)
    return pull_back(upstream)[0]


def gelu_tanh(values):
    return jax.nn.gelu(values, approximate=True)


def rotate(values, cosine, sine_part):
    half_width = values.shape[-1] // 2
    first_half = values[..., :half_width]
    second_half = values[..., half_width:]
    return jnp.concatenate(
        [
            first_half * cosine - second_half * sine_part,
            second_half * cosine + first_half * sine_part,
        ],
        axis=-1,
    )


def rounded(values):
    return lax.optimization_barrier(values.astype(jnp.bfloat16)).astype(jnp.float32)


def doc_start_of(starts, positions):
    return jnp.max(
        jnp.where(starts[:, None, :] <= positions[None, :, None], starts[:, None, :], 0), axis=-1
    )


def general_body(tokens, doc_starts, qkv_weight, out_weight, up_weight, down_weight, norm_gains, cotangent):
    rows_count = lax.axis_size("rows")
    cp_count = lax.axis_size("cp")
    qkv_rows, out_rows, up_rows, down_rows, gain_piece = (
        lax.all_gather(qkv_weight, "rows", axis=0, tiled=True),
        lax.all_gather(out_weight, "rows", axis=0, tiled=True),
        lax.all_gather(up_weight, "rows", axis=0, tiled=True),
        lax.all_gather(down_weight, "rows", axis=1, tiled=True),
        lax.all_gather(norm_gains, "rows", axis=0, tiled=True),
    )
    qkv_full, out_full, gain_mixed = (
        lax.all_gather(qkv_rows, "cp", axis=1, tiled=True),
        lax.all_gather(out_rows, "cp", axis=1, tiled=True),
        lax.all_gather(gain_piece, "cp", axis=0, tiled=True),
    )
    gain_full = jnp.transpose(gain_mixed.reshape(cp_count, rows_count, -1), (1, 0, 2)).reshape(-1)
    row_count, _, span_len, width = tokens.shape
    half_len = span_len * cp_count
    row_len = 2 * half_len
    queries_dev = 2 * span_len
    token_total = row_count * queries_dev
    group_total = row_count * row_len
    gain_rows = gain_full.astype(jnp.float32).reshape(4, width)
    score_scale = HEAD_DIM ** (-0.5)
    local_pos = lax.axis_index("cp") * span_len + jnp.arange(span_len, dtype=jnp.int32)
    query_pos = jnp.concatenate([local_pos, row_len - 1 - local_pos])
    half_pos = jnp.arange(half_len, dtype=jnp.int32)
    key_pos = jnp.concatenate([half_pos, row_len - 1 - half_pos])
    query_start = doc_start_of(doc_starts, query_pos)
    key_start = doc_start_of(doc_starts, key_pos)
    freq_index = jnp.arange(HEAD_DIM // 2, dtype=jnp.float32)
    inverse_freq = jnp.exp(-math.log(10000.0) * 2.0 * freq_index / HEAD_DIM)
    angles = (query_pos[None, :] - query_start).astype(jnp.float32)[..., None] * inverse_freq
    cosine = jnp.cos(angles)[:, :, None, :]
    sine_part = jnp.sin(angles)[:, :, None, :]
    head_shape = (row_count, queries_dev, HEADS, HEAD_DIM)
    flat_shape = (row_count, queries_dev, width)
    fold_shape = (row_count, 2, span_len, width)
    group_shape = (row_count, 2, half_len, width)
    full_shape = (row_count, row_len, HEADS, HEAD_DIM)
    inputs = tokens.astype(jnp.float32).reshape(flat_shape)
    normed_in = layer_norm(inputs)
    normed = (normed_in * gain_rows[0]).astype(jnp.bfloat16)
    linear = jnp.dot(normed, qkv_full, preferred_element_type=jnp.float32)
    query_rows = rotate(linear[..., :width].reshape(head_shape), cosine, sine_part).astype(
        jnp.bfloat16
    )
    key_local = rotate(
        linear[..., width : 2 * width].reshape(head_shape), cosine, sine_part
    ).astype(jnp.bfloat16)
    value_local = linear[..., 2 * width :].reshape(head_shape).astype(jnp.bfloat16)
    key_sent, value_sent = (
        lax.all_gather(key_local.reshape(fold_shape), "cp", axis=2, tiled=True),
        lax.all_gather(value_local.reshape(fold_shape), "cp", axis=2, tiled=True),
    )
    key_rows = key_sent.reshape(full_shape)
    value_rows = value_sent.reshape(full_shape)
    block_size = min(512, row_len)
    block_count = row_len // block_size
    block_range = jnp.arange(block_count)

    def block_scores(block_index):
        first_key = block_index * block_size
        key_block = lax.dynamic_slice_in_dim(key_rows, first_key, block_size, 1)
        pos_block = lax.dynamic_slice_in_dim(key_pos, first_key, block_size, 0)
        start_block = lax.dynamic_slice_in_dim(key_start, first_key, block_size, 1)
        raw_scores = jnp.einsum(
            "rqhd,rkhd->rhqk", query_rows, key_block, preferred_element_type=jnp.float32
        )
        allowed = (query_start[:, None, :, None] == start_block[:, None, None, :]) & (
            pos_block[None, None, None, :] <= query_pos[None, None, :, None]
        )
        return (raw_scores * score_scale, allowed)

    def max_step(carry, block_index):
        running_max, running_sum = carry
        scores, allowed = block_scores(block_index)
        scores = jnp.where(allowed, scores, MASKED)
        new_max = jnp.maximum(running_max, jnp.max(scores, axis=-1))
        running_sum = running_sum * jnp.exp(running_max - new_max) + jnp.sum(
            jnp.where(allowed, jnp.exp(scores - new_max[..., None]), 0.0), axis=-1
        )
        return ((new_max, running_sum), None)

    stat_shape = (row_count, HEADS, queries_dev)
    (running_max, running_sum), _ = lax.scan(
        max_step,
        (jnp.full(stat_shape, MASKED, jnp.float32), jnp.zeros(stat_shape, jnp.float32)),
        block_range,
    )
    log_total = running_max + jnp.log(running_sum)

    def value_step(totals, block_index):
        scores, allowed = block_scores(block_index)
        probs = jnp.where(allowed, jnp.exp(scores - log_total[..., None]), 0.0).astype(jnp.bfloat16)
        value_block = lax.dynamic_slice_in_dim(value_rows, block_index * block_size, block_size, 1)
        return (
            totals
            + jnp.einsum("rhqk,rkhd->rqhd", probs, value_block, preferred_element_type=jnp.float32),
            None,
        )

    attended, _ = lax.scan(value_step, jnp.zeros(head_shape, jnp.float32), block_range)
    mixed_heads = attended.reshape(flat_shape).astype(jnp.bfloat16)
    branch = jnp.dot(mixed_heads, out_full, preferred_element_type=jnp.float32)
    branch_hat = layer_norm(branch)
    hidden = inputs + branch_hat * gain_rows[1]
    hidden_hat = layer_norm(hidden)
    normed_mid = (hidden_hat * gain_rows[2]).astype(jnp.bfloat16)
    ffn_in = lax.all_gather(normed_mid.reshape(fold_shape), "cp", axis=2, tiled=True).reshape(
        group_total, width
    )
    up_proj = jnp.dot(ffn_in, up_rows, preferred_element_type=jnp.float32)
    activation = gelu_tanh(up_proj).astype(jnp.bfloat16)
    down_terms = jnp.dot(activation, down_rows, preferred_element_type=jnp.float32)
    down_proj = (
        lax.psum_scatter(
            down_terms.reshape(group_shape).astype(jnp.bfloat16),
            "cp",
            scatter_dimension=2,
            tiled=True,
        )
        .astype(jnp.float32)
        .reshape(flat_shape)
    )
    down_hat = layer_norm(down_proj)
    mixed = (hidden + down_hat * gain_rows[3]).astype(jnp.bfloat16).reshape(tokens.shape)
    upstream = cotangent.astype(jnp.float32).reshape(flat_shape)
    gain_four = jnp.sum(upstream * down_hat, axis=(0, 1))
    grad_down_out = norm_back(down_proj, upstream * gain_rows[3]).astype(jnp.bfloat16)
    grad_out_rows = lax.all_gather(
        grad_down_out.reshape(fold_shape), "cp", axis=2, tiled=True
    ).reshape(group_total, width)
    down_local = jnp.einsum(
        "tf,td->fd", activation, grad_out_rows, preferred_element_type=jnp.float32
    )
    grad_act = jnp.einsum("td,fd->tf", grad_out_rows, down_rows, preferred_element_type=jnp.float32)
    _, gelu_pull = jax.vjp(gelu_tanh, up_proj)
    grad_up = gelu_pull(grad_act)[0].astype(jnp.bfloat16)
    up_local = jnp.einsum("tc,tf->cf", ffn_in, grad_up, preferred_element_type=jnp.float32)
    mid_terms = jnp.einsum("tf,cf->tc", grad_up, up_rows, preferred_element_type=jnp.float32)
    grad_mid = (
        lax.psum_scatter(
            mid_terms.reshape(group_shape).astype(jnp.bfloat16),
            "cp",
            scatter_dimension=2,
            tiled=True,
        )
        .astype(jnp.float32)
        .reshape(flat_shape)
    )
    gain_three = jnp.sum(grad_mid * hidden_hat, axis=(0, 1))
    grad_hidden = upstream + norm_back(hidden, grad_mid * gain_rows[2])
    gain_two = jnp.sum(grad_hidden * branch_hat, axis=(0, 1))
    grad_branch = norm_back(branch, grad_hidden * gain_rows[1]).astype(jnp.bfloat16)
    out_local = jnp.einsum(
        "tc,te->ce",
        mixed_heads.reshape(token_total, width),
        grad_branch.reshape(token_total, width),
        preferred_element_type=jnp.float32,
    )
    grad_heads = (
        jnp.einsum("rqe,ce->rqc", grad_branch, out_full, preferred_element_type=jnp.float32)
        .astype(jnp.bfloat16)
        .reshape(head_shape)
    )
    delta_sum = jnp.transpose(
        jnp.sum(grad_heads.astype(jnp.float32) * attended, axis=-1), (0, 2, 1)
    )

    def score_grads(block_index):
        scores, allowed = block_scores(block_index)
        probs = jnp.where(allowed, jnp.exp(scores - log_total[..., None]), 0.0)
        first_key = block_index * block_size
        key_block = lax.dynamic_slice_in_dim(key_rows, first_key, block_size, 1)
        value_block = lax.dynamic_slice_in_dim(value_rows, first_key, block_size, 1)
        grad_probs = jnp.einsum(
            "rqhd,rkhd->rhqk", grad_heads, value_block, preferred_element_type=jnp.float32
        )
        grad_scores = (probs * (grad_probs - delta_sum[..., None]) * score_scale).astype(
            jnp.bfloat16
        )
        return (probs, grad_scores, key_block)

    def grad_step(grad_query, block_index):
        probs, grad_scores, key_block = score_grads(block_index)
        grad_query = grad_query + jnp.einsum(
            "rhqk,rkhd->rqhd", grad_scores, key_block, preferred_element_type=jnp.float32
        )
        key_part = jnp.einsum(
            "rhqk,rqhd->rkhd", grad_scores, query_rows, preferred_element_type=jnp.float32
        )
        value_part = jnp.einsum(
            "rhqk,rqhd->rkhd",
            probs.astype(jnp.bfloat16),
            grad_heads,
            preferred_element_type=jnp.float32,
        )
        return (grad_query, (key_part, value_part))

    grad_query, (key_parts, value_parts) = lax.scan(
        grad_step, jnp.zeros(head_shape, jnp.float32), block_range
    )
    key_terms = jnp.moveaxis(key_parts, 0, 1).reshape(group_shape)
    value_terms = jnp.moveaxis(value_parts, 0, 1).reshape(group_shape)
    key_sum, value_sum = (
        lax.psum_scatter(
            key_terms.astype(jnp.bfloat16), "cp", scatter_dimension=2, tiled=True
        ).astype(jnp.float32),
        lax.psum_scatter(
            value_terms.astype(jnp.bfloat16), "cp", scatter_dimension=2, tiled=True
        ).astype(jnp.float32),
    )
    query_unturned = rotate(rounded(grad_query), cosine, -sine_part).reshape(flat_shape)
    key_unturned = rotate(rounded(key_sum.reshape(head_shape)), cosine, -sine_part).reshape(
        flat_shape
    )
    grad_linear = jnp.concatenate(
        [query_unturned, key_unturned, value_sum.reshape(flat_shape)], axis=-1
    ).astype(jnp.bfloat16)
    qkv_local = jnp.einsum(
        "tc,te->ce",
        normed.reshape(token_total, width),
        grad_linear.reshape(token_total, 3 * width),
        preferred_element_type=jnp.float32,
    )
    grad_normed = jnp.einsum(
        "rqe,ce->rqc", grad_linear, qkv_full, preferred_element_type=jnp.float32
    )
    gain_one = jnp.sum(grad_normed * normed_in, axis=(0, 1))
    tokens_grad = (grad_hidden + norm_back(inputs, grad_normed * gain_rows[0])).reshape(
        tokens.shape
    )
    gain_local = jnp.concatenate([gain_one, gain_two, gain_three, gain_four])
    gain_order = jnp.transpose(gain_local.reshape(rows_count, cp_count, -1), (1, 0, 2)).reshape(-1)
    qkv_mid, out_mid, gain_mid = (
        lax.psum_scatter(
            qkv_local.astype(jnp.bfloat16), "cp", scatter_dimension=1, tiled=True
        ).astype(jnp.float32),
        lax.psum_scatter(
            out_local.astype(jnp.bfloat16), "cp", scatter_dimension=1, tiled=True
        ).astype(jnp.float32),
        lax.psum_scatter(
            gain_order.astype(jnp.bfloat16), "cp", scatter_dimension=0, tiled=True
        ).astype(jnp.float32),
    )
    qkv_sum, out_sum, up_sum, down_sum, gain_sum = (
        lax.psum_scatter(
            qkv_mid.astype(jnp.bfloat16), "rows", scatter_dimension=0, tiled=True
        ).astype(jnp.float32),
        lax.psum_scatter(
            out_mid.astype(jnp.bfloat16), "rows", scatter_dimension=0, tiled=True
        ).astype(jnp.float32),
        lax.psum_scatter(
            up_local.astype(jnp.bfloat16), "rows", scatter_dimension=0, tiled=True
        ).astype(jnp.float32),
        lax.psum_scatter(
            down_local.astype(jnp.bfloat16), "rows", scatter_dimension=1, tiled=True
        ).astype(jnp.float32),
        lax.psum_scatter(
            gain_mid.astype(jnp.bfloat16), "rows", scatter_dimension=0, tiled=True
        ).astype(jnp.float32),
    )
    return (mixed, tokens_grad, qkv_sum, out_sum, up_sum, down_sum, gain_sum)


F32 = jnp.float32
BF16 = jnp.bfloat16
MIB = 1024 * 1024


def params(grid_rank, mebibytes=24):
    return pltpu.CompilerParams(
        dimension_semantics=("arbitrary",) * grid_rank, vmem_limit_bytes=mebibytes * MIB
    )


def lasting(microseconds):
    return pl.CostEstimate(
        flops=int(microseconds * 1e7), bytes_accessed=1024, transcendentals=0
    )


def turned(x, cosine, sine):
    lane = lax.broadcasted_iota(jnp.int32, x.shape, 1)
    other = jnp.where((lane & 32) == 0, pltpu.roll(x, 96, 1), pltpu.roll(x, 32, 1))
    return x * cosine + other * sine


def attend_kernel(tile, bounds, slot_of, q_ref, k_ref, v_ref, pcol_ref, prow_ref, srow_ref,
                  o_ref, ob_ref, lse_ref, vt_ref):
    i = pl.program_id(1)

    @pl.when(i == 0)
    def _():
        vt_ref[...] = v_ref[...].astype(F32).T.astype(BF16)

    qt = q_ref[...].astype(F32).T
    row = lax.broadcasted_iota(jnp.int32, qt.shape, 0)
    lo = bounds[0, i]
    mid = jnp.minimum(bounds[1, i], i)
    qpos = prow_ref[...]
    qstart = srow_ref[...]
    qh = [jnp.where((row >= 64) == (h == 1), qt, 0.0).astype(BF16) for h in range(2)]

    def step(j, carry, masked):
        at = pl.multiple_of(j * tile, tile)
        k = k_ref[pl.ds(at, tile), :]
        scores = [jnp.dot(k, qh[h], preferred_element_type=F32) for h in range(2)]
        if masked:
            kpos = pcol_ref[pl.ds(at, tile), :]
            allowed = (kpos >= qstart) & (kpos <= qpos)
            scores = [jnp.where(allowed, s, MASKED) for s in scores]
        out = []
        for h in range(2):
            top, total, acc = carry[h]
            new = jnp.maximum(top, jnp.max(scores[h], axis=0, keepdims=True))
            p = jnp.exp(scores[h] - new)
            keep = jnp.exp(top - new)
            total = total * keep + jnp.sum(p, axis=0, keepdims=True)
            acc = acc * keep + jnp.dot(
                vt_ref[h * 64 : h * 64 + 64, pl.ds(at, tile)], p.astype(BF16),
                preferred_element_type=F32,
            )
            out.append((new, total, acc))
        return tuple(out)

    start = (
        jnp.full((1, tile), MASKED, F32), jnp.zeros((1, tile), F32), jnp.zeros((64, tile), F32)
    )
    carry = step(i, (start, start), True)
    carry = lax.fori_loop(lo, mid, functools.partial(step, masked=True), carry)
    carry = lax.fori_loop(mid, i, functools.partial(step, masked=False), carry)
    parts = []
    for h in range(2):
        top, total, acc = carry[h]
        lse_ref[0, h : h + 1, :] = top + jnp.log(total)
        parts.append(acc / total)
    out = jnp.concatenate(parts, axis=0).T
    o_ref[...] = out
    span = ob_ref.shape[1]
    for b in range(tile // span):
        ob_ref[slot_of[i * (tile // span) + b]] = out[b * span : (b + 1) * span].astype(BF16)


def attend(pair, q, k, v, pcol, prow, srow, bounds, slot_of, tile):
    rows, width = q.shape
    blocks = slot_of.shape[0]
    span = rows // blocks
    count = rows // tile
    grid_spec = pltpu.PrefetchScalarGridSpec(
        num_scalar_prefetch=2,
        grid=(1, count),
        in_specs=[
            pl.BlockSpec((tile, 128), lambda p, i, b, t: (i, pair)),
            pl.BlockSpec((rows, 128), lambda p, i, b, t: (0, pair)),
            pl.BlockSpec((rows, 128), lambda p, i, b, t: (0, pair)),
            pl.BlockSpec((rows, 1), lambda p, i, b, t: (0, 0)),
            pl.BlockSpec((1, tile), lambda p, i, b, t: (0, i)),
            pl.BlockSpec((1, tile), lambda p, i, b, t: (0, i)),
        ],
        out_specs=[
            pl.BlockSpec((tile, 128), lambda p, i, b, t: (i, p)),
            pl.BlockSpec((blocks, span, 128), lambda p, i, b, t: (0, 0, p)),
            pl.BlockSpec((1, 2, tile), lambda p, i, b, t: (p, 0, i)),
        ],
        scratch_shapes=[pltpu.VMEM((128, rows), BF16)],
    )
    return pl.pallas_call(
        functools.partial(attend_kernel, tile),
        grid_spec=grid_spec,
        out_shape=[
            jax.ShapeDtypeStruct((rows, 128), F32),
            jax.ShapeDtypeStruct((blocks, span, 128), BF16),
            jax.ShapeDtypeStruct((1, 2, rows), F32),
        ],
        compiler_params=params(2),
        cost_estimate=lasting(14),
        name="attend",
    )(bounds, slot_of, q, k, v, pcol, prow, srow)


def attend_back_kernel(tile, first, steps, bounds, slot_of, q_ref, k_ref, v_ref, do_ref, o_ref,
                       lse_ref, pcol_ref, prow_ref, srow_ref, cos_ref, sin_ref, *refs):
    qm, dom, qtm, dotm, delta, dqt = refs[-6:]
    count = q_ref.shape[0] // tile
    last = first + steps
    before = refs[0] if first else None
    g_ref = refs[1 if first else 0]
    after_ref = refs[1] if last < count else None
    j = first + pl.program_id(1)
    span = do_ref.shape[1]

    @pl.when(pl.program_id(1) == 0)
    def _():
        for t in range(first, count):
            part = pl.ds(t * tile, tile)
            q = q_ref[part, :].astype(F32)
            do = jnp.concatenate(
                [do_ref[slot_of[t * tile // span + b]] for b in range(tile // span)], axis=0
            ).astype(F32)
            qt, dot = q.T, do.T
            lane = lax.broadcasted_iota(jnp.int32, q.shape, 1)
            row = lax.broadcasted_iota(jnp.int32, qt.shape, 0)
            prod = dot * o_ref[part, :].T
            for h in range(2):
                mine = (lane >= 64) == (h == 1)
                mine_t = (row >= 64) == (h == 1)
                qm[h, part, :] = jnp.where(mine, q, 0.0).astype(BF16)
                dom[h, part, :] = jnp.where(mine, do, 0.0).astype(BF16)
                qtm[h, :, part] = jnp.where(mine_t, qt, 0.0).astype(BF16)
                dotm[h, :, part] = jnp.where(mine_t, dot, 0.0).astype(BF16)
                delta[h : h + 1, part] = jnp.sum(
                    prod[h * 64 : h * 64 + 64], axis=0, keepdims=True
                )
        if before is None:
            dqt[...] = jnp.zeros_like(dqt)
        else:
            dqt[:, first * tile :] = before[0]

    here = pl.ds(pl.multiple_of(j * tile, tile), tile)
    k = k_ref[here, :]
    v = v_ref[here, :]
    kt = k.astype(F32).T.astype(BF16)
    kpos = pcol_ref[here, :]
    full = jnp.maximum(bounds[2, j], j + 1)
    end = bounds[3, j]

    def step(i, carry, masked):
        dk, dv = carry
        part = pl.ds(pl.multiple_of(i * tile, tile), tile)
        if masked:
            allowed = (kpos >= srow_ref[:, part]) & (kpos <= prow_ref[:, part])
        for h in range(2):
            s = jnp.dot(k, qtm[h, :, part], preferred_element_type=F32)
            p = jnp.exp(s - lse_ref[0, h : h + 1, part])
            if masked:
                p = jnp.where(allowed, p, 0.0)
            dp = jnp.dot(v, dotm[h, :, part], preferred_element_type=F32)
            ds = (p * (dp - delta[h : h + 1, part])).astype(BF16)
            dv = dv + jnp.dot(p.astype(BF16), dom[h, part, :], preferred_element_type=F32)
            dk = dk + jnp.dot(ds, qm[h, part, :], preferred_element_type=F32)
            dqt[h * 64 : h * 64 + 64, part] += jnp.dot(
                kt[h * 64 : h * 64 + 64, :], ds, preferred_element_type=F32
            )
        return dk, dv

    carry = (jnp.zeros((tile, 128), F32), jnp.zeros((tile, 128), F32))
    carry = step(j, carry, True)
    carry = lax.fori_loop(j + 1, full, functools.partial(step, masked=False), carry)
    carry = lax.fori_loop(full, end, functools.partial(step, masked=True), carry)
    dk, dv = carry

    def unturned(x, at):
        x = x.astype(BF16).astype(F32)
        return turned(x, cos_ref[at, :], -sin_ref[at, :]).astype(BF16)

    grad_k, grad_v = unturned(dk, here), dv.astype(BF16)
    for b in range(tile // span):
        at = slot_of[j * (tile // span) + b] >> 1
        g_ref[at, :, 128:256] = grad_k[b * span : (b + 1) * span]
        g_ref[at, :, 256:384] = grad_v[b * span : (b + 1) * span]

    @pl.when(pl.program_id(1) == steps - 1)
    def _():
        for t in range(first, last):
            part = pl.ds(t * tile, tile)
            grad_q = unturned(dqt[:, part].T * 0.125, part)
            for b in range(tile // span):
                at = slot_of[t * (tile // span) + b] >> 1
                g_ref[at, :, 0:128] = grad_q[b * span : (b + 1) * span]
        if after_ref is not None:
            after_ref[0] = dqt[:, last * tile :]


def attend_back(half, q, k, v, do, o, lse, pcol, prow, srow, cosine, sine, bounds, slot_of, tile,
                before):
    rows, width = q.shape
    pairs = width // 128
    blocks, span, _ = do.shape
    count = rows // tile
    steps = count // 2
    first = half * steps
    whole = pl.BlockSpec((rows, 128), lambda p, j, b, t: (0, p))
    table = pl.BlockSpec((rows, 128), lambda p, j, b, t: (0, 0))
    line = pl.BlockSpec((1, rows), lambda p, j, b, t: (0, 0))
    rest = pl.BlockSpec((1, 128, rows // 2), lambda p, j, b, t: (p, 0, 0))
    outs = [
        (
            jax.ShapeDtypeStruct((blocks // 2, span, 3 * width), BF16),
            pl.BlockSpec((blocks // 2, span, 384), lambda p, j, b, t: (0, 0, p)),
        )
    ]
    if not half:
        outs.append((jax.ShapeDtypeStruct((pairs, 128, rows // 2), F32), rest))
    grid_spec = pltpu.PrefetchScalarGridSpec(
        num_scalar_prefetch=2,
        grid=(pairs, steps),
        in_specs=[
            whole, whole, whole,
            pl.BlockSpec((blocks, span, 128), lambda p, j, b, t: (0, 0, p)),
            whole,
            pl.BlockSpec((1, 2, rows), lambda p, j, b, t: (p, 0, 0)),
            pl.BlockSpec((rows, 1), lambda p, j, b, t: (0, 0)),
            line, line, table, table,
        ]
        + [rest] * len(before),
        out_specs=[spec for _, spec in outs],
        scratch_shapes=[
            pltpu.VMEM((2, rows, 128), BF16), pltpu.VMEM((2, rows, 128), BF16),
            pltpu.VMEM((2, 128, rows), BF16), pltpu.VMEM((2, 128, rows), BF16),
            pltpu.VMEM((2, rows), F32), pltpu.VMEM((128, rows), F32),
        ],
    )
    return pl.pallas_call(
        functools.partial(attend_back_kernel, tile, first, steps),
        grid_spec=grid_spec,
        out_shape=[shape for shape, _ in outs],
        compiler_params=params(2, 40),
        cost_estimate=lasting(23),
        name="attend_back",
    )(bounds, slot_of, q, k, v, do, o, lse, pcol, prow, srow, cosine, sine, *before)


def tile_bounds(starts_nat, tile):
    rows = starts_nat.shape[0]
    count = rows // tile
    tiles = starts_nat.reshape(count, tile)
    first, last = tiles[:, 0], tiles[:, -1]
    at = jnp.arange(count, dtype=jnp.int32) * tile
    lo = first // tile
    mid = (last + tile - 1) // tile
    full = jnp.sum((last[None, :] <= at[:, None]).astype(jnp.int32), axis=1)
    end = jnp.sum((first[None, :] <= at[:, None] + tile - 1).astype(jnp.int32), axis=1)
    return jnp.stack([lo, mid, full, end]).astype(jnp.int32)


def normalized(x):
    centred = x - jnp.mean(x, axis=1, keepdims=True)
    scale = lax.rsqrt(jnp.mean(centred * centred, axis=1, keepdims=True) + NORM_EPS)
    return centred * scale, scale


def normalized_back(hat, scale, upstream):
    level = jnp.mean(upstream, axis=1, keepdims=True)
    slant = jnp.mean(upstream * hat, axis=1, keepdims=True)
    return scale * (upstream - level - hat * slant)


def dot_nt(a, b):
    return lax.dot_general(a, b, (((1,), (1,)), ((), ())), preferred_element_type=F32)


def call(kernel, name, grid, tables, ins, outs, microseconds, *arrays):
    return pl.pallas_call(
        kernel,
        grid_spec=pltpu.PrefetchScalarGridSpec(
            num_scalar_prefetch=len(tables),
            grid=grid,
            in_specs=ins,
            out_specs=[spec for _, spec in outs],
        ),
        out_shape=[shape for shape, _ in outs],
        compiler_params=params(len(grid)),
        cost_estimate=lasting(microseconds),
        name=name,
    )(*tables, *arrays)


def shaped(dtype, *shape):
    return jax.ShapeDtypeStruct(shape, dtype)


def fixed(*shape):
    return pl.BlockSpec(shape, lambda *_: (0,) * len(shape))


def project_kernel(blocks, slots, near, far, gain_ref, w_ref, cos_ref, sin_ref, *refs):
    q_ref, k_ref, v_ref, n_ref = refs[-4:]
    width = q_ref.shape[1]
    x = jnp.where(slots[pl.program_id(0)] < 4, near[0], far[0]).astype(F32)
    normed = (normalized(x)[0] * gain_ref[0:1, :]).astype(BF16)
    n_ref[0] = normed
    linear = jnp.dot(normed, w_ref[...], preferred_element_type=F32)
    for at in range(0, width, 128):
        q = turned(linear[:, 3 * at : 3 * at + 128], cos_ref[...], sin_ref[...])
        k = turned(linear[:, 3 * at + 128 : 3 * at + 256], cos_ref[...], sin_ref[...])
        q_ref[:, at : at + 128] = q.astype(BF16) * jnp.asarray(0.125, BF16)
        k_ref[:, at : at + 128] = k.astype(BF16)
        v_ref[:, at : at + 128] = linear[:, 3 * at + 256 : 3 * at + 384].astype(BF16)


def project(near, far, gains, w, cosine, sine, blocks, slots, before):
    _, rows, depth = near.shape
    width = w.shape[1] // 3
    count = 2 * blocks.shape[0]
    piece = pl.BlockSpec((1, rows, depth), lambda i, b, s: (s[i] & 1, 0, 0))
    angle = pl.BlockSpec((rows, 128), lambda i, b, s: (b[i], 0))
    out = shaped(BF16, count * rows, width)
    normed = shaped(BF16, count, rows, depth)
    block = pl.BlockSpec((rows, width), lambda i, b, s: (b[i], 0))
    return pl.pallas_call(
        project_kernel,
        grid_spec=pltpu.PrefetchScalarGridSpec(
            num_scalar_prefetch=2,
            grid=blocks.shape,
            in_specs=[piece, piece, fixed(*gains.shape), fixed(*w.shape), angle, angle]
            + [pl.BlockSpec(memory_space=pl.ANY)] * len(before),
            out_specs=[
                block, block, block,
                pl.BlockSpec((1, rows, depth), lambda i, b, s: ((s[i] & 1) * 4 + (s[i] >> 1), 0, 0)),
            ],
        ),
        out_shape=[out, out, out, normed],
        input_output_aliases={8 + n: n for n in range(len(before))},
        compiler_params=params(1),
        cost_estimate=lasting(7),
        name="project",
    )(blocks, slots, near, far, gains, w, cosine, sine, *before)


def mix_kernel(group, own, near, far, both, w_ref, x_ref, gain_ref,
               heads_ref, hat_ref, scale_ref, hidden_ref, mid_ref):
    width = own.shape[2]
    for r, piece in enumerate((own[0], far[0], near[0], both[0])):
        at = pl.ds(pl.multiple_of((group[0] ^ r) * width, width), width)
        heads_ref[:, at] = piece
    branch = jnp.dot(heads_ref[...], w_ref[...], preferred_element_type=F32)
    hat, scale = normalized(branch)
    hidden = x_ref[0].astype(F32) + hat * gain_ref[1:2, :]
    hat_ref[...] = hat
    scale_ref[...] = scale
    hidden_ref[...] = hidden
    mid_ref[...] = (normalized(hidden)[0] * gain_ref[2:3, :]).astype(BF16)


def mix(group, local, near, far, both, w, x, gains):
    _, rows, part = local.shape
    count, _, width = x.shape
    block = pl.BlockSpec((1, rows, part), lambda i, g: (i, 0, 0))
    row = pl.BlockSpec((rows, width), lambda i, g: (i, 0))
    total = count * rows
    return call(
        mix_kernel, "mix", (count,), [group],
        [
            block, block, block, block, fixed(*w.shape), pl.BlockSpec((1, rows, width), lambda i, g: (i, 0, 0)),
            fixed(*gains.shape),
        ],
        [
            (shaped(BF16, total, width), row),
            (shaped(F32, total, width), row),
            (shaped(F32, total, 1), pl.BlockSpec((rows, 1), lambda i, g: (i, 0))),
            (shaped(F32, total, width), row),
            (shaped(BF16, total, width), row),
        ],
        6, local, near, far, both, w, x, gains,
    )


def finish_kernel(terms_ref, sent_ref, hidden_ref, dy_ref, gain_ref, mixed_ref, grad_ref, sum_ref):
    down = terms_ref[...] + sent_ref[...].astype(F32)
    hat, scale = normalized(down)
    gain = gain_ref[3:4, :]
    dy = dy_ref[...].astype(F32)
    mixed_ref[...] = (hidden_ref[...] + hat * gain).astype(BF16)
    grad_ref[...] = normalized_back(hat, scale, dy * gain).astype(BF16)

    @pl.when(pl.program_id(0) == 0)
    def _():
        sum_ref[...] = jnp.zeros_like(sum_ref)

    sum_ref[...] += jnp.sum(dy * hat, axis=0, keepdims=True)


def finish(terms, sent, hidden, dy, gains):
    total, width = terms.shape
    rows = total // 2
    row = pl.BlockSpec((rows, width), lambda i: (i, 0))
    return call(
        finish_kernel, "finish", (2,), [],
        [row, row, row, row, fixed(*gains.shape)],
        [
            (shaped(BF16, total, width), row), (shaped(BF16, total, width), row),
            (shaped(F32, 1, width), fixed(1, width)),
        ],
        5, terms, sent, hidden, dy, gains,
    )


def turn_kernel(group, terms_ref, sent_ref, hidden_ref, dy_ref, hat_ref, scale_ref, w_ref, gain_ref,
                keep_ref, branch_ref, heads_ref, three_ref, two_ref):
    upstream = terms_ref[...] + sent_ref[...].astype(F32)
    hat, scale = normalized(hidden_ref[...])

    @pl.when(pl.program_id(0) == 0)
    def _():
        three_ref[...] = jnp.zeros_like(three_ref)
        two_ref[...] = jnp.zeros_like(two_ref)

    three_ref[...] += jnp.sum(upstream * hat, axis=0, keepdims=True)
    grad = dy_ref[...].astype(F32) + normalized_back(hat, scale, upstream * gain_ref[2:3, :])
    keep_ref[...] = grad
    branch_hat = hat_ref[...]
    two_ref[...] += jnp.sum(grad * branch_hat, axis=0, keepdims=True)
    branch = normalized_back(branch_hat, scale_ref[...], grad * gain_ref[1:2, :]).astype(BF16)
    branch_ref[...] = branch
    part = heads_ref.shape[3]
    for r in range(4):
        at = pl.ds(pl.multiple_of((group[0] ^ r) * part, part), part)
        heads_ref[r, 0] = dot_nt(branch, w_ref[at, :]).astype(BF16)


def turn(group, terms, sent, hidden, dy, hat, scale, w, gains):
    total, width = terms.shape
    rows = total // 2
    part = width // 4
    row = pl.BlockSpec((rows, width), lambda i, g: (i, 0))
    return call(
        turn_kernel, "turn", (2,), [group],
        [
            row, row, row, row, row, pl.BlockSpec((rows, 1), lambda i, g: (i, 0)),
            fixed(*w.shape), fixed(*gains.shape),
        ],
        [
            (shaped(F32, total, width), row), (shaped(BF16, total, width), row),
            (
                shaped(BF16, 4, 2, rows, part),
                pl.BlockSpec((4, 1, rows, part), lambda i, g: (0, i, 0, 0)),
            ),
            (shaped(F32, 1, width), fixed(1, width)), (shaped(F32, 1, width), fixed(1, width)),
        ],
        8, terms, sent, hidden, dy, hat, scale, w, gains,
    )


def end_kernel(keep_ref, far_ref, x_ref, grad_ref, gain_ref, o_ref):
    upstream = keep_ref[...] + far_ref[...].astype(F32)
    hat, scale = normalized(x_ref[...].astype(F32))
    grad = grad_ref[...] + normalized_back(hat, scale, upstream * gain_ref[0:1, :])
    o_ref[...] = grad.astype(BF16)


def end(keep, far, x, grad, gains):
    total, width = x.shape
    rows = total // 2
    row = pl.BlockSpec((rows, width), lambda i: (i, 0))
    return call(
        end_kernel, "end", (2,), [], [row] * 4 + [fixed(*gains.shape)],
        [(shaped(BF16, total, width), row)], 20, keep, far, x, grad, gains,
    )[0]


def plain(x):
    return with_layout_constraint(x, Layout(tuple(range(x.ndim))))


QKV_BLOCKS, OVER_BLOCKS, OUT_BLOCKS = 12, 2, 8
LOW_BLOCKS = 11
ALL_BLOCKS = QKV_BLOCKS + OVER_BLOCKS + OUT_BLOCKS + 1
LEFT = ((0, 0), (0, 1), (1, 0))
RIGHT = ((1, 1), (2, 0), (2, 1))


def tiles(array):
    return [array[:, at : at + 128] for at in range(0, array.shape[1], 128)]


def plus(a, b):
    return (a.astype(F32) + b.astype(F32)).astype(BF16)


def spread_first_kernel(place, qkv_ref, out_ref, gain_ref, over_ref, far_ref, out_far,
                        low, low_away, high, high_away):
    lines = far_ref.shape[1]
    spare = over_ref.shape[0] // 8
    wide = qkv_ref.shape[1]
    x_bit, y_bit, core = place[0], place[1], place[2]

    def fill(line, low_out, high_out):
        at = pl.ds(pl.multiple_of((2 * line + core) * lines, lines), lines)
        near = tiles(qkv_ref[at, :])
        far = tiles(far_ref[line, :, :wide])
        blocks = [jnp.where(core == 0, a, b) for a, b in zip(near, far)]
        blocks += [jnp.where(core == 0, a, b) for a, b in zip(far, near)]
        for c in range(2):
            rows = pl.ds(pl.multiple_of((2 * line + c) * spare, spare), spare)
            blocks.append(jnp.concatenate(tiles(over_ref[rows, :]), axis=0))
        blocks += [
            plus(a, b)
            for a, b in zip(tiles(out_ref[at, :]), tiles(out_far[line]))
        ]
        count = gain_ref.shape[1]
        gain = jnp.concatenate(
            [gain_ref[2 * line + core], jnp.zeros((lines - count, 128), BF16)], axis=0
        )
        blocks.append(plus(gain, far_ref[line, :, -128:]))
        for n, block in enumerate(blocks):
            if n < LOW_BLOCKS and low_out is not None:
                low_out[n] = block
            if n >= LOW_BLOCKS and high_out is not None:
                high_out[n - LOW_BLOCKS] = block

    for n in range(2):
        fill(2 * n + x_bit, low.at[n], None)
        fill(2 * n + 1 - x_bit, low_away.at[n], None)
        fill(2 * y_bit + n, None, high.at[n])
        fill(2 * (1 - y_bit) + n, None, high_away.at[n])


def spread_first(place, qkv, out, gain, over, far, out_far):
    lines = far.shape[1]
    low = shaped(BF16, 2, LOW_BLOCKS, lines, 128), fixed(2, LOW_BLOCKS, lines, 128)
    rest = ALL_BLOCKS - LOW_BLOCKS
    high = shaped(BF16, 2, rest, lines, 128), fixed(2, rest, lines, 128)
    arrays = (qkv, out, gain, over, far, out_far)
    return call(
        spread_first_kernel, "spread_first", (1,), [place], [fixed(*a.shape) for a in arrays],
        [low, low, high, high], 2, *arrays,
    )


def spread_second_kernel(place, low, low_far, high, high_far, low_o, low_away, high_o, high_away):
    for source, far, bit, near_o, away_o in (
        (low, low_far, place[1], low_o, low_away), (high, high_far, place[0], high_o, high_away)
    ):
        near_o[...] = plus(source[bit], far[bit])
        away_o[...] = plus(source[1 - bit], far[1 - bit])


def spread_second(place, *arrays):
    lows, highs = arrays[0].shape[1:], arrays[2].shape[1:]
    outs = [(shaped(BF16, *s), fixed(*s)) for s in (lows, lows, highs, highs)]
    return call(
        spread_second_kernel, "spread_second", (1,), [place], [fixed(*a.shape) for a in arrays],
        outs, 2, *arrays,
    )


def spread_third_kernel(place, low, low_far, high, high_far, near_o, away_o, over_o):
    half = place[4]

    def block(n):
        if n < LOW_BLOCKS:
            return plus(low[n], low_far[n])
        return plus(high[n - LOW_BLOCKS], high_far[n - LOW_BLOCKS])

    at = 0
    for (left_t, left_c), (right_t, right_c) in zip(LEFT, RIGHT):
        for pair in range(2):
            left = block(left_c * 6 + pair * 3 + left_t)
            right = block(right_c * 6 + pair * 3 + right_t)
            near_o[at] = jnp.where(half == 0, left, right)
            away_o[at] = jnp.where(half == 0, right, left)
            at += 1
    for c in range(2):
        over_o[c] = block(QKV_BLOCKS + c)
    first = QKV_BLOCKS + OVER_BLOCKS
    for n in range(4):
        left, right = block(first + n), block(first + 4 + n)
        near_o[at] = jnp.where(half == 0, left, right)
        away_o[at] = jnp.where(half == 0, right, left)
        at += 1
    near_o[at] = block(first + 8)
    away_o[at] = block(first + 8)


def spread_third(place, *arrays):
    lines = arrays[0].shape[1]
    part = shaped(BF16, 11, lines, 128), fixed(11, lines, 128)
    over = shaped(BF16, 2, lines, 128), fixed(2, lines, 128)
    return call(
        spread_third_kernel, "spread_third", (1,), [place], [fixed(*a.shape) for a in arrays],
        [part, part, over], 2, *arrays,
    )


def spread_fourth_kernel(place, near, far, near_o, away_o):
    odd = place[3] == 1
    blocks = [plus(near[n], far[n]) for n in range(11)]
    for pair in range(2):
        one, two, three = blocks[pair], blocks[2 + pair], blocks[4 + pair]
        near_o[pair] = jnp.where(odd, two, one)
        near_o[2 + pair] = jnp.where(odd, three, two)
        away_o[pair] = jnp.where(odd, one, three)
        near_o[4 + pair] = jnp.where(odd, blocks[8 + pair], blocks[6 + pair])
        away_o[2 + pair] = jnp.where(odd, blocks[6 + pair], blocks[8 + pair])
    near_o[6] = blocks[10]
    away_o[4] = blocks[10]


def spread_fourth(place, near, far):
    lines = near.shape[1]
    return call(
        spread_fourth_kernel, "spread_fourth", (1,), [place], [fixed(*near.shape)] * 2,
        [
            (shaped(BF16, 7, lines, 128), fixed(7, lines, 128)),
            (shaped(BF16, 5, lines, 128), fixed(5, lines, 128)),
        ],
        2, near, far,
    )


def spread_fifth_kernel(place, near, far, qkv_o, out_o, gain_o, gain_all):
    for pair in range(2):
        first, second = near[pair].astype(F32), near[2 + pair].astype(F32)
        other = far[pair].astype(F32)
        at = 128 * pair
        qkv_o[:, at : at + 128] = first
        qkv_o[:, 256 + at : 384 + at] = other
        qkv_o[:, 512 + at : 640 + at] = second
        out_o[:, at : at + 128] = near[4 + pair].astype(F32) + far[2 + pair].astype(F32)
    gain_all[...] = near[6].astype(F32) + far[4].astype(F32)
    gain_o[...] = gain_all[pl.ds(2 * place[4] + place[3], 1), :]


def spread_fifth(place, near, far):
    lines = near.shape[1]
    outs = [(shaped(F32, *s), fixed(*s)) for s in ((lines, 768), (lines, 256), (1, 128))]
    return pl.pallas_call(
        spread_fifth_kernel,
        grid_spec=pltpu.PrefetchScalarGridSpec(
            num_scalar_prefetch=1,
            grid=(1,),
            in_specs=[fixed(*near.shape), fixed(*far.shape)],
            out_specs=[spec for _, spec in outs],
            scratch_shapes=[pltpu.VMEM((lines, 128), F32)],
        ),
        out_shape=[shape for shape, _ in outs],
        compiler_params=params(1),
        cost_estimate=lasting(2),
        name="spread_fifth",
    )(place, near, far)


def flip(x, axis, bit):
    return lax.ppermute(plain(x), axis, [(i, i ^ bit) for i in range(lax.axis_size(axis))])


def swap(x):
    cp = lax.axis_size("cp")
    half = cp // 2
    pairs = []
    for z in range(half):
        low, high = cp + z, z + half
        pairs += [(low, high), (high, low)]
    return lax.ppermute(plain(x), ("core", "cp"), pairs)


def settled(x, moved):
    stays = (lax.axis_index("core") == 1) == (lax.axis_index("cp") >= lax.axis_size("cp") // 2)
    return jnp.where(stays, x, moved)


def ordered(first, mine, other, axis):
    return jnp.concatenate(
        [jnp.where(first, mine, other), jnp.where(first, other, mine)], axis=axis
    )


def placed(first, mine, other, at):
    return ordered(first, jnp.expand_dims(mine, at), jnp.expand_dims(other, at), at)


def after(x, *others):
    return lax.optimization_barrier((x, *others))[0]


def all_after(group, *others):
    return lax.optimization_barrier((*group, *others))[: len(group)]


def total(a, b):
    return (a.astype(F32) + b.astype(F32)).astype(BF16)


def flip_both(x):
    cp = lax.axis_size("cp")
    return lax.ppermute(
        x, ("core", "cp"), [(c * cp + z, (1 - c) * cp + (z ^ 1)) for c in range(2) for z in range(cp)]
    )


def dot(a, b, dims):
    return lax.dot_general(a, b, ((dims[:1], dims[1:]), ((), ())), preferred_element_type=F32)


def gelu_and_slope(u):
    c = math.sqrt(2.0 / math.pi)
    square = u * u
    t = jnp.tanh(u * (c + (c * 0.044715) * square))
    half = 0.5 + 0.5 * t
    slope = half + (0.5 * u) * (1.0 - t * t) * (c + (3.0 * 0.044715 * c) * square)
    return lax.optimization_barrier(((u * half).astype(BF16), slope.astype(BF16)))


def pick(x, at, axis):
    return lax.dynamic_index_in_dim(x, at, axis, False)


def widened(z, x, other):
    first, second = jnp.where(z & 1 == 0, x, other), jnp.where(z & 1 == 0, other, x)
    half = x.shape[1] // 2
    return jnp.concatenate(
        [first[:, :half], second[:, :half], first[:, half:], second[:, half:]], axis=1
    )


def body(tokens, doc_starts, qkv_weight, out_weight, up_weight, down_weight, norm_gains, cotangent):
    xy, core, z = lax.axis_index("xy"), lax.axis_index("core"), lax.axis_index("cp")
    xy_count, cp_count = lax.axis_size("xy"), lax.axis_size("cp")
    _, _, span, width = tokens.shape
    blocks = 2 * cp_count
    row_len = blocks * span
    own = 2 * span
    parity = z & 1
    group = parity + 2 * core
    part = width // cp_count
    hidden_part = up_weight.shape[1] // 2
    lines_each = width // xy_count
    lines = lines_each // 2
    here = jnp.reshape(xy, (1,)).astype(jnp.int32)
    group_at = jnp.reshape(group, (1,)).astype(jnp.int32)

    gain_rows = jnp.zeros((16, qkv_weight.shape[1]), BF16)
    gain_rows = lax.dynamic_update_slice(gain_rows, norm_gains[None], (0, 0))
    w = jnp.concatenate([qkv_weight, gain_rows])
    w_far = flip(w, "cp", 2)

    x = settled(tokens[0], swap(after(tokens, w_far)[0]))
    w, w_far = jnp.where(z & 2 == 0, w, w_far), jnp.where(z & 2 == 0, w_far, w)
    near = [w[:, n * part : (n + 1) * part] for n in range(3)]
    near += [w_far[:, n * part : (n + 1) * part] for n in range(3)]
    even = parity == 0
    sent = jnp.concatenate([near[1], near[4]], axis=1)
    gain_near = jnp.stack([w[lines, :128], w_far[lines, :128]])
    sent = lax.dynamic_update_slice(sent, gain_near, (lines, 0))
    far = flip(sent, "cp", 1)
    up_weight, down_weight, out_weight = all_after((up_weight, down_weight, out_weight), far)
    out_far = flip(out_weight, "cp", 2)


    def half_of(which):
        up = lax.dynamic_slice_in_dim(up_weight, which * hidden_part, hidden_part, 1)
        down = lax.dynamic_slice_in_dim(down_weight, which * hidden_part, hidden_part, 0)
        return plain(jnp.stack([up, down.T]))

    ffn = ordered(core == 0, half_of(core), flip(half_of(1 - core), "core", 1), 1)

    def paired(mine, other):
        return jnp.concatenate(
            [jnp.where(z & 2 == 0, mine, other), jnp.where(z & 2 == 0, other, mine)], axis=1
        )

    gain_far = far[lines : lines + 2, :128]
    gain_near, gain_far = (
        jnp.where(even, gain_near, gain_far), jnp.where(even, gain_far, gain_near)
    )
    gain_rows = jnp.stack([gain_near[0], gain_far[0], gain_near[1], gain_far[1]])
    far = [far[:lines, n * part : (n + 1) * part] for n in range(2)]
    near = [block[:lines] for block in near]

    def by_pairs(*choices):
        picked = [jnp.where(even, a, b) for a, b in choices]
        return jnp.concatenate(
            [block[:, at : at + 128] for at in range(0, part, 128) for block in picked], axis=1
        )

    first_group = by_pairs((near[0], far[0]), (far[0], near[2]), (near[5], near[3]))
    second_group = by_pairs((near[2], near[0]), (near[3], far[1]), (far[1], near[5]))
    gain_block = jnp.zeros((16, 3 * part), BF16)
    gain_block = lax.dynamic_update_slice(gain_block, gain_rows, (0, 0))
    mine = jnp.concatenate([jnp.where(core == 0, first_group, second_group), gain_block])
    other = jnp.concatenate([jnp.where(core == 0, second_group, first_group), gain_block])

    other_starts = flip(after(doc_starts, w_far), "core", 1)
    starts = jnp.where(core == z // (cp_count // 2), doc_starts, other_starts)[0]

    block_id = jnp.arange(blocks, dtype=jnp.int32)[:, None]
    inside = jnp.arange(span, dtype=jnp.int32)[None, :]
    late = block_id >= cp_count
    positions = (block_id * span + jnp.where(late, span - 1 - inside, inside)).reshape(-1)

    def starts_at(at):
        return jnp.max(jnp.where(starts[None, :] <= at[:, None], starts[None, :], 0), axis=1)

    row_start = starts_at(positions)
    tile = min(512, row_len)
    bounds = tile_bounds(starts_at(jnp.arange(row_len, dtype=jnp.int32)), tile)
    freq = jnp.exp(
        -math.log(10000.0) * 2.0 * jnp.arange(HEAD_DIM // 2, dtype=F32) / HEAD_DIM
    )
    angles = (positions - row_start).astype(F32)[:, None] * freq
    cosine, sine = jnp.cos(angles), jnp.sin(angles)
    cosine = plain(jnp.tile(cosine, (1, 4)))
    sine = plain(jnp.tile(jnp.concatenate([-sine, sine], axis=1), (1, 2)))
    pcol, prow, srow = positions[:, None], positions[None, :], row_start[None, :]
    chunk = jnp.arange(blocks, dtype=jnp.int32)
    chunk = jnp.where(chunk < cp_count, chunk, blocks - 1 - chunk)
    slot_of = (
        2 * (2 * ((chunk >> 1) ^ core) + ((chunk & 1) ^ parity))
        + (jnp.arange(blocks) >= cp_count)
    ).astype(jnp.int32)
    slot = jnp.arange(blocks, dtype=jnp.int32)
    relative = slot >> 1
    chunk_of = 2 * ((relative >> 1) ^ core) + ((relative & 1) ^ parity)
    block_of = jnp.where(slot & 1 == 0, chunk_of, blocks - 1 - chunk_of).astype(jnp.int32)

    x = after(x, sent, cosine, sine)
    x_chip = flip(x, "cp", 1)
    x_core = flip(x, "core", 1)
    up_lines, out_w, out_far = all_after((ffn[0], out_weight, out_far), x)
    up_far = flip(up_lines, "cp", 2)
    out_w = paired(out_w, out_far)
    out_far = flip(out_w, "cp", 1)

    qkv = placed(core == 0, mine, flip(other, "core", 1), 0)
    cut = qkv.shape[2] // 2
    low, high = qkv[:, :, :cut], qkv[:, :, cut:]
    low = placed(xy & 1 == 0, low, flip(low, "xy", 1), 0)
    high = placed(xy & 2 == 0, high, flip(high, "xy", 2), 0)
    low = placed(xy & 2 == 0, low, flip(low, "xy", 2), 0)
    high = placed(xy & 1 == 0, high, flip(high, "xy", 1), 1)
    qkv = jnp.concatenate([low[:, :, :, :lines], high[:, :, :, :lines]], axis=4)
    qkv = qkv.reshape(width, 3 * part)
    gains = low[:, :, :, lines : lines + cp_count, :128]
    gains = gains.reshape(4, width).astype(F32)

    sooner, later = jnp.array([0, 1, 4, 5], jnp.int32), jnp.array([2, 3, 6, 7], jnp.int32)
    early = project(x, x_core, gains, qkv, cosine, sine, block_of[sooner], sooner, [])
    x_chip, up_far, *early = lax.optimization_barrier((x_chip, up_far, *early))
    x_both = flip(x_chip, "core", 1)
    up_lines, up_far, down_lines, out_w, out_far = all_after(
        (up_lines, up_far, ffn[1], out_w, out_far), x_chip, qkv
    )
    up_lines, out_w = paired(up_lines, up_far), widened(z, out_w, out_far)[None]
    up_far = flip(up_lines, "cp", 1)
    down_far = flip(down_lines, "cp", 2)
    out_far = flip(out_w, "xy", 1)

    def halves(x):
        return x[None, :lines], x[None, lines:]

    def send_lines(low, high):
        return flip(low, "xy", 1), flip(high, "xy", 2)

    def join_lines(low, high, low_far, high_far):
        low = ordered(xy & 1 == 0, low, low_far, 0)
        high = jnp.expand_dims(ordered(xy & 2 == 0, high, high_far, 0), 1)
        return low, high

    def send_more(low, high):
        return flip(low, "xy", 2), flip(high, "xy", 1)

    def join_all(low, high, low_far, high_far):
        low = ordered(xy & 2 == 0, low, low_far, 0)
        high = ordered(xy & 1 == 0, high, high_far, 1).reshape(low.shape)
        return jnp.stack([low, high], axis=1).reshape(width, -1)

    q, k, v, normed = project(
        x_chip, x_both, gains, qkv, cosine, sine, block_of[later], later, early
    )
    up_lines, up_far, out_w, out_far = all_after((up_lines, up_far, out_w, out_far), q)
    up_lines = widened(z, up_lines, up_far)
    up_full = lax.all_gather(up_lines, "xy", axis=0, tiled=True)
    out_w = ordered(xy & 1 == 0, out_w, out_far, 0)
    out_far = flip(out_w, "xy", 2)
    q = after(q, up_lines, out_w)
    first = attend(0, q, k, v, pcol, prow, srow, bounds, slot_of, tile)
    down_lines, down_far, out_w, out_far = all_after(
        (down_lines, down_far, out_w, out_far), first[0]
    )
    out_w = ordered(xy & 2 == 0, out_w, out_far, 0)
    out_far = flip(out_w, "core", 1)
    down_lines = paired(down_lines, down_far)
    down_far = flip(down_lines, "cp", 1)
    q = after(q, first[0], down_lines, out_w)
    second = attend(1, q, k, v, pcol, prow, srow, bounds, slot_of, tile)
    attended, local, lse = zip(first, second)
    local = jnp.concatenate(local, axis=2)
    out_w, out_far, down_lines, down_far = all_after((out_w, out_far, down_lines, down_far), local)
    out_w = placed(core == 0, out_w, out_far, 1).reshape(width, width)
    down_pair = halves(widened(z, down_lines, down_far))
    down_far = send_lines(*down_pair)
    heads, branch_hat, branch_scale, hidden, mid = mix(
        group_at, local[:2], flip(local[4:6], "core", 1), flip(local[2:4], "cp", 1),
        flip_both(local[6:]), out_w, x, gains,
    )

    cotangent = cotangent.reshape(own, width)
    dy_moved = swap(after(cotangent, mid))

    ffn_in = jnp.concatenate([mid, flip(mid, "core", 1)])
    down_pair, down_far = all_after(down_pair, mid), all_after(down_far, mid)
    down_pair = join_lines(*down_pair, *down_far)
    down_far = send_more(*down_pair)
    ffn_in = after(ffn_in, *down_pair)
    act, slope = gelu_and_slope(dot(ffn_in, up_full, (1, 0)))
    down_full = join_all(*down_pair, *all_after(down_far, act))
    sent = flip(dot(act[own:], down_full, (1, 1)).astype(BF16), "core", 1)
    terms = dot(act[:own], down_full, (1, 1))
    dy = settled(cotangent, dy_moved)
    mixed, grad_down, gain_four = finish(terms, sent, hidden, dy, gains)
    grad_down = jnp.concatenate([grad_down, flip(grad_down, "core", 1)])

    x_bit, y_bit = xy & 1, xy >> 1

    def cut_first(grads):
        grads = [g.reshape(2, 2, 2, -1, g.shape[-1]) for g in grads]
        low = [g[:, :, 0] for g in grads]
        high = [g[:, :, 1] for g in grads]

        def both(parts, at, axis):
            return jnp.concatenate([pick(part_of, at, axis) for part_of in parts], axis=1)

        away = both(low, 1 - x_bit, 1), both(high, 1 - y_bit, 0)
        return (both(low, x_bit, 1), both(high, y_bit, 0)), away

    def send_first(away):
        return flip(away[0], "xy", 1), flip(away[1], "xy", 2)

    def cut_second(near, far):
        away = (
            total(pick(near[0], 1 - y_bit, 0), pick(far[0], 1 - y_bit, 0)),
            total(pick(near[1], 1 - x_bit, 0), pick(far[1], 1 - x_bit, 0)),
        )
        near = (
            total(pick(near[0], y_bit, 0), pick(far[0], y_bit, 0)),
            total(pick(near[1], x_bit, 0), pick(far[1], x_bit, 0)),
        )
        return near, away

    def send_second(away):
        return flip(away[0], "xy", 2), flip(away[1], "xy", 1)

    def cut_third(near, far):
        return split_columns(
            jnp.concatenate([total(a, b) for a, b in zip(near, far)]), hidden_part
        )

    def split_columns(sums, each):
        blocks_of = [sums[:, n * each : (n + 1) * each] for n in range(cp_count)]
        odd = jnp.stack([blocks_of[1], blocks_of[3]])
        even = jnp.stack([blocks_of[0], blocks_of[2]])
        return jnp.where(parity == 0, even, odd), jnp.where(parity == 0, odd, even)

    def cut_fourth(near, far):
        return (
            total(pick(near, z >> 1, 0), pick(far, z >> 1, 0)),
            total(pick(near, 1 - (z >> 1), 0), pick(far, 1 - (z >> 1), 0)),
        )

    down_local = plain(dot(grad_down, act, (0, 0)).astype(BF16))
    grad_up = dot(after(grad_down, down_local), down_full, (1, 0)) * slope.astype(F32)
    grad_up = grad_up.astype(BF16)
    sent = flip(dot(grad_up[own:], up_full, (1, 1)).astype(BF16), "core", 1)
    up_local = plain(dot(ffn_in, grad_up, (0, 0)).astype(BF16))
    spare = lines // 4
    down_local = down_local.reshape(2 * xy_count, lines, -1)
    over_local = down_local[:, lines - spare :].reshape(2 * xy_count * spare, -1)
    down_local = down_local[:, : lines - spare].reshape(2 * xy_count * (lines - spare), -1)
    grad_near, grad_away = cut_first((up_local, down_local))
    grad_far = send_first(grad_away)
    terms = dot(after(grad_up, *grad_away)[:own], up_full, (1, 1))
    grad_hidden, grad_branch, grad_heads, gain_three, gain_two = turn(
        group_at, terms, sent, hidden, dy, branch_hat, branch_scale, out_w, gains
    )

    grad_local = [
        grad_heads[0], flip(grad_heads[1], "cp", 1), flip(grad_heads[2], "core", 1),
        flip_both(grad_heads[3]),
    ]
    out_local = dot(after(heads, grad_heads), grad_branch, (0, 0)).astype(BF16)
    grad_local = plain(jnp.concatenate(grad_local))
    out_away = pick(out_local.reshape(xy_count, 2, lines, width), 1 - core, 1)
    out_away, over_local, mixed, grad_local = lax.optimization_barrier(
        (out_away, over_local, mixed, grad_local)
    )
    over_near, over_away = split_columns(over_local, hidden_part)
    over_far = flip(over_away, "cp", 1)
    mixed_moved = swap(mixed)
    grad_local = after(grad_local, over_away)

    def back_to_tokens(grads):
        two = 2 * span
        rows = grads.reshape(4 * span, 3 * part)
        send = dot(rows[two:], qkv, (1, 1)).astype(BF16)
        sent = flip(send, "core", 1)
        rows = after(rows, send)
        own_sums = dot(rows[:two], qkv, (1, 1)) + sent.astype(F32)
        far_away = own_sums[span:].astype(BF16)
        return send, far_away, flip(far_away, "cp", 1), own_sums[:span]

    tables = (pcol, prow, srow, cosine, sine, bounds, slot_of, tile)
    attended, lse = jnp.concatenate(attended, axis=1), jnp.concatenate(lse, axis=0)
    first, unfinished = attend_back(0, q, k, v, grad_local, attended, lse, *tables, [])
    first, mixed_moved, over_far, *grad_far = lax.optimization_barrier(
        (first, mixed_moved, over_far, *grad_far)
    )
    over_near, over_away = cut_fourth(over_near, over_far)
    over_far = flip(over_away, "cp", 2)
    _, far_away, far_back, kept = back_to_tokens(after(first, over_away))
    grad_near, grad_away = cut_second(grad_near, all_after(grad_far, far_away))
    grad_far = send_second(grad_away)
    out_far = flip(after(out_away, far_away), "core", 1)
    second = attend_back(
        1, q, k, v, after(grad_local, first, *grad_away, over_away, kept), attended, lse, *tables,
        [unfinished],
    )[0]
    second, over_far, out_far, *grad_far = lax.optimization_barrier(
        (second, over_far, out_far, *grad_far)
    )

    ended = end(kept, after(far_back, second), x[0], grad_hidden[:span], gains)
    moved = swap(ended)
    second = after(second, ended)
    send, far_away, far, kept = back_to_tokens(second)
    qkv_local = sum(
        dot(normed[4 * h : 4 * h + 4].reshape(4 * span, width), g.reshape(4 * span, -1), (0, 0))
        for h, g in enumerate((first, after(second, send)))
    ).astype(BF16)
    gain_one = jnp.sum(qkv_local.astype(F32) * qkv.astype(F32), axis=1) / gains[0]
    gain_sum = jnp.concatenate([gain_one[None], gain_two, gain_three, gain_four])
    gain_sum = gain_sum.reshape(2 * xy_count, cp_count, 128).astype(BF16)
    place = jnp.stack([x_bit, y_bit, core, parity, z >> 1]).astype(jnp.int32)
    locals_ = (qkv_local, out_local, gain_sum)
    rest_away = jnp.concatenate(
        [
            pick(qkv_local.reshape(xy_count, 2, lines, 3 * part), 1 - core, 1),
            jnp.pad(
                pick(gain_sum.reshape(xy_count, 2, cp_count, 128), 1 - core, 1),
                ((0, 0), (0, lines - cp_count), (0, 0)),
            ),
        ],
        axis=2,
    )
    rest_far = flip(rest_away, "core", 1)

    over = total(over_near, over_far)
    rest_far, over = all_after((rest_far, over), kept)
    low, low_away, high, high_away = spread_first(place, *locals_, over, rest_far, out_far)
    rest_far = flip(low_away, "xy", 1), flip(high_away, "xy", 2)
    grad_near, grad_away = cut_third(grad_near, all_after(grad_far, low_away))
    grad_far = flip(grad_away, "cp", 1)
    ended_last = end(kept, after(far, moved), x[1], grad_hidden[span:], gains)
    moved_last = swap(ended_last)
    rest_far, grad_far = all_after(rest_far, ended_last), after(grad_far, ended_last)
    grad_near, grad_away = cut_fourth(grad_near, grad_far)
    grad_far = flip(grad_away, "cp", 2)
    rest_far = all_after(rest_far, grad_away)
    low, low_away, high, high_away = spread_second(place, low, rest_far[0], high, rest_far[1])
    rest_far = flip(low_away, "xy", 2), flip(high_away, "xy", 1)
    rest, rest_away, over = spread_third(place, low, rest_far[0], high, rest_far[1])
    gather_away = rest_away
    rest, rest_away = spread_fourth(place, rest, flip(rest_away, "cp", 2))
    moved_last = after(moved_last, rest_away)
    qkv_grad, out_grad, gains_grad = spread_fifth(place, rest, flip(rest_away, "cp", 1))
    gains_grad = gains_grad.reshape(-1)
    tokens_grad = jnp.stack([settled(ended, moved), settled(ended_last, moved_last)])
    tokens_grad = tokens_grad.astype(F32).reshape(tokens.shape)
    mixed = settled(after(mixed, gather_away), mixed_moved).reshape(tokens.shape)

    both = total(grad_near, after(grad_far, gather_away))
    both = plain(both).reshape(2, 2 * lines - spare, hidden_part)
    over = [
        jnp.concatenate([block[n * spare : (n + 1) * spare] for n in range(4)], axis=1)
        for block in over
    ]
    both = jnp.concatenate([both, jnp.stack(over)], axis=1).reshape(2, 2, lines, hidden_part)
    mine, other = pick(both, core, 0), flip(pick(both, 1 - core, 0), "core", 1)
    up_grad = ordered(core == 0, mine[0], other[0], 1).astype(F32)
    down_grad = ordered(core == 0, mine[1], other[1], 1).T.astype(F32)
    return mixed, tokens_grad, qkv_grad, out_grad, up_grad, down_grad, gains_grad


def solution(mesh):
    rows, cp = mesh.shape["rows"], mesh.shape["cp"]
    if (rows, cp) == (8, 4):
        grid = Mesh(mesh.devices.reshape(rows // 2, 2, cp), ("xy", "core", "cp"))
        run, lines = body, ("xy", "core")
    else:
        grid, run, lines = mesh, general_body, ("rows",)
    tokens = P(lines, None, "cp", None)
    weight, down, gains = P(lines, "cp"), P("cp", lines), P(lines + ("cp",))
    return jax.shard_map(
        run,
        mesh=grid,
        in_specs=(tokens, P(lines, None), weight, weight, weight, down, gains, tokens),
        out_specs=(tokens, tokens, weight, weight, weight, down, gains),
        check_vma=False,
    )
```

```python
import functools
import math

import jax
import jax.numpy as jnp
from jax import lax
from jax.experimental import pallas as pl
from jax.experimental.layout import Layout, with_layout_constraint
from jax.experimental.pallas import tpu as pltpu
from jax.sharding import Mesh, PartitionSpec as P

HEADS = 16
HEAD_DIM = 64


NORM_EPS = 1e-05
MASKED = -1e30


def layer_norm(values):
    average = jnp.mean(values, axis=-1, keepdims=True)
    centred = values - average
    spread = jnp.mean(centred * centred, axis=-1, keepdims=True)
    return centred * lax.rsqrt(spread + NORM_EPS)


def norm_back(values, upstream):
    _, pull_back = jax.vjp(layer_norm, values)
    return pull_back(upstream)[0]


def gelu_tanh(values):
    return jax.nn.gelu(values, approximate=True)


def rotate(values, cosine, sine_part):
    half_width = values.shape[-1] // 2
    first_half = values[..., :half_width]
    second_half = values[..., half_width:]
    return jnp.concatenate(
        [
            first_half * cosine - second_half * sine_part,
            second_half * cosine + first_half * sine_part,
        ],
        axis=-1,
    )


def rounded(values):
    return lax.optimization_barrier(values.astype(jnp.bfloat16)).astype(jnp.float32)


def doc_start_of(starts, positions):
    return jnp.max(
        jnp.where(starts[:, None, :] <= positions[None, :, None], starts[:, None, :], 0), axis=-1
    )


def general_body(tokens, doc_starts, qkv_weight, out_weight, up_weight, down_weight, norm_gains, cotangent):
    rows_count = lax.axis_size("rows")
    cp_count = lax.axis_size("cp")
    qkv_rows, out_rows, up_rows, down_rows, gain_piece = (
        lax.all_gather(qkv_weight, "rows", axis=0, tiled=True),
        lax.all_gather(out_weight, "rows", axis=0, tiled=True),
        lax.all_gather(up_weight, "rows", axis=0, tiled=True),
        lax.all_gather(down_weight, "rows", axis=1, tiled=True),
        lax.all_gather(norm_gains, "rows", axis=0, tiled=True),
    )
    qkv_full, out_full, gain_mixed = (
        lax.all_gather(qkv_rows, "cp", axis=1, tiled=True),
        lax.all_gather(out_rows, "cp", axis=1, tiled=True),
        lax.all_gather(gain_piece, "cp", axis=0, tiled=True),
    )
    gain_full = jnp.transpose(gain_mixed.reshape(cp_count, rows_count, -1), (1, 0, 2)).reshape(-1)
    row_count, _, span_len, width = tokens.shape
    half_len = span_len * cp_count
    row_len = 2 * half_len
    queries_dev = 2 * span_len
    token_total = row_count * queries_dev
    group_total = row_count * row_len
    gain_rows = gain_full.astype(jnp.float32).reshape(4, width)
    score_scale = HEAD_DIM ** (-0.5)
    local_pos = lax.axis_index("cp") * span_len + jnp.arange(span_len, dtype=jnp.int32)
    query_pos = jnp.concatenate([local_pos, row_len - 1 - local_pos])
    half_pos = jnp.arange(half_len, dtype=jnp.int32)
    key_pos = jnp.concatenate([half_pos, row_len - 1 - half_pos])
    query_start = doc_start_of(doc_starts, query_pos)
    key_start = doc_start_of(doc_starts, key_pos)
    freq_index = jnp.arange(HEAD_DIM // 2, dtype=jnp.float32)
    inverse_freq = jnp.exp(-math.log(10000.0) * 2.0 * freq_index / HEAD_DIM)
    angles = (query_pos[None, :] - query_start).astype(jnp.float32)[..., None] * inverse_freq
    cosine = jnp.cos(angles)[:, :, None, :]
    sine_part = jnp.sin(angles)[:, :, None, :]
    head_shape = (row_count, queries_dev, HEADS, HEAD_DIM)
    flat_shape = (row_count, queries_dev, width)
    fold_shape = (row_count, 2, span_len, width)
    group_shape = (row_count, 2, half_len, width)
    full_shape = (row_count, row_len, HEADS, HEAD_DIM)
    inputs = tokens.astype(jnp.float32).reshape(flat_shape)
    normed_in = layer_norm(inputs)
    normed = (normed_in * gain_rows[0]).astype(jnp.bfloat16)
    linear = jnp.dot(normed, qkv_full, preferred_element_type=jnp.float32)
    query_rows = rotate(linear[..., :width].reshape(head_shape), cosine, sine_part).astype(
        jnp.bfloat16
    )
    key_local = rotate(
        linear[..., width : 2 * width].reshape(head_shape), cosine, sine_part
    ).astype(jnp.bfloat16)
    value_local = linear[..., 2 * width :].reshape(head_shape).astype(jnp.bfloat16)
    key_sent, value_sent = (
        lax.all_gather(key_local.reshape(fold_shape), "cp", axis=2, tiled=True),
        lax.all_gather(value_local.reshape(fold_shape), "cp", axis=2, tiled=True),
    )
    key_rows = key_sent.reshape(full_shape)
    value_rows = value_sent.reshape(full_shape)
    block_size = min(512, row_len)
    block_count = row_len // block_size
    block_range = jnp.arange(block_count)

    def block_scores(block_index):
        first_key = block_index * block_size
        key_block = lax.dynamic_slice_in_dim(key_rows, first_key, block_size, 1)
        pos_block = lax.dynamic_slice_in_dim(key_pos, first_key, block_size, 0)
        start_block = lax.dynamic_slice_in_dim(key_start, first_key, block_size, 1)
        raw_scores = jnp.einsum(
            "rqhd,rkhd->rhqk", query_rows, key_block, preferred_element_type=jnp.float32
        )
        allowed = (query_start[:, None, :, None] == start_block[:, None, None, :]) & (
            pos_block[None, None, None, :] <= query_pos[None, None, :, None]
        )
        return (raw_scores * score_scale, allowed)

    def max_step(carry, block_index):
        running_max, running_sum = carry
        scores, allowed = block_scores(block_index)
        scores = jnp.where(allowed, scores, MASKED)
        new_max = jnp.maximum(running_max, jnp.max(scores, axis=-1))
        running_sum = running_sum * jnp.exp(running_max - new_max) + jnp.sum(
            jnp.where(allowed, jnp.exp(scores - new_max[..., None]), 0.0), axis=-1
        )
        return ((new_max, running_sum), None)

    stat_shape = (row_count, HEADS, queries_dev)
    (running_max, running_sum), _ = lax.scan(
        max_step,
        (jnp.full(stat_shape, MASKED, jnp.float32), jnp.zeros(stat_shape, jnp.float32)),
        block_range,
    )
    log_total = running_max + jnp.log(running_sum)

    def value_step(totals, block_index):
        scores, allowed = block_scores(block_index)
        probs = jnp.where(allowed, jnp.exp(scores - log_total[..., None]), 0.0).astype(jnp.bfloat16)
        value_block = lax.dynamic_slice_in_dim(value_rows, block_index * block_size, block_size, 1)
        return (
            totals
            + jnp.einsum("rhqk,rkhd->rqhd", probs, value_block, preferred_element_type=jnp.float32),
            None,
        )

    attended, _ = lax.scan(value_step, jnp.zeros(head_shape, jnp.float32), block_range)
    mixed_heads = attended.reshape(flat_shape).astype(jnp.bfloat16)
    branch = jnp.dot(mixed_heads, out_full, preferred_element_type=jnp.float32)
    branch_hat = layer_norm(branch)
    hidden = inputs + branch_hat * gain_rows[1]
    hidden_hat = layer_norm(hidden)
    normed_mid = (hidden_hat * gain_rows[2]).astype(jnp.bfloat16)
    ffn_in = lax.all_gather(normed_mid.reshape(fold_shape), "cp", axis=2, tiled=True).reshape(
        group_total, width
    )
    up_proj = jnp.dot(ffn_in, up_rows, preferred_element_type=jnp.float32)
    activation = gelu_tanh(up_proj).astype(jnp.bfloat16)
    down_terms = jnp.dot(activation, down_rows, preferred_element_type=jnp.float32)
    down_proj = (
        lax.psum_scatter(
            down_terms.reshape(group_shape).astype(jnp.bfloat16),
            "cp",
            scatter_dimension=2,
            tiled=True,
        )
        .astype(jnp.float32)
        .reshape(flat_shape)
    )
    down_hat = layer_norm(down_proj)
    mixed = (hidden + down_hat * gain_rows[3]).astype(jnp.bfloat16).reshape(tokens.shape)
    upstream = cotangent.astype(jnp.float32).reshape(flat_shape)
    gain_four = jnp.sum(upstream * down_hat, axis=(0, 1))
    grad_down_out = norm_back(down_proj, upstream * gain_rows[3]).astype(jnp.bfloat16)
    grad_out_rows = lax.all_gather(
        grad_down_out.reshape(fold_shape), "cp", axis=2, tiled=True
    ).reshape(group_total, width)
    down_local = jnp.einsum(
        "tf,td->fd", activation, grad_out_rows, preferred_element_type=jnp.float32
    )
    grad_act = jnp.einsum("td,fd->tf", grad_out_rows, down_rows, preferred_element_type=jnp.float32)
    _, gelu_pull = jax.vjp(gelu_tanh, up_proj)
    grad_up = gelu_pull(grad_act)[0].astype(jnp.bfloat16)
    up_local = jnp.einsum("tc,tf->cf", ffn_in, grad_up, preferred_element_type=jnp.float32)
    mid_terms = jnp.einsum("tf,cf->tc", grad_up, up_rows, preferred_element_type=jnp.float32)
    grad_mid = (
        lax.psum_scatter(
            mid_terms.reshape(group_shape).astype(jnp.bfloat16),
            "cp",
            scatter_dimension=2,
            tiled=True,
        )
        .astype(jnp.float32)
        .reshape(flat_shape)
    )
    gain_three = jnp.sum(grad_mid * hidden_hat, axis=(0, 1))
    grad_hidden = upstream + norm_back(hidden, grad_mid * gain_rows[2])
    gain_two = jnp.sum(grad_hidden * branch_hat, axis=(0, 1))
    grad_branch = norm_back(branch, grad_hidden * gain_rows[1]).astype(jnp.bfloat16)
    out_local = jnp.einsum(
        "tc,te->ce",
        mixed_heads.reshape(token_total, width),
        grad_branch.reshape(token_total, width),
        preferred_element_type=jnp.float32,
    )
    grad_heads = (
        jnp.einsum("rqe,ce->rqc", grad_branch, out_full, preferred_element_type=jnp.float32)
        .astype(jnp.bfloat16)
        .reshape(head_shape)
    )
    delta_sum = jnp.transpose(
        jnp.sum(grad_heads.astype(jnp.float32) * attended, axis=-1), (0, 2, 1)
    )

    def score_grads(block_index):
        scores, allowed = block_scores(block_index)
        probs = jnp.where(allowed, jnp.exp(scores - log_total[..., None]), 0.0)
        first_key = block_index * block_size
        key_block = lax.dynamic_slice_in_dim(key_rows, first_key, block_size, 1)
        value_block = lax.dynamic_slice_in_dim(value_rows, first_key, block_size, 1)
        grad_probs = jnp.einsum(
            "rqhd,rkhd->rhqk", grad_heads, value_block, preferred_element_type=jnp.float32
        )
        grad_scores = (probs * (grad_probs - delta_sum[..., None]) * score_scale).astype(
            jnp.bfloat16
        )
        return (probs, grad_scores, key_block)

    def grad_step(grad_query, block_index):
        probs, grad_scores, key_block = score_grads(block_index)
        grad_query = grad_query + jnp.einsum(
            "rhqk,rkhd->rqhd", grad_scores, key_block, preferred_element_type=jnp.float32
        )
        key_part = jnp.einsum(
            "rhqk,rqhd->rkhd", grad_scores, query_rows, preferred_element_type=jnp.float32
        )
        value_part = jnp.einsum(
            "rhqk,rqhd->rkhd",
            probs.astype(jnp.bfloat16),
            grad_heads,
            preferred_element_type=jnp.float32,
        )
        return (grad_query, (key_part, value_part))

    grad_query, (key_parts, value_parts) = lax.scan(
        grad_step, jnp.zeros(head_shape, jnp.float32), block_range
    )
    key_terms = jnp.moveaxis(key_parts, 0, 1).reshape(group_shape)
    value_terms = jnp.moveaxis(value_parts, 0, 1).reshape(group_shape)
    key_sum, value_sum = (
        lax.psum_scatter(
            key_terms.astype(jnp.bfloat16), "cp", scatter_dimension=2, tiled=True
        ).astype(jnp.float32),
        lax.psum_scatter(
            value_terms.astype(jnp.bfloat16), "cp", scatter_dimension=2, tiled=True
        ).astype(jnp.float32),
    )
    query_unturned = rotate(rounded(grad_query), cosine, -sine_part).reshape(flat_shape)
    key_unturned = rotate(rounded(key_sum.reshape(head_shape)), cosine, -sine_part).reshape(
        flat_shape
    )
    grad_linear = jnp.concatenate(
        [query_unturned, key_unturned, value_sum.reshape(flat_shape)], axis=-1
    ).astype(jnp.bfloat16)
    qkv_local = jnp.einsum(
        "tc,te->ce",
        normed.reshape(token_total, width),
        grad_linear.reshape(token_total, 3 * width),
        preferred_element_type=jnp.float32,
    )
    grad_normed = jnp.einsum(
        "rqe,ce->rqc", grad_linear, qkv_full, preferred_element_type=jnp.float32
    )
    gain_one = jnp.sum(grad_normed * normed_in, axis=(0, 1))
    tokens_grad = (grad_hidden + norm_back(inputs, grad_normed * gain_rows[0])).reshape(
        tokens.shape
    )
    gain_local = jnp.concatenate([gain_one, gain_two, gain_three, gain_four])
    gain_order = jnp.transpose(gain_local.reshape(rows_count, cp_count, -1), (1, 0, 2)).reshape(-1)
    qkv_mid, out_mid, gain_mid = (
        lax.psum_scatter(
            qkv_local.astype(jnp.bfloat16), "cp", scatter_dimension=1, tiled=True
        ).astype(jnp.float32),
        lax.psum_scatter(
            out_local.astype(jnp.bfloat16), "cp", scatter_dimension=1, tiled=True
        ).astype(jnp.float32),
        lax.psum_scatter(
            gain_order.astype(jnp.bfloat16), "cp", scatter_dimension=0, tiled=True
        ).astype(jnp.float32),
    )
    qkv_sum, out_sum, up_sum, down_sum, gain_sum = (
        lax.psum_scatter(
            qkv_mid.astype(jnp.bfloat16), "rows", scatter_dimension=0, tiled=True
        ).astype(jnp.float32),
        lax.psum_scatter(
            out_mid.astype(jnp.bfloat16), "rows", scatter_dimension=0, tiled=True
        ).astype(jnp.float32),
        lax.psum_scatter(
            up_local.astype(jnp.bfloat16), "rows", scatter_dimension=0, tiled=True
        ).astype(jnp.float32),
        lax.psum_scatter(
            down_local.astype(jnp.bfloat16), "rows", scatter_dimension=1, tiled=True
        ).astype(jnp.float32),
        lax.psum_scatter(
            gain_mid.astype(jnp.bfloat16), "rows", scatter_dimension=0, tiled=True
        ).astype(jnp.float32),
    )
    return (mixed, tokens_grad, qkv_sum, out_sum, up_sum, down_sum, gain_sum)


F32 = jnp.float32
BF16 = jnp.bfloat16
MIB = 1024 * 1024


def params(grid_rank, mebibytes=24):
    return pltpu.CompilerParams(
        dimension_semantics=("arbitrary",) * grid_rank, vmem_limit_bytes=mebibytes * MIB
    )


def lasting(microseconds):
    return pl.CostEstimate(
        flops=int(microseconds * 1e7), bytes_accessed=1024, transcendentals=0
    )


def turned(x, cosine, sine):
    lane = lax.broadcasted_iota(jnp.int32, x.shape, 1)
    other = jnp.where((lane & 32) == 0, pltpu.roll(x, 96, 1), pltpu.roll(x, 32, 1))
    return x * cosine + other * sine


def attend_kernel(tile, bounds, slot_of, q_ref, k_ref, v_ref, pcol_ref, prow_ref, srow_ref,
                  o_ref, ob_ref, lse_ref, vt_ref):
    i = pl.program_id(1)

    @pl.when(i == 0)
    def _():
        vt_ref[...] = v_ref[...].astype(F32).T.astype(BF16)

    qt = q_ref[...].astype(F32).T
    row = lax.broadcasted_iota(jnp.int32, qt.shape, 0)
    lo = bounds[0, i]
    mid = jnp.minimum(bounds[1, i], i)
    qpos = prow_ref[...]
    qstart = srow_ref[...]
    qh = [jnp.where((row >= 64) == (h == 1), qt, 0.0).astype(BF16) for h in range(2)]

    def step(j, carry, masked):
        at = pl.multiple_of(j * tile, tile)
        k = k_ref[pl.ds(at, tile), :]
        scores = [jnp.dot(k, qh[h], preferred_element_type=F32) for h in range(2)]
        if masked:
            kpos = pcol_ref[pl.ds(at, tile), :]
            allowed = (kpos >= qstart) & (kpos <= qpos)
            scores = [jnp.where(allowed, s, MASKED) for s in scores]
        out = []
        for h in range(2):
            top, total, acc = carry[h]
            new = jnp.maximum(top, jnp.max(scores[h], axis=0, keepdims=True))
            p = jnp.exp(scores[h] - new)
            keep = jnp.exp(top - new)
            total = total * keep + jnp.sum(p, axis=0, keepdims=True)
            acc = acc * keep + jnp.dot(
                vt_ref[h * 64 : h * 64 + 64, pl.ds(at, tile)], p.astype(BF16),
                preferred_element_type=F32,
            )
            out.append((new, total, acc))
        return tuple(out)

    start = (
        jnp.full((1, tile), MASKED, F32), jnp.zeros((1, tile), F32), jnp.zeros((64, tile), F32)
    )
    carry = step(i, (start, start), True)
    carry = lax.fori_loop(lo, mid, functools.partial(step, masked=True), carry)
    carry = lax.fori_loop(mid, i, functools.partial(step, masked=False), carry)
    parts = []
    for h in range(2):
        top, total, acc = carry[h]
        lse_ref[0, h : h + 1, :] = top + jnp.log(total)
        parts.append(acc / total)
    out = jnp.concatenate(parts, axis=0).T
    o_ref[...] = out
    span = ob_ref.shape[1]
    for b in range(tile // span):
        ob_ref[slot_of[i * (tile // span) + b]] = out[b * span : (b + 1) * span].astype(BF16)


def attend(pair, q, k, v, pcol, prow, srow, bounds, slot_of, tile):
    rows, width = q.shape
    blocks = slot_of.shape[0]
    span = rows // blocks
    count = rows // tile
    grid_spec = pltpu.PrefetchScalarGridSpec(
        num_scalar_prefetch=2,
        grid=(1, count),
        in_specs=[
            pl.BlockSpec((tile, 128), lambda p, i, b, t: (i, pair)),
            pl.BlockSpec((rows, 128), lambda p, i, b, t: (0, pair)),
            pl.BlockSpec((rows, 128), lambda p, i, b, t: (0, pair)),
            pl.BlockSpec((rows, 1), lambda p, i, b, t: (0, 0)),
            pl.BlockSpec((1, tile), lambda p, i, b, t: (0, i)),
            pl.BlockSpec((1, tile), lambda p, i, b, t: (0, i)),
        ],
        out_specs=[
            pl.BlockSpec((tile, 128), lambda p, i, b, t: (i, p)),
            pl.BlockSpec((blocks, span, 128), lambda p, i, b, t: (0, 0, p)),
            pl.BlockSpec((1, 2, tile), lambda p, i, b, t: (p, 0, i)),
        ],
        scratch_shapes=[pltpu.VMEM((128, rows), BF16)],
    )
    return pl.pallas_call(
        functools.partial(attend_kernel, tile),
        grid_spec=grid_spec,
        out_shape=[
            jax.ShapeDtypeStruct((rows, 128), F32),
            jax.ShapeDtypeStruct((blocks, span, 128), BF16),
            jax.ShapeDtypeStruct((1, 2, rows), F32),
        ],
        compiler_params=params(2),
        cost_estimate=lasting(14),
        name="attend",
    )(bounds, slot_of, q, k, v, pcol, prow, srow)


def attend_back_kernel(tile, first, steps, bounds, slot_of, q_ref, k_ref, v_ref, do_ref, o_ref,
                       lse_ref, pcol_ref, prow_ref, srow_ref, cos_ref, sin_ref, *refs):
    qm, dom, qtm, dotm, delta, dqt = refs[-6:]
    count = q_ref.shape[0] // tile
    last = first + steps
    before = refs[0] if first else None
    g_ref = refs[1 if first else 0]
    after_ref = refs[1] if last < count else None
    j = first + pl.program_id(1)
    span = do_ref.shape[1]

    @pl.when(pl.program_id(1) == 0)
    def _():
        for t in range(first, count):
            part = pl.ds(t * tile, tile)
            q = q_ref[part, :].astype(F32)
            do = jnp.concatenate(
                [do_ref[slot_of[t * tile // span + b]] for b in range(tile // span)], axis=0
            ).astype(F32)
            qt, dot = q.T, do.T
            lane = lax.broadcasted_iota(jnp.int32, q.shape, 1)
            row = lax.broadcasted_iota(jnp.int32, qt.shape, 0)
            prod = dot * o_ref[part, :].T
            for h in range(2):
                mine = (lane >= 64) == (h == 1)
                mine_t = (row >= 64) == (h == 1)
                qm[h, part, :] = jnp.where(mine, q, 0.0).astype(BF16)
                dom[h, part, :] = jnp.where(mine, do, 0.0).astype(BF16)
                qtm[h, :, part] = jnp.where(mine_t, qt, 0.0).astype(BF16)
                dotm[h, :, part] = jnp.where(mine_t, dot, 0.0).astype(BF16)
                delta[h : h + 1, part] = jnp.sum(
                    prod[h * 64 : h * 64 + 64], axis=0, keepdims=True
                )
        if before is None:
            dqt[...] = jnp.zeros_like(dqt)
        else:
            dqt[:, first * tile :] = before[0]

    here = pl.ds(pl.multiple_of(j * tile, tile), tile)
    k = k_ref[here, :]
    v = v_ref[here, :]
    kt = k.astype(F32).T.astype(BF16)
    kpos = pcol_ref[here, :]
    full = jnp.maximum(bounds[2, j], j + 1)
    end = bounds[3, j]

    def step(i, carry, masked):
        dk, dv = carry
        part = pl.ds(pl.multiple_of(i * tile, tile), tile)
        if masked:
            allowed = (kpos >= srow_ref[:, part]) & (kpos <= prow_ref[:, part])
        for h in range(2):
            s = jnp.dot(k, qtm[h, :, part], preferred_element_type=F32)
            p = jnp.exp(s - lse_ref[0, h : h + 1, part])
            if masked:
                p = jnp.where(allowed, p, 0.0)
            dp = jnp.dot(v, dotm[h, :, part], preferred_element_type=F32)
            ds = (p * (dp - delta[h : h + 1, part])).astype(BF16)
            dv = dv + jnp.dot(p.astype(BF16), dom[h, part, :], preferred_element_type=F32)
            dk = dk + jnp.dot(ds, qm[h, part, :], preferred_element_type=F32)
            dqt[h * 64 : h * 64 + 64, part] += jnp.dot(
                kt[h * 64 : h * 64 + 64, :], ds, preferred_element_type=F32
            )
        return dk, dv

    carry = (jnp.zeros((tile, 128), F32), jnp.zeros((tile, 128), F32))
    carry = step(j, carry, True)
    carry = lax.fori_loop(j + 1, full, functools.partial(step, masked=False), carry)
    carry = lax.fori_loop(full, end, functools.partial(step, masked=True), carry)
    dk, dv = carry

    def unturned(x, at):
        x = x.astype(BF16).astype(F32)
        return turned(x, cos_ref[at, :], -sin_ref[at, :]).astype(BF16)

    grad_k, grad_v = unturned(dk, here), dv.astype(BF16)
    for b in range(tile // span):
        at = slot_of[j * (tile // span) + b] >> 1
        g_ref[at, :, 128:256] = grad_k[b * span : (b + 1) * span]
        g_ref[at, :, 256:384] = grad_v[b * span : (b + 1) * span]

    @pl.when(pl.program_id(1) == steps - 1)
    def _():
        for t in range(first, last):
            part = pl.ds(t * tile, tile)
            grad_q = unturned(dqt[:, part].T * 0.125, part)
            for b in range(tile // span):
                at = slot_of[t * (tile // span) + b] >> 1
                g_ref[at, :, 0:128] = grad_q[b * span : (b + 1) * span]
        if after_ref is not None:
            after_ref[0] = dqt[:, last * tile :]


def attend_back(half, q, k, v, do, o, lse, pcol, prow, srow, cosine, sine, bounds, slot_of, tile,
                before):
    rows, width = q.shape
    pairs = width // 128
    blocks, span, _ = do.shape
    count = rows // tile
    steps = count // 2
    first = half * steps
    whole = pl.BlockSpec((rows, 128), lambda p, j, b, t: (0, p))
    table = pl.BlockSpec((rows, 128), lambda p, j, b, t: (0, 0))
    line = pl.BlockSpec((1, rows), lambda p, j, b, t: (0, 0))
    rest = pl.BlockSpec((1, 128, rows // 2), lambda p, j, b, t: (p, 0, 0))
    outs = [
        (
            jax.ShapeDtypeStruct((blocks // 2, span, 3 * width), BF16),
            pl.BlockSpec((blocks // 2, span, 384), lambda p, j, b, t: (0, 0, p)),
        )
    ]
    if not half:
        outs.append((jax.ShapeDtypeStruct((pairs, 128, rows // 2), F32), rest))
    grid_spec = pltpu.PrefetchScalarGridSpec(
        num_scalar_prefetch=2,
        grid=(pairs, steps),
        in_specs=[
            whole, whole, whole,
            pl.BlockSpec((blocks, span, 128), lambda p, j, b, t: (0, 0, p)),
            whole,
            pl.BlockSpec((1, 2, rows), lambda p, j, b, t: (p, 0, 0)),
            pl.BlockSpec((rows, 1), lambda p, j, b, t: (0, 0)),
            line, line, table, table,
        ]
        + [rest] * len(before),
        out_specs=[spec for _, spec in outs],
        scratch_shapes=[
            pltpu.VMEM((2, rows, 128), BF16), pltpu.VMEM((2, rows, 128), BF16),
            pltpu.VMEM((2, 128, rows), BF16), pltpu.VMEM((2, 128, rows), BF16),
            pltpu.VMEM((2, rows), F32), pltpu.VMEM((128, rows), F32),
        ],
    )
    return pl.pallas_call(
        functools.partial(attend_back_kernel, tile, first, steps),
        grid_spec=grid_spec,
        out_shape=[shape for shape, _ in outs],
        compiler_params=params(2, 40),
        cost_estimate=lasting(23),
        name="attend_back",
    )(bounds, slot_of, q, k, v, do, o, lse, pcol, prow, srow, cosine, sine, *before)


def tile_bounds(starts_nat, tile):
    rows = starts_nat.shape[0]
    count = rows // tile
    tiles = starts_nat.reshape(count, tile)
    first, last = tiles[:, 0], tiles[:, -1]
    at = jnp.arange(count, dtype=jnp.int32) * tile
    lo = first // tile
    mid = (last + tile - 1) // tile
    full = jnp.sum((last[None, :] <= at[:, None]).astype(jnp.int32), axis=1)
    end = jnp.sum((first[None, :] <= at[:, None] + tile - 1).astype(jnp.int32), axis=1)
    return jnp.stack([lo, mid, full, end]).astype(jnp.int32)


def normalized(x):
    centred = x - jnp.mean(x, axis=1, keepdims=True)
    scale = lax.rsqrt(jnp.mean(centred * centred, axis=1, keepdims=True) + NORM_EPS)
    return centred * scale, scale


def normalized_back(hat, scale, upstream):
    level = jnp.mean(upstream, axis=1, keepdims=True)
    slant = jnp.mean(upstream * hat, axis=1, keepdims=True)
    return scale * (upstream - level - hat * slant)


def dot_nt(a, b):
    return lax.dot_general(a, b, (((1,), (1,)), ((), ())), preferred_element_type=F32)


def call(kernel, name, grid, tables, ins, outs, microseconds, *arrays):
    return pl.pallas_call(
        kernel,
        grid_spec=pltpu.PrefetchScalarGridSpec(
            num_scalar_prefetch=len(tables),
            grid=grid,
            in_specs=ins,
            out_specs=[spec for _, spec in outs],
        ),
        out_shape=[shape for shape, _ in outs],
        compiler_params=params(len(grid)),
        cost_estimate=lasting(microseconds),
        name=name,
    )(*tables, *arrays)


def shaped(dtype, *shape):
    return jax.ShapeDtypeStruct(shape, dtype)


def fixed(*shape):
    return pl.BlockSpec(shape, lambda *_: (0,) * len(shape))


def project_kernel(blocks, slots, near, far, gain_ref, w_ref, cos_ref, sin_ref, *refs):
    q_ref, k_ref, v_ref, n_ref = refs[-4:]
    width = q_ref.shape[1]
    x = jnp.where(slots[pl.program_id(0)] < 4, near[0], far[0]).astype(F32)
    normed = (normalized(x)[0] * gain_ref[0:1, :]).astype(BF16)
    n_ref[0] = normed
    linear = jnp.dot(normed, w_ref[...], preferred_element_type=F32)
    for at in range(0, width, 128):
        q = turned(linear[:, 3 * at : 3 * at + 128], cos_ref[...], sin_ref[...])
        k = turned(linear[:, 3 * at + 128 : 3 * at + 256], cos_ref[...], sin_ref[...])
        q_ref[:, at : at + 128] = q.astype(BF16) * jnp.asarray(0.125, BF16)
        k_ref[:, at : at + 128] = k.astype(BF16)
        v_ref[:, at : at + 128] = linear[:, 3 * at + 256 : 3 * at + 384].astype(BF16)


def project(near, far, gains, w, cosine, sine, blocks, slots, before):
    _, rows, depth = near.shape
    width = w.shape[1] // 3
    count = 2 * blocks.shape[0]
    piece = pl.BlockSpec((1, rows, depth), lambda i, b, s: (s[i] & 1, 0, 0))
    angle = pl.BlockSpec((rows, 128), lambda i, b, s: (b[i], 0))
    out = shaped(BF16, count * rows, width)
    normed = shaped(BF16, count, rows, depth)
    block = pl.BlockSpec((rows, width), lambda i, b, s: (b[i], 0))
    return pl.pallas_call(
        project_kernel,
        grid_spec=pltpu.PrefetchScalarGridSpec(
            num_scalar_prefetch=2,
            grid=blocks.shape,
            in_specs=[piece, piece, fixed(*gains.shape), fixed(*w.shape), angle, angle]
            + [pl.BlockSpec(memory_space=pl.ANY)] * len(before),
            out_specs=[
                block, block, block,
                pl.BlockSpec((1, rows, depth), lambda i, b, s: ((s[i] & 1) * 4 + (s[i] >> 1), 0, 0)),
            ],
        ),
        out_shape=[out, out, out, normed],
        input_output_aliases={8 + n: n for n in range(len(before))},
        compiler_params=params(1),
        cost_estimate=lasting(7),
        name="project",
    )(blocks, slots, near, far, gains, w, cosine, sine, *before)


def mix_kernel(group, own, near, far, both, w_ref, x_ref, gain_ref,
               heads_ref, hat_ref, scale_ref, hidden_ref, mid_ref):
    width = own.shape[2]
    for r, piece in enumerate((own[0], far[0], near[0], both[0])):
        at = pl.ds(pl.multiple_of((group[0] ^ r) * width, width), width)
        heads_ref[:, at] = piece
    branch = jnp.dot(heads_ref[...], w_ref[...], preferred_element_type=F32)
    hat, scale = normalized(branch)
    hidden = x_ref[0].astype(F32) + hat * gain_ref[1:2, :]
    hat_ref[...] = hat
    scale_ref[...] = scale
    hidden_ref[...] = hidden
    mid_ref[...] = (normalized(hidden)[0] * gain_ref[2:3, :]).astype(BF16)


def mix(group, local, near, far, both, w, x, gains):
    _, rows, part = local.shape
    count, _, width = x.shape
    block = pl.BlockSpec((1, rows, part), lambda i, g: (i, 0, 0))
    row = pl.BlockSpec((rows, width), lambda i, g: (i, 0))
    total = count * rows
    return call(
        mix_kernel, "mix", (count,), [group],
        [
            block, block, block, block, fixed(*w.shape), pl.BlockSpec((1, rows, width), lambda i, g: (i, 0, 0)),
            fixed(*gains.shape),
        ],
        [
            (shaped(BF16, total, width), row),
            (shaped(F32, total, width), row),
            (shaped(F32, total, 1), pl.BlockSpec((rows, 1), lambda i, g: (i, 0))),
            (shaped(F32, total, width), row),
            (shaped(BF16, total, width), row),
        ],
        6, local, near, far, both, w, x, gains,
    )


def finish_kernel(terms_ref, sent_ref, hidden_ref, dy_ref, gain_ref, mixed_ref, grad_ref, sum_ref):
    down = terms_ref[...] + sent_ref[...].astype(F32)
    hat, scale = normalized(down)
    gain = gain_ref[3:4, :]
    dy = dy_ref[...].astype(F32)
    mixed_ref[...] = (hidden_ref[...] + hat * gain).astype(BF16)
    grad_ref[...] = normalized_back(hat, scale, dy * gain).astype(BF16)

    @pl.when(pl.program_id(0) == 0)
    def _():
        sum_ref[...] = jnp.zeros_like(sum_ref)

    sum_ref[...] += jnp.sum(dy * hat, axis=0, keepdims=True)


def finish(terms, sent, hidden, dy, gains):
    total, width = terms.shape
    rows = total // 2
    row = pl.BlockSpec((rows, width), lambda i: (i, 0))
    return call(
        finish_kernel, "finish", (2,), [],
        [row, row, row, row, fixed(*gains.shape)],
        [
            (shaped(BF16, total, width), row), (shaped(BF16, total, width), row),
            (shaped(F32, 1, width), fixed(1, width)),
        ],
        5, terms, sent, hidden, dy, gains,
    )


def turn_kernel(group, terms_ref, sent_ref, hidden_ref, dy_ref, hat_ref, scale_ref, w_ref, gain_ref,
                keep_ref, branch_ref, heads_ref, three_ref, two_ref):
    upstream = terms_ref[...] + sent_ref[...].astype(F32)
    hat, scale = normalized(hidden_ref[...])

    @pl.when(pl.program_id(0) == 0)
    def _():
        three_ref[...] = jnp.zeros_like(three_ref)
        two_ref[...] = jnp.zeros_like(two_ref)

    three_ref[...] += jnp.sum(upstream * hat, axis=0, keepdims=True)
    grad = dy_ref[...].astype(F32) + normalized_back(hat, scale, upstream * gain_ref[2:3, :])
    keep_ref[...] = grad
    branch_hat = hat_ref[...]
    two_ref[...] += jnp.sum(grad * branch_hat, axis=0, keepdims=True)
    branch = normalized_back(branch_hat, scale_ref[...], grad * gain_ref[1:2, :]).astype(BF16)
    branch_ref[...] = branch
    part = heads_ref.shape[3]
    for r in range(4):
        at = pl.ds(pl.multiple_of((group[0] ^ r) * part, part), part)
        heads_ref[r, 0] = dot_nt(branch, w_ref[at, :]).astype(BF16)


def turn(group, terms, sent, hidden, dy, hat, scale, w, gains):
    total, width = terms.shape
    rows = total // 2
    part = width // 4
    row = pl.BlockSpec((rows, width), lambda i, g: (i, 0))
    return call(
        turn_kernel, "turn", (2,), [group],
        [
            row, row, row, row, row, pl.BlockSpec((rows, 1), lambda i, g: (i, 0)),
            fixed(*w.shape), fixed(*gains.shape),
        ],
        [
            (shaped(F32, total, width), row), (shaped(BF16, total, width), row),
            (
                shaped(BF16, 4, 2, rows, part),
                pl.BlockSpec((4, 1, rows, part), lambda i, g: (0, i, 0, 0)),
            ),
            (shaped(F32, 1, width), fixed(1, width)), (shaped(F32, 1, width), fixed(1, width)),
        ],
        8, terms, sent, hidden, dy, hat, scale, w, gains,
    )


def end_kernel(keep_ref, far_ref, x_ref, grad_ref, gain_ref, o_ref):
    upstream = keep_ref[...] + far_ref[...].astype(F32)
    hat, scale = normalized(x_ref[...].astype(F32))
    grad = grad_ref[...] + normalized_back(hat, scale, upstream * gain_ref[0:1, :])
    o_ref[...] = grad.astype(BF16)


def end(keep, far, x, grad, gains):
    total, width = x.shape
    rows = total // 2
    row = pl.BlockSpec((rows, width), lambda i: (i, 0))
    return call(
        end_kernel, "end", (2,), [], [row] * 4 + [fixed(*gains.shape)],
        [(shaped(BF16, total, width), row)], 20, keep, far, x, grad, gains,
    )[0]


def plain(x):
    return with_layout_constraint(x, Layout(tuple(range(x.ndim))))


QKV_BLOCKS, OVER_BLOCKS, OUT_BLOCKS = 12, 2, 8
LOW_BLOCKS = 11
ALL_BLOCKS = QKV_BLOCKS + OVER_BLOCKS + OUT_BLOCKS + 1
LEFT = ((0, 0), (0, 1), (1, 0))
RIGHT = ((1, 1), (2, 0), (2, 1))


def tiles(array):
    return [array[:, at : at + 128] for at in range(0, array.shape[1], 128)]


def plus(a, b):
    return (a.astype(F32) + b.astype(F32)).astype(BF16)


def spread_first_kernel(place, qkv_ref, out_ref, gain_ref, over_ref, far_ref, out_far,
                        low, low_away, high, high_away):
    lines = far_ref.shape[1]
    spare = over_ref.shape[0] // 8
    wide = qkv_ref.shape[1]
    x_bit, y_bit, core = place[0], place[1], place[2]

    def fill(line, low_out, high_out):
        at = pl.ds(pl.multiple_of((2 * line + core) * lines, lines), lines)
        near = tiles(qkv_ref[at, :])
        far = tiles(far_ref[line, :, :wide])
        blocks = [jnp.where(core == 0, a, b) for a, b in zip(near, far)]
        blocks += [jnp.where(core == 0, a, b) for a, b in zip(far, near)]
        for c in range(2):
            rows = pl.ds(pl.multiple_of((2 * line + c) * spare, spare), spare)
            blocks.append(jnp.concatenate(tiles(over_ref[rows, :]), axis=0))
        blocks += [
            plus(a, b)
            for a, b in zip(tiles(out_ref[at, :]), tiles(out_far[line]))
        ]
        count = gain_ref.shape[1]
        gain = jnp.concatenate(
            [gain_ref[2 * line + core], jnp.zeros((lines - count, 128), BF16)], axis=0
        )
        blocks.append(plus(gain, far_ref[line, :, -128:]))
        for n, block in enumerate(blocks):
            if n < LOW_BLOCKS and low_out is not None:
                low_out[n] = block
            if n >= LOW_BLOCKS and high_out is not None:
                high_out[n - LOW_BLOCKS] = block

    for n in range(2):
        fill(2 * n + x_bit, low.at[n], None)
        fill(2 * n + 1 - x_bit, low_away.at[n], None)
        fill(2 * y_bit + n, None, high.at[n])
        fill(2 * (1 - y_bit) + n, None, high_away.at[n])


def spread_first(place, qkv, out, gain, over, far, out_far):
    lines = far.shape[1]
    low = shaped(BF16, 2, LOW_BLOCKS, lines, 128), fixed(2, LOW_BLOCKS, lines, 128)
    rest = ALL_BLOCKS - LOW_BLOCKS
    high = shaped(BF16, 2, rest, lines, 128), fixed(2, rest, lines, 128)
    arrays = (qkv, out, gain, over, far, out_far)
    return call(
        spread_first_kernel, "spread_first", (1,), [place], [fixed(*a.shape) for a in arrays],
        [low, low, high, high], 2, *arrays,
    )


def spread_second_kernel(place, low, low_far, high, high_far, low_o, low_away, high_o, high_away):
    for source, far, bit, near_o, away_o in (
        (low, low_far, place[1], low_o, low_away), (high, high_far, place[0], high_o, high_away)
    ):
        near_o[...] = plus(source[bit], far[bit])
        away_o[...] = plus(source[1 - bit], far[1 - bit])


def spread_second(place, *arrays):
    lows, highs = arrays[0].shape[1:], arrays[2].shape[1:]
    outs = [(shaped(BF16, *s), fixed(*s)) for s in (lows, lows, highs, highs)]
    return call(
        spread_second_kernel, "spread_second", (1,), [place], [fixed(*a.shape) for a in arrays],
        outs, 2, *arrays,
    )


def spread_third_kernel(place, low, low_far, high, high_far, near_o, away_o, over_o):
    half = place[4]

    def block(n):
        if n < LOW_BLOCKS:
            return plus(low[n], low_far[n])
        return plus(high[n - LOW_BLOCKS], high_far[n - LOW_BLOCKS])

    at = 0
    for (left_t, left_c), (right_t, right_c) in zip(LEFT, RIGHT):
        for pair in range(2):
            left = block(left_c * 6 + pair * 3 + left_t)
            right = block(right_c * 6 + pair * 3 + right_t)
            near_o[at] = jnp.where(half == 0, left, right)
            away_o[at] = jnp.where(half == 0, right, left)
            at += 1
    for c in range(2):
        over_o[c] = block(QKV_BLOCKS + c)
    first = QKV_BLOCKS + OVER_BLOCKS
    for n in range(4):
        left, right = block(first + n), block(first + 4 + n)
        near_o[at] = jnp.where(half == 0, left, right)
        away_o[at] = jnp.where(half == 0, right, left)
        at += 1
    near_o[at] = block(first + 8)
    away_o[at] = block(first + 8)


def spread_third(place, *arrays):
    lines = arrays[0].shape[1]
    part = shaped(BF16, 11, lines, 128), fixed(11, lines, 128)
    over = shaped(BF16, 2, lines, 128), fixed(2, lines, 128)
    return call(
        spread_third_kernel, "spread_third", (1,), [place], [fixed(*a.shape) for a in arrays],
        [part, part, over], 2, *arrays,
    )


def spread_fourth_kernel(place, near, far, near_o, away_o):
    odd = place[3] == 1
    blocks = [plus(near[n], far[n]) for n in range(11)]
    for pair in range(2):
        one, two, three = blocks[pair], blocks[2 + pair], blocks[4 + pair]
        near_o[pair] = jnp.where(odd, two, one)
        near_o[2 + pair] = jnp.where(odd, three, two)
        away_o[pair] = jnp.where(odd, one, three)
        near_o[4 + pair] = jnp.where(odd, blocks[8 + pair], blocks[6 + pair])
        away_o[2 + pair] = jnp.where(odd, blocks[6 + pair], blocks[8 + pair])
    near_o[6] = blocks[10]
    away_o[4] = blocks[10]


def spread_fourth(place, near, far):
    lines = near.shape[1]
    return call(
        spread_fourth_kernel, "spread_fourth", (1,), [place], [fixed(*near.shape)] * 2,
        [
            (shaped(BF16, 7, lines, 128), fixed(7, lines, 128)),
            (shaped(BF16, 5, lines, 128), fixed(5, lines, 128)),
        ],
        2, near, far,
    )


def spread_fifth_kernel(place, near, far, qkv_o, out_o, gain_o, gain_all):
    for pair in range(2):
        first, second = near[pair].astype(F32), near[2 + pair].astype(F32)
        other = far[pair].astype(F32)
        at = 128 * pair
        qkv_o[:, at : at + 128] = first
        qkv_o[:, 256 + at : 384 + at] = other
        qkv_o[:, 512 + at : 640 + at] = second
        out_o[:, at : at + 128] = near[4 + pair].astype(F32) + far[2 + pair].astype(F32)
    gain_all[...] = near[6].astype(F32) + far[4].astype(F32)
    gain_o[...] = gain_all[pl.ds(2 * place[4] + place[3], 1), :]


def spread_fifth(place, near, far):
    lines = near.shape[1]
    outs = [(shaped(F32, *s), fixed(*s)) for s in ((lines, 768), (lines, 256), (1, 128))]
    return pl.pallas_call(
        spread_fifth_kernel,
        grid_spec=pltpu.PrefetchScalarGridSpec(
            num_scalar_prefetch=1,
            grid=(1,),
            in_specs=[fixed(*near.shape), fixed(*far.shape)],
            out_specs=[spec for _, spec in outs],
            scratch_shapes=[pltpu.VMEM((lines, 128), F32)],
        ),
        out_shape=[shape for shape, _ in outs],
        compiler_params=params(1),
        cost_estimate=lasting(2),
        name="spread_fifth",
    )(place, near, far)


def flip(x, axis, bit):
    return lax.ppermute(plain(x), axis, [(i, i ^ bit) for i in range(lax.axis_size(axis))])


def swap(x):
    cp = lax.axis_size("cp")
    half = cp // 2
    pairs = []
    for z in range(half):
        low, high = cp + z, z + half
        pairs += [(low, high), (high, low)]
    return lax.ppermute(plain(x), ("core", "cp"), pairs)


def settled(x, moved):
    stays = (lax.axis_index("core") == 1) == (lax.axis_index("cp") >= lax.axis_size("cp") // 2)
    return jnp.where(stays, x, moved)


def ordered(first, mine, other, axis):
    return jnp.concatenate(
        [jnp.where(first, mine, other), jnp.where(first, other, mine)], axis=axis
    )


def placed(first, mine, other, at):
    return ordered(first, jnp.expand_dims(mine, at), jnp.expand_dims(other, at), at)


def after(x, *others):
    return lax.optimization_barrier((x, *others))[0]


def all_after(group, *others):
    return lax.optimization_barrier((*group, *others))[: len(group)]


def total(a, b):
    return (a.astype(F32) + b.astype(F32)).astype(BF16)


def flip_both(x):
    cp = lax.axis_size("cp")
    return lax.ppermute(
        x, ("core", "cp"), [(c * cp + z, (1 - c) * cp + (z ^ 1)) for c in range(2) for z in range(cp)]
    )


def dot(a, b, dims):
    return lax.dot_general(a, b, ((dims[:1], dims[1:]), ((), ())), preferred_element_type=F32)


def gelu_and_slope(u):
    c = math.sqrt(2.0 / math.pi)
    square = u * u
    t = jnp.tanh(u * (c + (c * 0.044715) * square))
    half = 0.5 + 0.5 * t
    slope = half + (0.5 * u) * (1.0 - t * t) * (c + (3.0 * 0.044715 * c) * square)
    return lax.optimization_barrier(((u * half).astype(BF16), slope.astype(BF16)))


def pick(x, at, axis):
    return lax.dynamic_index_in_dim(x, at, axis, False)


def widened(z, x, other):
    first, second = jnp.where(z & 1 == 0, x, other), jnp.where(z & 1 == 0, other, x)
    half = x.shape[1] // 2
    return jnp.concatenate(
        [first[:, :half], second[:, :half], first[:, half:], second[:, half:]], axis=1
    )


def body(tokens, doc_starts, qkv_weight, out_weight, up_weight, down_weight, norm_gains, cotangent):
    xy, core, z = lax.axis_index("xy"), lax.axis_index("core"), lax.axis_index("cp")
    xy_count, cp_count = lax.axis_size("xy"), lax.axis_size("cp")
    _, _, span, width = tokens.shape
    blocks = 2 * cp_count
    row_len = blocks * span
    own = 2 * span
    parity = z & 1
    group = parity + 2 * core
    part = width // cp_count
    hidden_part = up_weight.shape[1] // 2
    lines_each = width // xy_count
    lines = lines_each // 2
    here = jnp.reshape(xy, (1,)).astype(jnp.int32)
    group_at = jnp.reshape(group, (1,)).astype(jnp.int32)

    gain_rows = jnp.zeros((16, qkv_weight.shape[1]), BF16)
    gain_rows = lax.dynamic_update_slice(gain_rows, norm_gains[None], (0, 0))
    w = jnp.concatenate([qkv_weight, gain_rows])
    w_far = flip(w, "cp", 2)

    x = settled(tokens[0], swap(after(tokens, w_far)[0]))
    w, w_far = jnp.where(z & 2 == 0, w, w_far), jnp.where(z & 2 == 0, w_far, w)
    near = [w[:, n * part : (n + 1) * part] for n in range(3)]
    near += [w_far[:, n * part : (n + 1) * part] for n in range(3)]
    even = parity == 0
    sent = jnp.concatenate([near[1], near[4]], axis=1)
    gain_near = jnp.stack([w[lines, :128], w_far[lines, :128]])
    sent = lax.dynamic_update_slice(sent, gain_near, (lines, 0))
    far = flip(sent, "cp", 1)
    up_weight, down_weight, out_weight = all_after((up_weight, down_weight, out_weight), far)
    out_far = flip(out_weight, "cp", 2)


    def half_of(which):
        up = lax.dynamic_slice_in_dim(up_weight, which * hidden_part, hidden_part, 1)
        down = lax.dynamic_slice_in_dim(down_weight, which * hidden_part, hidden_part, 0)
        return plain(jnp.stack([up, down.T]))

    ffn = ordered(core == 0, half_of(core), flip(half_of(1 - core), "core", 1), 1)

    def paired(mine, other):
        return jnp.concatenate(
            [jnp.where(z & 2 == 0, mine, other), jnp.where(z & 2 == 0, other, mine)], axis=1
        )

    gain_far = far[lines : lines + 2, :128]
    gain_near, gain_far = (
        jnp.where(even, gain_near, gain_far), jnp.where(even, gain_far, gain_near)
    )
    gain_rows = jnp.stack([gain_near[0], gain_far[0], gain_near[1], gain_far[1]])
    far = [far[:lines, n * part : (n + 1) * part] for n in range(2)]
    near = [block[:lines] for block in near]

    def by_pairs(*choices):
        picked = [jnp.where(even, a, b) for a, b in choices]
        return jnp.concatenate(
            [block[:, at : at + 128] for at in range(0, part, 128) for block in picked], axis=1
        )

    first_group = by_pairs((near[0], far[0]), (far[0], near[2]), (near[5], near[3]))
    second_group = by_pairs((near[2], near[0]), (near[3], far[1]), (far[1], near[5]))
    gain_block = jnp.zeros((16, 3 * part), BF16)
    gain_block = lax.dynamic_update_slice(gain_block, gain_rows, (0, 0))
    mine = jnp.concatenate([jnp.where(core == 0, first_group, second_group), gain_block])
    other = jnp.concatenate([jnp.where(core == 0, second_group, first_group), gain_block])

    other_starts = flip(after(doc_starts, w_far), "core", 1)
    starts = jnp.where(core == z // (cp_count // 2), doc_starts, other_starts)[0]

    block_id = jnp.arange(blocks, dtype=jnp.int32)[:, None]
    inside = jnp.arange(span, dtype=jnp.int32)[None, :]
    late = block_id >= cp_count
    positions = (block_id * span + jnp.where(late, span - 1 - inside, inside)).reshape(-1)

    def starts_at(at):
        return jnp.max(jnp.where(starts[None, :] <= at[:, None], starts[None, :], 0), axis=1)

    row_start = starts_at(positions)
    tile = min(512, row_len)
    bounds = tile_bounds(starts_at(jnp.arange(row_len, dtype=jnp.int32)), tile)
    freq = jnp.exp(
        -math.log(10000.0) * 2.0 * jnp.arange(HEAD_DIM // 2, dtype=F32) / HEAD_DIM
    )
    angles = (positions - row_start).astype(F32)[:, None] * freq
    cosine, sine = jnp.cos(angles), jnp.sin(angles)
    cosine = plain(jnp.tile(cosine, (1, 4)))
    sine = plain(jnp.tile(jnp.concatenate([-sine, sine], axis=1), (1, 2)))
    pcol, prow, srow = positions[:, None], positions[None, :], row_start[None, :]
    chunk = jnp.arange(blocks, dtype=jnp.int32)
    chunk = jnp.where(chunk < cp_count, chunk, blocks - 1 - chunk)
    slot_of = (
        2 * (2 * ((chunk >> 1) ^ core) + ((chunk & 1) ^ parity))
        + (jnp.arange(blocks) >= cp_count)
    ).astype(jnp.int32)
    slot = jnp.arange(blocks, dtype=jnp.int32)
    relative = slot >> 1
    chunk_of = 2 * ((relative >> 1) ^ core) + ((relative & 1) ^ parity)
    block_of = jnp.where(slot & 1 == 0, chunk_of, blocks - 1 - chunk_of).astype(jnp.int32)

    x = after(x, sent, cosine, sine)
    x_chip = flip(x, "cp", 1)
    x_core = flip(x, "core", 1)
    up_lines, out_w, out_far = all_after((ffn[0], out_weight, out_far), x)
    up_far = flip(up_lines, "cp", 2)
    out_w = paired(out_w, out_far)
    out_far = flip(out_w, "cp", 1)

    qkv = placed(core == 0, mine, flip(other, "core", 1), 0)
    cut = qkv.shape[2] // 2
    low, high = qkv[:, :, :cut], qkv[:, :, cut:]
    low = placed(xy & 1 == 0, low, flip(low, "xy", 1), 0)
    high = placed(xy & 2 == 0, high, flip(high, "xy", 2), 0)
    low = placed(xy & 2 == 0, low, flip(low, "xy", 2), 0)
    high = placed(xy & 1 == 0, high, flip(high, "xy", 1), 1)
    qkv = jnp.concatenate([low[:, :, :, :lines], high[:, :, :, :lines]], axis=4)
    qkv = qkv.reshape(width, 3 * part)
    gains = low[:, :, :, lines : lines + cp_count, :128]
    gains = gains.reshape(4, width).astype(F32)

    sooner, later = jnp.array([0, 1, 4, 5], jnp.int32), jnp.array([2, 3, 6, 7], jnp.int32)
    early = project(x, x_core, gains, qkv, cosine, sine, block_of[sooner], sooner, [])
    x_chip, up_far, *early = lax.optimization_barrier((x_chip, up_far, *early))
    x_both = flip(x_chip, "core", 1)
    up_lines, up_far, down_lines, out_w, out_far = all_after(
        (up_lines, up_far, ffn[1], out_w, out_far), x_chip, qkv
    )
    up_lines, out_w = paired(up_lines, up_far), widened(z, out_w, out_far)[None]
    up_far = flip(up_lines, "cp", 1)
    down_far = flip(down_lines, "cp", 2)
    out_far = flip(out_w, "xy", 1)

    def halves(x):
        return x[None, :lines], x[None, lines:]

    def send_lines(low, high):
        return flip(low, "xy", 1), flip(high, "xy", 2)

    def join_lines(low, high, low_far, high_far):
        low = ordered(xy & 1 == 0, low, low_far, 0)
        high = jnp.expand_dims(ordered(xy & 2 == 0, high, high_far, 0), 1)
        return low, high

    def send_more(low, high):
        return flip(low, "xy", 2), flip(high, "xy", 1)

    def join_all(low, high, low_far, high_far):
        low = ordered(xy & 2 == 0, low, low_far, 0)
        high = ordered(xy & 1 == 0, high, high_far, 1).reshape(low.shape)
        return jnp.stack([low, high], axis=1).reshape(width, -1)

    q, k, v, normed = project(
        x_chip, x_both, gains, qkv, cosine, sine, block_of[later], later, early
    )
    up_lines, up_far, down_lines, down_far, out_w, out_far = all_after(
        (up_lines, up_far, down_lines, down_far, out_w, out_far), q
    )
    up_lines = widened(z, up_lines, up_far)
    up_full = lax.all_gather(up_lines, "xy", axis=0, tiled=True)
    out_w = ordered(xy & 1 == 0, out_w, out_far, 0)
    out_far = flip(out_w, "xy", 2)
    down_lines = paired(down_lines, down_far)
    down_far = flip(down_lines, "cp", 1)
    q = after(q, up_lines, out_w, down_lines)
    first = attend(0, q, k, v, pcol, prow, srow, bounds, slot_of, tile)
    down_lines, down_far, out_w, out_far = all_after(
        (down_lines, down_far, out_w, out_far), first[0]
    )
    out_w = ordered(xy & 2 == 0, out_w, out_far, 0)
    down_pair = halves(widened(z, down_lines, down_far))
    down_far = send_lines(*down_pair)
    q = after(q, first[0], *down_pair, out_w)
    second = attend(1, q, k, v, pcol, prow, srow, bounds, slot_of, tile)
    attended, local, lse = zip(first, second)
    local = jnp.concatenate(local, axis=2)
    out_w, down_pair, down_far = (
        after(out_w, local), all_after(down_pair, local), all_after(down_far, local)
    )
    out_w = placed(core == 0, out_w, flip(out_w, "core", 1), 1).reshape(width, width)
    down_pair = join_lines(*down_pair, *down_far)
    down_far = send_more(*down_pair)
    heads, branch_hat, branch_scale, hidden, mid = mix(
        group_at, after(local, *down_pair)[:2], flip(local[4:6], "core", 1), flip(local[2:4], "cp", 1),
        flip_both(local[6:]), out_w, x, gains,
    )

    cotangent = cotangent.reshape(own, width)
    dy_moved = swap(after(cotangent, mid))

    ffn_in = jnp.concatenate([mid, flip(mid, "core", 1)])
    act, slope = gelu_and_slope(dot(ffn_in, up_full, (1, 0)))
    down_full = join_all(*down_pair, *all_after(down_far, act))
    sent = flip(dot(act[own:], down_full, (1, 1)).astype(BF16), "core", 1)
    terms = dot(act[:own], down_full, (1, 1))
    dy = settled(cotangent, dy_moved)
    mixed, grad_down, gain_four = finish(terms, sent, hidden, dy, gains)
    grad_down = jnp.concatenate([grad_down, flip(grad_down, "core", 1)])

    x_bit, y_bit = xy & 1, xy >> 1

    def cut_first(grads):
        grads = [g.reshape(2, 2, 2, -1, g.shape[-1]) for g in grads]
        low = [g[:, :, 0] for g in grads]
        high = [g[:, :, 1] for g in grads]

        def both(parts, at, axis):
            return jnp.concatenate([pick(part_of, at, axis) for part_of in parts], axis=1)

        away = both(low, 1 - x_bit, 1), both(high, 1 - y_bit, 0)
        return (both(low, x_bit, 1), both(high, y_bit, 0)), away

    def send_first(away):
        return flip(away[0], "xy", 1), flip(away[1], "xy", 2)

    def cut_second(near, far):
        away = (
            total(pick(near[0], 1 - y_bit, 0), pick(far[0], 1 - y_bit, 0)),
            total(pick(near[1], 1 - x_bit, 0), pick(far[1], 1 - x_bit, 0)),
        )
        near = (
            total(pick(near[0], y_bit, 0), pick(far[0], y_bit, 0)),
            total(pick(near[1], x_bit, 0), pick(far[1], x_bit, 0)),
        )
        return near, away

    def send_second(away):
        return flip(away[0], "xy", 2), flip(away[1], "xy", 1)

    def cut_third(near, far):
        return split_columns(
            jnp.concatenate([total(a, b) for a, b in zip(near, far)]), hidden_part
        )

    def split_columns(sums, each):
        blocks_of = [sums[:, n * each : (n + 1) * each] for n in range(cp_count)]
        odd = jnp.stack([blocks_of[1], blocks_of[3]])
        even = jnp.stack([blocks_of[0], blocks_of[2]])
        return jnp.where(parity == 0, even, odd), jnp.where(parity == 0, odd, even)

    def cut_fourth(near, far):
        return (
            total(pick(near, z >> 1, 0), pick(far, z >> 1, 0)),
            total(pick(near, 1 - (z >> 1), 0), pick(far, 1 - (z >> 1), 0)),
        )

    down_local = plain(dot(grad_down, act, (0, 0)).astype(BF16))
    grad_up = dot(after(grad_down, down_local), down_full, (1, 0)) * slope.astype(F32)
    grad_up = grad_up.astype(BF16)
    sent = flip(dot(grad_up[own:], up_full, (1, 1)).astype(BF16), "core", 1)
    up_local = plain(dot(ffn_in, grad_up, (0, 0)).astype(BF16))
    spare = lines // 4
    down_local = down_local.reshape(2 * xy_count, lines, -1)
    over_local = down_local[:, lines - spare :].reshape(2 * xy_count * spare, -1)
    down_local = down_local[:, : lines - spare].reshape(2 * xy_count * (lines - spare), -1)
    grad_near, grad_away = cut_first((up_local, down_local))
    grad_far = send_first(grad_away)
    terms = dot(after(grad_up, *grad_away)[:own], up_full, (1, 1))
    grad_hidden, grad_branch, grad_heads, gain_three, gain_two = turn(
        group_at, terms, sent, hidden, dy, branch_hat, branch_scale, out_w, gains
    )

    grad_local = [
        grad_heads[0], flip(grad_heads[1], "cp", 1), flip(grad_heads[2], "core", 1),
        flip_both(grad_heads[3]),
    ]
    out_local = dot(after(heads, grad_heads), grad_branch, (0, 0)).astype(BF16)
    grad_local = plain(jnp.concatenate(grad_local))
    out_away = pick(out_local.reshape(xy_count, 2, lines, width), 1 - core, 1)
    out_away, over_local, mixed, grad_local = lax.optimization_barrier(
        (out_away, over_local, mixed, grad_local)
    )
    over_near, over_away = split_columns(over_local, hidden_part)
    over_far = flip(over_away, "cp", 1)
    mixed_moved = swap(mixed)
    grad_local = after(grad_local, over_away)

    def back_to_tokens(grads):
        two = 2 * span
        rows = grads.reshape(4 * span, 3 * part)
        send = dot(rows[two:], qkv, (1, 1)).astype(BF16)
        sent = flip(send, "core", 1)
        rows = after(rows, send)
        own_sums = dot(rows[:two], qkv, (1, 1)) + sent.astype(F32)
        far_away = own_sums[span:].astype(BF16)
        return send, far_away, flip(far_away, "cp", 1), own_sums[:span]

    tables = (pcol, prow, srow, cosine, sine, bounds, slot_of, tile)
    attended, lse = jnp.concatenate(attended, axis=1), jnp.concatenate(lse, axis=0)
    first, unfinished = attend_back(0, q, k, v, grad_local, attended, lse, *tables, [])
    first, mixed_moved, over_far, *grad_far = lax.optimization_barrier(
        (first, mixed_moved, over_far, *grad_far)
    )
    over_near, over_away = cut_fourth(over_near, over_far)
    over_far = flip(over_away, "cp", 2)
    _, far_away, far_back, kept = back_to_tokens(after(first, over_away))
    grad_near, grad_away = cut_second(grad_near, all_after(grad_far, far_away))
    grad_far = send_second(grad_away)
    out_far = flip(after(out_away, far_away), "core", 1)
    second = attend_back(
        1, q, k, v, after(grad_local, first, *grad_away, over_away, kept), attended, lse, *tables,
        [unfinished],
    )[0]
    second, over_far, out_far, *grad_far = lax.optimization_barrier(
        (second, over_far, out_far, *grad_far)
    )

    ended = end(kept, after(far_back, second), x[0], grad_hidden[:span], gains)
    moved = swap(ended)
    second = after(second, ended)
    send, far_away, far, kept = back_to_tokens(second)
    qkv_local = sum(
        dot(normed[4 * h : 4 * h + 4].reshape(4 * span, width), g.reshape(4 * span, -1), (0, 0))
        for h, g in enumerate((first, after(second, send)))
    ).astype(BF16)
    gain_one = jnp.sum(qkv_local.astype(F32) * qkv.astype(F32), axis=1) / gains[0]
    gain_sum = jnp.concatenate([gain_one[None], gain_two, gain_three, gain_four])
    gain_sum = gain_sum.reshape(2 * xy_count, cp_count, 128).astype(BF16)
    place = jnp.stack([x_bit, y_bit, core, parity, z >> 1]).astype(jnp.int32)
    locals_ = (qkv_local, out_local, gain_sum)
    rest_away = jnp.concatenate(
        [
            pick(qkv_local.reshape(xy_count, 2, lines, 3 * part), 1 - core, 1),
            jnp.pad(
                pick(gain_sum.reshape(xy_count, 2, cp_count, 128), 1 - core, 1),
                ((0, 0), (0, lines - cp_count), (0, 0)),
            ),
        ],
        axis=2,
    )
    rest_far = flip(rest_away, "core", 1)

    over = total(over_near, over_far)
    rest_far, over = all_after((rest_far, over), kept)
    low, low_away, high, high_away = spread_first(place, *locals_, over, rest_far, out_far)
    rest_far = flip(low_away, "xy", 1), flip(high_away, "xy", 2)
    low, low_away, high, high_away = spread_second(place, low, rest_far[0], high, rest_far[1])
    rest_far = flip(low_away, "xy", 2), flip(high_away, "xy", 1)
    grad_near, grad_away = cut_third(grad_near, all_after(grad_far, low_away))
    grad_far = flip(grad_away, "cp", 1)
    ended_last = end(
        kept, after(far, moved, low_away, high_away), x[1], grad_hidden[span:], gains
    )
    moved_last = swap(ended_last)
    rest_far = all_after(rest_far, moved_last)
    rest, rest_away, over = spread_third(place, low, rest_far[0], high, rest_far[1])
    grad_near, grad_away = cut_fourth(grad_near, after(grad_far, rest_away))
    grad_far = flip(grad_away, "cp", 2)
    gather_away = rest_away
    rest, rest_away = spread_fourth(place, rest, flip(rest_away, "cp", 2))
    moved_last = after(moved_last, rest_away)
    qkv_grad, out_grad, gains_grad = spread_fifth(place, rest, flip(rest_away, "cp", 1))
    gains_grad = gains_grad.reshape(-1)
    tokens_grad = jnp.stack([settled(ended, moved), settled(ended_last, moved_last)])
    tokens_grad = tokens_grad.astype(F32).reshape(tokens.shape)
    mixed = settled(after(mixed, gather_away), mixed_moved).reshape(tokens.shape)

    both = total(grad_near, after(grad_far, gather_away))
    both = plain(both).reshape(2, 2 * lines - spare, hidden_part)
    over = [
        jnp.concatenate([block[n * spare : (n + 1) * spare] for n in range(4)], axis=1)
        for block in over
    ]
    both = jnp.concatenate([both, jnp.stack(over)], axis=1).reshape(2, 2, lines, hidden_part)
    mine, other = pick(both, core, 0), flip(pick(both, 1 - core, 0), "core", 1)
    up_grad = ordered(core == 0, mine[0], other[0], 1).astype(F32)
    down_grad = ordered(core == 0, mine[1], other[1], 1).T.astype(F32)
    return mixed, tokens_grad, qkv_grad, out_grad, up_grad, down_grad, gains_grad


def solution(mesh):
    rows, cp = mesh.shape["rows"], mesh.shape["cp"]
    if (rows, cp) == (8, 4):
        grid = Mesh(mesh.devices.reshape(rows // 2, 2, cp), ("xy", "core", "cp"))
        run, lines = body, ("xy", "core")
    else:
        grid, run, lines = mesh, general_body, ("rows",)
    tokens = P(lines, None, "cp", None)
    weight, down, gains = P(lines, "cp"), P("cp", lines), P(lines + ("cp",))
    return jax.shard_map(
        run,
        mesh=grid,
        in_specs=(tokens, P(lines, None), weight, weight, weight, down, gains, tokens),
        out_specs=(tokens, tokens, weight, weight, weight, down, gains),
        check_vma=False,
    )
```

```python
import functools
import math

import jax
import jax.numpy as jnp
from jax import lax
from jax.experimental import pallas as pl
from jax.experimental.layout import Layout, with_layout_constraint
from jax.experimental.pallas import tpu as pltpu
from jax.sharding import Mesh, PartitionSpec as P

HEADS = 16
HEAD_DIM = 64


NORM_EPS = 1e-05
MASKED = -1e30


def layer_norm(values):
    average = jnp.mean(values, axis=-1, keepdims=True)
    centred = values - average
    spread = jnp.mean(centred * centred, axis=-1, keepdims=True)
    return centred * lax.rsqrt(spread + NORM_EPS)


def norm_back(values, upstream):
    _, pull_back = jax.vjp(layer_norm, values)
    return pull_back(upstream)[0]


def gelu_tanh(values):
    return jax.nn.gelu(values, approximate=True)


def rotate(values, cosine, sine_part):
    half_width = values.shape[-1] // 2
    first_half = values[..., :half_width]
    second_half = values[..., half_width:]
    return jnp.concatenate(
        [
            first_half * cosine - second_half * sine_part,
            second_half * cosine + first_half * sine_part,
        ],
        axis=-1,
    )


def rounded(values):
    return lax.optimization_barrier(values.astype(jnp.bfloat16)).astype(jnp.float32)


def doc_start_of(starts, positions):
    return jnp.max(
        jnp.where(starts[:, None, :] <= positions[None, :, None], starts[:, None, :], 0), axis=-1
    )


def general_body(tokens, doc_starts, qkv_weight, out_weight, up_weight, down_weight, norm_gains, cotangent):
    rows_count = lax.axis_size("rows")
    cp_count = lax.axis_size("cp")
    qkv_rows, out_rows, up_rows, down_rows, gain_piece = (
        lax.all_gather(qkv_weight, "rows", axis=0, tiled=True),
        lax.all_gather(out_weight, "rows", axis=0, tiled=True),
        lax.all_gather(up_weight, "rows", axis=0, tiled=True),
        lax.all_gather(down_weight, "rows", axis=1, tiled=True),
        lax.all_gather(norm_gains, "rows", axis=0, tiled=True),
    )
    qkv_full, out_full, gain_mixed = (
        lax.all_gather(qkv_rows, "cp", axis=1, tiled=True),
        lax.all_gather(out_rows, "cp", axis=1, tiled=True),
        lax.all_gather(gain_piece, "cp", axis=0, tiled=True),
    )
    gain_full = jnp.transpose(gain_mixed.reshape(cp_count, rows_count, -1), (1, 0, 2)).reshape(-1)
    row_count, _, span_len, width = tokens.shape
    half_len = span_len * cp_count
    row_len = 2 * half_len
    queries_dev = 2 * span_len
    token_total = row_count * queries_dev
    group_total = row_count * row_len
    gain_rows = gain_full.astype(jnp.float32).reshape(4, width)
    score_scale = HEAD_DIM ** (-0.5)
    local_pos = lax.axis_index("cp") * span_len + jnp.arange(span_len, dtype=jnp.int32)
    query_pos = jnp.concatenate([local_pos, row_len - 1 - local_pos])
    half_pos = jnp.arange(half_len, dtype=jnp.int32)
    key_pos = jnp.concatenate([half_pos, row_len - 1 - half_pos])
    query_start = doc_start_of(doc_starts, query_pos)
    key_start = doc_start_of(doc_starts, key_pos)
    freq_index = jnp.arange(HEAD_DIM // 2, dtype=jnp.float32)
    inverse_freq = jnp.exp(-math.log(10000.0) * 2.0 * freq_index / HEAD_DIM)
    angles = (query_pos[None, :] - query_start).astype(jnp.float32)[..., None] * inverse_freq
    cosine = jnp.cos(angles)[:, :, None, :]
    sine_part = jnp.sin(angles)[:, :, None, :]
    head_shape = (row_count, queries_dev, HEADS, HEAD_DIM)
    flat_shape = (row_count, queries_dev, width)
    fold_shape = (row_count, 2, span_len, width)
    group_shape = (row_count, 2, half_len, width)
    full_shape = (row_count, row_len, HEADS, HEAD_DIM)
    inputs = tokens.astype(jnp.float32).reshape(flat_shape)
    normed_in = layer_norm(inputs)
    normed = (normed_in * gain_rows[0]).astype(jnp.bfloat16)
    linear = jnp.dot(normed, qkv_full, preferred_element_type=jnp.float32)
    query_rows = rotate(linear[..., :width].reshape(head_shape), cosine, sine_part).astype(
        jnp.bfloat16
    )
    key_local = rotate(
        linear[..., width : 2 * width].reshape(head_shape), cosine, sine_part
    ).astype(jnp.bfloat16)
    value_local = linear[..., 2 * width :].reshape(head_shape).astype(jnp.bfloat16)
    key_sent, value_sent = (
        lax.all_gather(key_local.reshape(fold_shape), "cp", axis=2, tiled=True),
        lax.all_gather(value_local.reshape(fold_shape), "cp", axis=2, tiled=True),
    )
    key_rows = key_sent.reshape(full_shape)
    value_rows = value_sent.reshape(full_shape)
    block_size = min(512, row_len)
    block_count = row_len // block_size
    block_range = jnp.arange(block_count)

    def block_scores(block_index):
        first_key = block_index * block_size
        key_block = lax.dynamic_slice_in_dim(key_rows, first_key, block_size, 1)
        pos_block = lax.dynamic_slice_in_dim(key_pos, first_key, block_size, 0)
        start_block = lax.dynamic_slice_in_dim(key_start, first_key, block_size, 1)
        raw_scores = jnp.einsum(
            "rqhd,rkhd->rhqk", query_rows, key_block, preferred_element_type=jnp.float32
        )
        allowed = (query_start[:, None, :, None] == start_block[:, None, None, :]) & (
            pos_block[None, None, None, :] <= query_pos[None, None, :, None]
        )
        return (raw_scores * score_scale, allowed)

    def max_step(carry, block_index):
        running_max, running_sum = carry
        scores, allowed = block_scores(block_index)
        scores = jnp.where(allowed, scores, MASKED)
        new_max = jnp.maximum(running_max, jnp.max(scores, axis=-1))
        running_sum = running_sum * jnp.exp(running_max - new_max) + jnp.sum(
            jnp.where(allowed, jnp.exp(scores - new_max[..., None]), 0.0), axis=-1
        )
        return ((new_max, running_sum), None)

    stat_shape = (row_count, HEADS, queries_dev)
    (running_max, running_sum), _ = lax.scan(
        max_step,
        (jnp.full(stat_shape, MASKED, jnp.float32), jnp.zeros(stat_shape, jnp.float32)),
        block_range,
    )
    log_total = running_max + jnp.log(running_sum)

    def value_step(totals, block_index):
        scores, allowed = block_scores(block_index)
        probs = jnp.where(allowed, jnp.exp(scores - log_total[..., None]), 0.0).astype(jnp.bfloat16)
        value_block = lax.dynamic_slice_in_dim(value_rows, block_index * block_size, block_size, 1)
        return (
            totals
            + jnp.einsum("rhqk,rkhd->rqhd", probs, value_block, preferred_element_type=jnp.float32),
            None,
        )

    attended, _ = lax.scan(value_step, jnp.zeros(head_shape, jnp.float32), block_range)
    mixed_heads = attended.reshape(flat_shape).astype(jnp.bfloat16)
    branch = jnp.dot(mixed_heads, out_full, preferred_element_type=jnp.float32)
    branch_hat = layer_norm(branch)
    hidden = inputs + branch_hat * gain_rows[1]
    hidden_hat = layer_norm(hidden)
    normed_mid = (hidden_hat * gain_rows[2]).astype(jnp.bfloat16)
    ffn_in = lax.all_gather(normed_mid.reshape(fold_shape), "cp", axis=2, tiled=True).reshape(
        group_total, width
    )
    up_proj = jnp.dot(ffn_in, up_rows, preferred_element_type=jnp.float32)
    activation = gelu_tanh(up_proj).astype(jnp.bfloat16)
    down_terms = jnp.dot(activation, down_rows, preferred_element_type=jnp.float32)
    down_proj = (
        lax.psum_scatter(
            down_terms.reshape(group_shape).astype(jnp.bfloat16),
            "cp",
            scatter_dimension=2,
            tiled=True,
        )
        .astype(jnp.float32)
        .reshape(flat_shape)
    )
    down_hat = layer_norm(down_proj)
    mixed = (hidden + down_hat * gain_rows[3]).astype(jnp.bfloat16).reshape(tokens.shape)
    upstream = cotangent.astype(jnp.float32).reshape(flat_shape)
    gain_four = jnp.sum(upstream * down_hat, axis=(0, 1))
    grad_down_out = norm_back(down_proj, upstream * gain_rows[3]).astype(jnp.bfloat16)
    grad_out_rows = lax.all_gather(
        grad_down_out.reshape(fold_shape), "cp", axis=2, tiled=True
    ).reshape(group_total, width)
    down_local = jnp.einsum(
        "tf,td->fd", activation, grad_out_rows, preferred_element_type=jnp.float32
    )
    grad_act = jnp.einsum("td,fd->tf", grad_out_rows, down_rows, preferred_element_type=jnp.float32)
    _, gelu_pull = jax.vjp(gelu_tanh, up_proj)
    grad_up = gelu_pull(grad_act)[0].astype(jnp.bfloat16)
    up_local = jnp.einsum("tc,tf->cf", ffn_in, grad_up, preferred_element_type=jnp.float32)
    mid_terms = jnp.einsum("tf,cf->tc", grad_up, up_rows, preferred_element_type=jnp.float32)
    grad_mid = (
        lax.psum_scatter(
            mid_terms.reshape(group_shape).astype(jnp.bfloat16),
            "cp",
            scatter_dimension=2,
            tiled=True,
        )
        .astype(jnp.float32)
        .reshape(flat_shape)
    )
    gain_three = jnp.sum(grad_mid * hidden_hat, axis=(0, 1))
    grad_hidden = upstream + norm_back(hidden, grad_mid * gain_rows[2])
    gain_two = jnp.sum(grad_hidden * branch_hat, axis=(0, 1))
    grad_branch = norm_back(branch, grad_hidden * gain_rows[1]).astype(jnp.bfloat16)
    out_local = jnp.einsum(
        "tc,te->ce",
        mixed_heads.reshape(token_total, width),
        grad_branch.reshape(token_total, width),
        preferred_element_type=jnp.float32,
    )
    grad_heads = (
        jnp.einsum("rqe,ce->rqc", grad_branch, out_full, preferred_element_type=jnp.float32)
        .astype(jnp.bfloat16)
        .reshape(head_shape)
    )
    delta_sum = jnp.transpose(
        jnp.sum(grad_heads.astype(jnp.float32) * attended, axis=-1), (0, 2, 1)
    )

    def score_grads(block_index):
        scores, allowed = block_scores(block_index)
        probs = jnp.where(allowed, jnp.exp(scores - log_total[..., None]), 0.0)
        first_key = block_index * block_size
        key_block = lax.dynamic_slice_in_dim(key_rows, first_key, block_size, 1)
        value_block = lax.dynamic_slice_in_dim(value_rows, first_key, block_size, 1)
        grad_probs = jnp.einsum(
            "rqhd,rkhd->rhqk", grad_heads, value_block, preferred_element_type=jnp.float32
        )
        grad_scores = (probs * (grad_probs - delta_sum[..., None]) * score_scale).astype(
            jnp.bfloat16
        )
        return (probs, grad_scores, key_block)

    def grad_step(grad_query, block_index):
        probs, grad_scores, key_block = score_grads(block_index)
        grad_query = grad_query + jnp.einsum(
            "rhqk,rkhd->rqhd", grad_scores, key_block, preferred_element_type=jnp.float32
        )
        key_part = jnp.einsum(
            "rhqk,rqhd->rkhd", grad_scores, query_rows, preferred_element_type=jnp.float32
        )
        value_part = jnp.einsum(
            "rhqk,rqhd->rkhd",
            probs.astype(jnp.bfloat16),
            grad_heads,
            preferred_element_type=jnp.float32,
        )
        return (grad_query, (key_part, value_part))

    grad_query, (key_parts, value_parts) = lax.scan(
        grad_step, jnp.zeros(head_shape, jnp.float32), block_range
    )
    key_terms = jnp.moveaxis(key_parts, 0, 1).reshape(group_shape)
    value_terms = jnp.moveaxis(value_parts, 0, 1).reshape(group_shape)
    key_sum, value_sum = (
        lax.psum_scatter(
            key_terms.astype(jnp.bfloat16), "cp", scatter_dimension=2, tiled=True
        ).astype(jnp.float32),
        lax.psum_scatter(
            value_terms.astype(jnp.bfloat16), "cp", scatter_dimension=2, tiled=True
        ).astype(jnp.float32),
    )
    query_unturned = rotate(rounded(grad_query), cosine, -sine_part).reshape(flat_shape)
    key_unturned = rotate(rounded(key_sum.reshape(head_shape)), cosine, -sine_part).reshape(
        flat_shape
    )
    grad_linear = jnp.concatenate(
        [query_unturned, key_unturned, value_sum.reshape(flat_shape)], axis=-1
    ).astype(jnp.bfloat16)
    qkv_local = jnp.einsum(
        "tc,te->ce",
        normed.reshape(token_total, width),
        grad_linear.reshape(token_total, 3 * width),
        preferred_element_type=jnp.float32,
    )
    grad_normed = jnp.einsum(
        "rqe,ce->rqc", grad_linear, qkv_full, preferred_element_type=jnp.float32
    )
    gain_one = jnp.sum(grad_normed * normed_in, axis=(0, 1))
    tokens_grad = (grad_hidden + norm_back(inputs, grad_normed * gain_rows[0])).reshape(
        tokens.shape
    )
    gain_local = jnp.concatenate([gain_one, gain_two, gain_three, gain_four])
    gain_order = jnp.transpose(gain_local.reshape(rows_count, cp_count, -1), (1, 0, 2)).reshape(-1)
    qkv_mid, out_mid, gain_mid = (
        lax.psum_scatter(
            qkv_local.astype(jnp.bfloat16), "cp", scatter_dimension=1, tiled=True
        ).astype(jnp.float32),
        lax.psum_scatter(
            out_local.astype(jnp.bfloat16), "cp", scatter_dimension=1, tiled=True
        ).astype(jnp.float32),
        lax.psum_scatter(
            gain_order.astype(jnp.bfloat16), "cp", scatter_dimension=0, tiled=True
        ).astype(jnp.float32),
    )
    qkv_sum, out_sum, up_sum, down_sum, gain_sum = (
        lax.psum_scatter(
            qkv_mid.astype(jnp.bfloat16), "rows", scatter_dimension=0, tiled=True
        ).astype(jnp.float32),
        lax.psum_scatter(
            out_mid.astype(jnp.bfloat16), "rows", scatter_dimension=0, tiled=True
        ).astype(jnp.float32),
        lax.psum_scatter(
            up_local.astype(jnp.bfloat16), "rows", scatter_dimension=0, tiled=True
        ).astype(jnp.float32),
        lax.psum_scatter(
            down_local.astype(jnp.bfloat16), "rows", scatter_dimension=1, tiled=True
        ).astype(jnp.float32),
        lax.psum_scatter(
            gain_mid.astype(jnp.bfloat16), "rows", scatter_dimension=0, tiled=True
        ).astype(jnp.float32),
    )
    return (mixed, tokens_grad, qkv_sum, out_sum, up_sum, down_sum, gain_sum)


F32 = jnp.float32
BF16 = jnp.bfloat16
MIB = 1024 * 1024


def params(grid_rank, mebibytes=24):
    return pltpu.CompilerParams(
        dimension_semantics=("arbitrary",) * grid_rank, vmem_limit_bytes=mebibytes * MIB
    )


def lasting(microseconds):
    return pl.CostEstimate(
        flops=int(microseconds * 1e7), bytes_accessed=1024, transcendentals=0
    )


def turned(x, cosine, sine):
    lane = lax.broadcasted_iota(jnp.int32, x.shape, 1)
    other = jnp.where((lane & 32) == 0, pltpu.roll(x, 96, 1), pltpu.roll(x, 32, 1))
    return x * cosine + other * sine


def attend_kernel(tile, bounds, slot_of, q_ref, k_ref, v_ref, pcol_ref, prow_ref, srow_ref,
                  o_ref, ob_ref, lse_ref, vt_ref):
    i = pl.program_id(1)

    @pl.when(i == 0)
    def _():
        vt_ref[...] = v_ref[...].astype(F32).T.astype(BF16)

    qt = q_ref[...].astype(F32).T
    row = lax.broadcasted_iota(jnp.int32, qt.shape, 0)
    lo = bounds[0, i]
    mid = jnp.minimum(bounds[1, i], i)
    qpos = prow_ref[...]
    qstart = srow_ref[...]
    qh = [jnp.where((row >= 64) == (h == 1), qt, 0.0).astype(BF16) for h in range(2)]

    def step(j, carry, masked):
        at = pl.multiple_of(j * tile, tile)
        k = k_ref[pl.ds(at, tile), :]
        scores = [jnp.dot(k, qh[h], preferred_element_type=F32) for h in range(2)]
        if masked:
            kpos = pcol_ref[pl.ds(at, tile), :]
            allowed = (kpos >= qstart) & (kpos <= qpos)
            scores = [jnp.where(allowed, s, MASKED) for s in scores]
        out = []
        for h in range(2):
            top, total, acc = carry[h]
            new = jnp.maximum(top, jnp.max(scores[h], axis=0, keepdims=True))
            p = jnp.exp(scores[h] - new)
            keep = jnp.exp(top - new)
            total = total * keep + jnp.sum(p, axis=0, keepdims=True)
            acc = acc * keep + jnp.dot(
                vt_ref[h * 64 : h * 64 + 64, pl.ds(at, tile)], p.astype(BF16),
                preferred_element_type=F32,
            )
            out.append((new, total, acc))
        return tuple(out)

    start = (
        jnp.full((1, tile), MASKED, F32), jnp.zeros((1, tile), F32), jnp.zeros((64, tile), F32)
    )
    carry = step(i, (start, start), True)
    carry = lax.fori_loop(lo, mid, functools.partial(step, masked=True), carry)
    carry = lax.fori_loop(mid, i, functools.partial(step, masked=False), carry)
    parts = []
    for h in range(2):
        top, total, acc = carry[h]
        lse_ref[0, h : h + 1, :] = top + jnp.log(total)
        parts.append(acc / total)
    out = jnp.concatenate(parts, axis=0).T
    o_ref[...] = out
    span = ob_ref.shape[1]
    for b in range(tile // span):
        ob_ref[slot_of[i * (tile // span) + b]] = out[b * span : (b + 1) * span].astype(BF16)


def attend(pair, q, k, v, pcol, prow, srow, bounds, slot_of, tile):
    rows, width = q.shape
    blocks = slot_of.shape[0]
    span = rows // blocks
    count = rows // tile
    grid_spec = pltpu.PrefetchScalarGridSpec(
        num_scalar_prefetch=2,
        grid=(1, count),
        in_specs=[
            pl.BlockSpec((tile, 128), lambda p, i, b, t: (i, pair)),
            pl.BlockSpec((rows, 128), lambda p, i, b, t: (0, pair)),
            pl.BlockSpec((rows, 128), lambda p, i, b, t: (0, pair)),
            pl.BlockSpec((rows, 1), lambda p, i, b, t: (0, 0)),
            pl.BlockSpec((1, tile), lambda p, i, b, t: (0, i)),
            pl.BlockSpec((1, tile), lambda p, i, b, t: (0, i)),
        ],
        out_specs=[
            pl.BlockSpec((tile, 128), lambda p, i, b, t: (i, p)),
            pl.BlockSpec((blocks, span, 128), lambda p, i, b, t: (0, 0, p)),
            pl.BlockSpec((1, 2, tile), lambda p, i, b, t: (p, 0, i)),
        ],
        scratch_shapes=[pltpu.VMEM((128, rows), BF16)],
    )
    return pl.pallas_call(
        functools.partial(attend_kernel, tile),
        grid_spec=grid_spec,
        out_shape=[
            jax.ShapeDtypeStruct((rows, 128), F32),
            jax.ShapeDtypeStruct((blocks, span, 128), BF16),
            jax.ShapeDtypeStruct((1, 2, rows), F32),
        ],
        compiler_params=params(2),
        cost_estimate=lasting(14),
        name="attend",
    )(bounds, slot_of, q, k, v, pcol, prow, srow)


def attend_back_kernel(tile, first, steps, bounds, slot_of, q_ref, k_ref, v_ref, do_ref, o_ref,
                       lse_ref, pcol_ref, prow_ref, srow_ref, cos_ref, sin_ref, *refs):
    qm, dom, qtm, dotm, delta, dqt = refs[-6:]
    count = q_ref.shape[0] // tile
    last = first + steps
    before = refs[0] if first else None
    g_ref = refs[1 if first else 0]
    after_ref = refs[1] if last < count else None
    j = first + pl.program_id(1)
    span = do_ref.shape[1]

    @pl.when(pl.program_id(1) == 0)
    def _():
        for t in range(first, count):
            part = pl.ds(t * tile, tile)
            q = q_ref[part, :].astype(F32)
            do = jnp.concatenate(
                [do_ref[slot_of[t * tile // span + b]] for b in range(tile // span)], axis=0
            ).astype(F32)
            qt, dot = q.T, do.T
            lane = lax.broadcasted_iota(jnp.int32, q.shape, 1)
            row = lax.broadcasted_iota(jnp.int32, qt.shape, 0)
            prod = dot * o_ref[part, :].T
            for h in range(2):
                mine = (lane >= 64) == (h == 1)
                mine_t = (row >= 64) == (h == 1)
                qm[h, part, :] = jnp.where(mine, q, 0.0).astype(BF16)
                dom[h, part, :] = jnp.where(mine, do, 0.0).astype(BF16)
                qtm[h, :, part] = jnp.where(mine_t, qt, 0.0).astype(BF16)
                dotm[h, :, part] = jnp.where(mine_t, dot, 0.0).astype(BF16)
                delta[h : h + 1, part] = jnp.sum(
                    prod[h * 64 : h * 64 + 64], axis=0, keepdims=True
                )
        if before is None:
            dqt[...] = jnp.zeros_like(dqt)
        else:
            dqt[:, first * tile :] = before[0]

    here = pl.ds(pl.multiple_of(j * tile, tile), tile)
    k = k_ref[here, :]
    v = v_ref[here, :]
    kt = k.astype(F32).T.astype(BF16)
    kpos = pcol_ref[here, :]
    full = jnp.maximum(bounds[2, j], j + 1)
    end = bounds[3, j]

    def step(i, carry, masked):
        dk, dv = carry
        part = pl.ds(pl.multiple_of(i * tile, tile), tile)
        if masked:
            allowed = (kpos >= srow_ref[:, part]) & (kpos <= prow_ref[:, part])
        for h in range(2):
            s = jnp.dot(k, qtm[h, :, part], preferred_element_type=F32)
            p = jnp.exp(s - lse_ref[0, h : h + 1, part])
            if masked:
                p = jnp.where(allowed, p, 0.0)
            dp = jnp.dot(v, dotm[h, :, part], preferred_element_type=F32)
            ds = (p * (dp - delta[h : h + 1, part])).astype(BF16)
            dv = dv + jnp.dot(p.astype(BF16), dom[h, part, :], preferred_element_type=F32)
            dk = dk + jnp.dot(ds, qm[h, part, :], preferred_element_type=F32)
            dqt[h * 64 : h * 64 + 64, part] += jnp.dot(
                kt[h * 64 : h * 64 + 64, :], ds, preferred_element_type=F32
            )
        return dk, dv

    carry = (jnp.zeros((tile, 128), F32), jnp.zeros((tile, 128), F32))
    carry = step(j, carry, True)
    carry = lax.fori_loop(j + 1, full, functools.partial(step, masked=False), carry)
    carry = lax.fori_loop(full, end, functools.partial(step, masked=True), carry)
    dk, dv = carry

    def unturned(x, at):
        x = x.astype(BF16).astype(F32)
        return turned(x, cos_ref[at, :], -sin_ref[at, :]).astype(BF16)

    grad_k, grad_v = unturned(dk, here), dv.astype(BF16)
    for b in range(tile // span):
        at = slot_of[j * (tile // span) + b] >> 1
        g_ref[at, :, 128:256] = grad_k[b * span : (b + 1) * span]
        g_ref[at, :, 256:384] = grad_v[b * span : (b + 1) * span]

    @pl.when(pl.program_id(1) == steps - 1)
    def _():
        for t in range(first, last):
            part = pl.ds(t * tile, tile)
            grad_q = unturned(dqt[:, part].T * 0.125, part)
            for b in range(tile // span):
                at = slot_of[t * (tile // span) + b] >> 1
                g_ref[at, :, 0:128] = grad_q[b * span : (b + 1) * span]
        if after_ref is not None:
            after_ref[0] = dqt[:, last * tile :]


def attend_back(half, q, k, v, do, o, lse, pcol, prow, srow, cosine, sine, bounds, slot_of, tile,
                before):
    rows, width = q.shape
    pairs = width // 128
    blocks, span, _ = do.shape
    count = rows // tile
    steps = count // 2
    first = half * steps
    whole = pl.BlockSpec((rows, 128), lambda p, j, b, t: (0, p))
    table = pl.BlockSpec((rows, 128), lambda p, j, b, t: (0, 0))
    line = pl.BlockSpec((1, rows), lambda p, j, b, t: (0, 0))
    rest = pl.BlockSpec((1, 128, rows // 2), lambda p, j, b, t: (p, 0, 0))
    outs = [
        (
            jax.ShapeDtypeStruct((blocks // 2, span, 3 * width), BF16),
            pl.BlockSpec((blocks // 2, span, 384), lambda p, j, b, t: (0, 0, p)),
        )
    ]
    if not half:
        outs.append((jax.ShapeDtypeStruct((pairs, 128, rows // 2), F32), rest))
    grid_spec = pltpu.PrefetchScalarGridSpec(
        num_scalar_prefetch=2,
        grid=(pairs, steps),
        in_specs=[
            whole, whole, whole,
            pl.BlockSpec((blocks, span, 128), lambda p, j, b, t: (0, 0, p)),
            whole,
            pl.BlockSpec((1, 2, rows), lambda p, j, b, t: (p, 0, 0)),
            pl.BlockSpec((rows, 1), lambda p, j, b, t: (0, 0)),
            line, line, table, table,
        ]
        + [rest] * len(before),
        out_specs=[spec for _, spec in outs],
        scratch_shapes=[
            pltpu.VMEM((2, rows, 128), BF16), pltpu.VMEM((2, rows, 128), BF16),
            pltpu.VMEM((2, 128, rows), BF16), pltpu.VMEM((2, 128, rows), BF16),
            pltpu.VMEM((2, rows), F32), pltpu.VMEM((128, rows), F32),
        ],
    )
    return pl.pallas_call(
        functools.partial(attend_back_kernel, tile, first, steps),
        grid_spec=grid_spec,
        out_shape=[shape for shape, _ in outs],
        compiler_params=params(2, 40),
        cost_estimate=lasting(23),
        name="attend_back",
    )(bounds, slot_of, q, k, v, do, o, lse, pcol, prow, srow, cosine, sine, *before)


def tile_bounds(starts_nat, tile):
    rows = starts_nat.shape[0]
    count = rows // tile
    tiles = starts_nat.reshape(count, tile)
    first, last = tiles[:, 0], tiles[:, -1]
    at = jnp.arange(count, dtype=jnp.int32) * tile
    lo = first // tile
    mid = (last + tile - 1) // tile
    full = jnp.sum((last[None, :] <= at[:, None]).astype(jnp.int32), axis=1)
    end = jnp.sum((first[None, :] <= at[:, None] + tile - 1).astype(jnp.int32), axis=1)
    return jnp.stack([lo, mid, full, end]).astype(jnp.int32)


def normalized(x):
    centred = x - jnp.mean(x, axis=1, keepdims=True)
    scale = lax.rsqrt(jnp.mean(centred * centred, axis=1, keepdims=True) + NORM_EPS)
    return centred * scale, scale


def normalized_back(hat, scale, upstream):
    level = jnp.mean(upstream, axis=1, keepdims=True)
    slant = jnp.mean(upstream * hat, axis=1, keepdims=True)
    return scale * (upstream - level - hat * slant)


def dot_nt(a, b):
    return lax.dot_general(a, b, (((1,), (1,)), ((), ())), preferred_element_type=F32)


def call(kernel, name, grid, tables, ins, outs, microseconds, *arrays):
    return pl.pallas_call(
        kernel,
        grid_spec=pltpu.PrefetchScalarGridSpec(
            num_scalar_prefetch=len(tables),
            grid=grid,
            in_specs=ins,
            out_specs=[spec for _, spec in outs],
        ),
        out_shape=[shape for shape, _ in outs],
        compiler_params=params(len(grid)),
        cost_estimate=lasting(microseconds),
        name=name,
    )(*tables, *arrays)


def shaped(dtype, *shape):
    return jax.ShapeDtypeStruct(shape, dtype)


def fixed(*shape):
    return pl.BlockSpec(shape, lambda *_: (0,) * len(shape))


def project_kernel(blocks, slots, near, far, gain_ref, w_ref, cos_ref, sin_ref, *refs):
    q_ref, k_ref, v_ref, n_ref = refs[-4:]
    width = q_ref.shape[1]
    x = jnp.where(slots[pl.program_id(0)] < 4, near[0], far[0]).astype(F32)
    normed = (normalized(x)[0] * gain_ref[0:1, :]).astype(BF16)
    n_ref[0] = normed
    linear = jnp.dot(normed, w_ref[...], preferred_element_type=F32)
    for at in range(0, width, 128):
        q = turned(linear[:, 3 * at : 3 * at + 128], cos_ref[...], sin_ref[...])
        k = turned(linear[:, 3 * at + 128 : 3 * at + 256], cos_ref[...], sin_ref[...])
        q_ref[:, at : at + 128] = q.astype(BF16) * jnp.asarray(0.125, BF16)
        k_ref[:, at : at + 128] = k.astype(BF16)
        v_ref[:, at : at + 128] = linear[:, 3 * at + 256 : 3 * at + 384].astype(BF16)


def project(near, far, gains, w, cosine, sine, blocks, slots, before):
    _, rows, depth = near.shape
    width = w.shape[1] // 3
    count = 2 * blocks.shape[0]
    piece = pl.BlockSpec((1, rows, depth), lambda i, b, s: (s[i] & 1, 0, 0))
    angle = pl.BlockSpec((rows, 128), lambda i, b, s: (b[i], 0))
    out = shaped(BF16, count * rows, width)
    normed = shaped(BF16, count, rows, depth)
    block = pl.BlockSpec((rows, width), lambda i, b, s: (b[i], 0))
    return pl.pallas_call(
        project_kernel,
        grid_spec=pltpu.PrefetchScalarGridSpec(
            num_scalar_prefetch=2,
            grid=blocks.shape,
            in_specs=[piece, piece, fixed(*gains.shape), fixed(*w.shape), angle, angle]
            + [pl.BlockSpec(memory_space=pl.ANY)] * len(before),
            out_specs=[
                block, block, block,
                pl.BlockSpec((1, rows, depth), lambda i, b, s: ((s[i] & 1) * 4 + (s[i] >> 1), 0, 0)),
            ],
        ),
        out_shape=[out, out, out, normed],
        input_output_aliases={8 + n: n for n in range(len(before))},
        compiler_params=params(1),
        cost_estimate=lasting(7),
        name="project",
    )(blocks, slots, near, far, gains, w, cosine, sine, *before)


def mix_kernel(group, own, near, far, both, w_ref, x_ref, gain_ref,
               heads_ref, hat_ref, scale_ref, hidden_ref, mid_ref):
    width = own.shape[2]
    for r, piece in enumerate((own[0], far[0], near[0], both[0])):
        at = pl.ds(pl.multiple_of((group[0] ^ r) * width, width), width)
        heads_ref[:, at] = piece
    branch = jnp.dot(heads_ref[...], w_ref[...], preferred_element_type=F32)
    hat, scale = normalized(branch)
    hidden = x_ref[0].astype(F32) + hat * gain_ref[1:2, :]
    hat_ref[...] = hat
    scale_ref[...] = scale
    hidden_ref[...] = hidden
    mid_ref[...] = (normalized(hidden)[0] * gain_ref[2:3, :]).astype(BF16)


def mix(group, local, near, far, both, w, x, gains):
    _, rows, part = local.shape
    count, _, width = x.shape
    block = pl.BlockSpec((1, rows, part), lambda i, g: (i, 0, 0))
    row = pl.BlockSpec((rows, width), lambda i, g: (i, 0))
    total = count * rows
    return call(
        mix_kernel, "mix", (count,), [group],
        [
            block, block, block, block, fixed(*w.shape), pl.BlockSpec((1, rows, width), lambda i, g: (i, 0, 0)),
            fixed(*gains.shape),
        ],
        [
            (shaped(BF16, total, width), row),
            (shaped(F32, total, width), row),
            (shaped(F32, total, 1), pl.BlockSpec((rows, 1), lambda i, g: (i, 0))),
            (shaped(F32, total, width), row),
            (shaped(BF16, total, width), row),
        ],
        6, local, near, far, both, w, x, gains,
    )


def finish_kernel(terms_ref, sent_ref, hidden_ref, dy_ref, gain_ref, mixed_ref, grad_ref, sum_ref):
    down = terms_ref[...] + sent_ref[...].astype(F32)
    hat, scale = normalized(down)
    gain = gain_ref[3:4, :]
    dy = dy_ref[...].astype(F32)
    mixed_ref[...] = (hidden_ref[...] + hat * gain).astype(BF16)
    grad_ref[...] = normalized_back(hat, scale, dy * gain).astype(BF16)

    @pl.when(pl.program_id(0) == 0)
    def _():
        sum_ref[...] = jnp.zeros_like(sum_ref)

    sum_ref[...] += jnp.sum(dy * hat, axis=0, keepdims=True)


def finish(terms, sent, hidden, dy, gains):
    total, width = terms.shape
    rows = total // 2
    row = pl.BlockSpec((rows, width), lambda i: (i, 0))
    return call(
        finish_kernel, "finish", (2,), [],
        [row, row, row, row, fixed(*gains.shape)],
        [
            (shaped(BF16, total, width), row), (shaped(BF16, total, width), row),
            (shaped(F32, 1, width), fixed(1, width)),
        ],
        5, terms, sent, hidden, dy, gains,
    )


def turn_kernel(group, terms_ref, sent_ref, hidden_ref, dy_ref, hat_ref, scale_ref, w_ref, gain_ref,
                keep_ref, branch_ref, heads_ref, three_ref, two_ref):
    upstream = terms_ref[...] + sent_ref[...].astype(F32)
    hat, scale = normalized(hidden_ref[...])

    @pl.when(pl.program_id(0) == 0)
    def _():
        three_ref[...] = jnp.zeros_like(three_ref)
        two_ref[...] = jnp.zeros_like(two_ref)

    three_ref[...] += jnp.sum(upstream * hat, axis=0, keepdims=True)
    grad = dy_ref[...].astype(F32) + normalized_back(hat, scale, upstream * gain_ref[2:3, :])
    keep_ref[...] = grad
    branch_hat = hat_ref[...]
    two_ref[...] += jnp.sum(grad * branch_hat, axis=0, keepdims=True)
    branch = normalized_back(branch_hat, scale_ref[...], grad * gain_ref[1:2, :]).astype(BF16)
    branch_ref[...] = branch
    part = heads_ref.shape[3]
    for r in range(4):
        at = pl.ds(pl.multiple_of((group[0] ^ r) * part, part), part)
        heads_ref[r, 0] = dot_nt(branch, w_ref[at, :]).astype(BF16)


def turn(group, terms, sent, hidden, dy, hat, scale, w, gains):
    total, width = terms.shape
    rows = total // 2
    part = width // 4
    row = pl.BlockSpec((rows, width), lambda i, g: (i, 0))
    return call(
        turn_kernel, "turn", (2,), [group],
        [
            row, row, row, row, row, pl.BlockSpec((rows, 1), lambda i, g: (i, 0)),
            fixed(*w.shape), fixed(*gains.shape),
        ],
        [
            (shaped(F32, total, width), row), (shaped(BF16, total, width), row),
            (
                shaped(BF16, 4, 2, rows, part),
                pl.BlockSpec((4, 1, rows, part), lambda i, g: (0, i, 0, 0)),
            ),
            (shaped(F32, 1, width), fixed(1, width)), (shaped(F32, 1, width), fixed(1, width)),
        ],
        8, terms, sent, hidden, dy, hat, scale, w, gains,
    )


def end_kernel(keep_ref, far_ref, x_ref, grad_ref, gain_ref, o_ref):
    upstream = keep_ref[...] + far_ref[...].astype(F32)
    hat, scale = normalized(x_ref[...].astype(F32))
    grad = grad_ref[...] + normalized_back(hat, scale, upstream * gain_ref[0:1, :])
    o_ref[...] = grad.astype(BF16)


def end(keep, far, x, grad, gains):
    total, width = x.shape
    rows = total // 2
    row = pl.BlockSpec((rows, width), lambda i: (i, 0))
    return call(
        end_kernel, "end", (2,), [], [row] * 4 + [fixed(*gains.shape)],
        [(shaped(BF16, total, width), row)], 20, keep, far, x, grad, gains,
    )[0]


def plain(x):
    return with_layout_constraint(x, Layout(tuple(range(x.ndim))))


def cut_lines_kernel(place, *refs):
    for n, out in enumerate(refs[8:]):
        up, down = refs[2 * n], refs[2 * n + 1]
        lines = up.shape[0]
        out[0, :lines] = up[...]
        out[0, lines:] = down[: out.shape[1] - lines]


def cut_lines(place, up, down, spare):
    width = up.shape[1]
    lines = up.shape[0] // 8
    at = (
        lambda i, p: (2 * (2 * i + p[0]), 0),
        lambda i, p: (2 * (2 * i + 1 - p[0]), 0),
        lambda i, p: (2 * (2 * p[1] + i) + 1, 0),
        lambda i, p: (2 * (2 * (1 - p[1]) + i) + 1, 0),
    )
    rows = 2 * lines - spare
    out = shaped(BF16, 2, rows, width), pl.BlockSpec((1, rows, width), lambda i, p: (i, 0, 0))
    return call(
        cut_lines_kernel, "cut_lines", (2,), [place],
        [pl.BlockSpec((lines, width), index) for index in at for _ in range(2)],
        [out] * 4, 4, *([up, down] * 4),
    )


QKV_BLOCKS, OVER_BLOCKS, OUT_BLOCKS = 12, 2, 8
LOW_BLOCKS = 11
ALL_BLOCKS = QKV_BLOCKS + OVER_BLOCKS + OUT_BLOCKS + 1
LEFT = ((0, 0), (0, 1), (1, 0))
RIGHT = ((1, 1), (2, 0), (2, 1))


def tiles(array):
    return [array[:, at : at + 128] for at in range(0, array.shape[1], 128)]


def plus(a, b):
    return (a.astype(F32) + b.astype(F32)).astype(BF16)


def spread_first_kernel(place, qkv_ref, out_ref, gain_ref, over_ref, far_ref, out_far,
                        low, low_away, high, high_away):
    lines = far_ref.shape[1]
    spare = over_ref.shape[0] // 8
    wide = qkv_ref.shape[1]
    x_bit, y_bit, core = place[0], place[1], place[2]

    def fill(line, low_out, high_out):
        at = pl.ds(pl.multiple_of((2 * line + core) * lines, lines), lines)
        near = tiles(qkv_ref[at, :])
        far = tiles(far_ref[line, :, :wide])
        blocks = [jnp.where(core == 0, a, b) for a, b in zip(near, far)]
        blocks += [jnp.where(core == 0, a, b) for a, b in zip(far, near)]
        for c in range(2):
            rows = pl.ds(pl.multiple_of((2 * line + c) * spare, spare), spare)
            blocks.append(jnp.concatenate(tiles(over_ref[rows, :]), axis=0))
        blocks += [
            plus(a, b)
            for a, b in zip(tiles(out_ref[at, :]), tiles(out_far[line]))
        ]
        count = gain_ref.shape[1]
        gain = jnp.concatenate(
            [gain_ref[2 * line + core], jnp.zeros((lines - count, 128), BF16)], axis=0
        )
        blocks.append(plus(gain, far_ref[line, :, -128:]))
        for n, block in enumerate(blocks):
            if n < LOW_BLOCKS and low_out is not None:
                low_out[n] = block
            if n >= LOW_BLOCKS and high_out is not None:
                high_out[n - LOW_BLOCKS] = block

    for n in range(2):
        fill(2 * n + x_bit, low.at[n], None)
        fill(2 * n + 1 - x_bit, low_away.at[n], None)
        fill(2 * y_bit + n, None, high.at[n])
        fill(2 * (1 - y_bit) + n, None, high_away.at[n])


def spread_first(place, qkv, out, gain, over, far, out_far):
    lines = far.shape[1]
    low = shaped(BF16, 2, LOW_BLOCKS, lines, 128), fixed(2, LOW_BLOCKS, lines, 128)
    rest = ALL_BLOCKS - LOW_BLOCKS
    high = shaped(BF16, 2, rest, lines, 128), fixed(2, rest, lines, 128)
    arrays = (qkv, out, gain, over, far, out_far)
    return call(
        spread_first_kernel, "spread_first", (1,), [place], [fixed(*a.shape) for a in arrays],
        [low, low, high, high], 2, *arrays,
    )


def spread_second_kernel(place, low, low_far, high, high_far, low_o, low_away, high_o, high_away):
    for source, far, bit, near_o, away_o in (
        (low, low_far, place[1], low_o, low_away), (high, high_far, place[0], high_o, high_away)
    ):
        near_o[...] = plus(source[bit], far[bit])
        away_o[...] = plus(source[1 - bit], far[1 - bit])


def spread_second(place, *arrays):
    lows, highs = arrays[0].shape[1:], arrays[2].shape[1:]
    outs = [(shaped(BF16, *s), fixed(*s)) for s in (lows, lows, highs, highs)]
    return call(
        spread_second_kernel, "spread_second", (1,), [place], [fixed(*a.shape) for a in arrays],
        outs, 2, *arrays,
    )


def spread_third_kernel(place, low, low_far, high, high_far, near_o, away_o, over_o):
    half = place[4]

    def block(n):
        if n < LOW_BLOCKS:
            return plus(low[n], low_far[n])
        return plus(high[n - LOW_BLOCKS], high_far[n - LOW_BLOCKS])

    at = 0
    for (left_t, left_c), (right_t, right_c) in zip(LEFT, RIGHT):
        for pair in range(2):
            left = block(left_c * 6 + pair * 3 + left_t)
            right = block(right_c * 6 + pair * 3 + right_t)
            near_o[at] = jnp.where(half == 0, left, right)
            away_o[at] = jnp.where(half == 0, right, left)
            at += 1
    for c in range(2):
        over_o[c] = block(QKV_BLOCKS + c)
    first = QKV_BLOCKS + OVER_BLOCKS
    for n in range(4):
        left, right = block(first + n), block(first + 4 + n)
        near_o[at] = jnp.where(half == 0, left, right)
        away_o[at] = jnp.where(half == 0, right, left)
        at += 1
    near_o[at] = block(first + 8)
    away_o[at] = block(first + 8)


def spread_third(place, *arrays):
    lines = arrays[0].shape[1]
    part = shaped(BF16, 11, lines, 128), fixed(11, lines, 128)
    over = shaped(BF16, 2, lines, 128), fixed(2, lines, 128)
    return call(
        spread_third_kernel, "spread_third", (1,), [place], [fixed(*a.shape) for a in arrays],
        [part, part, over], 2, *arrays,
    )


def spread_fourth_kernel(place, near, far, near_o, away_o):
    odd = place[3] == 1
    blocks = [plus(near[n], far[n]) for n in range(11)]
    for pair in range(2):
        one, two, three = blocks[pair], blocks[2 + pair], blocks[4 + pair]
        near_o[pair] = jnp.where(odd, two, one)
        near_o[2 + pair] = jnp.where(odd, three, two)
        away_o[pair] = jnp.where(odd, one, three)
        near_o[4 + pair] = jnp.where(odd, blocks[8 + pair], blocks[6 + pair])
        away_o[2 + pair] = jnp.where(odd, blocks[6 + pair], blocks[8 + pair])
    near_o[6] = blocks[10]
    away_o[4] = blocks[10]


def spread_fourth(place, near, far):
    lines = near.shape[1]
    return call(
        spread_fourth_kernel, "spread_fourth", (1,), [place], [fixed(*near.shape)] * 2,
        [
            (shaped(BF16, 7, lines, 128), fixed(7, lines, 128)),
            (shaped(BF16, 5, lines, 128), fixed(5, lines, 128)),
        ],
        2, near, far,
    )


def spread_fifth_kernel(place, near, far, qkv_o, out_o, gain_o, gain_all):
    for pair in range(2):
        first, second = near[pair].astype(F32), near[2 + pair].astype(F32)
        other = far[pair].astype(F32)
        at = 128 * pair
        qkv_o[:, at : at + 128] = first
        qkv_o[:, 256 + at : 384 + at] = other
        qkv_o[:, 512 + at : 640 + at] = second
        out_o[:, at : at + 128] = near[4 + pair].astype(F32) + far[2 + pair].astype(F32)
    gain_all[...] = near[6].astype(F32) + far[4].astype(F32)
    gain_o[...] = gain_all[pl.ds(2 * place[4] + place[3], 1), :]


def spread_fifth(place, near, far):
    lines = near.shape[1]
    outs = [(shaped(F32, *s), fixed(*s)) for s in ((lines, 768), (lines, 256), (1, 128))]
    return pl.pallas_call(
        spread_fifth_kernel,
        grid_spec=pltpu.PrefetchScalarGridSpec(
            num_scalar_prefetch=1,
            grid=(1,),
            in_specs=[fixed(*near.shape), fixed(*far.shape)],
            out_specs=[spec for _, spec in outs],
            scratch_shapes=[pltpu.VMEM((lines, 128), F32)],
        ),
        out_shape=[shape for shape, _ in outs],
        compiler_params=params(1),
        cost_estimate=lasting(2),
        name="spread_fifth",
    )(place, near, far)


def flip(x, axis, bit):
    return lax.ppermute(plain(x), axis, [(i, i ^ bit) for i in range(lax.axis_size(axis))])


def swap(x):
    cp = lax.axis_size("cp")
    half = cp // 2
    pairs = []
    for z in range(half):
        low, high = cp + z, z + half
        pairs += [(low, high), (high, low)]
    return lax.ppermute(plain(x), ("core", "cp"), pairs)


def settled(x, moved):
    stays = (lax.axis_index("core") == 1) == (lax.axis_index("cp") >= lax.axis_size("cp") // 2)
    return jnp.where(stays, x, moved)


def ordered(first, mine, other, axis):
    return jnp.concatenate(
        [jnp.where(first, mine, other), jnp.where(first, other, mine)], axis=axis
    )


def placed(first, mine, other, at):
    return ordered(first, jnp.expand_dims(mine, at), jnp.expand_dims(other, at), at)


def after(x, *others):
    return lax.optimization_barrier((x, *others))[0]


def all_after(group, *others):
    return lax.optimization_barrier((*group, *others))[: len(group)]


def total(a, b):
    return (a.astype(F32) + b.astype(F32)).astype(BF16)


def flip_both(x):
    cp = lax.axis_size("cp")
    return lax.ppermute(
        x, ("core", "cp"), [(c * cp + z, (1 - c) * cp + (z ^ 1)) for c in range(2) for z in range(cp)]
    )


def dot(a, b, dims):
    return lax.dot_general(a, b, ((dims[:1], dims[1:]), ((), ())), preferred_element_type=F32)


def gelu_and_slope(u):
    c = math.sqrt(2.0 / math.pi)
    square = u * u
    t = jnp.tanh(u * (c + (c * 0.044715) * square))
    half = 0.5 + 0.5 * t
    slope = half + (0.5 * u) * (1.0 - t * t) * (c + (3.0 * 0.044715 * c) * square)
    return lax.optimization_barrier(((u * half).astype(BF16), slope.astype(BF16)))


def pick(x, at, axis):
    return lax.dynamic_index_in_dim(x, at, axis, False)


def widened(z, x, other):
    first, second = jnp.where(z & 1 == 0, x, other), jnp.where(z & 1 == 0, other, x)
    half = x.shape[1] // 2
    return jnp.concatenate(
        [first[:, :half], second[:, :half], first[:, half:], second[:, half:]], axis=1
    )


def body(tokens, doc_starts, qkv_weight, out_weight, up_weight, down_weight, norm_gains, cotangent):
    xy, core, z = lax.axis_index("xy"), lax.axis_index("core"), lax.axis_index("cp")
    xy_count, cp_count = lax.axis_size("xy"), lax.axis_size("cp")
    _, _, span, width = tokens.shape
    blocks = 2 * cp_count
    row_len = blocks * span
    own = 2 * span
    parity = z & 1
    group = parity + 2 * core
    part = width // cp_count
    hidden_part = up_weight.shape[1] // 2
    lines_each = width // xy_count
    lines = lines_each // 2
    here = jnp.reshape(xy, (1,)).astype(jnp.int32)
    group_at = jnp.reshape(group, (1,)).astype(jnp.int32)

    gain_rows = jnp.zeros((16, qkv_weight.shape[1]), BF16)
    gain_rows = lax.dynamic_update_slice(gain_rows, norm_gains[None], (0, 0))
    w = jnp.concatenate([qkv_weight, gain_rows])
    w_far = flip(w, "cp", 2)

    x = settled(tokens[0], swap(after(tokens, w_far)[0]))
    w, w_far = jnp.where(z & 2 == 0, w, w_far), jnp.where(z & 2 == 0, w_far, w)
    near = [w[:, n * part : (n + 1) * part] for n in range(3)]
    near += [w_far[:, n * part : (n + 1) * part] for n in range(3)]
    even = parity == 0
    sent = jnp.concatenate([near[1], near[4]], axis=1)
    gain_near = jnp.stack([w[lines, :128], w_far[lines, :128]])
    sent = lax.dynamic_update_slice(sent, gain_near, (lines, 0))
    far = flip(sent, "cp", 1)
    up_weight, down_weight, out_weight = all_after((up_weight, down_weight, out_weight), far)
    out_far = flip(out_weight, "cp", 2)


    def half_of(which):
        up = lax.dynamic_slice_in_dim(up_weight, which * hidden_part, hidden_part, 1)
        down = lax.dynamic_slice_in_dim(down_weight, which * hidden_part, hidden_part, 0)
        return plain(jnp.stack([up, down.T]))

    ffn = ordered(core == 0, half_of(core), flip(half_of(1 - core), "core", 1), 1)

    def paired(mine, other):
        return jnp.concatenate(
            [jnp.where(z & 2 == 0, mine, other), jnp.where(z & 2 == 0, other, mine)], axis=1
        )

    gain_far = far[lines : lines + 2, :128]
    gain_near, gain_far = (
        jnp.where(even, gain_near, gain_far), jnp.where(even, gain_far, gain_near)
    )
    gain_rows = jnp.stack([gain_near[0], gain_far[0], gain_near[1], gain_far[1]])
    far = [far[:lines, n * part : (n + 1) * part] for n in range(2)]
    near = [block[:lines] for block in near]

    def by_pairs(*choices):
        picked = [jnp.where(even, a, b) for a, b in choices]
        return jnp.concatenate(
            [block[:, at : at + 128] for at in range(0, part, 128) for block in picked], axis=1
        )

    first_group = by_pairs((near[0], far[0]), (far[0], near[2]), (near[5], near[3]))
    second_group = by_pairs((near[2], near[0]), (near[3], far[1]), (far[1], near[5]))
    gain_block = jnp.zeros((16, 3 * part), BF16)
    gain_block = lax.dynamic_update_slice(gain_block, gain_rows, (0, 0))
    mine = jnp.concatenate([jnp.where(core == 0, first_group, second_group), gain_block])
    other = jnp.concatenate([jnp.where(core == 0, second_group, first_group), gain_block])

    other_starts = flip(after(doc_starts, w_far), "core", 1)
    starts = jnp.where(core == z // (cp_count // 2), doc_starts, other_starts)[0]

    block_id = jnp.arange(blocks, dtype=jnp.int32)[:, None]
    inside = jnp.arange(span, dtype=jnp.int32)[None, :]
    late = block_id >= cp_count
    positions = (block_id * span + jnp.where(late, span - 1 - inside, inside)).reshape(-1)

    def starts_at(at):
        return jnp.max(jnp.where(starts[None, :] <= at[:, None], starts[None, :], 0), axis=1)

    row_start = starts_at(positions)
    tile = min(512, row_len)
    bounds = tile_bounds(starts_at(jnp.arange(row_len, dtype=jnp.int32)), tile)
    freq = jnp.exp(
        -math.log(10000.0) * 2.0 * jnp.arange(HEAD_DIM // 2, dtype=F32) / HEAD_DIM
    )
    angles = (positions - row_start).astype(F32)[:, None] * freq
    cosine, sine = jnp.cos(angles), jnp.sin(angles)
    cosine = plain(jnp.tile(cosine, (1, 4)))
    sine = plain(jnp.tile(jnp.concatenate([-sine, sine], axis=1), (1, 2)))
    pcol, prow, srow = positions[:, None], positions[None, :], row_start[None, :]
    chunk = jnp.arange(blocks, dtype=jnp.int32)
    chunk = jnp.where(chunk < cp_count, chunk, blocks - 1 - chunk)
    slot_of = (
        2 * (2 * ((chunk >> 1) ^ core) + ((chunk & 1) ^ parity))
        + (jnp.arange(blocks) >= cp_count)
    ).astype(jnp.int32)
    slot = jnp.arange(blocks, dtype=jnp.int32)
    relative = slot >> 1
    chunk_of = 2 * ((relative >> 1) ^ core) + ((relative & 1) ^ parity)
    block_of = jnp.where(slot & 1 == 0, chunk_of, blocks - 1 - chunk_of).astype(jnp.int32)

    x = after(x, sent, cosine, sine)
    x_chip = flip(x, "cp", 1)
    x_core = flip(x, "core", 1)
    up_lines, out_w, out_far = all_after((ffn[0], out_weight, out_far), x)
    up_far = flip(up_lines, "cp", 2)
    out_w = paired(out_w, out_far)
    out_far = flip(out_w, "cp", 1)

    qkv = placed(core == 0, mine, flip(other, "core", 1), 0)
    cut = qkv.shape[2] // 2
    low, high = qkv[:, :, :cut], qkv[:, :, cut:]
    low = placed(xy & 1 == 0, low, flip(low, "xy", 1), 0)
    high = placed(xy & 2 == 0, high, flip(high, "xy", 2), 0)
    low = placed(xy & 2 == 0, low, flip(low, "xy", 2), 0)
    high = placed(xy & 1 == 0, high, flip(high, "xy", 1), 1)
    qkv = jnp.concatenate([low[:, :, :, :lines], high[:, :, :, :lines]], axis=4)
    qkv = qkv.reshape(width, 3 * part)
    gains = low[:, :, :, lines : lines + cp_count, :128]
    gains = gains.reshape(4, width).astype(F32)

    sooner, later = jnp.array([0, 1, 4, 5], jnp.int32), jnp.array([2, 3, 6, 7], jnp.int32)
    early = project(x, x_core, gains, qkv, cosine, sine, block_of[sooner], sooner, [])
    x_chip, up_far, *early = lax.optimization_barrier((x_chip, up_far, *early))
    x_both = flip(x_chip, "core", 1)
    up_lines, up_far, down_lines, out_w, out_far = all_after(
        (up_lines, up_far, ffn[1], out_w, out_far), x_chip, qkv
    )
    up_lines, out_w = paired(up_lines, up_far), widened(z, out_w, out_far)[None]
    up_far = flip(up_lines, "cp", 1)
    down_far = flip(down_lines, "cp", 2)
    out_far = flip(out_w, "xy", 1)

    def halves(x):
        return x[None, :lines], x[None, lines:]

    def send_lines(low, high):
        return flip(low, "xy", 1), flip(high, "xy", 2)

    def join_lines(low, high, low_far, high_far):
        low = ordered(xy & 1 == 0, low, low_far, 0)
        high = jnp.expand_dims(ordered(xy & 2 == 0, high, high_far, 0), 1)
        return low, high

    def send_more(low, high):
        return flip(low, "xy", 2), flip(high, "xy", 1)

    def join_all(low, high, low_far, high_far):
        low = ordered(xy & 2 == 0, low, low_far, 0)
        high = ordered(xy & 1 == 0, high, high_far, 1).reshape(low.shape)
        return jnp.stack([low, high], axis=1).reshape(width, -1)

    q, k, v, normed = project(
        x_chip, x_both, gains, qkv, cosine, sine, block_of[later], later, early
    )
    up_lines, up_far, down_lines, down_far, out_w, out_far = all_after(
        (up_lines, up_far, down_lines, down_far, out_w, out_far), q
    )
    up_lines = widened(z, up_lines, up_far)
    up_full = lax.all_gather(up_lines, "xy", axis=0, tiled=True)
    out_w = ordered(xy & 1 == 0, out_w, out_far, 0)
    out_far = flip(out_w, "xy", 2)
    down_lines = paired(down_lines, down_far)
    down_far = flip(down_lines, "cp", 1)
    q = after(q, up_lines, out_w, down_lines)
    first = attend(0, q, k, v, pcol, prow, srow, bounds, slot_of, tile)
    down_lines, down_far, out_w, out_far = all_after(
        (down_lines, down_far, out_w, out_far), first[0]
    )
    out_w = ordered(xy & 2 == 0, out_w, out_far, 0)
    down_pair = halves(widened(z, down_lines, down_far))
    down_far = send_lines(*down_pair)
    q = after(q, first[0], *down_pair, out_w)
    second = attend(1, q, k, v, pcol, prow, srow, bounds, slot_of, tile)
    attended, local, lse = zip(first, second)
    local = jnp.concatenate(local, axis=2)
    out_w, down_pair, down_far = (
        after(out_w, local), all_after(down_pair, local), all_after(down_far, local)
    )
    out_w = placed(core == 0, out_w, flip(out_w, "core", 1), 1).reshape(width, width)
    down_pair = join_lines(*down_pair, *down_far)
    down_far = send_more(*down_pair)
    heads, branch_hat, branch_scale, hidden, mid = mix(
        group_at, after(local, *down_pair)[:2], flip(local[4:6], "core", 1), flip(local[2:4], "cp", 1),
        flip_both(local[6:]), out_w, x, gains,
    )

    cotangent = cotangent.reshape(own, width)
    dy_moved = swap(after(cotangent, mid))

    ffn_in = jnp.concatenate([mid, flip(mid, "core", 1)])
    act, slope = gelu_and_slope(dot(ffn_in, up_full, (1, 0)))
    down_full = join_all(*down_pair, *all_after(down_far, act))
    sent = flip(dot(act[own:], down_full, (1, 1)).astype(BF16), "core", 1)
    terms = dot(act[:own], down_full, (1, 1))
    dy = settled(cotangent, dy_moved)
    mixed, grad_down, gain_four = finish(terms, sent, hidden, dy, gains)
    grad_down = jnp.concatenate([grad_down, flip(grad_down, "core", 1)])

    x_bit, y_bit = xy & 1, xy >> 1

    def send_first(away):
        return flip(away[0], "xy", 1), flip(away[1], "xy", 2)

    def cut_second(near, far):
        away = (
            total(pick(near[0], 1 - y_bit, 0), pick(far[0], 1 - y_bit, 0)),
            total(pick(near[1], 1 - x_bit, 0), pick(far[1], 1 - x_bit, 0)),
        )
        near = (
            total(pick(near[0], y_bit, 0), pick(far[0], y_bit, 0)),
            total(pick(near[1], x_bit, 0), pick(far[1], x_bit, 0)),
        )
        return near, away

    def send_second(away):
        return flip(away[0], "xy", 2), flip(away[1], "xy", 1)

    def cut_third(near, far):
        return split_columns(
            jnp.concatenate([total(a, b) for a, b in zip(near, far)]), hidden_part
        )

    def split_columns(sums, each):
        blocks_of = [sums[:, n * each : (n + 1) * each] for n in range(cp_count)]
        odd = jnp.stack([blocks_of[1], blocks_of[3]])
        even = jnp.stack([blocks_of[0], blocks_of[2]])
        return jnp.where(parity == 0, even, odd), jnp.where(parity == 0, odd, even)

    def cut_fourth(near, far):
        return (
            total(pick(near, z >> 1, 0), pick(far, z >> 1, 0)),
            total(pick(near, 1 - (z >> 1), 0), pick(far, 1 - (z >> 1), 0)),
        )

    down_local = plain(dot(grad_down, act, (0, 0)).astype(BF16))
    grad_up = dot(after(grad_down, down_local), down_full, (1, 0)) * slope.astype(F32)
    grad_up = grad_up.astype(BF16)
    sent = flip(dot(grad_up[own:], up_full, (1, 1)).astype(BF16), "core", 1)
    up_local = plain(dot(ffn_in, grad_up, (0, 0)).astype(BF16))
    spare = lines // 4
    place = jnp.stack([x_bit, y_bit]).astype(jnp.int32)
    low, low_away, high, high_away = cut_lines(place, up_local, down_local, spare)
    grad_near, grad_away = (low, high), (low_away, high_away)
    over_local = down_local.reshape(2 * xy_count, lines, -1)[:, lines - spare :]
    over_local = over_local.reshape(2 * xy_count * spare, -1)
    grad_far = send_first(grad_away)
    terms = dot(after(grad_up, *grad_away)[:own], up_full, (1, 1))
    grad_hidden, grad_branch, grad_heads, gain_three, gain_two = turn(
        group_at, terms, sent, hidden, dy, branch_hat, branch_scale, out_w, gains
    )

    grad_local = [
        grad_heads[0], flip(grad_heads[1], "cp", 1), flip(grad_heads[2], "core", 1),
        flip_both(grad_heads[3]),
    ]
    out_local = dot(after(heads, grad_heads), grad_branch, (0, 0)).astype(BF16)
    grad_local = plain(jnp.concatenate(grad_local))
    out_away = pick(out_local.reshape(xy_count, 2, lines, width), 1 - core, 1)
    out_away, over_local, mixed, grad_local = lax.optimization_barrier(
        (out_away, over_local, mixed, grad_local)
    )
    over_near, over_away = split_columns(over_local, hidden_part)
    over_far = flip(over_away, "cp", 1)
    mixed_moved = swap(mixed)
    grad_local = after(grad_local, over_away)

    def back_to_tokens(grads):
        two = 2 * span
        rows = grads.reshape(4 * span, 3 * part)
        send = dot(rows[two:], qkv, (1, 1)).astype(BF16)
        sent = flip(send, "core", 1)
        rows = after(rows, send)
        far_away = total(dot(rows[span:two], qkv, (1, 1)), sent[span:])
        kept = dot(after(rows, far_away)[:span], qkv, (1, 1)) + sent[:span].astype(F32)
        return send, far_away, flip(far_away, "cp", 1), kept

    tables = (pcol, prow, srow, cosine, sine, bounds, slot_of, tile)
    attended, lse = jnp.concatenate(attended, axis=1), jnp.concatenate(lse, axis=0)
    first, unfinished = attend_back(0, q, k, v, grad_local, attended, lse, *tables, [])
    first, mixed_moved, over_far, *grad_far = lax.optimization_barrier(
        (first, mixed_moved, over_far, *grad_far)
    )
    over_near, over_away = cut_fourth(over_near, over_far)
    over_far = flip(over_away, "cp", 2)
    _, far_away, far_back, kept = back_to_tokens(after(first, over_away))
    grad_near, grad_away = cut_second(grad_near, all_after(grad_far, far_away))
    grad_far = send_second(grad_away)
    out_far = flip(after(out_away, far_away), "core", 1)
    second = attend_back(
        1, q, k, v, after(grad_local, first, *grad_away, over_away, kept), attended, lse, *tables,
        [unfinished],
    )[0]
    second, over_far, out_far, *grad_far = lax.optimization_barrier(
        (second, over_far, out_far, *grad_far)
    )

    ended = end(kept, after(far_back, second), x[0], grad_hidden[:span], gains)
    moved = swap(ended)
    second = after(second, ended)
    send, far_away, far, kept = back_to_tokens(second)
    qkv_local = sum(
        dot(normed[4 * h : 4 * h + 4].reshape(4 * span, width), g.reshape(4 * span, -1), (0, 0))
        for h, g in enumerate((first, after(second, send)))
    ).astype(BF16)
    gain_one = jnp.sum(qkv_local.astype(F32) * qkv.astype(F32), axis=1) / gains[0]
    gain_sum = jnp.concatenate([gain_one[None], gain_two, gain_three, gain_four])
    gain_sum = gain_sum.reshape(2 * xy_count, cp_count, 128).astype(BF16)
    place = jnp.stack([x_bit, y_bit, core, parity, z >> 1]).astype(jnp.int32)
    locals_ = (qkv_local, out_local, gain_sum)
    rest_away = jnp.concatenate(
        [
            pick(qkv_local.reshape(xy_count, 2, lines, 3 * part), 1 - core, 1),
            jnp.pad(
                pick(gain_sum.reshape(xy_count, 2, cp_count, 128), 1 - core, 1),
                ((0, 0), (0, lines - cp_count), (0, 0)),
            ),
        ],
        axis=2,
    )
    rest_far = flip(rest_away, "core", 1)

    over = total(over_near, over_far)
    rest_far, over = all_after((rest_far, over), kept)
    low, low_away, high, high_away = spread_first(place, *locals_, over, rest_far, out_far)
    rest_far = flip(low_away, "xy", 1), flip(high_away, "xy", 2)
    low, low_away, high, high_away = spread_second(place, low, rest_far[0], high, rest_far[1])
    rest_far = flip(low_away, "xy", 2), flip(high_away, "xy", 1)
    grad_near, grad_away = cut_third(grad_near, all_after(grad_far, low_away))
    grad_far = flip(grad_away, "cp", 1)
    ended_last = end(
        kept, after(far, moved, low_away, high_away), x[1], grad_hidden[span:], gains
    )
    moved_last = swap(ended_last)
    rest_far = all_after(rest_far, moved_last)
    rest, rest_away, over = spread_third(place, low, rest_far[0], high, rest_far[1])
    grad_near, grad_away = cut_fourth(grad_near, after(grad_far, rest_away))
    grad_far = flip(grad_away, "cp", 2)
    gather_away = rest_away
    rest, rest_away = spread_fourth(place, rest, flip(rest_away, "cp", 2))
    moved_last = after(moved_last, rest_away)
    qkv_grad, out_grad, gains_grad = spread_fifth(place, rest, flip(rest_away, "cp", 1))
    gains_grad = gains_grad.reshape(-1)
    tokens_grad = jnp.stack([settled(ended, moved), settled(ended_last, moved_last)])
    tokens_grad = tokens_grad.astype(F32).reshape(tokens.shape)
    mixed = settled(after(mixed, gather_away), mixed_moved).reshape(tokens.shape)

    both = total(grad_near, after(grad_far, gather_away))
    both = plain(both).reshape(2, 2 * lines - spare, hidden_part)
    over = [
        jnp.concatenate([block[n * spare : (n + 1) * spare] for n in range(4)], axis=1)
        for block in over
    ]
    both = jnp.concatenate([both, jnp.stack(over)], axis=1).reshape(2, 2, lines, hidden_part)
    mine, other = pick(both, core, 0), flip(pick(both, 1 - core, 0), "core", 1)
    up_grad = ordered(core == 0, mine[0], other[0], 1).astype(F32)
    down_grad = ordered(core == 0, mine[1], other[1], 1).T.astype(F32)
    return mixed, tokens_grad, qkv_grad, out_grad, up_grad, down_grad, gains_grad


def solution(mesh):
    rows, cp = mesh.shape["rows"], mesh.shape["cp"]
    if (rows, cp) == (8, 4):
        grid = Mesh(mesh.devices.reshape(rows // 2, 2, cp), ("xy", "core", "cp"))
        run, lines = body, ("xy", "core")
    else:
        grid, run, lines = mesh, general_body, ("rows",)
    tokens = P(lines, None, "cp", None)
    weight, down, gains = P(lines, "cp"), P("cp", lines), P(lines + ("cp",))
    return jax.shard_map(
        run,
        mesh=grid,
        in_specs=(tokens, P(lines, None), weight, weight, weight, down, gains, tokens),
        out_specs=(tokens, tokens, weight, weight, weight, down, gains),
        check_vma=False,
    )
```

```python
import functools
import math

import jax
import jax.numpy as jnp
from jax import lax
from jax.experimental import pallas as pl
from jax.experimental.layout import Layout, with_layout_constraint
from jax.experimental.pallas import tpu as pltpu
from jax.sharding import Mesh, PartitionSpec as P

HEADS = 16
HEAD_DIM = 64


NORM_EPS = 1e-05
MASKED = -1e30


def layer_norm(values):
    average = jnp.mean(values, axis=-1, keepdims=True)
    centred = values - average
    spread = jnp.mean(centred * centred, axis=-1, keepdims=True)
    return centred * lax.rsqrt(spread + NORM_EPS)


def norm_back(values, upstream):
    _, pull_back = jax.vjp(layer_norm, values)
    return pull_back(upstream)[0]


def gelu_tanh(values):
    return jax.nn.gelu(values, approximate=True)


def rotate(values, cosine, sine_part):
    half_width = values.shape[-1] // 2
    first_half = values[..., :half_width]
    second_half = values[..., half_width:]
    return jnp.concatenate(
        [
            first_half * cosine - second_half * sine_part,
            second_half * cosine + first_half * sine_part,
        ],
        axis=-1,
    )


def rounded(values):
    return lax.optimization_barrier(values.astype(jnp.bfloat16)).astype(jnp.float32)


def doc_start_of(starts, positions):
    return jnp.max(
        jnp.where(starts[:, None, :] <= positions[None, :, None], starts[:, None, :], 0), axis=-1
    )


def general_body(tokens, doc_starts, qkv_weight, out_weight, up_weight, down_weight, norm_gains, cotangent):
    rows_count = lax.axis_size("rows")
    cp_count = lax.axis_size("cp")
    qkv_rows, out_rows, up_rows, down_rows, gain_piece = (
        lax.all_gather(qkv_weight, "rows", axis=0, tiled=True),
        lax.all_gather(out_weight, "rows", axis=0, tiled=True),
        lax.all_gather(up_weight, "rows", axis=0, tiled=True),
        lax.all_gather(down_weight, "rows", axis=1, tiled=True),
        lax.all_gather(norm_gains, "rows", axis=0, tiled=True),
    )
    qkv_full, out_full, gain_mixed = (
        lax.all_gather(qkv_rows, "cp", axis=1, tiled=True),
        lax.all_gather(out_rows, "cp", axis=1, tiled=True),
        lax.all_gather(gain_piece, "cp", axis=0, tiled=True),
    )
    gain_full = jnp.transpose(gain_mixed.reshape(cp_count, rows_count, -1), (1, 0, 2)).reshape(-1)
    row_count, _, span_len, width = tokens.shape
    half_len = span_len * cp_count
    row_len = 2 * half_len
    queries_dev = 2 * span_len
    token_total = row_count * queries_dev
    group_total = row_count * row_len
    gain_rows = gain_full.astype(jnp.float32).reshape(4, width)
    score_scale = HEAD_DIM ** (-0.5)
    local_pos = lax.axis_index("cp") * span_len + jnp.arange(span_len, dtype=jnp.int32)
    query_pos = jnp.concatenate([local_pos, row_len - 1 - local_pos])
    half_pos = jnp.arange(half_len, dtype=jnp.int32)
    key_pos = jnp.concatenate([half_pos, row_len - 1 - half_pos])
    query_start = doc_start_of(doc_starts, query_pos)
    key_start = doc_start_of(doc_starts, key_pos)
    freq_index = jnp.arange(HEAD_DIM // 2, dtype=jnp.float32)
    inverse_freq = jnp.exp(-math.log(10000.0) * 2.0 * freq_index / HEAD_DIM)
    angles = (query_pos[None, :] - query_start).astype(jnp.float32)[..., None] * inverse_freq
    cosine = jnp.cos(angles)[:, :, None, :]
    sine_part = jnp.sin(angles)[:, :, None, :]
    head_shape = (row_count, queries_dev, HEADS, HEAD_DIM)
    flat_shape = (row_count, queries_dev, width)
    fold_shape = (row_count, 2, span_len, width)
    group_shape = (row_count, 2, half_len, width)
    full_shape = (row_count, row_len, HEADS, HEAD_DIM)
    inputs = tokens.astype(jnp.float32).reshape(flat_shape)
    normed_in = layer_norm(inputs)
    normed = (normed_in * gain_rows[0]).astype(jnp.bfloat16)
    linear = jnp.dot(normed, qkv_full, preferred_element_type=jnp.float32)
    query_rows = rotate(linear[..., :width].reshape(head_shape), cosine, sine_part).astype(
        jnp.bfloat16
    )
    key_local = rotate(
        linear[..., width : 2 * width].reshape(head_shape), cosine, sine_part
    ).astype(jnp.bfloat16)
    value_local = linear[..., 2 * width :].reshape(head_shape).astype(jnp.bfloat16)
    key_sent, value_sent = (
        lax.all_gather(key_local.reshape(fold_shape), "cp", axis=2, tiled=True),
        lax.all_gather(value_local.reshape(fold_shape), "cp", axis=2, tiled=True),
    )
    key_rows = key_sent.reshape(full_shape)
    value_rows = value_sent.reshape(full_shape)
    block_size = min(512, row_len)
    block_count = row_len // block_size
    block_range = jnp.arange(block_count)

    def block_scores(block_index):
        first_key = block_index * block_size
        key_block = lax.dynamic_slice_in_dim(key_rows, first_key, block_size, 1)
        pos_block = lax.dynamic_slice_in_dim(key_pos, first_key, block_size, 0)
        start_block = lax.dynamic_slice_in_dim(key_start, first_key, block_size, 1)
        raw_scores = jnp.einsum(
            "rqhd,rkhd->rhqk", query_rows, key_block, preferred_element_type=jnp.float32
        )
        allowed = (query_start[:, None, :, None] == start_block[:, None, None, :]) & (
            pos_block[None, None, None, :] <= query_pos[None, None, :, None]
        )
        return (raw_scores * score_scale, allowed)

    def max_step(carry, block_index):
        running_max, running_sum = carry
        scores, allowed = block_scores(block_index)
        scores = jnp.where(allowed, scores, MASKED)
        new_max = jnp.maximum(running_max, jnp.max(scores, axis=-1))
        running_sum = running_sum * jnp.exp(running_max - new_max) + jnp.sum(
            jnp.where(allowed, jnp.exp(scores - new_max[..., None]), 0.0), axis=-1
        )
        return ((new_max, running_sum), None)

    stat_shape = (row_count, HEADS, queries_dev)
    (running_max, running_sum), _ = lax.scan(
        max_step,
        (jnp.full(stat_shape, MASKED, jnp.float32), jnp.zeros(stat_shape, jnp.float32)),
        block_range,
    )
    log_total = running_max + jnp.log(running_sum)

    def value_step(totals, block_index):
        scores, allowed = block_scores(block_index)
        probs = jnp.where(allowed, jnp.exp(scores - log_total[..., None]), 0.0).astype(jnp.bfloat16)
        value_block = lax.dynamic_slice_in_dim(value_rows, block_index * block_size, block_size, 1)
        return (
            totals
            + jnp.einsum("rhqk,rkhd->rqhd", probs, value_block, preferred_element_type=jnp.float32),
            None,
        )

    attended, _ = lax.scan(value_step, jnp.zeros(head_shape, jnp.float32), block_range)
    mixed_heads = attended.reshape(flat_shape).astype(jnp.bfloat16)
    branch = jnp.dot(mixed_heads, out_full, preferred_element_type=jnp.float32)
    branch_hat = layer_norm(branch)
    hidden = inputs + branch_hat * gain_rows[1]
    hidden_hat = layer_norm(hidden)
    normed_mid = (hidden_hat * gain_rows[2]).astype(jnp.bfloat16)
    ffn_in = lax.all_gather(normed_mid.reshape(fold_shape), "cp", axis=2, tiled=True).reshape(
        group_total, width
    )
    up_proj = jnp.dot(ffn_in, up_rows, preferred_element_type=jnp.float32)
    activation = gelu_tanh(up_proj).astype(jnp.bfloat16)
    down_terms = jnp.dot(activation, down_rows, preferred_element_type=jnp.float32)
    down_proj = (
        lax.psum_scatter(
            down_terms.reshape(group_shape).astype(jnp.bfloat16),
            "cp",
            scatter_dimension=2,
            tiled=True,
        )
        .astype(jnp.float32)
        .reshape(flat_shape)
    )
    down_hat = layer_norm(down_proj)
    mixed = (hidden + down_hat * gain_rows[3]).astype(jnp.bfloat16).reshape(tokens.shape)
    upstream = cotangent.astype(jnp.float32).reshape(flat_shape)
    gain_four = jnp.sum(upstream * down_hat, axis=(0, 1))
    grad_down_out = norm_back(down_proj, upstream * gain_rows[3]).astype(jnp.bfloat16)
    grad_out_rows = lax.all_gather(
        grad_down_out.reshape(fold_shape), "cp", axis=2, tiled=True
    ).reshape(group_total, width)
    down_local = jnp.einsum(
        "tf,td->fd", activation, grad_out_rows, preferred_element_type=jnp.float32
    )
    grad_act = jnp.einsum("td,fd->tf", grad_out_rows, down_rows, preferred_element_type=jnp.float32)
    _, gelu_pull = jax.vjp(gelu_tanh, up_proj)
    grad_up = gelu_pull(grad_act)[0].astype(jnp.bfloat16)
    up_local = jnp.einsum("tc,tf->cf", ffn_in, grad_up, preferred_element_type=jnp.float32)
    mid_terms = jnp.einsum("tf,cf->tc", grad_up, up_rows, preferred_element_type=jnp.float32)
    grad_mid = (
        lax.psum_scatter(
            mid_terms.reshape(group_shape).astype(jnp.bfloat16),
            "cp",
            scatter_dimension=2,
            tiled=True,
        )
        .astype(jnp.float32)
        .reshape(flat_shape)
    )
    gain_three = jnp.sum(grad_mid * hidden_hat, axis=(0, 1))
    grad_hidden = upstream + norm_back(hidden, grad_mid * gain_rows[2])
    gain_two = jnp.sum(grad_hidden * branch_hat, axis=(0, 1))
    grad_branch = norm_back(branch, grad_hidden * gain_rows[1]).astype(jnp.bfloat16)
    out_local = jnp.einsum(
        "tc,te->ce",
        mixed_heads.reshape(token_total, width),
        grad_branch.reshape(token_total, width),
        preferred_element_type=jnp.float32,
    )
    grad_heads = (
        jnp.einsum("rqe,ce->rqc", grad_branch, out_full, preferred_element_type=jnp.float32)
        .astype(jnp.bfloat16)
        .reshape(head_shape)
    )
    delta_sum = jnp.transpose(
        jnp.sum(grad_heads.astype(jnp.float32) * attended, axis=-1), (0, 2, 1)
    )

    def score_grads(block_index):
        scores, allowed = block_scores(block_index)
        probs = jnp.where(allowed, jnp.exp(scores - log_total[..., None]), 0.0)
        first_key = block_index * block_size
        key_block = lax.dynamic_slice_in_dim(key_rows, first_key, block_size, 1)
        value_block = lax.dynamic_slice_in_dim(value_rows, first_key, block_size, 1)
        grad_probs = jnp.einsum(
            "rqhd,rkhd->rhqk", grad_heads, value_block, preferred_element_type=jnp.float32
        )
        grad_scores = (probs * (grad_probs - delta_sum[..., None]) * score_scale).astype(
            jnp.bfloat16
        )
        return (probs, grad_scores, key_block)

    def grad_step(grad_query, block_index):
        probs, grad_scores, key_block = score_grads(block_index)
        grad_query = grad_query + jnp.einsum(
            "rhqk,rkhd->rqhd", grad_scores, key_block, preferred_element_type=jnp.float32
        )
        key_part = jnp.einsum(
            "rhqk,rqhd->rkhd", grad_scores, query_rows, preferred_element_type=jnp.float32
        )
        value_part = jnp.einsum(
            "rhqk,rqhd->rkhd",
            probs.astype(jnp.bfloat16),
            grad_heads,
            preferred_element_type=jnp.float32,
        )
        return (grad_query, (key_part, value_part))

    grad_query, (key_parts, value_parts) = lax.scan(
        grad_step, jnp.zeros(head_shape, jnp.float32), block_range
    )
    key_terms = jnp.moveaxis(key_parts, 0, 1).reshape(group_shape)
    value_terms = jnp.moveaxis(value_parts, 0, 1).reshape(group_shape)
    key_sum, value_sum = (
        lax.psum_scatter(
            key_terms.astype(jnp.bfloat16), "cp", scatter_dimension=2, tiled=True
        ).astype(jnp.float32),
        lax.psum_scatter(
            value_terms.astype(jnp.bfloat16), "cp", scatter_dimension=2, tiled=True
        ).astype(jnp.float32),
    )
    query_unturned = rotate(rounded(grad_query), cosine, -sine_part).reshape(flat_shape)
    key_unturned = rotate(rounded(key_sum.reshape(head_shape)), cosine, -sine_part).reshape(
        flat_shape
    )
    grad_linear = jnp.concatenate(
        [query_unturned, key_unturned, value_sum.reshape(flat_shape)], axis=-1
    ).astype(jnp.bfloat16)
    qkv_local = jnp.einsum(
        "tc,te->ce",
        normed.reshape(token_total, width),
        grad_linear.reshape(token_total, 3 * width),
        preferred_element_type=jnp.float32,
    )
    grad_normed = jnp.einsum(
        "rqe,ce->rqc", grad_linear, qkv_full, preferred_element_type=jnp.float32
    )
    gain_one = jnp.sum(grad_normed * normed_in, axis=(0, 1))
    tokens_grad = (grad_hidden + norm_back(inputs, grad_normed * gain_rows[0])).reshape(
        tokens.shape
    )
    gain_local = jnp.concatenate([gain_one, gain_two, gain_three, gain_four])
    gain_order = jnp.transpose(gain_local.reshape(rows_count, cp_count, -1), (1, 0, 2)).reshape(-1)
    qkv_mid, out_mid, gain_mid = (
        lax.psum_scatter(
            qkv_local.astype(jnp.bfloat16), "cp", scatter_dimension=1, tiled=True
        ).astype(jnp.float32),
        lax.psum_scatter(
            out_local.astype(jnp.bfloat16), "cp", scatter_dimension=1, tiled=True
        ).astype(jnp.float32),
        lax.psum_scatter(
            gain_order.astype(jnp.bfloat16), "cp", scatter_dimension=0, tiled=True
        ).astype(jnp.float32),
    )
    qkv_sum, out_sum, up_sum, down_sum, gain_sum = (
        lax.psum_scatter(
            qkv_mid.astype(jnp.bfloat16), "rows", scatter_dimension=0, tiled=True
        ).astype(jnp.float32),
        lax.psum_scatter(
            out_mid.astype(jnp.bfloat16), "rows", scatter_dimension=0, tiled=True
        ).astype(jnp.float32),
        lax.psum_scatter(
            up_local.astype(jnp.bfloat16), "rows", scatter_dimension=0, tiled=True
        ).astype(jnp.float32),
        lax.psum_scatter(
            down_local.astype(jnp.bfloat16), "rows", scatter_dimension=1, tiled=True
        ).astype(jnp.float32),
        lax.psum_scatter(
            gain_mid.astype(jnp.bfloat16), "rows", scatter_dimension=0, tiled=True
        ).astype(jnp.float32),
    )
    return (mixed, tokens_grad, qkv_sum, out_sum, up_sum, down_sum, gain_sum)


F32 = jnp.float32
BF16 = jnp.bfloat16
MIB = 1024 * 1024


def params(grid_rank, mebibytes=24):
    return pltpu.CompilerParams(
        dimension_semantics=("arbitrary",) * grid_rank, vmem_limit_bytes=mebibytes * MIB
    )


def lasting(microseconds):
    return pl.CostEstimate(
        flops=int(microseconds * 1e7), bytes_accessed=1024, transcendentals=0
    )


def turned(x, cosine, sine):
    lane = lax.broadcasted_iota(jnp.int32, x.shape, 1)
    other = jnp.where((lane & 32) == 0, pltpu.roll(x, 96, 1), pltpu.roll(x, 32, 1))
    return x * cosine + other * sine


def attend_kernel(tile, bounds, slot_of, q_ref, k_ref, v_ref, pcol_ref, prow_ref, srow_ref,
                  o_ref, ob_ref, lse_ref, vt_ref):
    i = pl.program_id(1)

    @pl.when(i == 0)
    def _():
        vt_ref[...] = v_ref[...].astype(F32).T.astype(BF16)

    qt = q_ref[...].astype(F32).T
    row = lax.broadcasted_iota(jnp.int32, qt.shape, 0)
    lo = bounds[0, i]
    mid = jnp.minimum(bounds[1, i], i)
    qpos = prow_ref[...]
    qstart = srow_ref[...]
    qh = [jnp.where((row >= 64) == (h == 1), qt, 0.0).astype(BF16) for h in range(2)]

    def step(j, carry, masked):
        at = pl.multiple_of(j * tile, tile)
        k = k_ref[pl.ds(at, tile), :]
        scores = [jnp.dot(k, qh[h], preferred_element_type=F32) for h in range(2)]
        if masked:
            kpos = pcol_ref[pl.ds(at, tile), :]
            allowed = (kpos >= qstart) & (kpos <= qpos)
            scores = [jnp.where(allowed, s, MASKED) for s in scores]
        out = []
        for h in range(2):
            top, total, acc = carry[h]
            new = jnp.maximum(top, jnp.max(scores[h], axis=0, keepdims=True))
            p = jnp.exp(scores[h] - new)
            keep = jnp.exp(top - new)
            total = total * keep + jnp.sum(p, axis=0, keepdims=True)
            acc = acc * keep + jnp.dot(
                vt_ref[h * 64 : h * 64 + 64, pl.ds(at, tile)], p.astype(BF16),
                preferred_element_type=F32,
            )
            out.append((new, total, acc))
        return tuple(out)

    start = (
        jnp.full((1, tile), MASKED, F32), jnp.zeros((1, tile), F32), jnp.zeros((64, tile), F32)
    )
    carry = step(i, (start, start), True)
    carry = lax.fori_loop(lo, mid, functools.partial(step, masked=True), carry)
    carry = lax.fori_loop(mid, i, functools.partial(step, masked=False), carry)
    parts = []
    for h in range(2):
        top, total, acc = carry[h]
        lse_ref[0, h : h + 1, :] = top + jnp.log(total)
        parts.append(acc / total)
    out = jnp.concatenate(parts, axis=0).T
    o_ref[...] = out
    span = ob_ref.shape[1]
    for b in range(tile // span):
        ob_ref[slot_of[i * (tile // span) + b]] = out[b * span : (b + 1) * span].astype(BF16)


def attend(pair, q, k, v, pcol, prow, srow, bounds, slot_of, tile):
    rows, width = q.shape
    blocks = slot_of.shape[0]
    span = rows // blocks
    count = rows // tile
    grid_spec = pltpu.PrefetchScalarGridSpec(
        num_scalar_prefetch=2,
        grid=(1, count),
        in_specs=[
            pl.BlockSpec((tile, 128), lambda p, i, b, t: (i, pair)),
            pl.BlockSpec((rows, 128), lambda p, i, b, t: (0, pair)),
            pl.BlockSpec((rows, 128), lambda p, i, b, t: (0, pair)),
            pl.BlockSpec((rows, 1), lambda p, i, b, t: (0, 0)),
            pl.BlockSpec((1, tile), lambda p, i, b, t: (0, i)),
            pl.BlockSpec((1, tile), lambda p, i, b, t: (0, i)),
        ],
        out_specs=[
            pl.BlockSpec((tile, 128), lambda p, i, b, t: (i, p)),
            pl.BlockSpec((blocks, span, 128), lambda p, i, b, t: (0, 0, p)),
            pl.BlockSpec((1, 2, tile), lambda p, i, b, t: (p, 0, i)),
        ],
        scratch_shapes=[pltpu.VMEM((128, rows), BF16)],
    )
    return pl.pallas_call(
        functools.partial(attend_kernel, tile),
        grid_spec=grid_spec,
        out_shape=[
            jax.ShapeDtypeStruct((rows, 128), F32),
            jax.ShapeDtypeStruct((blocks, span, 128), BF16),
            jax.ShapeDtypeStruct((1, 2, rows), F32),
        ],
        compiler_params=params(2),
        cost_estimate=lasting(14),
        name="attend",
    )(bounds, slot_of, q, k, v, pcol, prow, srow)


def attend_back_kernel(tile, first, steps, bounds, slot_of, q_ref, k_ref, v_ref, do_ref, o_ref,
                       lse_ref, pcol_ref, prow_ref, srow_ref, cos_ref, sin_ref, *refs):
    qm, dom, qtm, dotm, delta, dqt = refs[-6:]
    count = q_ref.shape[0] // tile
    last = first + steps
    before = refs[0] if first else None
    g_ref = refs[1 if first else 0]
    after_ref = refs[1] if last < count else None
    j = first + pl.program_id(1)
    span = do_ref.shape[1]

    @pl.when(pl.program_id(1) == 0)
    def _():
        for t in range(first, count):
            part = pl.ds(t * tile, tile)
            q = q_ref[part, :].astype(F32)
            do = jnp.concatenate(
                [do_ref[slot_of[t * tile // span + b]] for b in range(tile // span)], axis=0
            ).astype(F32)
            qt, dot = q.T, do.T
            lane = lax.broadcasted_iota(jnp.int32, q.shape, 1)
            row = lax.broadcasted_iota(jnp.int32, qt.shape, 0)
            prod = dot * o_ref[part, :].T
            for h in range(2):
                mine = (lane >= 64) == (h == 1)
                mine_t = (row >= 64) == (h == 1)
                qm[h, part, :] = jnp.where(mine, q, 0.0).astype(BF16)
                dom[h, part, :] = jnp.where(mine, do, 0.0).astype(BF16)
                qtm[h, :, part] = jnp.where(mine_t, qt, 0.0).astype(BF16)
                dotm[h, :, part] = jnp.where(mine_t, dot, 0.0).astype(BF16)
                delta[h : h + 1, part] = jnp.sum(
                    prod[h * 64 : h * 64 + 64], axis=0, keepdims=True
                )
        if before is None:
            dqt[...] = jnp.zeros_like(dqt)
        else:
            dqt[:, first * tile :] = before[0]

    here = pl.ds(pl.multiple_of(j * tile, tile), tile)
    k = k_ref[here, :]
    v = v_ref[here, :]
    kt = k.astype(F32).T.astype(BF16)
    kpos = pcol_ref[here, :]
    full = jnp.maximum(bounds[2, j], j + 1)
    end = bounds[3, j]

    def step(i, carry, masked):
        dk, dv = carry
        part = pl.ds(pl.multiple_of(i * tile, tile), tile)
        if masked:
            allowed = (kpos >= srow_ref[:, part]) & (kpos <= prow_ref[:, part])
        for h in range(2):
            s = jnp.dot(k, qtm[h, :, part], preferred_element_type=F32)
            p = jnp.exp(s - lse_ref[0, h : h + 1, part])
            if masked:
                p = jnp.where(allowed, p, 0.0)
            dp = jnp.dot(v, dotm[h, :, part], preferred_element_type=F32)
            ds = (p * (dp - delta[h : h + 1, part])).astype(BF16)
            dv = dv + jnp.dot(p.astype(BF16), dom[h, part, :], preferred_element_type=F32)
            dk = dk + jnp.dot(ds, qm[h, part, :], preferred_element_type=F32)
            dqt[h * 64 : h * 64 + 64, part] += jnp.dot(
                kt[h * 64 : h * 64 + 64, :], ds, preferred_element_type=F32
            )
        return dk, dv

    carry = (jnp.zeros((tile, 128), F32), jnp.zeros((tile, 128), F32))
    carry = step(j, carry, True)
    carry = lax.fori_loop(j + 1, full, functools.partial(step, masked=False), carry)
    carry = lax.fori_loop(full, end, functools.partial(step, masked=True), carry)
    dk, dv = carry

    def unturned(x, at):
        x = x.astype(BF16).astype(F32)
        return turned(x, cos_ref[at, :], -sin_ref[at, :]).astype(BF16)

    grad_k, grad_v = unturned(dk, here), dv.astype(BF16)
    for b in range(tile // span):
        at = slot_of[j * (tile // span) + b] >> 1
        g_ref[at, :, 128:256] = grad_k[b * span : (b + 1) * span]
        g_ref[at, :, 256:384] = grad_v[b * span : (b + 1) * span]

    @pl.when(pl.program_id(1) == steps - 1)
    def _():
        for t in range(first, last):
            part = pl.ds(t * tile, tile)
            grad_q = unturned(dqt[:, part].T * 0.125, part)
            for b in range(tile // span):
                at = slot_of[t * (tile // span) + b] >> 1
                g_ref[at, :, 0:128] = grad_q[b * span : (b + 1) * span]
        if after_ref is not None:
            after_ref[0] = dqt[:, last * tile :]


def attend_back(half, q, k, v, do, o, lse, pcol, prow, srow, cosine, sine, bounds, slot_of, tile,
                before):
    rows, width = q.shape
    pairs = width // 128
    blocks, span, _ = do.shape
    count = rows // tile
    steps = count // 2
    first = half * steps
    whole = pl.BlockSpec((rows, 128), lambda p, j, b, t: (0, p))
    table = pl.BlockSpec((rows, 128), lambda p, j, b, t: (0, 0))
    line = pl.BlockSpec((1, rows), lambda p, j, b, t: (0, 0))
    rest = pl.BlockSpec((1, 128, rows // 2), lambda p, j, b, t: (p, 0, 0))
    outs = [
        (
            jax.ShapeDtypeStruct((blocks // 2, span, 3 * width), BF16),
            pl.BlockSpec((blocks // 2, span, 384), lambda p, j, b, t: (0, 0, p)),
        )
    ]
    if not half:
        outs.append((jax.ShapeDtypeStruct((pairs, 128, rows // 2), F32), rest))
    grid_spec = pltpu.PrefetchScalarGridSpec(
        num_scalar_prefetch=2,
        grid=(pairs, steps),
        in_specs=[
            whole, whole, whole,
            pl.BlockSpec((blocks, span, 128), lambda p, j, b, t: (0, 0, p)),
            whole,
            pl.BlockSpec((1, 2, rows), lambda p, j, b, t: (p, 0, 0)),
            pl.BlockSpec((rows, 1), lambda p, j, b, t: (0, 0)),
            line, line, table, table,
        ]
        + [rest] * len(before),
        out_specs=[spec for _, spec in outs],
        scratch_shapes=[
            pltpu.VMEM((2, rows, 128), BF16), pltpu.VMEM((2, rows, 128), BF16),
            pltpu.VMEM((2, 128, rows), BF16), pltpu.VMEM((2, 128, rows), BF16),
            pltpu.VMEM((2, rows), F32), pltpu.VMEM((128, rows), F32),
        ],
    )
    return pl.pallas_call(
        functools.partial(attend_back_kernel, tile, first, steps),
        grid_spec=grid_spec,
        out_shape=[shape for shape, _ in outs],
        compiler_params=params(2, 40),
        cost_estimate=lasting(23),
        name="attend_back",
    )(bounds, slot_of, q, k, v, do, o, lse, pcol, prow, srow, cosine, sine, *before)


def tile_bounds(starts_nat, tile):
    rows = starts_nat.shape[0]
    count = rows // tile
    tiles = starts_nat.reshape(count, tile)
    first, last = tiles[:, 0], tiles[:, -1]
    at = jnp.arange(count, dtype=jnp.int32) * tile
    lo = first // tile
    mid = (last + tile - 1) // tile
    full = jnp.sum((last[None, :] <= at[:, None]).astype(jnp.int32), axis=1)
    end = jnp.sum((first[None, :] <= at[:, None] + tile - 1).astype(jnp.int32), axis=1)
    return jnp.stack([lo, mid, full, end]).astype(jnp.int32)


def normalized(x):
    centred = x - jnp.mean(x, axis=1, keepdims=True)
    scale = lax.rsqrt(jnp.mean(centred * centred, axis=1, keepdims=True) + NORM_EPS)
    return centred * scale, scale


def normalized_back(hat, scale, upstream):
    level = jnp.mean(upstream, axis=1, keepdims=True)
    slant = jnp.mean(upstream * hat, axis=1, keepdims=True)
    return scale * (upstream - level - hat * slant)


def dot_nt(a, b):
    return lax.dot_general(a, b, (((1,), (1,)), ((), ())), preferred_element_type=F32)


def call(kernel, name, grid, tables, ins, outs, microseconds, *arrays):
    return pl.pallas_call(
        kernel,
        grid_spec=pltpu.PrefetchScalarGridSpec(
            num_scalar_prefetch=len(tables),
            grid=grid,
            in_specs=ins,
            out_specs=[spec for _, spec in outs],
        ),
        out_shape=[shape for shape, _ in outs],
        compiler_params=params(len(grid)),
        cost_estimate=lasting(microseconds),
        name=name,
    )(*tables, *arrays)


def shaped(dtype, *shape):
    return jax.ShapeDtypeStruct(shape, dtype)


def fixed(*shape):
    return pl.BlockSpec(shape, lambda *_: (0,) * len(shape))


def project_kernel(blocks, slots, near, far, gain_ref, w_ref, cos_ref, sin_ref, *refs):
    q_ref, k_ref, v_ref, n_ref = refs[-4:]
    width = q_ref.shape[1]
    x = jnp.where(slots[pl.program_id(0)] < 4, near[0], far[0]).astype(F32)
    normed = (normalized(x)[0] * gain_ref[0:1, :]).astype(BF16)
    n_ref[0] = normed
    linear = jnp.dot(normed, w_ref[...], preferred_element_type=F32)
    for at in range(0, width, 128):
        q = turned(linear[:, 3 * at : 3 * at + 128], cos_ref[...], sin_ref[...])
        k = turned(linear[:, 3 * at + 128 : 3 * at + 256], cos_ref[...], sin_ref[...])
        q_ref[:, at : at + 128] = q.astype(BF16) * jnp.asarray(0.125, BF16)
        k_ref[:, at : at + 128] = k.astype(BF16)
        v_ref[:, at : at + 128] = linear[:, 3 * at + 256 : 3 * at + 384].astype(BF16)


def project(near, far, gains, w, cosine, sine, blocks, slots, before):
    _, rows, depth = near.shape
    width = w.shape[1] // 3
    count = 2 * blocks.shape[0]
    piece = pl.BlockSpec((1, rows, depth), lambda i, b, s: (s[i] & 1, 0, 0))
    angle = pl.BlockSpec((rows, 128), lambda i, b, s: (b[i], 0))
    out = shaped(BF16, count * rows, width)
    normed = shaped(BF16, count, rows, depth)
    block = pl.BlockSpec((rows, width), lambda i, b, s: (b[i], 0))
    return pl.pallas_call(
        project_kernel,
        grid_spec=pltpu.PrefetchScalarGridSpec(
            num_scalar_prefetch=2,
            grid=blocks.shape,
            in_specs=[piece, piece, fixed(*gains.shape), fixed(*w.shape), angle, angle]
            + [pl.BlockSpec(memory_space=pl.ANY)] * len(before),
            out_specs=[
                block, block, block,
                pl.BlockSpec((1, rows, depth), lambda i, b, s: ((s[i] & 1) * 4 + (s[i] >> 1), 0, 0)),
            ],
        ),
        out_shape=[out, out, out, normed],
        input_output_aliases={8 + n: n for n in range(len(before))},
        compiler_params=params(1),
        cost_estimate=lasting(7),
        name="project",
    )(blocks, slots, near, far, gains, w, cosine, sine, *before)


def mix_kernel(group, own, near, far, both, w_ref, x_ref, gain_ref,
               heads_ref, hat_ref, scale_ref, hidden_ref, mid_ref):
    width = own.shape[2]
    for r, piece in enumerate((own[0], far[0], near[0], both[0])):
        at = pl.ds(pl.multiple_of((group[0] ^ r) * width, width), width)
        heads_ref[:, at] = piece
    branch = jnp.dot(heads_ref[...], w_ref[...], preferred_element_type=F32)
    hat, scale = normalized(branch)
    hidden = x_ref[0].astype(F32) + hat * gain_ref[1:2, :]
    hat_ref[...] = hat
    scale_ref[...] = scale
    hidden_ref[...] = hidden
    mid_ref[...] = (normalized(hidden)[0] * gain_ref[2:3, :]).astype(BF16)


def mix(group, local, near, far, both, w, x, gains):
    _, rows, part = local.shape
    count, _, width = x.shape
    block = pl.BlockSpec((1, rows, part), lambda i, g: (i, 0, 0))
    row = pl.BlockSpec((rows, width), lambda i, g: (i, 0))
    total = count * rows
    return call(
        mix_kernel, "mix", (count,), [group],
        [
            block, block, block, block, fixed(*w.shape), pl.BlockSpec((1, rows, width), lambda i, g: (i, 0, 0)),
            fixed(*gains.shape),
        ],
        [
            (shaped(BF16, total, width), row),
            (shaped(F32, total, width), row),
            (shaped(F32, total, 1), pl.BlockSpec((rows, 1), lambda i, g: (i, 0))),
            (shaped(F32, total, width), row),
            (shaped(BF16, total, width), row),
        ],
        6, local, near, far, both, w, x, gains,
    )


def finish_kernel(stays, terms_ref, sent_ref, hidden_ref, own_ref, moved_ref, gain_ref,
                  mixed_ref, grad_ref, dy_ref, sum_ref):
    down = terms_ref[...] + sent_ref[...].astype(F32)
    hat, scale = normalized(down)
    gain = gain_ref[3:4, :]
    low = jnp.where(stays[0] == 1, own_ref[...], moved_ref[...])
    dy_ref[...] = low
    dy = low.astype(F32)
    mixed_ref[...] = (hidden_ref[...] + hat * gain).astype(BF16)
    grad_ref[...] = normalized_back(hat, scale, dy * gain).astype(BF16)

    @pl.when(pl.program_id(0) == 0)
    def _():
        sum_ref[...] = jnp.zeros_like(sum_ref)

    sum_ref[...] += jnp.sum(dy * hat, axis=0, keepdims=True)


def finish(stays, terms, sent, hidden, own, moved, gains):
    total, width = terms.shape
    rows = total // 2
    row = pl.BlockSpec((rows, width), lambda i, s: (i, 0))
    return call(
        finish_kernel, "finish", (2,), [stays],
        [row] * 5 + [fixed(*gains.shape)],
        [
            (shaped(BF16, total, width), row), (shaped(BF16, total, width), row),
            (shaped(BF16, total, width), row),
            (shaped(F32, 1, width), fixed(1, width)),
        ],
        5, terms, sent, hidden, own, moved, gains,
    )


def turn_kernel(group, terms_ref, sent_ref, hidden_ref, dy_ref, hat_ref, scale_ref, w_ref, gain_ref,
                keep_ref, branch_ref, heads_ref, three_ref, two_ref):
    upstream = terms_ref[...] + sent_ref[...].astype(F32)
    hat, scale = normalized(hidden_ref[...])

    @pl.when(pl.program_id(0) == 0)
    def _():
        three_ref[...] = jnp.zeros_like(three_ref)
        two_ref[...] = jnp.zeros_like(two_ref)

    three_ref[...] += jnp.sum(upstream * hat, axis=0, keepdims=True)
    grad = dy_ref[...].astype(F32) + normalized_back(hat, scale, upstream * gain_ref[2:3, :])
    keep_ref[...] = grad
    branch_hat = hat_ref[...]
    two_ref[...] += jnp.sum(grad * branch_hat, axis=0, keepdims=True)
    branch = normalized_back(branch_hat, scale_ref[...], grad * gain_ref[1:2, :]).astype(BF16)
    branch_ref[...] = branch
    part = heads_ref.shape[3]
    for r in range(4):
        at = pl.ds(pl.multiple_of((group[0] ^ r) * part, part), part)
        heads_ref[r, 0] = dot_nt(branch, w_ref[at, :]).astype(BF16)


def turn(group, terms, sent, hidden, dy, hat, scale, w, gains):
    total, width = terms.shape
    rows = total // 2
    part = width // 4
    row = pl.BlockSpec((rows, width), lambda i, g: (i, 0))
    return call(
        turn_kernel, "turn", (2,), [group],
        [
            row, row, row, row, row, pl.BlockSpec((rows, 1), lambda i, g: (i, 0)),
            fixed(*w.shape), fixed(*gains.shape),
        ],
        [
            (shaped(F32, total, width), row), (shaped(BF16, total, width), row),
            (
                shaped(BF16, 4, 2, rows, part),
                pl.BlockSpec((4, 1, rows, part), lambda i, g: (0, i, 0, 0)),
            ),
            (shaped(F32, 1, width), fixed(1, width)), (shaped(F32, 1, width), fixed(1, width)),
        ],
        8, terms, sent, hidden, dy, hat, scale, w, gains,
    )


def end_kernel(keep_ref, far_ref, x_ref, grad_ref, gain_ref, o_ref):
    upstream = keep_ref[...] + far_ref[...].astype(F32)
    hat, scale = normalized(x_ref[...].astype(F32))
    grad = grad_ref[...] + normalized_back(hat, scale, upstream * gain_ref[0:1, :])
    o_ref[...] = grad.astype(BF16)


def end(keep, far, x, grad, gains):
    total, width = x.shape
    rows = total // 2
    row = pl.BlockSpec((rows, width), lambda i: (i, 0))
    return call(
        end_kernel, "end", (2,), [], [row] * 4 + [fixed(*gains.shape)],
        [(shaped(BF16, total, width), row)], 20, keep, far, x, grad, gains,
    )[0]


def plain(x):
    return with_layout_constraint(x, Layout(tuple(range(x.ndim))))


def cut_lines_kernel(place, *refs):
    for n, out in enumerate(refs[8:]):
        up, down = refs[2 * n], refs[2 * n + 1]
        lines = up.shape[0]
        out[0, :lines] = up[...]
        out[0, lines:] = down[: out.shape[1] - lines]


def cut_lines(place, up, down, spare):
    width = up.shape[1]
    lines = up.shape[0] // 8
    at = (
        lambda i, p: (2 * (2 * i + p[0]), 0),
        lambda i, p: (2 * (2 * i + 1 - p[0]), 0),
        lambda i, p: (2 * (2 * p[1] + i) + 1, 0),
        lambda i, p: (2 * (2 * (1 - p[1]) + i) + 1, 0),
    )
    rows = 2 * lines - spare
    out = shaped(BF16, 2, rows, width), pl.BlockSpec((1, rows, width), lambda i, p: (i, 0, 0))
    return call(
        cut_lines_kernel, "cut_lines", (2,), [place],
        [pl.BlockSpec((lines, width), index) for index in at for _ in range(2)],
        [out] * 4, 4, *([up, down] * 4),
    )


QKV_BLOCKS, OVER_BLOCKS, OUT_BLOCKS = 12, 2, 8
LOW_BLOCKS = 11
ALL_BLOCKS = QKV_BLOCKS + OVER_BLOCKS + OUT_BLOCKS + 1
LEFT = ((0, 0), (0, 1), (1, 0))
RIGHT = ((1, 1), (2, 0), (2, 1))


def tiles(array):
    return [array[:, at : at + 128] for at in range(0, array.shape[1], 128)]


def plus(a, b):
    return (a.astype(F32) + b.astype(F32)).astype(BF16)


def spread_first_kernel(place, qkv_ref, out_ref, gain_ref, over_ref, far_ref, out_far,
                        low, low_away, high, high_away):
    lines = far_ref.shape[1]
    spare = over_ref.shape[0] // 8
    wide = qkv_ref.shape[1]
    x_bit, y_bit, core = place[0], place[1], place[2]

    def fill(line, low_out, high_out):
        at = pl.ds(pl.multiple_of((2 * line + core) * lines, lines), lines)
        near = tiles(qkv_ref[at, :])
        far = tiles(far_ref[line, :, :wide])
        blocks = [jnp.where(core == 0, a, b) for a, b in zip(near, far)]
        blocks += [jnp.where(core == 0, a, b) for a, b in zip(far, near)]
        for c in range(2):
            rows = pl.ds(pl.multiple_of((2 * line + c) * spare, spare), spare)
            blocks.append(jnp.concatenate(tiles(over_ref[rows, :]), axis=0))
        blocks += [
            plus(a, b)
            for a, b in zip(tiles(out_ref[at, :]), tiles(out_far[line]))
        ]
        count = gain_ref.shape[1]
        gain = jnp.concatenate(
            [gain_ref[2 * line + core], jnp.zeros((lines - count, 128), BF16)], axis=0
        )
        blocks.append(plus(gain, far_ref[line, :, -128:]))
        for n, block in enumerate(blocks):
            if n < LOW_BLOCKS and low_out is not None:
                low_out[n] = block
            if n >= LOW_BLOCKS and high_out is not None:
                high_out[n - LOW_BLOCKS] = block

    for n in range(2):
        fill(2 * n + x_bit, low.at[n], None)
        fill(2 * n + 1 - x_bit, low_away.at[n], None)
        fill(2 * y_bit + n, None, high.at[n])
        fill(2 * (1 - y_bit) + n, None, high_away.at[n])


def spread_first(place, qkv, out, gain, over, far, out_far):
    lines = far.shape[1]
    low = shaped(BF16, 2, LOW_BLOCKS, lines, 128), fixed(2, LOW_BLOCKS, lines, 128)
    rest = ALL_BLOCKS - LOW_BLOCKS
    high = shaped(BF16, 2, rest, lines, 128), fixed(2, rest, lines, 128)
    arrays = (qkv, out, gain, over, far, out_far)
    return call(
        spread_first_kernel, "spread_first", (1,), [place], [fixed(*a.shape) for a in arrays],
        [low, low, high, high], 2, *arrays,
    )


def spread_second_kernel(place, low, low_far, high, high_far, low_o, low_away, high_o, high_away):
    for source, far, bit, near_o, away_o in (
        (low, low_far, place[1], low_o, low_away), (high, high_far, place[0], high_o, high_away)
    ):
        near_o[...] = plus(source[bit], far[bit])
        away_o[...] = plus(source[1 - bit], far[1 - bit])


def spread_second(place, *arrays):
    lows, highs = arrays[0].shape[1:], arrays[2].shape[1:]
    outs = [(shaped(BF16, *s), fixed(*s)) for s in (lows, lows, highs, highs)]
    return call(
        spread_second_kernel, "spread_second", (1,), [place], [fixed(*a.shape) for a in arrays],
        outs, 2, *arrays,
    )


def spread_third_kernel(place, low, low_far, high, high_far, near_o, away_o, over_o):
    half = place[4]

    def block(n):
        if n < LOW_BLOCKS:
            return plus(low[n], low_far[n])
        return plus(high[n - LOW_BLOCKS], high_far[n - LOW_BLOCKS])

    at = 0
    for (left_t, left_c), (right_t, right_c) in zip(LEFT, RIGHT):
        for pair in range(2):
            left = block(left_c * 6 + pair * 3 + left_t)
            right = block(right_c * 6 + pair * 3 + right_t)
            near_o[at] = jnp.where(half == 0, left, right)
            away_o[at] = jnp.where(half == 0, right, left)
            at += 1
    for c in range(2):
        over_o[c] = block(QKV_BLOCKS + c)
    first = QKV_BLOCKS + OVER_BLOCKS
    for n in range(4):
        left, right = block(first + n), block(first + 4 + n)
        near_o[at] = jnp.where(half == 0, left, right)
        away_o[at] = jnp.where(half == 0, right, left)
        at += 1
    near_o[at] = block(first + 8)
    away_o[at] = block(first + 8)


def spread_third(place, *arrays):
    lines = arrays[0].shape[1]
    part = shaped(BF16, 11, lines, 128), fixed(11, lines, 128)
    over = shaped(BF16, 2, lines, 128), fixed(2, lines, 128)
    return call(
        spread_third_kernel, "spread_third", (1,), [place], [fixed(*a.shape) for a in arrays],
        [part, part, over], 2, *arrays,
    )


def spread_fourth_kernel(place, near, far, near_o, away_o):
    odd = place[3] == 1
    blocks = [plus(near[n], far[n]) for n in range(11)]
    for pair in range(2):
        one, two, three = blocks[pair], blocks[2 + pair], blocks[4 + pair]
        near_o[pair] = jnp.where(odd, two, one)
        near_o[2 + pair] = jnp.where(odd, three, two)
        away_o[pair] = jnp.where(odd, one, three)
        near_o[4 + pair] = jnp.where(odd, blocks[8 + pair], blocks[6 + pair])
        away_o[2 + pair] = jnp.where(odd, blocks[6 + pair], blocks[8 + pair])
    near_o[6] = blocks[10]
    away_o[4] = blocks[10]


def spread_fourth(place, near, far):
    lines = near.shape[1]
    return call(
        spread_fourth_kernel, "spread_fourth", (1,), [place], [fixed(*near.shape)] * 2,
        [
            (shaped(BF16, 7, lines, 128), fixed(7, lines, 128)),
            (shaped(BF16, 5, lines, 128), fixed(5, lines, 128)),
        ],
        2, near, far,
    )


def spread_fifth_kernel(place, near, far, qkv_o, out_o, gain_o, gain_all):
    for pair in range(2):
        first, second = near[pair].astype(F32), near[2 + pair].astype(F32)
        other = far[pair].astype(F32)
        at = 128 * pair
        qkv_o[:, at : at + 128] = first
        qkv_o[:, 256 + at : 384 + at] = other
        qkv_o[:, 512 + at : 640 + at] = second
        out_o[:, at : at + 128] = near[4 + pair].astype(F32) + far[2 + pair].astype(F32)
    gain_all[...] = near[6].astype(F32) + far[4].astype(F32)
    gain_o[...] = gain_all[pl.ds(2 * place[4] + place[3], 1), :]


def spread_fifth(place, near, far):
    lines = near.shape[1]
    outs = [(shaped(F32, *s), fixed(*s)) for s in ((lines, 768), (lines, 256), (1, 128))]
    return pl.pallas_call(
        spread_fifth_kernel,
        grid_spec=pltpu.PrefetchScalarGridSpec(
            num_scalar_prefetch=1,
            grid=(1,),
            in_specs=[fixed(*near.shape), fixed(*far.shape)],
            out_specs=[spec for _, spec in outs],
            scratch_shapes=[pltpu.VMEM((lines, 128), F32)],
        ),
        out_shape=[shape for shape, _ in outs],
        compiler_params=params(1),
        cost_estimate=lasting(2),
        name="spread_fifth",
    )(place, near, far)


def flip(x, axis, bit):
    return lax.ppermute(plain(x), axis, [(i, i ^ bit) for i in range(lax.axis_size(axis))])


def swap(x):
    cp = lax.axis_size("cp")
    half = cp // 2
    pairs = []
    for z in range(half):
        low, high = cp + z, z + half
        pairs += [(low, high), (high, low)]
    return lax.ppermute(plain(x), ("core", "cp"), pairs)


def settled(x, moved):
    stays = (lax.axis_index("core") == 1) == (lax.axis_index("cp") >= lax.axis_size("cp") // 2)
    return jnp.where(stays, x, moved)


def ordered(first, mine, other, axis):
    return jnp.concatenate(
        [jnp.where(first, mine, other), jnp.where(first, other, mine)], axis=axis
    )


def placed(first, mine, other, at):
    return ordered(first, jnp.expand_dims(mine, at), jnp.expand_dims(other, at), at)


def after(x, *others):
    return lax.optimization_barrier((x, *others))[0]


def all_after(group, *others):
    return lax.optimization_barrier((*group, *others))[: len(group)]


def total(a, b):
    return (a.astype(F32) + b.astype(F32)).astype(BF16)


def flip_both(x):
    cp = lax.axis_size("cp")
    return lax.ppermute(
        x, ("core", "cp"), [(c * cp + z, (1 - c) * cp + (z ^ 1)) for c in range(2) for z in range(cp)]
    )


def dot(a, b, dims):
    return lax.dot_general(a, b, ((dims[:1], dims[1:]), ((), ())), preferred_element_type=F32)


def gelu_and_slope(u):
    c = math.sqrt(2.0 / math.pi)
    square = u * u
    t = jnp.tanh(u * (c + (c * 0.044715) * square))
    half = 0.5 + 0.5 * t
    slope = half + (0.5 * u) * (1.0 - t * t) * (c + (3.0 * 0.044715 * c) * square)
    return lax.optimization_barrier(((u * half).astype(BF16), slope.astype(BF16)))


def pick(x, at, axis):
    return lax.dynamic_index_in_dim(x, at, axis, False)


def widened(z, x, other):
    first, second = jnp.where(z & 1 == 0, x, other), jnp.where(z & 1 == 0, other, x)
    half = x.shape[1] // 2
    return jnp.concatenate(
        [first[:, :half], second[:, :half], first[:, half:], second[:, half:]], axis=1
    )


def body(tokens, doc_starts, qkv_weight, out_weight, up_weight, down_weight, norm_gains, cotangent):
    xy, core, z = lax.axis_index("xy"), lax.axis_index("core"), lax.axis_index("cp")
    xy_count, cp_count = lax.axis_size("xy"), lax.axis_size("cp")
    _, _, span, width = tokens.shape
    blocks = 2 * cp_count
    row_len = blocks * span
    own = 2 * span
    parity = z & 1
    group = parity + 2 * core
    part = width // cp_count
    hidden_part = up_weight.shape[1] // 2
    lines_each = width // xy_count
    lines = lines_each // 2
    here = jnp.reshape(xy, (1,)).astype(jnp.int32)
    group_at = jnp.reshape(group, (1,)).astype(jnp.int32)

    gain_rows = jnp.zeros((16, qkv_weight.shape[1]), BF16)
    gain_rows = lax.dynamic_update_slice(gain_rows, norm_gains[None], (0, 0))
    w = jnp.concatenate([qkv_weight, gain_rows])
    w_far = flip(w, "cp", 2)

    x = settled(tokens[0], swap(after(tokens, w_far)[0]))
    w, w_far = jnp.where(z & 2 == 0, w, w_far), jnp.where(z & 2 == 0, w_far, w)
    near = [w[:, n * part : (n + 1) * part] for n in range(3)]
    near += [w_far[:, n * part : (n + 1) * part] for n in range(3)]
    even = parity == 0
    sent = jnp.concatenate([near[1], near[4]], axis=1)
    gain_near = jnp.stack([w[lines, :128], w_far[lines, :128]])
    sent = lax.dynamic_update_slice(sent, gain_near, (lines, 0))
    far = flip(sent, "cp", 1)
    up_weight, down_weight, out_weight = all_after((up_weight, down_weight, out_weight), far)
    out_far = flip(out_weight, "cp", 2)


    def half_of(which):
        up = lax.dynamic_slice_in_dim(up_weight, which * hidden_part, hidden_part, 1)
        down = lax.dynamic_slice_in_dim(down_weight, which * hidden_part, hidden_part, 0)
        return plain(jnp.stack([up, down.T]))

    ffn = ordered(core == 0, half_of(core), flip(half_of(1 - core), "core", 1), 1)

    def paired(mine, other):
        return jnp.concatenate(
            [jnp.where(z & 2 == 0, mine, other), jnp.where(z & 2 == 0, other, mine)], axis=1
        )

    gain_far = far[lines : lines + 2, :128]
    gain_near, gain_far = (
        jnp.where(even, gain_near, gain_far), jnp.where(even, gain_far, gain_near)
    )
    gain_rows = jnp.stack([gain_near[0], gain_far[0], gain_near[1], gain_far[1]])
    far = [far[:lines, n * part : (n + 1) * part] for n in range(2)]
    near = [block[:lines] for block in near]

    def by_pairs(*choices):
        picked = [jnp.where(even, a, b) for a, b in choices]
        return jnp.concatenate(
            [block[:, at : at + 128] for at in range(0, part, 128) for block in picked], axis=1
        )

    first_group = by_pairs((near[0], far[0]), (far[0], near[2]), (near[5], near[3]))
    second_group = by_pairs((near[2], near[0]), (near[3], far[1]), (far[1], near[5]))
    gain_block = jnp.zeros((16, 3 * part), BF16)
    gain_block = lax.dynamic_update_slice(gain_block, gain_rows, (0, 0))
    mine = jnp.concatenate([jnp.where(core == 0, first_group, second_group), gain_block])
    other = jnp.concatenate([jnp.where(core == 0, second_group, first_group), gain_block])

    other_starts = flip(after(doc_starts, w_far), "core", 1)
    starts = jnp.where(core == z // (cp_count // 2), doc_starts, other_starts)[0]

    block_id = jnp.arange(blocks, dtype=jnp.int32)[:, None]
    inside = jnp.arange(span, dtype=jnp.int32)[None, :]
    late = block_id >= cp_count
    positions = (block_id * span + jnp.where(late, span - 1 - inside, inside)).reshape(-1)

    def starts_at(at):
        return jnp.max(jnp.where(starts[None, :] <= at[:, None], starts[None, :], 0), axis=1)

    row_start = starts_at(positions)
    tile = min(512, row_len)
    bounds = tile_bounds(starts_at(jnp.arange(row_len, dtype=jnp.int32)), tile)
    freq = jnp.exp(
        -math.log(10000.0) * 2.0 * jnp.arange(HEAD_DIM // 2, dtype=F32) / HEAD_DIM
    )
    angles = (positions - row_start).astype(F32)[:, None] * freq
    cosine, sine = jnp.cos(angles), jnp.sin(angles)
    cosine = plain(jnp.tile(cosine, (1, 4)))
    sine = plain(jnp.tile(jnp.concatenate([-sine, sine], axis=1), (1, 2)))
    pcol, prow, srow = positions[:, None], positions[None, :], row_start[None, :]
    chunk = jnp.arange(blocks, dtype=jnp.int32)
    chunk = jnp.where(chunk < cp_count, chunk, blocks - 1 - chunk)
    slot_of = (
        2 * (2 * ((chunk >> 1) ^ core) + ((chunk & 1) ^ parity))
        + (jnp.arange(blocks) >= cp_count)
    ).astype(jnp.int32)
    slot = jnp.arange(blocks, dtype=jnp.int32)
    relative = slot >> 1
    chunk_of = 2 * ((relative >> 1) ^ core) + ((relative & 1) ^ parity)
    block_of = jnp.where(slot & 1 == 0, chunk_of, blocks - 1 - chunk_of).astype(jnp.int32)

    x = after(x, sent, cosine, sine)
    x_chip = flip(x, "cp", 1)
    x_core = flip(x, "core", 1)
    up_lines, out_w, out_far = all_after((ffn[0], out_weight, out_far), x)
    up_far = flip(up_lines, "cp", 2)
    out_w = paired(out_w, out_far)
    out_far = flip(out_w, "cp", 1)

    qkv = placed(core == 0, mine, flip(other, "core", 1), 0)
    cut = qkv.shape[2] // 2
    low, high = qkv[:, :, :cut], qkv[:, :, cut:]
    low = placed(xy & 1 == 0, low, flip(low, "xy", 1), 0)
    high = placed(xy & 2 == 0, high, flip(high, "xy", 2), 0)
    low = placed(xy & 2 == 0, low, flip(low, "xy", 2), 0)
    high = placed(xy & 1 == 0, high, flip(high, "xy", 1), 1)
    qkv = jnp.concatenate([low[:, :, :, :lines], high[:, :, :, :lines]], axis=4)
    qkv = qkv.reshape(width, 3 * part)
    gains = low[:, :, :, lines : lines + cp_count, :128]
    gains = gains.reshape(4, width).astype(F32)

    sooner, later = jnp.array([0, 1, 4, 5], jnp.int32), jnp.array([2, 3, 6, 7], jnp.int32)
    early = project(x, x_core, gains, qkv, cosine, sine, block_of[sooner], sooner, [])
    x_chip, up_far, *early = lax.optimization_barrier((x_chip, up_far, *early))
    x_both = flip(x_chip, "core", 1)
    up_lines, up_far, down_lines, out_w, out_far = all_after(
        (up_lines, up_far, ffn[1], out_w, out_far), x_chip, qkv
    )
    up_lines, out_w = paired(up_lines, up_far), widened(z, out_w, out_far)[None]
    up_far = flip(up_lines, "cp", 1)
    down_far = flip(down_lines, "cp", 2)
    out_far = flip(out_w, "xy", 1)

    def halves(x):
        return x[None, :lines], x[None, lines:]

    def send_lines(low, high):
        return flip(low, "xy", 1), flip(high, "xy", 2)

    def join_lines(low, high, low_far, high_far):
        low = ordered(xy & 1 == 0, low, low_far, 0)
        high = jnp.expand_dims(ordered(xy & 2 == 0, high, high_far, 0), 1)
        return low, high

    def send_more(low, high):
        return flip(low, "xy", 2), flip(high, "xy", 1)

    def join_all(low, high, low_far, high_far):
        low = ordered(xy & 2 == 0, low, low_far, 0)
        high = ordered(xy & 1 == 0, high, high_far, 1).reshape(low.shape)
        return jnp.stack([low, high], axis=1).reshape(width, -1)

    q, k, v, normed = project(
        x_chip, x_both, gains, qkv, cosine, sine, block_of[later], later, early
    )
    up_lines, up_far, down_lines, down_far, out_w, out_far = all_after(
        (up_lines, up_far, down_lines, down_far, out_w, out_far), q
    )
    up_lines = widened(z, up_lines, up_far)
    up_full = lax.all_gather(up_lines, "xy", axis=0, tiled=True)
    out_w = ordered(xy & 1 == 0, out_w, out_far, 0)
    out_far = flip(out_w, "xy", 2)
    down_lines = paired(down_lines, down_far)
    down_far = flip(down_lines, "cp", 1)
    q = after(q, up_lines, out_w, down_lines)
    first = attend(0, q, k, v, pcol, prow, srow, bounds, slot_of, tile)
    down_lines, down_far, out_w, out_far = all_after(
        (down_lines, down_far, out_w, out_far), first[0]
    )
    out_w = ordered(xy & 2 == 0, out_w, out_far, 0)
    down_pair = halves(widened(z, down_lines, down_far))
    down_far = send_lines(*down_pair)
    q = after(q, first[0], *down_pair, out_w)
    second = attend(1, q, k, v, pcol, prow, srow, bounds, slot_of, tile)
    attended, local, lse = zip(first, second)
    local = jnp.concatenate(local, axis=2)
    out_w, down_pair, down_far = (
        after(out_w, local), all_after(down_pair, local), all_after(down_far, local)
    )
    out_w = placed(core == 0, out_w, flip(out_w, "core", 1), 1).reshape(width, width)
    down_pair = join_lines(*down_pair, *down_far)
    down_far = send_more(*down_pair)
    heads, branch_hat, branch_scale, hidden, mid = mix(
        group_at, after(local, *down_pair)[:2], flip(local[4:6], "core", 1), flip(local[2:4], "cp", 1),
        flip_both(local[6:]), out_w, x, gains,
    )

    cotangent = cotangent.reshape(own, width)
    dy_moved = swap(after(cotangent, mid))

    ffn_in = jnp.concatenate([mid, flip(mid, "core", 1)])
    act, slope = gelu_and_slope(dot(ffn_in, up_full, (1, 0)))
    down_full = join_all(*down_pair, *all_after(down_far, act))
    sent = flip(dot(act[own:], down_full, (1, 1)).astype(BF16), "core", 1)
    terms = dot(act[:own], down_full, (1, 1))
    stays = ((core == 1) == (z >= cp_count // 2)).astype(jnp.int32).reshape(1)
    mixed, grad_down, dy, gain_four = finish(
        stays, terms, sent, hidden, cotangent, dy_moved, gains
    )
    grad_down = jnp.concatenate([grad_down, flip(grad_down, "core", 1)])

    x_bit, y_bit = xy & 1, xy >> 1

    def send_first(away):
        return flip(away[0], "xy", 1), flip(away[1], "xy", 2)

    def cut_second(near, far):
        away = (
            total(pick(near[0], 1 - y_bit, 0), pick(far[0], 1 - y_bit, 0)),
            total(pick(near[1], 1 - x_bit, 0), pick(far[1], 1 - x_bit, 0)),
        )
        near = (
            total(pick(near[0], y_bit, 0), pick(far[0], y_bit, 0)),
            total(pick(near[1], x_bit, 0), pick(far[1], x_bit, 0)),
        )
        return near, away

    def send_second(away):
        return flip(away[0], "xy", 2), flip(away[1], "xy", 1)

    def cut_third(near, far):
        return split_columns(
            jnp.concatenate([total(a, b) for a, b in zip(near, far)]), hidden_part
        )

    def split_columns(sums, each):
        blocks_of = [sums[:, n * each : (n + 1) * each] for n in range(cp_count)]
        odd = jnp.stack([blocks_of[1], blocks_of[3]])
        even = jnp.stack([blocks_of[0], blocks_of[2]])
        return jnp.where(parity == 0, even, odd), jnp.where(parity == 0, odd, even)

    def cut_fourth(near, far):
        return (
            total(pick(near, z >> 1, 0), pick(far, z >> 1, 0)),
            total(pick(near, 1 - (z >> 1), 0), pick(far, 1 - (z >> 1), 0)),
        )

    down_local = plain(dot(grad_down, act, (0, 0)).astype(BF16))
    grad_up = dot(after(grad_down, down_local), down_full, (1, 0)) * slope.astype(F32)
    grad_up = grad_up.astype(BF16)
    sent = flip(dot(grad_up[own:], up_full, (1, 1)).astype(BF16), "core", 1)
    up_local = plain(dot(ffn_in, grad_up, (0, 0)).astype(BF16))
    spare = lines // 4
    place = jnp.stack([x_bit, y_bit]).astype(jnp.int32)
    low, low_away, high, high_away = cut_lines(place, up_local, down_local, spare)
    grad_near, grad_away = (low, high), (low_away, high_away)
    over_local = down_local.reshape(2 * xy_count, lines, -1)[:, lines - spare :]
    over_local = over_local.reshape(2 * xy_count * spare, -1)
    grad_far = send_first(grad_away)
    terms = dot(after(grad_up, *grad_away)[:own], up_full, (1, 1))
    grad_hidden, grad_branch, grad_heads, gain_three, gain_two = turn(
        group_at, terms, sent, hidden, dy, branch_hat, branch_scale, out_w, gains
    )

    grad_local = [
        grad_heads[0], flip(grad_heads[1], "cp", 1), flip(grad_heads[2], "core", 1),
        flip_both(grad_heads[3]),
    ]
    out_local = dot(after(heads, grad_heads), grad_branch, (0, 0)).astype(BF16)
    grad_local = plain(jnp.concatenate(grad_local))
    out_away = pick(out_local.reshape(xy_count, 2, lines, width), 1 - core, 1)
    out_away, over_local, mixed, grad_local = lax.optimization_barrier(
        (out_away, over_local, mixed, grad_local)
    )
    over_near, over_away = split_columns(over_local, hidden_part)
    over_far = flip(over_away, "cp", 1)
    mixed_moved = swap(mixed)
    grad_local = after(grad_local, over_away)

    def back_to_tokens(grads):
        two = 2 * span
        rows = grads.reshape(4 * span, 3 * part)
        send = dot(rows[two:], qkv, (1, 1)).astype(BF16)
        sent = flip(send, "core", 1)
        rows = after(rows, send)
        far_away = total(dot(rows[span:two], qkv, (1, 1)), sent[span:])
        kept = dot(after(rows, far_away)[:span], qkv, (1, 1)) + sent[:span].astype(F32)
        return send, far_away, flip(far_away, "cp", 1), kept

    tables = (pcol, prow, srow, cosine, sine, bounds, slot_of, tile)
    attended, lse = jnp.concatenate(attended, axis=1), jnp.concatenate(lse, axis=0)
    first, unfinished = attend_back(0, q, k, v, grad_local, attended, lse, *tables, [])
    first, mixed_moved, over_far, *grad_far = lax.optimization_barrier(
        (first, mixed_moved, over_far, *grad_far)
    )
    over_near, over_away = cut_fourth(over_near, over_far)
    over_far = flip(over_away, "cp", 2)
    _, far_away, far_back, kept = back_to_tokens(after(first, over_away))
    grad_near, grad_away = cut_second(grad_near, all_after(grad_far, far_away))
    grad_far = send_second(grad_away)
    out_far = flip(after(out_away, far_away), "core", 1)
    second = attend_back(
        1, q, k, v, after(grad_local, first, *grad_away, over_away, kept), attended, lse, *tables,
        [unfinished],
    )[0]
    second, over_far, out_far, *grad_far = lax.optimization_barrier(
        (second, over_far, out_far, *grad_far)
    )

    ended = end(kept, after(far_back, second), x[0], grad_hidden[:span], gains)
    moved = swap(ended)
    second = after(second, ended)
    send, far_away, far, kept = back_to_tokens(second)
    qkv_local = sum(
        dot(normed[4 * h : 4 * h + 4].reshape(4 * span, width), g.reshape(4 * span, -1), (0, 0))
        for h, g in enumerate((first, after(second, send)))
    ).astype(BF16)
    gain_one = jnp.sum(qkv_local.astype(F32) * qkv.astype(F32), axis=1) / gains[0]
    gain_sum = jnp.concatenate([gain_one[None], gain_two, gain_three, gain_four])
    gain_sum = gain_sum.reshape(2 * xy_count, cp_count, 128).astype(BF16)
    place = jnp.stack([x_bit, y_bit, core, parity, z >> 1]).astype(jnp.int32)
    locals_ = (qkv_local, out_local, gain_sum)
    rest_away = jnp.concatenate(
        [
            pick(qkv_local.reshape(xy_count, 2, lines, 3 * part), 1 - core, 1),
            jnp.pad(
                pick(gain_sum.reshape(xy_count, 2, cp_count, 128), 1 - core, 1),
                ((0, 0), (0, lines - cp_count), (0, 0)),
            ),
        ],
        axis=2,
    )
    rest_far = flip(rest_away, "core", 1)

    over = total(over_near, over_far)
    rest_far, over = all_after((rest_far, over), kept)
    low, low_away, high, high_away = spread_first(place, *locals_, over, rest_far, out_far)
    rest_far = flip(low_away, "xy", 1), flip(high_away, "xy", 2)
    low, low_away, high, high_away = spread_second(place, low, rest_far[0], high, rest_far[1])
    rest_far = flip(low_away, "xy", 2), flip(high_away, "xy", 1)
    grad_near, grad_away = cut_third(grad_near, all_after(grad_far, low_away))
    grad_far = flip(grad_away, "cp", 1)
    ended_last = end(
        kept, after(far, moved, low_away, high_away), x[1], grad_hidden[span:], gains
    )
    moved_last = swap(ended_last)
    rest_far = all_after(rest_far, moved_last)
    rest, rest_away, over = spread_third(place, low, rest_far[0], high, rest_far[1])
    grad_near, grad_away = cut_fourth(grad_near, after(grad_far, rest_away))
    grad_far = flip(grad_away, "cp", 2)
    gather_away = rest_away
    rest, rest_away = spread_fourth(place, rest, flip(rest_away, "cp", 2))
    moved_last = after(moved_last, rest_away)
    qkv_grad, out_grad, gains_grad = spread_fifth(place, rest, flip(rest_away, "cp", 1))
    gains_grad = gains_grad.reshape(-1)
    tokens_grad = jnp.stack([settled(ended, moved), settled(ended_last, moved_last)])
    tokens_grad = tokens_grad.astype(F32).reshape(tokens.shape)
    mixed = settled(after(mixed, gather_away), mixed_moved).reshape(tokens.shape)

    both = total(grad_near, after(grad_far, gather_away))
    both = plain(both).reshape(2, 2 * lines - spare, hidden_part)
    over = [
        jnp.concatenate([block[n * spare : (n + 1) * spare] for n in range(4)], axis=1)
        for block in over
    ]
    both = jnp.concatenate([both, jnp.stack(over)], axis=1).reshape(2, 2, lines, hidden_part)
    mine, other = pick(both, core, 0), flip(pick(both, 1 - core, 0), "core", 1)
    up_grad = ordered(core == 0, mine[0], other[0], 1).astype(F32)
    down_grad = ordered(core == 0, mine[1], other[1], 1).T.astype(F32)
    return mixed, tokens_grad, qkv_grad, out_grad, up_grad, down_grad, gains_grad


def solution(mesh):
    rows, cp = mesh.shape["rows"], mesh.shape["cp"]
    if (rows, cp) == (8, 4):
        grid = Mesh(mesh.devices.reshape(rows // 2, 2, cp), ("xy", "core", "cp"))
        run, lines = body, ("xy", "core")
    else:
        grid, run, lines = mesh, general_body, ("rows",)
    tokens = P(lines, None, "cp", None)
    weight, down, gains = P(lines, "cp"), P("cp", lines), P(lines + ("cp",))
    return jax.shard_map(
        run,
        mesh=grid,
        in_specs=(tokens, P(lines, None), weight, weight, weight, down, gains, tokens),
        out_specs=(tokens, tokens, weight, weight, weight, down, gains),
        check_vma=False,
    )
```
